32 devices in a mesh: seq: 8 (over y, x, core), hid: 4 (over z).
Axes of the slice: x: 2, y: 2, z: 4, core: 2. Of those that a mesh axis runs over, the one named last changes fastest.
Arguments:
- hidden: bfloat16 [2048, 4096], P('seq', 'hid'), may hold values from -6 to 6
- w_in: bfloat16 [2, 4096, 1024], P(None, 'hid'), may hold values from -0.09863281 to 0.09863281
- embedding: bfloat16 [1, 2048, 1024], replicated, may hold values from -6 to 6
- depth_gain: float32 [2, 1024], replicated, may hold values from 0.25 to 1.75
- w_out: bfloat16 [1024, 2, 2048], P(('seq', 'hid')), may hold values from -0.43554688 to 0.43554688
- codebook_ids: int32 [2, 2048], P(None, ('seq', 'hid')), may hold values from 0 to 2047
Outputs:
- grad_hidden: bfloat16 [2048, 4096], P('seq', 'hid')
- grad_in: float32 [2, 4096, 1024], P(None, 'hid', 'seq')
- grad_out: float32 [1024, 2, 2048], P(('seq', 'hid'))
The draws below stay inside these ranges and needn't reach their ends.
All inputs are finite; a program needn't handle non-finite values.
Results may differ from the reference program's by a relative error of at most 0.01.
Values may be sent and summed in bfloat16 or wider, within the bound.
No kernel may reach another device: no remote copies, remote signals or barrier semaphores. Data moves between devices by JAX's collectives and lax.ppermute only.
A program may use at most 128 MiB of HBM per device.

```python
import jax
import jax.numpy as jnp
from jax import lax

DT = 4096
DD = 1024
CARD = 2048
STEPS = 2
FRAMES = 2048


def draw_hidden(key, part):
    values = jnp.clip(jax.random.normal(jax.random.fold_in(key, 11), (FRAMES, DT), jnp.float32), -6.0, 6.0)
    return values.astype(jnp.bfloat16)


def draw_w_in(key, part):
    values = jnp.clip(jax.random.normal(jax.random.fold_in(key, 21), (STEPS, DT, DD), jnp.float32), -6.0, 6.0) * DT ** (-0.5)
    return values.astype(jnp.bfloat16)


def draw_embedding(key, part):
    values = jnp.clip(jax.random.normal(jax.random.fold_in(key, 41), (STEPS - 1, CARD, DD), jnp.float32), -6.0, 6.0)
    return values.astype(jnp.bfloat16)


def draw_w_out(key, part):
    values = jnp.clip(jax.random.normal(jax.random.fold_in(key, 31), (DD, STEPS, CARD), jnp.float32), -6.0, 6.0) * DD ** (-0.5)
    return values.astype(jnp.bfloat16)


def touch_ends(values, stream_key, smallest, top_value):
    longest = values.shape.index(max(values.shape))
    spots = []
    for shift in (0, 1):
        where = [jax.random.randint(jax.random.fold_in(stream_key, axis), (), 0, length) for axis, length in enumerate(values.shape)]
        where[longest] = (where[longest] + shift) % values.shape[longest]
        spots.append(tuple(where))
    return values.at[spots[0]].set(smallest).at[spots[1]].set(top_value)


def setup_inputs(seed: int = 0) -> dict:
    seeds = jax.random.split(jax.random.key(seed), 7)
    return {
        "hidden": draw_hidden(jax.random.fold_in(seeds[6], 71), 0),
        "w_in": draw_w_in(jax.random.fold_in(seeds[6], 71), 0),
        "embedding": draw_embedding(jax.random.fold_in(seeds[6], 71), 0),
        "depth_gain": jnp.clip(1.0 + 0.15 * jax.random.normal(seeds[3], (STEPS, DD), jnp.float32), 0.25, 1.75),
        "w_out": draw_w_out(jax.random.fold_in(seeds[6], 71), 0),
        "codebook_ids": touch_ends(jax.random.randint(seeds[5], (STEPS, FRAMES), 0, CARD), jax.random.fold_in(seeds[5], 1), 0, CARD - 1).astype(jnp.int32),
    }


def reference(hidden, w_in, embedding, depth_gain, w_out, codebook_ids):
    hidden_f = hidden.astype(jnp.float32)
    squares = lax.optimization_barrier(jnp.sum(hidden_f * hidden_f, axis=1))
    ratio = lax.rsqrt(squares / DT + 1e-06)
    proj = jnp.einsum('fd,kde->fke', hidden_f, w_in.astype(jnp.float32))
    x_rows = ratio[:, None, None] * proj
    for step in range(1, STEPS):
        looked = jnp.take(embedding[step - 1], codebook_ids[step - 1], axis=0).astype(jnp.float32)
        x_rows = x_rows.at[:, step].add(looked)
    scale = lax.rsqrt(lax.optimization_barrier(jnp.mean(x_rows * x_rows, axis=2, keepdims=True)) + 1e-06)
    normed = (x_rows * scale * depth_gain[None]).astype(jnp.bfloat16)
    logits = jnp.einsum('fkd,dkc->fkc', normed.astype(jnp.float32), w_out.astype(jnp.float32))
    targets = codebook_ids.T
    lse = jax.nn.logsumexp(logits, axis=2)
    onehot = (targets[:, :, None] == jnp.arange(CARD, dtype=jnp.int32)[None, None, :]).astype(jnp.float32)
    loss_weight = 2.0 * CARD / FRAMES
    d_logit = ((jnp.exp(logits - lse[:, :, None]) - onehot) * loss_weight).astype(jnp.bfloat16)
    grad_out = jnp.einsum('fkd,fkc->dkc', normed.astype(jnp.float32), d_logit.astype(jnp.float32))
    d_norm = jnp.einsum('fkc,dkc->fkd', d_logit.astype(jnp.float32), w_out.astype(jnp.float32))
    gated = depth_gain[None] * d_norm
    d_x = scale * gated - x_rows * scale ** 3 * lax.optimization_barrier(jnp.mean(gated * x_rows, axis=2, keepdims=True))
    d_round = d_x.astype(jnp.bfloat16)
    d_ratio = lax.optimization_barrier(jnp.sum(d_x * proj, axis=(1, 2)))
    scaled = (ratio[:, None, None] * d_round.astype(jnp.float32)).astype(jnp.bfloat16)
    grad_in = jnp.einsum('fd,fke->kde', hidden_f, scaled.astype(jnp.float32))
    back = jnp.einsum('fke,kde->fd', d_round.astype(jnp.float32), w_in.astype(jnp.float32))
    grad_hidden = (ratio[:, None] * back - (ratio ** 3 * d_ratio / DT)[:, None] * hidden_f).astype(jnp.bfloat16)
    return (grad_hidden, grad_in, grad_out)
```

```python
import jax
import jax.numpy as jnp
from jax import lax
from jax.sharding import PartitionSpec as P

F32 = jnp.float32
BF16 = jnp.bfloat16


def pick(values, index):
    return lax.dynamic_index_in_dim(values, index, axis=0, keepdims=False)


def matmul(a, b, contract):
    return lax.dot_general(a, b, (contract, ((), ())), preferred_element_type=F32)


def shards(hidden, w_in, embedding, depth_gain, w_out, codebook_ids):
    hids = lax.axis_size("hid")
    seqs = lax.axis_size("seq")
    steps, units, depth = w_in.shape
    entries = w_out.shape[2]
    rows = hidden.shape[0]
    part = rows // hids
    width_in = units * hids
    frames = rows * seqs
    halves = 2 if hids % 2 == 0 else 1
    block = entries // halves
    head_rows = w_out.shape[0]
    i = lax.axis_index("seq")
    j = lax.axis_index("hid")
    step = i % steps
    first = i - step
    half = j % halves

    def along_hid(values, shift):
        return lax.ppermute(values, "hid", [(a, (a + shift) % hids) for a in range(hids)])

    def turn_hid(values, shift):
        return lax.ppermute(
            values,
            "hid",
            [(a, a - a % halves + (a % halves + shift) % halves) for a in range(hids)],
        )

    def both(values, flip, shift):
        pairs = []
        for a in range(seqs):
            to = a - a % steps + (a % steps + flip) % steps
            for b in range(hids):
                pairs.append((a * hids + b, to * hids + (b + shift) % hids))
        return lax.ppermute(values, ("seq", "hid"), pairs)

    def flip_seq(values, flip):
        return lax.ppermute(
            values,
            "seq",
            [(a, a - a % steps + (a % steps + flip) % steps) for a in range(seqs)],
        )

    group = [hidden] + [flip_seq(hidden, -r) for r in range(1, steps)]

    squares_part = jnp.sum(jnp.square(hidden.astype(F32)), axis=1)
    small = jnp.concatenate([codebook_ids.reshape(-1).astype(F32), squares_part])
    small_all = lax.all_gather(small, ("seq", "hid"), axis=0).reshape(seqs, hids, -1)
    ids_all = small_all[:, :, : steps * part].astype(jnp.int32).reshape(seqs, hids, steps, part)
    squares = jnp.sum(small_all[:, :, steps * part :], axis=1)
    ratio_all = lax.rsqrt(squares / width_in + 1e-06)
    members = [first + (step + r) % steps for r in range(steps)]
    ratio_group = [pick(ratio_all, m) for m in members]

    head_parts = w_out.reshape(head_rows, steps, halves, block)
    head_send = jnp.stack([head_parts[:, :, b % halves] for b in range(hids)])
    head_mid = lax.all_to_all(head_send, "hid", 0, 0).reshape(hids * head_rows, steps, block)
    head_send = jnp.stack([head_mid[:, a % steps] for a in range(seqs)])
    head = lax.all_to_all(head_send, "seq", 0, 0).reshape(depth, block)

    w_own = pick(w_in, step)
    proj_parts = [matmul(h, w_own, ((1,), (0,))) for h in group]

    def owner_block(index):
        return jnp.concatenate(
            [lax.dynamic_slice_in_dim(p, index * part, part, 0) for p in proj_parts]
        )

    proj = owner_block(j)
    for shift in range(1, hids):
        proj += along_hid(owner_block((j + shift) % hids).astype(BF16), shift).astype(F32)

    ratio = jnp.concatenate([lax.dynamic_slice_in_dim(r, j * part, part, 0) for r in ratio_group])
    before = jnp.maximum(step - 1, 0)
    table = pick(embedding, before)
    ids_before = jnp.concatenate([pick(pick(pick(ids_all, m), j), before) for m in members])
    looked = jnp.take(table, ids_before, axis=0).astype(F32)
    x_rows = ratio[:, None] * proj + jnp.where(step > 0, looked, 0.0)
    scale = lax.rsqrt(jnp.mean(x_rows * x_rows, axis=1, keepdims=True) + 1e-06)
    gain = pick(depth_gain, step)[None, :]
    normed = (x_rows * scale * gain).astype(BF16)

    owners = [j - half + (half + k) % halves for k in range(halves)]
    normed_rows = jnp.concatenate([normed] + [turn_hid(normed, -k) for k in range(1, halves)])
    targets = jnp.concatenate([pick(pick(pick(ids_all, m), o), step) for o in owners for m in members])
    logits = matmul(normed_rows, head, ((1,), (0,)))
    top = jnp.max(logits, axis=1)
    total = jnp.sum(jnp.exp(logits - top[:, None]), axis=1)
    stats = jnp.stack([top, total]).reshape(2, halves, -1)
    every = [stats] + [jnp.roll(turn_hid(stats, -t), t, axis=1) for t in range(1, halves)]
    tops = jnp.stack([e[0] for e in every]).reshape(halves, -1)
    totals = jnp.stack([e[1] for e in every]).reshape(halves, -1)
    top_all = jnp.max(tops, axis=0)
    lse = top_all + jnp.log(jnp.sum(totals * jnp.exp(tops - top_all), axis=0))
    entry = lax.broadcasted_iota(jnp.int32, logits.shape, 1) + half * block
    onehot = (targets[:, None] == entry).astype(F32)
    loss_weight = 2.0 * entries / frames
    d_logit = ((jnp.exp(logits - lse[:, None]) - onehot) * loss_weight).astype(BF16)

    owned = steps * part
    d_norm_rows = matmul(d_logit, head, ((1,), (1,)))
    d_norm = d_norm_rows[:owned]
    for k in range(1, halves):
        d_norm += turn_hid(d_norm_rows[k * owned : (k + 1) * owned].astype(BF16), k).astype(F32)

    gated = gain * d_norm
    d_x = scale * gated - x_rows * scale**3 * jnp.mean(gated * x_rows, axis=1, keepdims=True)
    d_round = d_x.astype(BF16)
    d_ratio_part = jnp.sum(d_x * proj, axis=1)
    d_ratio_all = lax.all_gather(d_ratio_part, ("seq", "hid"), axis=0).reshape(seqs, hids, steps, part)

    back_rows = jnp.zeros((steps, hids, part, depth), BF16)
    for r in range(steps):
        for shift in range(hids):
            piece = d_round[r * part : (r + 1) * part]
            if r or shift:
                piece = both(piece, r, shift)
            back_rows = lax.dynamic_update_slice(
                back_rows, piece[None, None], ((step - r) % steps, (j - shift) % hids, 0, 0)
            )
    back_rows = back_rows.reshape(steps, rows, depth)
    ratio_own = ratio_group[0]
    d_ratio = jnp.zeros((hids, part), F32)
    for r in range(steps):
        d_ratio += pick(d_ratio_all, first + (step - r) % steps)[:, r]
    correction = ratio_own**3 * d_ratio.reshape(rows) / width_in
    back = matmul(back_rows[0], w_in[0], ((1,), (1,)))
    for s in range(1, steps):
        back += matmul(back_rows[s], w_in[s], ((1,), (1,)))
    grad_hidden = (ratio_own[:, None] * back - correction[:, None] * hidden.astype(F32)).astype(BF16)

    hidden_all = lax.all_gather(hidden, "seq", axis=0, tiled=True)
    scaled = (ratio_own[None, :, None] * back_rows.astype(F32)).astype(BF16)
    scaled = scaled.reshape(steps, rows, seqs, depth // seqs).transpose(2, 0, 1, 3)
    scaled = lax.all_to_all(scaled, "seq", 0, 0)
    scaled = scaled.transpose(1, 0, 2, 3).reshape(steps, frames, depth // seqs)
    grad_in = jnp.stack([matmul(hidden_all, scaled[s], ((0,), (0,))) for s in range(steps)])

    part_out = matmul(normed_rows, d_logit, ((0,), (0,))).astype(BF16)
    part_out = lax.all_to_all(part_out.reshape(seqs, depth // seqs, block), "seq", 0, 0)
    part_out = part_out.reshape(seqs // steps, steps, hids, head_rows, block).astype(F32).sum(0)
    part_out = part_out.transpose(1, 0, 2, 3).astype(BF16)
    part_out = lax.all_to_all(part_out, "hid", 0, 0)
    part_out = part_out.reshape(hids // halves, halves, steps, head_rows, block).astype(F32).sum(0)
    grad_out = part_out.transpose(2, 1, 0, 3).reshape(head_rows, steps, entries)
    return (grad_hidden, grad_in, grad_out)


def solution(mesh):
    placed = (
        P("seq", "hid"),
        P(None, "hid", None),
        P(),
        P(),
        P(("seq", "hid"), None, None),
        P(None, ("seq", "hid")),
    )
    return jax.shard_map(
        shards,
        mesh=mesh,
        in_specs=placed,
        out_specs=(P("seq", "hid"), P(None, "hid", "seq"), P(("seq", "hid"), None, None)),
        check_vma=False,
    )
```

```python
import jax
import jax.numpy as jnp
from jax import lax
from jax.sharding import PartitionSpec as P

F32 = jnp.float32
BF16 = jnp.bfloat16


def pick(values, index):
    return lax.dynamic_index_in_dim(values, index, axis=0, keepdims=False)


def matmul(a, b, contract):
    return lax.dot_general(a, b, (contract, ((), ())), preferred_element_type=F32)


def shards(hidden, w_in, embedding, depth_gain, w_out, codebook_ids):
    hids = lax.axis_size("hid")
    seqs = lax.axis_size("seq")
    steps, units, depth = w_in.shape
    entries = w_out.shape[2]
    rows = hidden.shape[0]
    part = rows // hids
    width_in = units * hids
    frames = rows * seqs
    halves = 2 if hids % 2 == 0 else 1
    block = entries // halves
    head_rows = w_out.shape[0]
    i = lax.axis_index("seq")
    j = lax.axis_index("hid")
    step = i % steps
    half = j % halves

    def along_hid(values, shift):
        return lax.ppermute(values, "hid", [(a, (a + shift) % hids) for a in range(hids)])

    def turn_hid(values, shift):
        return lax.ppermute(
            values,
            "hid",
            [(a, a - a % halves + (a % halves + shift) % halves) for a in range(hids)],
        )

    def both(values, flip, shift):
        pairs = []
        for a in range(seqs):
            to = a - a % steps + (a % steps + flip) % steps
            for b in range(hids):
                pairs.append((a * hids + b, to * hids + (b + shift) % hids))
        return lax.ppermute(values, ("seq", "hid"), pairs)

    def flip_seq(values, flip):
        return lax.ppermute(
            values,
            "seq",
            [(a, a - a % steps + (a % steps + flip) % steps) for a in range(seqs)],
        )

    group = [hidden] + [flip_seq(hidden, -r) for r in range(1, steps)]

    squares_part = jnp.sum(jnp.square(hidden.astype(F32)), axis=1)
    small = jnp.concatenate([codebook_ids.reshape(-1).astype(F32), squares_part])
    small = jnp.stack([small] + [flip_seq(small, -r) for r in range(1, steps)])
    small = lax.all_to_all(jnp.broadcast_to(small, (hids,) + small.shape), "hid", 0, 0)
    ids_group = small[:, :, : steps * part].astype(jnp.int32).reshape(hids, steps, steps, part)
    squares = jnp.sum(small[:, :, steps * part :], axis=0)
    ratio_group = lax.rsqrt(squares / width_in + 1e-06)

    head_send = w_out.reshape(head_rows, steps, halves, block).transpose(2, 1, 0, 3)
    head_send = jnp.broadcast_to(head_send, (hids // halves,) + head_send.shape)
    head_send = head_send.reshape(hids, steps, head_rows, block)
    head_mid = lax.all_to_all(head_send, "hid", 0, 0).transpose(1, 0, 2, 3)
    head_send = head_mid.reshape(steps, hids * head_rows, block)
    head_send = jnp.broadcast_to(head_send, (seqs // steps,) + head_send.shape)
    head_send = head_send.reshape(seqs, hids * head_rows, block)
    head = lax.all_to_all(head_send, "seq", 0, 0).reshape(depth, block)

    w_own = pick(w_in, step)
    proj_parts = [matmul(h, w_own, ((1,), (0,))) for h in group]

    def owner_block(index):
        return jnp.concatenate(
            [lax.dynamic_slice_in_dim(p, index * part, part, 0) for p in proj_parts]
        )

    proj = owner_block(j)
    for shift in range(1, hids):
        proj += along_hid(owner_block((j + shift) % hids).astype(BF16), shift).astype(F32)

    ratio = jnp.concatenate([lax.dynamic_slice_in_dim(r, j * part, part, 0) for r in ratio_group])
    before = jnp.maximum(step - 1, 0)
    table = pick(embedding, before)
    ids_before = pick(pick(ids_group, j).transpose(1, 0, 2), before).reshape(-1)
    looked = jnp.take(table, ids_before, axis=0).astype(F32)
    x_rows = ratio[:, None] * proj + jnp.where(step > 0, looked, 0.0)
    scale = lax.rsqrt(jnp.mean(x_rows * x_rows, axis=1, keepdims=True) + 1e-06)
    gain = pick(depth_gain, step)[None, :]
    normed = (x_rows * scale * gain).astype(BF16)

    owners = [j - half + (half + k) % halves for k in range(halves)]
    normed_rows = jnp.concatenate([normed] + [turn_hid(normed, -k) for k in range(1, halves)])
    targets = jnp.concatenate(
        [pick(pick(ids_group, o).transpose(1, 0, 2), step).reshape(-1) for o in owners]
    )
    logits = matmul(normed_rows, head, ((1,), (0,)))
    top = jnp.max(logits, axis=1)
    total = jnp.sum(jnp.exp(logits - top[:, None]), axis=1)
    stats = jnp.stack([top, total]).reshape(2, halves, -1)
    every = [stats] + [jnp.roll(turn_hid(stats, -t), t, axis=1) for t in range(1, halves)]
    tops = jnp.stack([e[0] for e in every]).reshape(halves, -1)
    totals = jnp.stack([e[1] for e in every]).reshape(halves, -1)
    top_all = jnp.max(tops, axis=0)
    lse = top_all + jnp.log(jnp.sum(totals * jnp.exp(tops - top_all), axis=0))
    entry = lax.broadcasted_iota(jnp.int32, logits.shape, 1) + half * block
    onehot = (targets[:, None] == entry).astype(F32)
    loss_weight = 2.0 * entries / frames
    d_logit = ((jnp.exp(logits - lse[:, None]) - onehot) * loss_weight).astype(BF16)

    owned = steps * part
    d_norm_rows = matmul(d_logit, head, ((1,), (1,)))
    d_norm = d_norm_rows[:owned]
    for k in range(1, halves):
        d_norm += turn_hid(d_norm_rows[k * owned : (k + 1) * owned].astype(BF16), k).astype(F32)

    gated = gain * d_norm
    d_x = scale * gated - x_rows * scale**3 * jnp.mean(gated * x_rows, axis=1, keepdims=True)
    d_round = d_x.astype(BF16)
    d_ratio_part = jnp.sum(d_x * proj, axis=1)
    d_ratio = d_ratio_part[:part]
    for r in range(1, steps):
        d_ratio += flip_seq(d_ratio_part[r * part : (r + 1) * part], r)
    d_ratio = lax.all_to_all(jnp.broadcast_to(d_ratio, (hids, part)), "hid", 0, 0).reshape(rows)

    back_rows = jnp.zeros((steps, hids, part, depth), BF16)
    for r in range(steps):
        for shift in range(hids):
            piece = d_round[r * part : (r + 1) * part]
            if r or shift:
                piece = both(piece, r, shift)
            back_rows = lax.dynamic_update_slice(
                back_rows, piece[None, None], ((step - r) % steps, (j - shift) % hids, 0, 0)
            )
    back_rows = back_rows.reshape(steps, rows, depth)
    ratio_own = ratio_group[0]
    correction = ratio_own**3 * d_ratio / width_in
    back = matmul(back_rows[0], w_in[0], ((1,), (1,)))
    for s in range(1, steps):
        back += matmul(back_rows[s], w_in[s], ((1,), (1,)))
    grad_hidden = (ratio_own[:, None] * back - correction[:, None] * hidden.astype(F32)).astype(BF16)

    hidden_all = lax.all_gather(hidden, "seq", axis=0, tiled=True)
    scaled = (ratio_own[None, :, None] * back_rows.astype(F32)).astype(BF16)
    scaled = scaled.reshape(steps, rows, seqs, depth // seqs).transpose(2, 0, 1, 3)
    scaled = lax.all_to_all(scaled, "seq", 0, 0)
    scaled = scaled.transpose(1, 0, 2, 3).reshape(steps, frames, depth // seqs)
    grad_in = jnp.stack([matmul(hidden_all, scaled[s], ((0,), (0,))) for s in range(steps)])

    part_out = matmul(normed_rows, d_logit, ((0,), (0,))).astype(BF16)
    part_out = lax.all_to_all(part_out.reshape(seqs, depth // seqs, block), "seq", 0, 0)
    part_out = part_out.reshape(seqs // steps, steps, hids, head_rows, block).astype(F32).sum(0)
    part_out = part_out.transpose(1, 0, 2, 3).astype(BF16)
    part_out = lax.all_to_all(part_out, "hid", 0, 0)
    part_out = part_out.reshape(hids // halves, halves, steps, head_rows, block).astype(F32).sum(0)
    grad_out = part_out.transpose(2, 1, 0, 3).reshape(head_rows, steps, entries)
    return (grad_hidden, grad_in, grad_out)


def solution(mesh):
    placed = (
        P("seq", "hid"),
        P(None, "hid", None),
        P(),
        P(),
        P(("seq", "hid"), None, None),
        P(None, ("seq", "hid")),
    )
    return jax.shard_map(
        shards,
        mesh=mesh,
        in_specs=placed,
        out_specs=(P("seq", "hid"), P(None, "hid", "seq"), P(("seq", "hid"), None, None)),
        check_vma=False,
    )
```

```python
import jax
import jax.numpy as jnp
from jax import lax
from jax.sharding import PartitionSpec as P

F32 = jnp.float32
BF16 = jnp.bfloat16


def pick(values, index):
    return lax.dynamic_index_in_dim(values, index, axis=0, keepdims=False)


def matmul(a, b, contract):
    return lax.dot_general(a, b, (contract, ((), ())), preferred_element_type=F32)


def shards(hidden, w_in, embedding, depth_gain, w_out, codebook_ids):
    hids = lax.axis_size("hid")
    seqs = lax.axis_size("seq")
    steps, units, depth = w_in.shape
    entries = w_out.shape[2]
    rows = hidden.shape[0]
    part = rows // hids
    width_in = units * hids
    frames = rows * seqs
    halves = 2 if hids % 2 == 0 else 1
    block = entries // halves
    head_rows = w_out.shape[0]
    groups = seqs // steps
    i = lax.axis_index("seq")
    j = lax.axis_index("hid")
    step = i % steps
    half = j % halves

    def along_hid(values, shift):
        return lax.ppermute(values, "hid", [(a, (a + shift) % hids) for a in range(hids)])

    def turn_hid(values, shift):
        return lax.ppermute(
            values,
            "hid",
            [(a, a - a % halves + (a % halves + shift) % halves) for a in range(hids)],
        )

    def flip_seq(values, flip):
        return lax.ppermute(
            values,
            "seq",
            [(a, a - a % steps + (a % steps + flip) % steps) for a in range(seqs)],
        )

    def gather_flips(values, position):
        out = jnp.broadcast_to(values, (steps,) + values.shape)
        for r in range(1, steps):
            out = lax.dynamic_update_index_in_dim(
                out, flip_seq(values, -r), (position + r) % steps, 0
            )
        return out

    def gather_hid(values):
        out = jnp.broadcast_to(values, (hids,) + values.shape)
        for shift in range(1, hids):
            out = lax.dynamic_update_index_in_dim(
                out, along_hid(values, shift), (j - shift) % hids, 0
            )
        return out

    head_send = w_out.reshape(head_rows, steps, halves, block).transpose(2, 1, 0, 3)
    head_send = jnp.broadcast_to(head_send, (hids // halves,) + head_send.shape)
    head_send = head_send.reshape(hids, steps, head_rows, block)
    head_mid = lax.all_to_all(head_send, "hid", 0, 0).transpose(1, 0, 2, 3)

    same = [[g * steps + s for g in range(groups)] for s in range(steps)]
    hidden_part = lax.all_gather(hidden, "seq", axis=0, axis_index_groups=same)

    pair = gather_flips(hidden, step)
    w_own = pick(w_in, step)
    proj_parts = matmul(pair.reshape(steps * rows, units), w_own, ((1,), (0,)))
    proj_parts = proj_parts.reshape(steps, hids, part, depth)
    owned = steps * part

    def owner_block(index):
        return lax.dynamic_index_in_dim(proj_parts, index, 1, False).reshape(owned, depth)

    send = [owner_block((j + shift) % hids).astype(BF16) for shift in range(1, hids)]
    proj = owner_block(j)

    squares_part = jnp.sum(jnp.square(hidden.astype(F32)), axis=1)
    small = jnp.concatenate([codebook_ids.reshape(-1).astype(F32), squares_part])
    small = gather_flips(small, step)
    *send, head_mid, small = lax.optimization_barrier((*send, head_mid, small))
    for shift in range(1, hids):
        proj += along_hid(send[shift - 1], shift).astype(F32)
    small = gather_hid(small)
    ids_group = small[:, :, : steps * part].astype(jnp.int32).reshape(hids, steps, steps, part)
    squares = jnp.sum(small[:, :, steps * part :], axis=0)
    ratio_group = lax.rsqrt(squares / width_in + 1e-06).reshape(steps, hids, part)
    ratio_own = pick(ratio_group, step).reshape(rows)

    head_send = head_mid.reshape(steps, hids * head_rows, block)
    head_send = jnp.broadcast_to(head_send, (groups,) + head_send.shape)
    head_send = head_send.reshape(seqs, hids * head_rows, block)
    head = lax.all_to_all(head_send, "seq", 0, 0).reshape(depth, block)

    ratio = lax.dynamic_index_in_dim(ratio_group, j, 1, False).reshape(owned)
    before = jnp.maximum(step - 1, 0)
    table = pick(embedding, before)
    ids_before = pick(pick(ids_group, j).transpose(1, 0, 2), before).reshape(-1)
    looked = jnp.take(table, ids_before, axis=0).astype(F32)
    x_rows = ratio[:, None] * proj + jnp.where(step > 0, looked, 0.0)
    scale = lax.rsqrt(jnp.mean(x_rows * x_rows, axis=1, keepdims=True) + 1e-06)
    gain = pick(depth_gain, step)[None, :]
    normed = (x_rows * scale * gain).astype(BF16)

    owners = [j - half + (half + k) % halves for k in range(halves)]
    normed_rows = jnp.concatenate([normed] + [turn_hid(normed, -k) for k in range(1, halves)])
    targets = jnp.concatenate(
        [pick(pick(ids_group, o).transpose(1, 0, 2), step).reshape(-1) for o in owners]
    )
    logits = matmul(normed_rows, head, ((1,), (0,)))
    top = jnp.max(logits, axis=1)
    total = jnp.sum(jnp.exp(logits - top[:, None]), axis=1)
    stats = jnp.stack([top, total]).reshape(2, halves, -1)
    every = [stats] + [jnp.roll(turn_hid(stats, -t), t, axis=1) for t in range(1, halves)]
    tops = jnp.stack([e[0] for e in every]).reshape(halves, -1)
    totals = jnp.stack([e[1] for e in every]).reshape(halves, -1)
    top_all = jnp.max(tops, axis=0)
    lse = top_all + jnp.log(jnp.sum(totals * jnp.exp(tops - top_all), axis=0))
    entry = lax.broadcasted_iota(jnp.int32, logits.shape, 1) + half * block
    onehot = (targets[:, None] == entry).astype(F32)
    loss_weight = 2.0 * entries / frames
    d_logit = ((jnp.exp(logits - lse[:, None]) - onehot) * loss_weight).astype(BF16)

    d_norm_rows = matmul(d_logit, head, ((1,), (1,)))
    d_norm = d_norm_rows[:owned]
    for k in range(1, halves):
        d_norm += turn_hid(d_norm_rows[k * owned : (k + 1) * owned].astype(BF16), k).astype(F32)

    gated = gain * d_norm
    d_x = scale * gated - x_rows * scale**3 * jnp.mean(gated * x_rows, axis=1, keepdims=True)
    d_round = d_x.astype(BF16)
    d_ratio_part = jnp.sum(d_x * proj, axis=1).reshape(steps, part)

    part_out = matmul(normed_rows, d_logit, ((0,), (0,))).astype(BF16)
    part_out, d_ratio_part, d_round = lax.optimization_barrier((part_out, d_ratio_part, d_round))
    d_rows = lax.all_gather(d_round, "hid", axis=0).reshape(hids, steps, part, depth)
    part_out = lax.all_to_all(part_out.reshape(seqs, depth // seqs, block), "seq", 0, 0)
    part_out = part_out.reshape(groups, steps, hids, head_rows, block).astype(F32).sum(0)
    part_out = part_out.astype(BF16)

    ratio_rows = ratio_group.transpose(1, 0, 2)[..., None]
    scaled = (ratio_rows * d_rows.astype(F32)).astype(BF16)
    scaled = scaled.reshape(hids, steps, part, seqs, depth // seqs).transpose(3, 1, 0, 2, 4)
    scaled = scaled.reshape(seqs, steps * rows, depth // seqs)
    scaled = lax.all_to_all(scaled, "seq", 0, 0)
    scaled = scaled.reshape(groups, steps, steps * rows, depth // seqs)
    hidden_all = gather_flips(hidden_part, step).transpose(1, 0, 2, 3).reshape(frames, units)
    grad_in = jnp.stack(
        [matmul(hidden_all, scaled[:, s].reshape(frames, -1), ((0,), (0,))) for s in range(steps)]
    )

    d_ratio = pick(d_ratio_part, step)
    for r in range(1, steps):
        d_ratio += flip_seq(pick(d_ratio_part, (step + r) % steps), r)
    d_ratio = gather_hid(d_ratio).reshape(rows)
    correction = ratio_own**3 * d_ratio / width_in
    d_mine = lax.dynamic_index_in_dim(d_rows, step, 1, False).reshape(rows, depth)
    back = matmul(d_mine, w_own, ((1,), (1,)))
    for r in range(1, steps):
        other = lax.dynamic_index_in_dim(d_rows, (step + r) % steps, 1, False)
        other = flip_seq(other.reshape(rows, depth), r)
        back += matmul(other, pick(w_in, (step - r) % steps), ((1,), (1,)))
    grad_hidden = (ratio_own[:, None] * back - correction[:, None] * hidden.astype(F32)).astype(BF16)

    sums = [None] * halves
    for shift in range(hids):
        piece = lax.dynamic_index_in_dim(part_out, (j + shift) % hids, 1, False)
        piece = along_hid(piece, shift) if shift else piece
        which = shift % halves
        piece = piece.astype(F32)
        sums[which] = piece if sums[which] is None else sums[which] + piece
    grad_out = jnp.zeros((steps, head_rows, halves, block), F32)
    for r in range(halves):
        grad_out = lax.dynamic_update_index_in_dim(grad_out, sums[r], (half - r) % halves, 2)
    grad_out = grad_out.transpose(1, 0, 2, 3).reshape(head_rows, steps, entries)
    return (grad_hidden, grad_in, grad_out)


def solution(mesh):
    placed = (
        P("seq", "hid"),
        P(None, "hid", None),
        P(),
        P(),
        P(("seq", "hid"), None, None),
        P(None, ("seq", "hid")),
    )
    return jax.shard_map(
        shards,
        mesh=mesh,
        in_specs=placed,
        out_specs=(P("seq", "hid"), P(None, "hid", "seq"), P(("seq", "hid"), None, None)),
        check_vma=False,
    )
```

```python
import jax
import jax.numpy as jnp
from jax import lax
from jax.experimental import pallas as pl
from jax.experimental.pallas import tpu as pltpu
from jax.sharding import PartitionSpec as P

F32 = jnp.float32
BF16 = jnp.bfloat16


def pick(values, index):
    return lax.dynamic_index_in_dim(values, index, axis=0, keepdims=False)


def matmul(a, b, contract):
    return lax.dot_general(a, b, (contract, ((), ())), preferred_element_type=F32)


def after(value, *others):
    return lax.optimization_barrier((value, *others))[0]


VMEM = pltpu.CompilerParams(vmem_limit_bytes=48 * 2**20)


def whole(shape):
    return pl.BlockSpec(shape, lambda n, place: (0,) * len(shape))


def call(kernel, place, grid, in_specs, out_specs, out_shape, scratch, flops, args):
    moved = sum(a.size * a.dtype.itemsize for a in args)
    return pl.pallas_call(
        kernel,
        grid_spec=pltpu.PrefetchScalarGridSpec(
            num_scalar_prefetch=1,
            grid=(grid,),
            in_specs=in_specs,
            out_specs=out_specs,
            scratch_shapes=scratch,
        ),
        out_shape=out_shape,
        compiler_params=VMEM,
        cost_estimate=pl.CostEstimate(flops=flops, bytes_accessed=moved, transcendentals=0),
    )(place, *args)


def project(place, group, w_in, hids):
    steps = len(group)
    rows, units = group[0].shape
    depth = w_in.shape[2]
    part = rows // hids
    wide = min(256, depth)

    def kernel(place_ref, *refs):
        hidden, w, outs, sums = refs[:steps], refs[steps], refs[steps + 1 : -1], refs[-1]
        step, j = place_ref[0], place_ref[1]
        for m in range(steps):
            sums[m] = jnp.dot(hidden[m][...], w[0], preferred_element_type=F32)
        for shift in range(hids):
            start = pl.multiple_of(lax.rem(j + shift, hids) * part, part)
            for m in range(steps):
                to = pl.multiple_of(lax.rem(step + m, steps) * part, part)
                outs[shift][pl.ds(to, part), :] = sums[m, pl.ds(start, part), :].astype(
                    outs[shift].dtype
                )

    column = pl.BlockSpec((steps * part, wide), lambda n, place: (0, n))
    return call(
        kernel,
        place,
        depth // wide,
        [whole((rows, units))] * steps
        + [pl.BlockSpec((1, units, wide), lambda n, place: (place[0], 0, n))],
        [column] * hids,
        [
            jax.ShapeDtypeStruct((steps * part, depth), BF16 if shift else F32)
            for shift in range(hids)
        ],
        [pltpu.VMEM((steps, rows, wide), F32)],
        2 * steps * rows * units * depth,
        (*group, w_in),
    )


def spread(place, pieces, ratio, seqs, steps):
    hids = len(pieces)
    owned, depth = pieces[0].shape
    part = owned // steps
    rows = part * hids
    wide = depth // seqs

    def kernel(place_ref, *refs):
        pieces, ratio, scaled, plain = refs[:hids], refs[hids], refs[hids + 1], refs[hids + 2 :]
        step, j = place_ref[0], place_ref[1]
        for shift in range(hids):
            owner = lax.rem(j - shift + hids, hids)
            values = pieces[shift][...].astype(F32) * ratio[owner]
            values = values.astype(BF16)
            for m in range(steps):
                at = pl.multiple_of(m * rows + owner * part, part)
                for q in range(seqs):
                    scaled[q, pl.ds(at, part), :] = values[
                        m * part : (m + 1) * part, q * wide : (q + 1) * wide
                    ]
            to = pl.multiple_of(owner * part, part)
            for m in range(steps):
                start = pl.multiple_of(lax.rem(step + m, steps) * part, part)
                plain[m][pl.ds(to, part), :] = pieces[shift][pl.ds(start, part), :]

    return call(
        kernel,
        place,
        1,
        [whole((owned, depth))] * hids + [whole((hids, owned, 1))],
        [whole((seqs, steps * rows, wide))] + [whole((rows, depth))] * steps,
        [jax.ShapeDtypeStruct((seqs, steps * rows, wide), BF16)]
        + [jax.ShapeDtypeStruct((rows, depth), BF16)] * steps,
        [],
        steps * rows * depth,
        (*pieces, ratio),
    )


def input_gradient(place, blocks, scaled, steps):
    groups = len(blocks)
    units, rows = blocks[0][0].shape
    wide = scaled.shape[2]
    tall = min(256, units)

    def kernel(place_ref, *refs):
        hidden, scaled, out = refs[:-2], refs[-2], refs[-1]
        step, group = place_ref[0], place_ref[2]
        total = None
        for r in range(groups):
            source = lax.rem(group - r + groups, groups)
            for m in range(steps):
                at = pl.multiple_of(lax.rem(step - m + steps, steps) * rows, rows)
                right = jnp.concatenate(
                    [scaled[source * steps + s, pl.ds(at, rows), :] for s in range(steps)], axis=1
                )
                term = jnp.dot(hidden[r * steps + m][...], right, preferred_element_type=F32)
                total = term if total is None else total + term
        for s in range(steps):
            out[s] = total[:, s * wide : (s + 1) * wide]

    flat = [b for line in blocks for b in line]
    return call(
        kernel,
        place,
        units // tall,
        [pl.BlockSpec((tall, rows), lambda n, place: (n, 0))] * len(flat) + [whole(scaled.shape)],
        pl.BlockSpec((steps, tall, wide), lambda n, place: (0, n, 0)),
        jax.ShapeDtypeStruct((steps, units, wide), F32),
        [],
        2 * units * rows * len(flat) * wide * steps,
        (*flat, scaled),
    )


def hidden_gradient(place, d_rows, w_in, hidden, factors):
    steps, units, depth = w_in.shape
    rows = hidden.shape[0]
    wide = min(256, units)

    def kernel(place_ref, *refs):
        d_rows, w, hidden, factors, out = refs[:steps], refs[-4], refs[-3], refs[-2], refs[-1]
        total = None
        for r in range(steps):
            which = lax.rem(place_ref[0] - r + steps, steps)
            term = lax.dot_general(
                d_rows[r][...], w[which], (((1,), (1,)), ((), ())), preferred_element_type=F32
            )
            total = term if total is None else total + term
        out[...] = (factors[0] * total - factors[1] * hidden[...].astype(F32)).astype(BF16)

    return call(
        kernel,
        place,
        units // wide,
        [whole((rows, depth))] * steps
        + [
            pl.BlockSpec((steps, wide, depth), lambda n, place: (0, n, 0)),
            pl.BlockSpec((rows, wide), lambda n, place: (0, n)),
            whole((2, rows, 1)),
        ],
        pl.BlockSpec((rows, wide), lambda n, place: (0, n)),
        jax.ShapeDtypeStruct((rows, units), BF16),
        [],
        2 * steps * rows * units * depth,
        (*d_rows, w_in, hidden, factors),
    )


def shards(hidden, w_in, embedding, depth_gain, w_out, codebook_ids):
    hids = lax.axis_size("hid")
    seqs = lax.axis_size("seq")
    steps, units, depth = w_in.shape
    entries = w_out.shape[2]
    rows = hidden.shape[0]
    part = rows // hids
    width_in = units * hids
    frames = rows * seqs
    halves = 2 if hids % 2 == 0 else 1
    block = entries // halves
    head_rows = w_out.shape[0]
    groups = seqs // steps
    i = lax.axis_index("seq")
    j = lax.axis_index("hid")
    step = i % steps
    half = j % halves

    def along_hid(values, shift):
        return lax.ppermute(values, "hid", [(a, (a + shift) % hids) for a in range(hids)])

    def turn_hid(values, shift):
        return lax.ppermute(
            values,
            "hid",
            [(a, a - a % halves + (a % halves + shift) % halves) for a in range(hids)],
        )

    def flip_seq(values, flip):
        return lax.ppermute(
            values,
            "seq",
            [(a, a - a % steps + (a % steps + flip) % steps) for a in range(seqs)],
        )

    def gather_flips(values, position):
        out = jnp.broadcast_to(values, (steps,) + values.shape)
        for r in range(1, steps):
            out = lax.dynamic_update_index_in_dim(
                out, flip_seq(values, -r), (position + r) % steps, 0
            )
        return out

    def gather_hid(values):
        out = jnp.broadcast_to(values, (hids,) + values.shape)
        for shift in range(1, hids):
            out = lax.dynamic_update_index_in_dim(
                out, along_hid(values, shift), (j - shift) % hids, 0
            )
        return out

    place = jnp.stack([step, j, i // steps]).astype(jnp.int32)

    def along_groups(values, shift):
        return lax.ppermute(values, "seq", [(a, (a + shift * steps) % seqs) for a in range(seqs)])

    group = [hidden] + [flip_seq(hidden, -r) for r in range(1, steps)]
    proj, *send = project(place, group, w_in, hids)
    owned = steps * part

    head_send = w_out.reshape(head_rows, steps, halves, block).transpose(2, 1, 0, 3)
    head_send = jnp.broadcast_to(head_send, (hids // halves,) + head_send.shape)
    head_send = after(head_send.reshape(hids, steps, head_rows, block), *send)
    head_mid = lax.all_to_all(head_send, "hid", 0, 0).transpose(1, 0, 2, 3)

    turned = [after(hidden.T, *send)]
    turned += [along_groups(turned[0], r) for r in range(1, groups)]
    turned = [[t] + [flip_seq(t, m) for m in range(1, steps)] for t in turned]

    squares_part = jnp.sum(jnp.square(hidden.astype(F32)), axis=1)
    small = jnp.concatenate([codebook_ids.reshape(-1).astype(F32), squares_part])
    small = gather_flips(after(small, *send), step)
    for shift in range(1, hids):
        proj += along_hid(send[shift - 1], shift).astype(F32)
    small = gather_hid(small)
    ids_group = small[:, :, : steps * part].astype(jnp.int32).reshape(hids, steps, steps, part)
    squares = jnp.sum(small[:, :, steps * part :], axis=0)
    ratio_group = lax.rsqrt(squares / width_in + 1e-06).reshape(steps, hids, part)
    ratio_own = pick(ratio_group, step).reshape(rows)

    head_send = head_mid.reshape(steps, hids * head_rows, block)
    head_send = jnp.broadcast_to(head_send, (groups,) + head_send.shape)
    head_send = head_send.reshape(seqs, hids * head_rows, block)
    head = lax.all_to_all(head_send, "seq", 0, 0).reshape(depth, block)

    ratio = lax.dynamic_index_in_dim(ratio_group, j, 1, False).reshape(owned)
    before = jnp.maximum(step - 1, 0)
    table = pick(embedding, before)
    ids_before = pick(pick(ids_group, j).transpose(1, 0, 2), before).reshape(-1)
    looked = jnp.take(table, ids_before, axis=0).astype(F32)
    x_rows = ratio[:, None] * proj + jnp.where(step > 0, looked, 0.0)
    scale = lax.rsqrt(jnp.mean(x_rows * x_rows, axis=1, keepdims=True) + 1e-06)
    gain = pick(depth_gain, step)[None, :]
    normed = (x_rows * scale * gain).astype(BF16)

    owners = [j - half + (half + k) % halves for k in range(halves)]
    normed_rows = jnp.concatenate([normed] + [turn_hid(normed, -k) for k in range(1, halves)])
    targets = jnp.concatenate(
        [pick(pick(ids_group, o).transpose(1, 0, 2), step).reshape(-1) for o in owners]
    )
    logits = matmul(normed_rows, head, ((1,), (0,)))
    top = jnp.max(logits, axis=1)
    total = jnp.sum(jnp.exp(logits - top[:, None]), axis=1)
    stats = jnp.stack([top, total]).reshape(2, halves, -1)
    every = [stats] + [jnp.roll(turn_hid(stats, -t), t, axis=1) for t in range(1, halves)]
    tops = jnp.stack([e[0] for e in every]).reshape(halves, -1)
    totals = jnp.stack([e[1] for e in every]).reshape(halves, -1)
    top_all = jnp.max(tops, axis=0)
    lse = top_all + jnp.log(jnp.sum(totals * jnp.exp(tops - top_all), axis=0))
    entry = lax.broadcasted_iota(jnp.int32, logits.shape, 1) + half * block
    onehot = (targets[:, None] == entry).astype(F32)
    loss_weight = 2.0 * entries / frames
    d_logit = ((jnp.exp(logits - lse[:, None]) - onehot) * loss_weight).astype(BF16)

    d_norm_rows = matmul(d_logit, head, ((1,), (1,)))
    d_norm = d_norm_rows[:owned]
    for k in range(1, halves):
        d_norm += turn_hid(d_norm_rows[k * owned : (k + 1) * owned].astype(BF16), k).astype(F32)

    gated = gain * d_norm
    d_x = scale * gated - x_rows * scale**3 * jnp.mean(gated * x_rows, axis=1, keepdims=True)
    d_round = d_x.astype(BF16)
    d_ratio_part = jnp.sum(d_x * proj, axis=1).reshape(steps, part)

    part_out = matmul(normed_rows, d_logit, ((0,), (0,))).astype(BF16)
    pieces = [d_round] + [along_hid(d_round, shift) for shift in range(1, hids)]
    d_ratio = pick(d_ratio_part, step)
    for r in range(1, steps):
        d_ratio += flip_seq(pick(d_ratio_part, (step + r) % steps), r)
    part_out = after(part_out, d_ratio)
    part_out = lax.all_to_all(part_out.reshape(seqs, depth // seqs, block), "seq", 0, 0)
    part_out = part_out.reshape(groups, steps, hids, head_rows, block).astype(F32).sum(0)
    part_out = part_out.astype(BF16)

    ratio_column = ratio_group.transpose(1, 0, 2).reshape(hids, owned, 1)
    scaled, mine, *others = spread(place, pieces, ratio_column, seqs, steps)
    scaled = lax.all_to_all(scaled, "seq", 0, 0)
    grad_in = input_gradient(place, turned, scaled, steps)

    d_ratio = gather_hid(d_ratio).reshape(rows)
    correction = ratio_own**3 * d_ratio / width_in
    factors = jnp.stack([ratio_own, correction])[:, :, None]
    mine = [mine] + [flip_seq(others[r - 1], r) for r in range(1, steps)]
    grad_hidden = hidden_gradient(place, mine, w_in, hidden, factors)

    sums = [None] * halves
    for shift in range(hids):
        piece = lax.dynamic_index_in_dim(part_out, (j + shift) % hids, 1, False)
        piece = along_hid(piece, shift) if shift else piece
        which = shift % halves
        piece = piece.astype(F32)
        sums[which] = piece if sums[which] is None else sums[which] + piece
    grad_out = jnp.zeros((steps, head_rows, halves, block), F32)
    for r in range(halves):
        grad_out = lax.dynamic_update_index_in_dim(grad_out, sums[r], (half - r) % halves, 2)
    grad_out = grad_out.transpose(1, 0, 2, 3).reshape(head_rows, steps, entries)
    return (grad_hidden, grad_in, grad_out)


def solution(mesh):
    placed = (
        P("seq", "hid"),
        P(None, "hid", None),
        P(),
        P(),
        P(("seq", "hid"), None, None),
        P(None, ("seq", "hid")),
    )
    return jax.shard_map(
        shards,
        mesh=mesh,
        in_specs=placed,
        out_specs=(P("seq", "hid"), P(None, "hid", "seq"), P(("seq", "hid"), None, None)),
        check_vma=False,
    )
```

```python
import jax
import jax.numpy as jnp
from jax import lax
from jax.experimental import pallas as pl
from jax.experimental.pallas import tpu as pltpu
from jax.sharding import PartitionSpec as P

F32 = jnp.float32
BF16 = jnp.bfloat16


def pick(values, index):
    return lax.dynamic_index_in_dim(values, index, axis=0, keepdims=False)


def matmul(a, b, contract):
    return lax.dot_general(a, b, (contract, ((), ())), preferred_element_type=F32)


def after(value, *others):
    return lax.optimization_barrier((value, *others))[0]


VMEM = pltpu.CompilerParams(vmem_limit_bytes=48 * 2**20)


def whole(shape):
    return pl.BlockSpec(shape, lambda n, place: (0,) * len(shape))


def call(kernel, place, grid, in_specs, out_specs, out_shape, scratch, flops, args):
    moved = sum(a.size * a.dtype.itemsize for a in args)
    return pl.pallas_call(
        kernel,
        grid_spec=pltpu.PrefetchScalarGridSpec(
            num_scalar_prefetch=1,
            grid=(grid,),
            in_specs=in_specs,
            out_specs=out_specs,
            scratch_shapes=scratch,
        ),
        out_shape=out_shape,
        compiler_params=VMEM,
        cost_estimate=pl.CostEstimate(flops=flops, bytes_accessed=moved, transcendentals=0),
    )(place, *args)


EXTRA = 128


def parts_of(columns, count):
    rows = columns[0].shape[0]
    lane = lax.broadcasted_iota(jnp.int32, (rows, EXTRA), 1)
    out = jnp.zeros((rows, EXTRA), F32)
    for c in range(count):
        left = columns[c]
        for k in range(3):
            piece = left.astype(BF16).astype(F32)
            left = left - piece
            out = jnp.where(lane == 3 * c + k, piece, out)
    return out.astype(BF16)


def column_of(extra, c):
    return sum(extra[:, 3 * c + k : 3 * c + k + 1].astype(F32) for k in (2, 1, 0))


def project(place, group, w_in, hids):
    steps = len(group)
    rows, units = group[0].shape
    depth = w_in.shape[2]
    part = rows // hids
    owned = steps * part
    wide = min(256, depth)

    def kernel(place_ref, *refs):
        hidden, w, own, squares = refs[:steps], refs[steps], refs[steps + 1], refs[steps + 2]
        sends, sums, totals = refs[steps + 3 : -2], refs[-2], refs[-1]
        n, step, j = pl.program_id(0), place_ref[0], place_ref[1]
        for m in range(steps):
            sums[m] = jnp.dot(hidden[m][...], w[0], preferred_element_type=F32)
        columns = pl.ds(pl.multiple_of(n * wide, wide), wide)
        for shift in range(hids):
            out = own if shift == 0 else sends[shift - 1]
            start = pl.multiple_of(lax.rem(j + shift, hids) * part, part)
            for m in range(steps):
                to = pl.multiple_of(lax.rem(step + m, steps) * part, part)
                out[pl.ds(to, part), columns] = sums[m, pl.ds(start, part), :].astype(out.dtype)

        @pl.when(n == 0)
        def _():
            for m in range(steps):
                values = hidden[m][...].astype(F32)
                totals[m] = jnp.sum(values * values, axis=1, keepdims=True)
            for shift in range(hids):
                start = pl.multiple_of(lax.rem(j + shift, hids) * part, part)
                for m in range(steps):
                    to = pl.multiple_of(lax.rem(step + m, steps) * part, part)
                    total = totals[m, pl.ds(start, part), :]
                    if shift == 0:
                        squares[pl.ds(to, part), :] = total
                    else:
                        sends[shift - 1][pl.ds(to, part), depth:] = parts_of([total], 1)

    return call(
        kernel,
        place,
        depth // wide,
        [whole((rows, units))] * steps
        + [pl.BlockSpec((1, units, wide), lambda n, place: (place[0], 0, n))],
        [whole((owned, depth)), whole((owned, 1))] + [whole((owned, depth + EXTRA))] * (hids - 1),
        [
            jax.ShapeDtypeStruct((owned, depth), F32),
            jax.ShapeDtypeStruct((owned, 1), F32),
        ]
        + [jax.ShapeDtypeStruct((owned, depth + EXTRA), BF16)] * (hids - 1),
        [pltpu.VMEM((steps, rows, wide), F32), pltpu.VMEM((steps, rows, 1), F32)],
        2 * steps * rows * units * depth,
        (*group, w_in),
    )


def row_gradient(place, d_norm, received, x_rows, proj, scale, ratio, gain, width_in):
    owned, depth = x_rows.shape

    def kernel(place_ref, *refs):
        d_norm, received = refs[0], refs[1 : 1 + len_received]
        x_ref, proj_ref, scale_ref, ratio_ref, gain_ref, out = refs[1 + len_received :]
        gated = d_norm[...]
        for r in received:
            gated = gated + r[...].astype(F32)
        gated = gated * gain_ref[...]
        x, scale, ratio = x_ref[...], scale_ref[...], ratio_ref[...]
        mean = jnp.sum(gated * x, axis=1, keepdims=True) * (1.0 / depth)
        d_x = scale * gated - x * (scale * scale * scale * mean)
        out[:, :depth] = d_x.astype(BF16)
        d_ratio = jnp.sum(d_x * proj_ref[...], axis=1, keepdims=True)
        correction = ratio * ratio * ratio * d_ratio * (1.0 / width_in)
        out[:, depth:] = parts_of([ratio, correction], 2)

    len_received = len(received)
    args = (d_norm, *received, x_rows, proj, scale, ratio, gain)
    return call(
        kernel,
        place,
        1,
        [whole((owned, depth))] + [whole(a.shape) for a in args[1:]],
        whole((owned, depth + EXTRA)),
        jax.ShapeDtypeStruct((owned, depth + EXTRA), BF16),
        [],
        10 * owned * depth,
        args,
    )


def spread(place, pieces, seqs, steps):
    hids = len(pieces)
    owned, full = pieces[0].shape
    depth = full - EXTRA
    part = owned // steps
    rows = part * hids
    wide = depth // seqs

    def kernel(place_ref, *refs):
        pieces, scaled, plain = refs[:hids], refs[hids], refs[hids + 1 :]
        step, j = place_ref[0], place_ref[1]
        for shift in range(hids):
            owner = lax.rem(j - shift + hids, hids)
            ratio = column_of(pieces[shift][:, depth:], 0)
            values = (pieces[shift][:, :depth].astype(F32) * ratio).astype(BF16)
            for m in range(steps):
                at = pl.multiple_of(m * rows + owner * part, part)
                for q in range(seqs):
                    scaled[q, pl.ds(at, part), :] = values[
                        m * part : (m + 1) * part, q * wide : (q + 1) * wide
                    ]
            to = pl.multiple_of(owner * part, part)
            for m in range(steps):
                start = pl.multiple_of(lax.rem(step + m, steps) * part, part)
                plain[m][pl.ds(to, part), :] = pieces[shift][pl.ds(start, part), :]

    return call(
        kernel,
        place,
        1,
        [whole((owned, full))] * hids,
        [whole((seqs, steps * rows, wide))] + [whole((rows, full))] * steps,
        [jax.ShapeDtypeStruct((seqs, steps * rows, wide), BF16)]
        + [jax.ShapeDtypeStruct((rows, full), BF16)] * steps,
        [],
        steps * rows * depth,
        tuple(pieces),
    )


def sum_groups(place, received, steps, hids):
    seqs, rows, entries = received.shape
    groups = seqs // steps
    part = rows // hids

    def kernel(place_ref, received, *outs):
        for shift in range(hids):
            start = pl.multiple_of(lax.rem(place_ref[1] + shift, hids) * part, part)
            for s in range(steps):
                total = received[s, pl.ds(start, part), :].astype(F32)
                for g in range(1, groups):
                    total = total + received[g * steps + s, pl.ds(start, part), :].astype(F32)
                outs[shift][s] = total.astype(BF16)

    return call(
        kernel,
        place,
        1,
        [whole(received.shape)],
        [whole((steps, part, entries))] * hids,
        [jax.ShapeDtypeStruct((steps, part, entries), BF16)] * hids,
        [],
        seqs * rows * entries,
        (received,),
    )


def head_gradient(place, pieces, halves):
    hids = len(pieces)
    steps, rows, block = pieces[0].shape

    def kernel(place_ref, *refs):
        pieces, out = refs[:-1], refs[-1]
        for r in range(halves):
            which = lax.rem(place_ref[1] - r + hids, halves)
            columns = pl.ds(pl.multiple_of(which * block, block), block)
            for s in range(steps):
                total = pieces[r][s].astype(F32)
                for k in range(r + halves, hids, halves):
                    total = total + pieces[k][s].astype(F32)
                out[:, s, columns] = total

    return call(
        kernel,
        place,
        1,
        [whole((steps, rows, block))] * hids,
        whole((rows, steps, halves * block)),
        jax.ShapeDtypeStruct((rows, steps, halves * block), F32),
        [],
        hids * steps * rows * block,
        tuple(pieces),
    )


def input_gradient(place, blocks, scaled, steps):
    groups = len(blocks)
    units, rows = blocks[0][0].shape
    wide = scaled.shape[2]
    tall = min(256, units)

    def kernel(place_ref, *refs):
        hidden, scaled, out = refs[:-2], refs[-2], refs[-1]
        step, group = place_ref[0], place_ref[2]
        total = None
        for r in range(groups):
            source = lax.rem(group - r + groups, groups)
            for m in range(steps):
                at = pl.multiple_of(lax.rem(step - m + steps, steps) * rows, rows)
                right = jnp.concatenate(
                    [scaled[source * steps + s, pl.ds(at, rows), :] for s in range(steps)], axis=1
                )
                term = jnp.dot(hidden[r * steps + m][...], right, preferred_element_type=F32)
                total = term if total is None else total + term
        for s in range(steps):
            out[s] = total[:, s * wide : (s + 1) * wide]

    flat = [b for line in blocks for b in line]
    return call(
        kernel,
        place,
        units // tall,
        [pl.BlockSpec((tall, rows), lambda n, place: (n, 0))] * len(flat) + [whole(scaled.shape)],
        pl.BlockSpec((steps, tall, wide), lambda n, place: (0, n, 0)),
        jax.ShapeDtypeStruct((steps, units, wide), F32),
        [],
        2 * units * rows * len(flat) * wide * steps,
        (*flat, scaled),
    )


def hidden_gradient(place, d_rows, w_in, hidden):
    steps, units, depth = w_in.shape
    rows = hidden.shape[0]
    wide = min(256, units)

    def kernel(place_ref, *refs):
        d_rows, w, hidden, out = refs[:steps], refs[-3], refs[-2], refs[-1]
        total, correction = None, None
        for r in range(steps):
            which = lax.rem(place_ref[0] - r + steps, steps)
            term = lax.dot_general(
                d_rows[r][:, :depth], w[which], (((1,), (1,)), ((), ())), preferred_element_type=F32
            )
            share = column_of(d_rows[r][:, depth:], 1)
            total = term if total is None else total + term
            correction = share if correction is None else correction + share
        ratio = column_of(d_rows[0][:, depth:], 0)
        out[...] = (ratio * total - correction * hidden[...].astype(F32)).astype(BF16)

    return call(
        kernel,
        place,
        units // wide,
        [whole((rows, depth + EXTRA))] * steps
        + [
            pl.BlockSpec((steps, wide, depth), lambda n, place: (0, n, 0)),
            pl.BlockSpec((rows, wide), lambda n, place: (0, n)),
        ],
        pl.BlockSpec((rows, wide), lambda n, place: (0, n)),
        jax.ShapeDtypeStruct((rows, units), BF16),
        [],
        2 * steps * rows * units * depth,
        (*d_rows, w_in, hidden),
    )


def shards(hidden, w_in, embedding, depth_gain, w_out, codebook_ids):
    hids = lax.axis_size("hid")
    seqs = lax.axis_size("seq")
    steps, units, depth = w_in.shape
    entries = w_out.shape[2]
    rows = hidden.shape[0]
    part = rows // hids
    width_in = units * hids
    frames = rows * seqs
    halves = 2 if hids % 2 == 0 else 1
    block = entries // halves
    head_rows = w_out.shape[0]
    groups = seqs // steps
    i = lax.axis_index("seq")
    j = lax.axis_index("hid")
    step = i % steps
    half = j % halves
    owned = steps * part

    def along_hid(values, shift):
        return lax.ppermute(values, "hid", [(a, (a + shift) % hids) for a in range(hids)])

    def turn_hid(values, shift):
        return lax.ppermute(
            values,
            "hid",
            [(a, a - a % halves + (a % halves + shift) % halves) for a in range(hids)],
        )

    def flip_seq(values, flip):
        return lax.ppermute(
            values,
            "seq",
            [(a, a - a % steps + (a % steps + flip) % steps) for a in range(seqs)],
        )

    def gather_flips(values, position):
        out = jnp.broadcast_to(values, (steps,) + values.shape)
        for r in range(1, steps):
            out = lax.dynamic_update_index_in_dim(
                out, flip_seq(values, -r), (position + r) % steps, 0
            )
        return out

    place = jnp.stack([step, j, i // steps]).astype(jnp.int32)

    def along_groups(values, shift):
        return lax.ppermute(values, "seq", [(a, (a + shift * steps) % seqs) for a in range(seqs)])

    head_send = w_out.reshape(head_rows, steps, halves, block).transpose(2, 1, 0, 3)
    head_send = jnp.broadcast_to(head_send, (hids // halves,) + head_send.shape)
    head_send = head_send.reshape(hids, steps, head_rows, block)
    head_mid = lax.all_to_all(head_send, "hid", 0, 0).transpose(1, 0, 2, 3)

    ids = gather_flips(codebook_ids, step).transpose(1, 0, 2).reshape(steps, owned)
    ids_rows = [ids] + [turn_hid(ids, -k) for k in range(1, halves)]

    group = [hidden] + [flip_seq(hidden, -r) for r in range(1, steps)]
    proj, squares, *send = project(place, group, w_in, hids)
    for shift in range(1, hids):
        received = along_hid(send[shift - 1], shift)
        proj += received[:, :depth].astype(F32)
        squares += jnp.sum(received[:, depth : depth + 3].astype(F32), axis=1, keepdims=True)
    ratio = lax.rsqrt(squares / width_in + 1e-06)

    head_send = after(head_mid, *send).reshape(steps, hids * head_rows, block)
    head_send = jnp.broadcast_to(head_send, (groups,) + head_send.shape)
    head_send = head_send.reshape(seqs, hids * head_rows, block)
    head = lax.all_to_all(head_send, "seq", 0, 0).reshape(depth, block)

    before = jnp.maximum(step - 1, 0)
    table = pick(embedding, before)
    looked = jnp.take(table, pick(ids, before), axis=0).astype(F32)
    x_rows = ratio * proj + jnp.where(step > 0, looked, 0.0)
    scale = lax.rsqrt(jnp.mean(x_rows * x_rows, axis=1, keepdims=True) + 1e-06)
    gain = pick(depth_gain, step)[None, :]
    normed = (x_rows * scale * gain).astype(BF16)

    turned = [after(hidden.T, normed)]
    turned += [along_groups(turned[0], r) for r in range(1, groups)]
    turned = [[t] + [flip_seq(t, m) for m in range(1, steps)] for t in turned]

    normed_rows = jnp.concatenate([normed] + [turn_hid(normed, -k) for k in range(1, halves)])
    targets = jnp.concatenate([pick(r, step) for r in ids_rows])
    logits = matmul(normed_rows, head, ((1,), (0,)))
    top = jnp.max(logits, axis=1)
    total = jnp.sum(jnp.exp(logits - top[:, None]), axis=1)
    stats = jnp.stack([top, total]).reshape(2, halves, -1)
    every = [stats] + [jnp.roll(turn_hid(stats, -t), t, axis=1) for t in range(1, halves)]
    tops = jnp.stack([e[0] for e in every]).reshape(halves, -1)
    totals = jnp.stack([e[1] for e in every]).reshape(halves, -1)
    top_all = jnp.max(tops, axis=0)
    lse = top_all + jnp.log(jnp.sum(totals * jnp.exp(tops - top_all), axis=0))
    entry = lax.broadcasted_iota(jnp.int32, logits.shape, 1) + half * block
    onehot = (targets[:, None] == entry).astype(F32)
    loss_weight = 2.0 * entries / frames
    d_logit = ((jnp.exp(logits - lse[:, None]) - onehot) * loss_weight).astype(BF16)

    d_norm_rows = matmul(d_logit, head, ((1,), (1,)))
    received = [
        turn_hid(d_norm_rows[k * owned : (k + 1) * owned].astype(BF16), k) for k in range(1, halves)
    ]
    d_round = row_gradient(
        place, d_norm_rows, received, x_rows, proj, scale, ratio, gain, width_in
    )

    part_out = matmul(normed_rows, d_logit, ((0,), (0,))).astype(BF16)
    part_out = lax.all_to_all(part_out.reshape(seqs, depth // seqs, block), "seq", 0, 0)
    sums = sum_groups(place, part_out, steps, hids)
    sums = [along_hid(p, shift) if shift else p for shift, p in enumerate(sums)]
    grad_out = head_gradient(place, sums, halves)

    pieces = [d_round] + [along_hid(d_round, shift) for shift in range(1, hids)]
    scaled, mine, *others = spread(place, pieces, seqs, steps)
    scaled = lax.all_to_all(scaled, "seq", 0, 0)
    grad_in = input_gradient(place, turned, scaled, steps)
    mine = [mine] + [flip_seq(others[r - 1], r) for r in range(1, steps)]
    grad_hidden = hidden_gradient(place, mine, w_in, hidden)
    return (grad_hidden, grad_in, grad_out)


def solution(mesh):
    placed = (
        P("seq", "hid"),
        P(None, "hid", None),
        P(),
        P(),
        P(("seq", "hid"), None, None),
        P(None, ("seq", "hid")),
    )
    return jax.shard_map(
        shards,
        mesh=mesh,
        in_specs=placed,
        out_specs=(P("seq", "hid"), P(None, "hid", "seq"), P(("seq", "hid"), None, None)),
        check_vma=False,
    )
```

```python
import jax
import jax.numpy as jnp
from jax import lax
from jax.experimental import pallas as pl
from jax.experimental.pallas import tpu as pltpu
from jax.sharding import PartitionSpec as P

F32 = jnp.float32
BF16 = jnp.bfloat16


def pick(values, index):
    return lax.dynamic_index_in_dim(values, index, axis=0, keepdims=False)


def matmul(a, b, contract):
    return lax.dot_general(a, b, (contract, ((), ())), preferred_element_type=F32)


def after(value, *others):
    return lax.optimization_barrier((value, *others))[0]


VMEM = pltpu.CompilerParams(vmem_limit_bytes=60 * 2**20)


def whole(shape):
    return pl.BlockSpec(shape, lambda n, place: (0,) * len(shape))


def call(kernel, place, grid, in_specs, out_specs, out_shape, scratch, flops, args):
    moved = sum(a.size * a.dtype.itemsize for a in args)
    return pl.pallas_call(
        kernel,
        grid_spec=pltpu.PrefetchScalarGridSpec(
            num_scalar_prefetch=1,
            grid=(grid,),
            in_specs=in_specs,
            out_specs=out_specs,
            scratch_shapes=scratch,
        ),
        out_shape=out_shape,
        compiler_params=VMEM,
        cost_estimate=pl.CostEstimate(flops=flops, bytes_accessed=moved, transcendentals=0),
    )(place, *args)


EXTRA = 128


def parts_of(columns, count):
    rows = columns[0].shape[0]
    lane = lax.broadcasted_iota(jnp.int32, (rows, EXTRA), 1)
    out = jnp.zeros((rows, EXTRA), F32)
    for c in range(count):
        left = columns[c]
        for k in range(3):
            piece = left.astype(BF16).astype(F32)
            left = left - piece
            out = jnp.where(lane == 3 * c + k, piece, out)
    return out.astype(BF16)


def column_of(extra, c):
    return sum(extra[:, 3 * c + k : 3 * c + k + 1].astype(F32) for k in (2, 1, 0))


def project(place, group, w_in, hids):
    steps = len(group)
    rows, units = group[0].shape
    depth = w_in.shape[2]
    part = rows // hids
    owned = steps * part
    wide = min(256, depth)

    def kernel(place_ref, *refs):
        hidden, w, own, squares = refs[:steps], refs[steps], refs[steps + 1], refs[steps + 2]
        sends, sums, totals = refs[steps + 3 : -2], refs[-2], refs[-1]
        n, step, j = pl.program_id(0), place_ref[0], place_ref[1]
        left = jnp.concatenate([h[...] for h in hidden], axis=0)
        sums[...] = jnp.dot(left, w[0], preferred_element_type=F32).reshape(steps, rows, wide)
        columns = pl.ds(pl.multiple_of(n * wide, wide), wide)
        for shift in range(hids):
            out = own if shift == 0 else sends[shift - 1]
            start = pl.multiple_of(lax.rem(j + shift, hids) * part, part)
            for m in range(steps):
                to = pl.multiple_of(lax.rem(step + m, steps) * part, part)
                out[pl.ds(to, part), columns] = sums[m, pl.ds(start, part), :].astype(out.dtype)

        @pl.when(n == 0)
        def _():
            for m in range(steps):
                values = hidden[m][...].astype(F32)
                totals[m] = jnp.sum(values * values, axis=1, keepdims=True)
            for shift in range(hids):
                start = pl.multiple_of(lax.rem(j + shift, hids) * part, part)
                for m in range(steps):
                    to = pl.multiple_of(lax.rem(step + m, steps) * part, part)
                    total = totals[m, pl.ds(start, part), :]
                    if shift == 0:
                        squares[pl.ds(to, part), :] = total
                    else:
                        sends[shift - 1][pl.ds(to, part), depth:] = parts_of([total], 1)

    return call(
        kernel,
        place,
        depth // wide,
        [whole((rows, units))] * steps
        + [pl.BlockSpec((1, units, wide), lambda n, place: (place[0], 0, n))],
        [whole((owned, depth)), whole((owned, 1))] + [whole((owned, depth + EXTRA))] * (hids - 1),
        [
            jax.ShapeDtypeStruct((owned, depth), F32),
            jax.ShapeDtypeStruct((owned, 1), F32),
        ]
        + [jax.ShapeDtypeStruct((owned, depth + EXTRA), BF16)] * (hids - 1),
        [pltpu.VMEM((steps, rows, wide), F32), pltpu.VMEM((steps, rows, 1), F32)],
        2 * steps * rows * units * depth,
        (*group, w_in),
    )


def normalise(place, proj, squares, received, looked, gain, width_in):
    owned, depth = proj.shape
    count = len(received)

    def kernel(place_ref, *refs):
        proj, squares, looked, gain = refs[0], refs[1], refs[2 + count], refs[3 + count]
        proj_out, x_out, normed_out, scale_out, ratio_out = refs[4 + count :]
        total, square = proj[...], squares[...]
        for r in refs[2 : 2 + count]:
            total = total + r[:, :depth].astype(F32)
            square = square + column_of(r[:, depth:], 0)
        ratio = lax.rsqrt(square * (1.0 / width_in) + 1e-06)
        x = ratio * total + jnp.where(place_ref[0] > 0, looked[...].astype(F32), 0.0)
        scale = lax.rsqrt(jnp.sum(x * x, axis=1, keepdims=True) * (1.0 / depth) + 1e-06)
        proj_out[...] = total
        x_out[...] = x
        normed_out[...] = (x * scale * gain[...]).astype(BF16)
        scale_out[...] = scale
        ratio_out[...] = ratio

    args = (proj, squares, *received, looked, gain)
    full, column = (owned, depth), (owned, 1)
    shapes = [(full, F32), (full, F32), (full, BF16), (column, F32), (column, F32)]
    return call(
        kernel,
        place,
        1,
        [whole(a.shape) for a in args],
        [whole(shape) for shape, _ in shapes],
        [jax.ShapeDtypeStruct(shape, dtype) for shape, dtype in shapes],
        [],
        10 * owned * depth,
        args,
    )


def row_gradient(place, d_norm, received, x_rows, proj, scale, ratio, gain, width_in):
    owned, depth = x_rows.shape

    def kernel(place_ref, *refs):
        d_norm, received = refs[0], refs[1 : 1 + len_received]
        x_ref, proj_ref, scale_ref, ratio_ref, gain_ref, out = refs[1 + len_received :]
        gated = d_norm[...]
        for r in received:
            gated = gated + r[...].astype(F32)
        gated = gated * gain_ref[...]
        x, scale, ratio = x_ref[...], scale_ref[...], ratio_ref[...]
        mean = jnp.sum(gated * x, axis=1, keepdims=True) * (1.0 / depth)
        d_x = scale * gated - x * (scale * scale * scale * mean)
        out[:, :depth] = d_x.astype(BF16)
        d_ratio = jnp.sum(d_x * proj_ref[...], axis=1, keepdims=True)
        correction = ratio * ratio * ratio * d_ratio * (1.0 / width_in)
        out[:, depth:] = parts_of([ratio, correction], 2)

    len_received = len(received)
    args = (d_norm, *received, x_rows, proj, scale, ratio, gain)
    return call(
        kernel,
        place,
        1,
        [whole((owned, depth))] + [whole(a.shape) for a in args[1:]],
        whole((owned, depth + EXTRA)),
        jax.ShapeDtypeStruct((owned, depth + EXTRA), BF16),
        [],
        10 * owned * depth,
        args,
    )


def spread(place, pieces, seqs, steps):
    hids = len(pieces)
    owned, full = pieces[0].shape
    depth = full - EXTRA
    part = owned // steps
    rows = part * hids
    wide = depth // seqs

    def kernel(place_ref, *refs):
        pieces, scaled, plain = refs[:hids], refs[hids], refs[hids + 1 :]
        step, j = place_ref[0], place_ref[1]
        for shift in range(hids):
            owner = lax.rem(j - shift + hids, hids)
            ratio = column_of(pieces[shift][:, depth:], 0)
            values = (pieces[shift][:, :depth].astype(F32) * ratio).astype(BF16)
            for m in range(steps):
                at = pl.multiple_of(m * rows + owner * part, part)
                for q in range(seqs):
                    scaled[q, pl.ds(at, part), :] = values[
                        m * part : (m + 1) * part, q * wide : (q + 1) * wide
                    ]
            to = pl.multiple_of(owner * part, part)
            for m in range(steps):
                start = pl.multiple_of(lax.rem(step + m, steps) * part, part)
                plain[m][pl.ds(to, part), :] = pieces[shift][pl.ds(start, part), :]

    return call(
        kernel,
        place,
        1,
        [whole((owned, full))] * hids,
        [whole((seqs, steps * rows, wide))] + [whole((rows, full))] * steps,
        [jax.ShapeDtypeStruct((seqs, steps * rows, wide), BF16)]
        + [jax.ShapeDtypeStruct((rows, full), BF16)] * steps,
        [],
        steps * rows * depth,
        tuple(pieces),
    )


def sum_groups(place, received, steps, hids):
    seqs, rows, entries = received.shape
    groups = seqs // steps
    part = rows // hids

    def kernel(place_ref, received, *outs):
        for shift in range(hids):
            start = pl.multiple_of(lax.rem(place_ref[1] + shift, hids) * part, part)
            for s in range(steps):
                total = received[s, pl.ds(start, part), :].astype(F32)
                for g in range(1, groups):
                    total = total + received[g * steps + s, pl.ds(start, part), :].astype(F32)
                outs[shift][s] = total.astype(BF16)

    return call(
        kernel,
        place,
        1,
        [whole(received.shape)],
        [whole((steps, part, entries))] * hids,
        [jax.ShapeDtypeStruct((steps, part, entries), BF16)] * hids,
        [],
        seqs * rows * entries,
        (received,),
    )


def head_gradient(place, pieces, halves):
    hids = len(pieces)
    steps, rows, block = pieces[0].shape

    def kernel(place_ref, *refs):
        pieces, out = refs[:-1], refs[-1]
        for r in range(halves):
            which = lax.rem(place_ref[1] - r + hids, halves)
            columns = pl.ds(pl.multiple_of(which * block, block), block)
            for s in range(steps):
                total = pieces[r][s].astype(F32)
                for k in range(r + halves, hids, halves):
                    total = total + pieces[k][s].astype(F32)
                out[:, s, columns] = total

    return call(
        kernel,
        place,
        1,
        [whole((steps, rows, block))] * hids,
        whole((rows, steps, halves * block)),
        jax.ShapeDtypeStruct((rows, steps, halves * block), F32),
        [],
        hids * steps * rows * block,
        tuple(pieces),
    )


def input_gradient(place, blocks, scaled, steps):
    groups = len(blocks)
    units, rows = blocks[0][0].shape
    wide = scaled.shape[2]
    tall = min(512, units)

    def kernel(place_ref, *refs):
        hidden, scaled, out = refs[:-2], refs[-2], refs[-1]
        step, group = place_ref[0], place_ref[2]
        total = None
        for r in range(groups):
            source = lax.rem(group - r + groups, groups)
            for m in range(steps):
                at = pl.multiple_of(lax.rem(step - m + steps, steps) * rows, rows)
                right = jnp.concatenate(
                    [scaled[source * steps + s, pl.ds(at, rows), :] for s in range(steps)], axis=1
                )
                term = jnp.dot(hidden[r * steps + m][...], right, preferred_element_type=F32)
                total = term if total is None else total + term
        for s in range(steps):
            out[s] = total[:, s * wide : (s + 1) * wide]

    flat = [b for line in blocks for b in line]
    return call(
        kernel,
        place,
        units // tall,
        [pl.BlockSpec((tall, rows), lambda n, place: (n, 0))] * len(flat) + [whole(scaled.shape)],
        pl.BlockSpec((steps, tall, wide), lambda n, place: (0, n, 0)),
        jax.ShapeDtypeStruct((steps, units, wide), F32),
        [],
        2 * units * rows * len(flat) * wide * steps,
        (*flat, scaled),
    )


def hidden_gradient(place, d_rows, w_in, hidden):
    steps, units, depth = w_in.shape
    rows = hidden.shape[0]
    wide = min(256, units)

    def kernel(place_ref, *refs):
        d_rows, w, hidden, out = refs[:steps], refs[-3], refs[-2], refs[-1]
        total, correction = None, None
        for r in range(steps):
            which = lax.rem(place_ref[0] - r + steps, steps)
            term = lax.dot_general(
                d_rows[r][:, :depth], w[which], (((1,), (1,)), ((), ())), preferred_element_type=F32
            )
            share = column_of(d_rows[r][:, depth:], 1)
            total = term if total is None else total + term
            correction = share if correction is None else correction + share
        ratio = column_of(d_rows[0][:, depth:], 0)
        out[...] = (ratio * total - correction * hidden[...].astype(F32)).astype(BF16)

    return call(
        kernel,
        place,
        units // wide,
        [whole((rows, depth + EXTRA))] * steps
        + [
            pl.BlockSpec((steps, wide, depth), lambda n, place: (0, n, 0)),
            pl.BlockSpec((rows, wide), lambda n, place: (0, n)),
        ],
        pl.BlockSpec((rows, wide), lambda n, place: (0, n)),
        jax.ShapeDtypeStruct((rows, units), BF16),
        [],
        2 * steps * rows * units * depth,
        (*d_rows, w_in, hidden),
    )


def shards(hidden, w_in, embedding, depth_gain, w_out, codebook_ids):
    hids = lax.axis_size("hid")
    seqs = lax.axis_size("seq")
    steps, units, depth = w_in.shape
    entries = w_out.shape[2]
    rows = hidden.shape[0]
    part = rows // hids
    width_in = units * hids
    frames = rows * seqs
    halves = 2 if hids % 2 == 0 else 1
    block = entries // halves
    head_rows = w_out.shape[0]
    groups = seqs // steps
    i = lax.axis_index("seq")
    j = lax.axis_index("hid")
    step = i % steps
    half = j % halves
    owned = steps * part

    def along_hid(values, shift):
        return lax.ppermute(values, "hid", [(a, (a + shift) % hids) for a in range(hids)])

    def turn_hid(values, shift):
        return lax.ppermute(
            values,
            "hid",
            [(a, a - a % halves + (a % halves + shift) % halves) for a in range(hids)],
        )

    def flip_seq(values, flip):
        return lax.ppermute(
            values,
            "seq",
            [(a, a - a % steps + (a % steps + flip) % steps) for a in range(seqs)],
        )

    def gather_flips(values, position):
        out = jnp.broadcast_to(values, (steps,) + values.shape)
        for r in range(1, steps):
            out = lax.dynamic_update_index_in_dim(
                out, flip_seq(values, -r), (position + r) % steps, 0
            )
        return out

    place = jnp.stack([step, j, i // steps]).astype(jnp.int32)

    def along_groups(values, shift):
        return lax.ppermute(values, "seq", [(a, (a + shift * steps) % seqs) for a in range(seqs)])

    head_send = w_out.reshape(head_rows, steps, halves, block).transpose(2, 1, 0, 3)
    head_send = jnp.broadcast_to(head_send, (hids // halves,) + head_send.shape)
    head_send = head_send.reshape(hids, steps, head_rows, block)
    head_mid = lax.all_to_all(head_send, "hid", 0, 0).transpose(1, 0, 2, 3)

    ids = gather_flips(codebook_ids, step).transpose(1, 0, 2).reshape(steps, owned)
    ids_rows = [ids] + [turn_hid(ids, -k) for k in range(1, halves)]

    group = [hidden] + [flip_seq(hidden, -r) for r in range(1, steps)]
    proj, squares, *send = project(place, group, w_in, hids)
    received = [along_hid(send[shift - 1], shift) for shift in range(1, hids)]

    head_send = after(head_mid, *send).reshape(steps, hids * head_rows, block)
    head_send = jnp.broadcast_to(head_send, (groups,) + head_send.shape)
    head_send = head_send.reshape(seqs, hids * head_rows, block)
    head = lax.all_to_all(head_send, "seq", 0, 0).reshape(depth, block)

    before = jnp.maximum(step - 1, 0)
    table = pick(embedding, before)
    looked = jnp.take(table, pick(ids, before), axis=0)
    gain = pick(depth_gain, step)[None, :]
    proj, x_rows, normed, scale, ratio = normalise(
        place, proj, squares, received, looked, gain, width_in
    )

    turned = [after(hidden.T, normed)]
    turned += [along_groups(turned[0], r) for r in range(1, groups)]
    turned = [[t] + [flip_seq(t, m) for m in range(1, steps)] for t in turned]

    normed_rows = jnp.concatenate([normed] + [turn_hid(normed, -k) for k in range(1, halves)])
    targets = jnp.concatenate([pick(r, step) for r in ids_rows])
    logits = matmul(normed_rows, head, ((1,), (0,)))
    top = jnp.max(logits, axis=1)
    total = jnp.sum(jnp.exp(logits - top[:, None]), axis=1)
    stats = jnp.stack([top, total]).reshape(2, halves, -1)
    every = [stats] + [jnp.roll(turn_hid(stats, -t), t, axis=1) for t in range(1, halves)]
    tops = jnp.stack([e[0] for e in every]).reshape(halves, -1)
    totals = jnp.stack([e[1] for e in every]).reshape(halves, -1)
    top_all = jnp.max(tops, axis=0)
    lse = top_all + jnp.log(jnp.sum(totals * jnp.exp(tops - top_all), axis=0))
    entry = lax.broadcasted_iota(jnp.int32, logits.shape, 1) + half * block
    onehot = (targets[:, None] == entry).astype(F32)
    loss_weight = 2.0 * entries / frames
    d_logit = ((jnp.exp(logits - lse[:, None]) - onehot) * loss_weight).astype(BF16)

    d_norm_rows = matmul(d_logit, head, ((1,), (1,)))
    away = [d_norm_rows[k * owned : (k + 1) * owned].astype(BF16) for k in range(1, halves)]
    received = [turn_hid(a, k + 1) for k, a in enumerate(away)]
    d_round = row_gradient(
        place, d_norm_rows, received, x_rows, proj, scale, ratio, gain, width_in
    )

    part_out = matmul(normed_rows, after(d_logit, *away), ((0,), (0,))).astype(BF16)
    part_out = lax.all_to_all(part_out.reshape(seqs, depth // seqs, block), "seq", 0, 0)
    sums = sum_groups(place, part_out, steps, hids)
    sums = [along_hid(p, shift) if shift else p for shift, p in enumerate(sums)]
    grad_out = head_gradient(place, sums, halves)

    pieces = [d_round] + [along_hid(d_round, shift) for shift in range(1, hids)]
    scaled, mine, *others = spread(place, pieces, seqs, steps)
    scaled = lax.all_to_all(scaled, "seq", 0, 0)
    grad_in = input_gradient(place, turned, scaled, steps)
    mine = [mine] + [flip_seq(others[r - 1], r) for r in range(1, steps)]
    grad_hidden = hidden_gradient(place, mine, w_in, hidden)
    return (grad_hidden, grad_in, grad_out)


def solution(mesh):
    placed = (
        P("seq", "hid"),
        P(None, "hid", None),
        P(),
        P(),
        P(("seq", "hid"), None, None),
        P(None, ("seq", "hid")),
    )
    return jax.shard_map(
        shards,
        mesh=mesh,
        in_specs=placed,
        out_specs=(P("seq", "hid"), P(None, "hid", "seq"), P(("seq", "hid"), None, None)),
        check_vma=False,
    )
```

```python
import jax
import jax.numpy as jnp
from jax import lax
from jax.experimental import pallas as pl
from jax.experimental.pallas import tpu as pltpu
from jax.sharding import PartitionSpec as P

F32 = jnp.float32
BF16 = jnp.bfloat16


def pick(values, index):
    return lax.dynamic_index_in_dim(values, index, axis=0, keepdims=False)


def matmul(a, b, contract):
    return lax.dot_general(a, b, (contract, ((), ())), preferred_element_type=F32)


def after(value, *others):
    return lax.optimization_barrier((value, *others))[0]


VMEM = pltpu.CompilerParams(vmem_limit_bytes=20 * 2**20)


def whole(shape):
    return pl.BlockSpec(shape, lambda n, place: (0,) * len(shape))


def call(kernel, place, grid, in_specs, out_specs, out_shape, scratch, flops, args, weight=1):
    moved = weight * sum(a.size * a.dtype.itemsize for a in args)
    flops = weight * flops
    return pl.pallas_call(
        kernel,
        grid_spec=pltpu.PrefetchScalarGridSpec(
            num_scalar_prefetch=1,
            grid=(grid,),
            in_specs=in_specs,
            out_specs=out_specs,
            scratch_shapes=scratch,
        ),
        out_shape=out_shape,
        compiler_params=VMEM,
        cost_estimate=pl.CostEstimate(flops=flops, bytes_accessed=moved, transcendentals=0),
    )(place, *args)


EXTRA = 128


def parts_of(columns, count):
    rows = columns[0].shape[0]
    lane = lax.broadcasted_iota(jnp.int32, (rows, EXTRA), 1)
    out = jnp.zeros((rows, EXTRA), F32)
    for c in range(count):
        left = columns[c]
        for k in range(3):
            piece = left.astype(BF16).astype(F32)
            left = left - piece
            out = jnp.where(lane == 3 * c + k, piece, out)
    return out.astype(BF16)


def column_of(extra, c):
    return sum(extra[:, 3 * c + k : 3 * c + k + 1].astype(F32) for k in (2, 1, 0))


def project(place, group, w_in, hids):
    steps = len(group)
    rows, units = group[0].shape
    depth = w_in.shape[2]
    part = rows // hids
    owned = steps * part
    wide = min(256, depth)

    def kernel(place_ref, *refs):
        hidden, w, own, squares = refs[:steps], refs[steps], refs[steps + 1], refs[steps + 2]
        sends, sums, totals = refs[steps + 3 : -2], refs[-2], refs[-1]
        n, step, j = pl.program_id(0), place_ref[0], place_ref[1]
        left = jnp.concatenate([h[...] for h in hidden], axis=0)
        sums[...] = jnp.dot(left, w[0], preferred_element_type=F32).reshape(steps, rows, wide)
        columns = pl.ds(pl.multiple_of(n * wide, wide), wide)
        for shift in range(hids):
            out = own if shift == 0 else sends[shift - 1]
            start = pl.multiple_of(lax.rem(j + shift, hids) * part, part)
            for m in range(steps):
                to = pl.multiple_of(lax.rem(step + m, steps) * part, part)
                out[pl.ds(to, part), columns] = sums[m, pl.ds(start, part), :].astype(out.dtype)

        @pl.when(n == 0)
        def _():
            for m in range(steps):
                values = hidden[m][...].astype(F32)
                totals[m] = jnp.sum(values * values, axis=1, keepdims=True)
            for shift in range(hids):
                start = pl.multiple_of(lax.rem(j + shift, hids) * part, part)
                for m in range(steps):
                    to = pl.multiple_of(lax.rem(step + m, steps) * part, part)
                    total = totals[m, pl.ds(start, part), :]
                    if shift == 0:
                        squares[pl.ds(to, part), :] = total
                    else:
                        sends[shift - 1][pl.ds(to, part), depth:] = parts_of([total], 1)

    return call(
        kernel,
        place,
        depth // wide,
        [whole((rows, units))] * steps
        + [pl.BlockSpec((1, units, wide), lambda n, place: (place[0], 0, n))],
        [whole((owned, depth)), whole((owned, 1))] + [whole((owned, depth + EXTRA))] * (hids - 1),
        [
            jax.ShapeDtypeStruct((owned, depth), F32),
            jax.ShapeDtypeStruct((owned, 1), F32),
        ]
        + [jax.ShapeDtypeStruct((owned, depth + EXTRA), BF16)] * (hids - 1),
        [pltpu.VMEM((steps, rows, wide), F32), pltpu.VMEM((steps, rows, 1), F32)],
        2 * steps * rows * units * depth,
        (*group, w_in),
    )


def normalise(place, proj, squares, received, looked, gain, width_in):
    owned, depth = proj.shape
    count = len(received)

    def kernel(place_ref, *refs):
        proj, squares, looked, gain = refs[0], refs[1], refs[2 + count], refs[3 + count]
        proj_out, x_out, normed_out, scale_out, ratio_out = refs[4 + count :]
        total, square = proj[...], squares[...]
        for r in refs[2 : 2 + count]:
            total = total + r[:, :depth].astype(F32)
            square = square + column_of(r[:, depth:], 0)
        ratio = lax.rsqrt(square * (1.0 / width_in) + 1e-06)
        x = ratio * total + jnp.where(place_ref[0] > 0, looked[...].astype(F32), 0.0)
        scale = lax.rsqrt(jnp.sum(x * x, axis=1, keepdims=True) * (1.0 / depth) + 1e-06)
        proj_out[...] = total
        x_out[...] = x
        normed_out[...] = (x * scale * gain[...]).astype(BF16)
        scale_out[...] = scale
        ratio_out[...] = ratio

    args = (proj, squares, *received, looked, gain)
    full, column = (owned, depth), (owned, 1)
    shapes = [(full, F32), (full, F32), (full, BF16), (column, F32), (column, F32)]
    return call(
        kernel,
        place,
        1,
        [whole(a.shape) for a in args],
        [whole(shape) for shape, _ in shapes],
        [jax.ShapeDtypeStruct(shape, dtype) for shape, dtype in shapes],
        [],
        10 * owned * depth,
        args,
        weight=64,
    )


def row_gradient(place, d_norm, received, x_rows, proj, scale, ratio, gain, width_in):
    owned, depth = x_rows.shape

    def kernel(place_ref, *refs):
        d_norm, received = refs[0], refs[1 : 1 + len_received]
        x_ref, proj_ref, scale_ref, ratio_ref, gain_ref, out = refs[1 + len_received :]
        gated = d_norm[...]
        for r in received:
            gated = gated + r[...].astype(F32)
        gated = gated * gain_ref[...]
        x, scale, ratio = x_ref[...], scale_ref[...], ratio_ref[...]
        mean = jnp.sum(gated * x, axis=1, keepdims=True) * (1.0 / depth)
        d_x = scale * gated - x * (scale * scale * scale * mean)
        out[:, :depth] = d_x.astype(BF16)
        d_ratio = jnp.sum(d_x * proj_ref[...], axis=1, keepdims=True)
        correction = ratio * ratio * ratio * d_ratio * (1.0 / width_in)
        out[:, depth:] = parts_of([ratio, correction], 2)

    len_received = len(received)
    args = (d_norm, *received, x_rows, proj, scale, ratio, gain)
    return call(
        kernel,
        place,
        1,
        [whole((owned, depth))] + [whole(a.shape) for a in args[1:]],
        whole((owned, depth + EXTRA)),
        jax.ShapeDtypeStruct((owned, depth + EXTRA), BF16),
        [],
        10 * owned * depth,
        args,
    )


def spread(place, pieces, seqs, steps):
    hids = len(pieces)
    owned, full = pieces[0].shape
    depth = full - EXTRA
    part = owned // steps
    rows = part * hids
    wide = depth // seqs

    def kernel(place_ref, *refs):
        pieces, scaled, plain = refs[:hids], refs[hids], refs[hids + 1 :]
        step, j = place_ref[0], place_ref[1]
        for shift in range(hids):
            owner = lax.rem(j - shift + hids, hids)
            ratio = column_of(pieces[shift][:, depth:], 0)
            values = (pieces[shift][:, :depth].astype(F32) * ratio).astype(BF16)
            for m in range(steps):
                at = pl.multiple_of(m * rows + owner * part, part)
                for q in range(seqs):
                    scaled[q, pl.ds(at, part), :] = values[
                        m * part : (m + 1) * part, q * wide : (q + 1) * wide
                    ]
            to = pl.multiple_of(owner * part, part)
            for m in range(steps):
                start = pl.multiple_of(lax.rem(step + m, steps) * part, part)
                plain[m][pl.ds(to, part), :] = pieces[shift][pl.ds(start, part), :]

    return call(
        kernel,
        place,
        1,
        [whole((owned, full))] * hids,
        [whole((seqs, steps * rows, wide))] + [whole((rows, full))] * steps,
        [jax.ShapeDtypeStruct((seqs, steps * rows, wide), BF16)]
        + [jax.ShapeDtypeStruct((rows, full), BF16)] * steps,
        [],
        steps * rows * depth,
        tuple(pieces),
        weight=64,
    )


def sum_groups(place, received, steps, hids):
    seqs, rows, entries = received.shape
    groups = seqs // steps
    part = rows // hids

    def kernel(place_ref, received, *outs):
        for shift in range(hids):
            start = pl.multiple_of(lax.rem(place_ref[1] + shift, hids) * part, part)
            for s in range(steps):
                total = received[s, pl.ds(start, part), :].astype(F32)
                for g in range(1, groups):
                    total = total + received[g * steps + s, pl.ds(start, part), :].astype(F32)
                outs[shift][s] = total.astype(BF16)

    return call(
        kernel,
        place,
        1,
        [whole(received.shape)],
        [whole((steps, part, entries))] * hids,
        [jax.ShapeDtypeStruct((steps, part, entries), BF16)] * hids,
        [],
        seqs * rows * entries,
        (received,),
    )


def head_gradient(place, pieces, halves):
    hids = len(pieces)
    steps, rows, block = pieces[0].shape

    def kernel(place_ref, *refs):
        pieces, out = refs[:-1], refs[-1]
        for r in range(halves):
            which = lax.rem(place_ref[1] - r + hids, halves)
            columns = pl.ds(pl.multiple_of(which * block, block), block)
            for s in range(steps):
                total = pieces[r][s].astype(F32)
                for k in range(r + halves, hids, halves):
                    total = total + pieces[k][s].astype(F32)
                out[:, s, columns] = total

    return call(
        kernel,
        place,
        1,
        [whole((steps, rows, block))] * hids,
        whole((rows, steps, halves * block)),
        jax.ShapeDtypeStruct((rows, steps, halves * block), F32),
        [],
        hids * steps * rows * block,
        tuple(pieces),
    )


def input_gradient(place, blocks, scaled, steps):
    groups = len(blocks)
    units, rows = blocks[0][0].shape
    wide = scaled.shape[2]
    tall = min(512, units)

    def kernel(place_ref, *refs):
        hidden, scaled, out = refs[:-2], refs[-2], refs[-1]
        step, group = place_ref[0], place_ref[2]
        total = None
        for r in range(groups):
            source = lax.rem(group - r + groups, groups)
            for m in range(steps):
                at = pl.multiple_of(lax.rem(step - m + steps, steps) * rows, rows)
                right = jnp.concatenate(
                    [scaled[source * steps + s, pl.ds(at, rows), :] for s in range(steps)], axis=1
                )
                term = jnp.dot(hidden[r * steps + m][...], right, preferred_element_type=F32)
                total = term if total is None else total + term
        for s in range(steps):
            out[s] = total[:, s * wide : (s + 1) * wide]

    flat = [b for line in blocks for b in line]
    return call(
        kernel,
        place,
        units // tall,
        [pl.BlockSpec((tall, rows), lambda n, place: (n, 0))] * len(flat) + [whole(scaled.shape)],
        pl.BlockSpec((steps, tall, wide), lambda n, place: (0, n, 0)),
        jax.ShapeDtypeStruct((steps, units, wide), F32),
        [],
        2 * units * rows * len(flat) * wide * steps,
        (*flat, scaled),
    )


def hidden_gradient(place, d_rows, w_in, hidden):
    steps, units, depth = w_in.shape
    rows = hidden.shape[0]
    wide = min(256, units)

    def kernel(place_ref, *refs):
        d_rows, w, hidden, out = refs[:steps], refs[-3], refs[-2], refs[-1]
        total, correction = None, None
        for r in range(steps):
            which = lax.rem(place_ref[0] - r + steps, steps)
            term = lax.dot_general(
                d_rows[r][:, :depth], w[which], (((1,), (1,)), ((), ())), preferred_element_type=F32
            )
            share = column_of(d_rows[r][:, depth:], 1)
            total = term if total is None else total + term
            correction = share if correction is None else correction + share
        ratio = column_of(d_rows[0][:, depth:], 0)
        out[...] = (ratio * total - correction * hidden[...].astype(F32)).astype(BF16)

    return call(
        kernel,
        place,
        units // wide,
        [whole((rows, depth + EXTRA))] * steps
        + [
            pl.BlockSpec((steps, wide, depth), lambda n, place: (0, n, 0)),
            pl.BlockSpec((rows, wide), lambda n, place: (0, n)),
        ],
        pl.BlockSpec((rows, wide), lambda n, place: (0, n)),
        jax.ShapeDtypeStruct((rows, units), BF16),
        [],
        2 * steps * rows * units * depth,
        (*d_rows, w_in, hidden),
    )


def shards(hidden, w_in, embedding, depth_gain, w_out, codebook_ids):
    hids = lax.axis_size("hid")
    seqs = lax.axis_size("seq")
    steps, units, depth = w_in.shape
    entries = w_out.shape[2]
    rows = hidden.shape[0]
    part = rows // hids
    width_in = units * hids
    frames = rows * seqs
    halves = 2 if hids % 2 == 0 else 1
    block = entries // halves
    head_rows = w_out.shape[0]
    groups = seqs // steps
    i = lax.axis_index("seq")
    j = lax.axis_index("hid")
    step = i % steps
    half = j % halves
    owned = steps * part

    def along_hid(values, shift):
        return lax.ppermute(values, "hid", [(a, (a + shift) % hids) for a in range(hids)])

    def turn_hid(values, shift):
        return lax.ppermute(
            values,
            "hid",
            [(a, a - a % halves + (a % halves + shift) % halves) for a in range(hids)],
        )

    def flip_seq(values, flip):
        return lax.ppermute(
            values,
            "seq",
            [(a, a - a % steps + (a % steps + flip) % steps) for a in range(seqs)],
        )

    def gather_flips(values, position):
        out = jnp.broadcast_to(values, (steps,) + values.shape)
        for r in range(1, steps):
            out = lax.dynamic_update_index_in_dim(
                out, flip_seq(values, -r), (position + r) % steps, 0
            )
        return out

    place = jnp.stack([step, j, i // steps]).astype(jnp.int32)

    def along_groups(values, shift):
        return lax.ppermute(values, "seq", [(a, (a + shift * steps) % seqs) for a in range(seqs)])

    head_send = w_out.reshape(head_rows, steps, halves, block).transpose(2, 1, 0, 3)
    head_send = jnp.broadcast_to(head_send, (hids // halves,) + head_send.shape)
    head_send = head_send.reshape(hids, steps, head_rows, block)
    head_mid = lax.all_to_all(head_send, "hid", 0, 0).transpose(1, 0, 2, 3)

    ids = gather_flips(codebook_ids, step).transpose(1, 0, 2).reshape(steps, owned)
    ids_rows = [ids] + [turn_hid(ids, -k) for k in range(1, halves)]

    group = [hidden] + [flip_seq(hidden, -r) for r in range(1, steps)]
    proj, squares, *send = project(place, group, w_in, hids)
    received = [along_hid(send[shift - 1], shift) for shift in range(1, hids)]

    head_send = after(head_mid, *send).reshape(steps, hids * head_rows, block)
    head_send = jnp.broadcast_to(head_send, (groups,) + head_send.shape)
    head_send = head_send.reshape(seqs, hids * head_rows, block)
    head = lax.all_to_all(head_send, "seq", 0, 0).reshape(depth, block)

    before = jnp.maximum(step - 1, 0)
    table = pick(embedding, before)
    looked = jnp.take(table, pick(ids, before), axis=0)
    gain = pick(depth_gain, step)[None, :]
    proj, x_rows, normed, scale, ratio = normalise(
        place, proj, squares, received, looked, gain, width_in
    )

    turned = [after(hidden.T, normed)]
    turned += [along_groups(turned[0], r) for r in range(1, groups)]
    turned = [[t] + [flip_seq(t, m) for m in range(1, steps)] for t in turned]

    normed_rows = jnp.concatenate([normed] + [turn_hid(normed, -k) for k in range(1, halves)])
    targets = jnp.concatenate([pick(r, step) for r in ids_rows])
    logits = matmul(normed_rows, head, ((1,), (0,)))
    top = jnp.max(logits, axis=1)
    total = jnp.sum(jnp.exp(logits - top[:, None]), axis=1)
    stats = jnp.stack([top, total]).reshape(2, halves, -1)
    every = [stats] + [jnp.roll(turn_hid(stats, -t), t, axis=1) for t in range(1, halves)]
    tops = jnp.stack([e[0] for e in every]).reshape(halves, -1)
    totals = jnp.stack([e[1] for e in every]).reshape(halves, -1)
    top_all = jnp.max(tops, axis=0)
    lse = top_all + jnp.log(jnp.sum(totals * jnp.exp(tops - top_all), axis=0))
    entry = lax.broadcasted_iota(jnp.int32, logits.shape, 1) + half * block
    onehot = (targets[:, None] == entry).astype(F32)
    loss_weight = 2.0 * entries / frames
    d_logit = ((jnp.exp(logits - lse[:, None]) - onehot) * loss_weight).astype(BF16)

    d_norm_rows = matmul(d_logit, head, ((1,), (1,)))
    away = [d_norm_rows[k * owned : (k + 1) * owned].astype(BF16) for k in range(1, halves)]
    received = [turn_hid(a, k + 1) for k, a in enumerate(away)]
    d_round = row_gradient(
        place, d_norm_rows, received, x_rows, proj, scale, ratio, gain, width_in
    )

    part_out = matmul(normed_rows, after(d_logit, *received), ((0,), (0,))).astype(BF16)
    part_out = lax.all_to_all(part_out.reshape(seqs, depth // seqs, block), "seq", 0, 0)
    sums = sum_groups(place, part_out, steps, hids)
    sums = [along_hid(p, shift) if shift else p for shift, p in enumerate(sums)]
    grad_out = head_gradient(place, sums, halves)

    pieces = [d_round] + [along_hid(d_round, shift) for shift in range(1, hids)]
    scaled, mine, *others = spread(place, pieces, seqs, steps)
    scaled = lax.all_to_all(scaled, "seq", 0, 0)
    grad_in = input_gradient(place, turned, scaled, steps)
    mine = [mine] + [flip_seq(others[r - 1], r) for r in range(1, steps)]
    grad_hidden = hidden_gradient(place, mine, w_in, hidden)
    return (grad_hidden, grad_in, grad_out)


def solution(mesh):
    placed = (
        P("seq", "hid"),
        P(None, "hid", None),
        P(),
        P(),
        P(("seq", "hid"), None, None),
        P(None, ("seq", "hid")),
    )
    return jax.shard_map(
        shards,
        mesh=mesh,
        in_specs=placed,
        out_specs=(P("seq", "hid"), P(None, "hid", "seq"), P(("seq", "hid"), None, None)),
        check_vma=False,
    )
```

```python
import jax
import jax.numpy as jnp
from jax import lax
from jax.experimental import pallas as pl
from jax.experimental.pallas import tpu as pltpu
from jax.sharding import PartitionSpec as P

F32 = jnp.float32
BF16 = jnp.bfloat16


def pick(values, index):
    return lax.dynamic_index_in_dim(values, index, axis=0, keepdims=False)


def matmul(a, b, contract):
    return lax.dot_general(a, b, (contract, ((), ())), preferred_element_type=F32)


def after(value, *others):
    return lax.optimization_barrier((value, *others))[0]


VMEM = pltpu.CompilerParams(vmem_limit_bytes=60 * 2**20)


def whole(shape):
    return pl.BlockSpec(shape, lambda n, place: (0,) * len(shape))


def rows_of(shape, some):
    return pl.BlockSpec((some, shape[1]), lambda n, place: (n, 0))


def call(kernel, place, grid, in_specs, out_specs, out_shape, scratch, flops, args):
    moved = sum(a.size * a.dtype.itemsize for a in args)
    return pl.pallas_call(
        kernel,
        grid_spec=pltpu.PrefetchScalarGridSpec(
            num_scalar_prefetch=1,
            grid=(grid,),
            in_specs=in_specs,
            out_specs=out_specs,
            scratch_shapes=scratch,
        ),
        out_shape=out_shape,
        compiler_params=VMEM,
        cost_estimate=pl.CostEstimate(flops=flops, bytes_accessed=moved, transcendentals=0),
    )(place, *args)


EXTRA = 128


def parts_of(columns, count):
    rows = columns[0].shape[0]
    lane = lax.broadcasted_iota(jnp.int32, (rows, EXTRA), 1)
    out = jnp.zeros((rows, EXTRA), F32)
    for c in range(count):
        left = columns[c]
        for k in range(3):
            piece = left.astype(BF16).astype(F32)
            left = left - piece
            out = jnp.where(lane == 3 * c + k, piece, out)
    return out.astype(BF16)


def column_of(extra, c):
    return sum(extra[:, 3 * c + k : 3 * c + k + 1].astype(F32) for k in (2, 1, 0))


def project(place, group, w_in, hids):
    steps = len(group)
    rows, units = group[0].shape
    depth = w_in.shape[2]
    part = rows // hids
    owned = steps * part
    wide = min(256, depth)

    def kernel(place_ref, *refs):
        hidden, w, own, squares = refs[:steps], refs[steps], refs[steps + 1], refs[steps + 2]
        sends, sums, totals = refs[steps + 3 : -2], refs[-2], refs[-1]
        n, step, j = pl.program_id(0), place_ref[0], place_ref[1]
        for m in range(steps):
            sums[m] = jnp.dot(hidden[m][...], w[0], preferred_element_type=F32)
        columns = pl.ds(pl.multiple_of(n * wide, wide), wide)
        for shift in range(hids):
            out = own if shift == 0 else sends[shift - 1]
            start = pl.multiple_of(lax.rem(j + shift, hids) * part, part)
            for m in range(steps):
                to = pl.multiple_of(lax.rem(step + m, steps) * part, part)
                out[pl.ds(to, part), columns] = sums[m, pl.ds(start, part), :].astype(out.dtype)

        @pl.when(n == 0)
        def _():
            for m in range(steps):
                values = hidden[m][...].astype(F32)
                totals[m] = jnp.sum(values * values, axis=1, keepdims=True)
            for shift in range(hids):
                start = pl.multiple_of(lax.rem(j + shift, hids) * part, part)
                for m in range(steps):
                    to = pl.multiple_of(lax.rem(step + m, steps) * part, part)
                    total = totals[m, pl.ds(start, part), :]
                    if shift == 0:
                        squares[pl.ds(to, part), :] = total
                    else:
                        sends[shift - 1][pl.ds(to, part), depth:] = parts_of([total], 1)

    return call(
        kernel,
        place,
        depth // wide,
        [whole((rows, units))] * steps
        + [pl.BlockSpec((1, units, wide), lambda n, place: (place[0], 0, n))],
        [whole((owned, depth)), whole((owned, 1))] + [whole((owned, depth + EXTRA))] * (hids - 1),
        [
            jax.ShapeDtypeStruct((owned, depth), F32),
            jax.ShapeDtypeStruct((owned, 1), F32),
        ]
        + [jax.ShapeDtypeStruct((owned, depth + EXTRA), BF16)] * (hids - 1),
        [pltpu.VMEM((steps, rows, wide), F32), pltpu.VMEM((steps, rows, 1), F32)],
        2 * steps * rows * units * depth,
        (*group, w_in),
    )


def normalise(place, proj, squares, received, looked, gain, width_in):
    owned, depth = proj.shape
    count = len(received)
    some = min(32, owned)

    def kernel(place_ref, *refs):
        proj, squares, looked, gain = refs[0], refs[1], refs[2 + count], refs[3 + count]
        proj_out, x_out, normed_out, scale_out, ratio_out = refs[4 + count :]
        total, square = proj[...], squares[...]
        for r in refs[2 : 2 + count]:
            total = total + r[:, :depth].astype(F32)
            square = square + column_of(r[:, depth:], 0)
        ratio = lax.rsqrt(square * (1.0 / width_in) + 1e-06)
        x = ratio * total + jnp.where(place_ref[0] > 0, looked[...].astype(F32), 0.0)
        scale = lax.rsqrt(jnp.sum(x * x, axis=1, keepdims=True) * (1.0 / depth) + 1e-06)
        proj_out[...] = total
        x_out[...] = x
        normed_out[...] = (x * scale * gain[...]).astype(BF16)
        scale_out[...] = scale
        ratio_out[...] = ratio

    args = (proj, squares, *received, looked, gain)
    full, column = (owned, depth), (owned, 1)
    shapes = [(full, F32), (full, F32), (full, BF16), (column, F32), (column, F32)]
    return call(
        kernel,
        place,
        owned // some,
        [rows_of(a.shape, some) for a in args[:-1]] + [whole(gain.shape)],
        [rows_of(shape, some) for shape, _ in shapes],
        [jax.ShapeDtypeStruct(shape, dtype) for shape, dtype in shapes],
        [],
        10 * owned * depth,
        args,
    )


def row_gradient(place, d_norm, received, x_rows, proj, scale, ratio, gain, width_in):
    owned, depth = x_rows.shape

    def kernel(place_ref, *refs):
        d_norm, received = refs[0], refs[1 : 1 + len_received]
        x_ref, proj_ref, scale_ref, ratio_ref, gain_ref, out = refs[1 + len_received :]
        gated = d_norm[...]
        for r in received:
            gated = gated + r[...].astype(F32)
        gated = gated * gain_ref[...]
        x, scale, ratio = x_ref[...], scale_ref[...], ratio_ref[...]
        mean = jnp.sum(gated * x, axis=1, keepdims=True) * (1.0 / depth)
        d_x = scale * gated - x * (scale * scale * scale * mean)
        out[:, :depth] = d_x.astype(BF16)
        d_ratio = jnp.sum(d_x * proj_ref[...], axis=1, keepdims=True)
        correction = ratio * ratio * ratio * d_ratio * (1.0 / width_in)
        out[:, depth:] = parts_of([ratio, correction], 2)

    len_received = len(received)
    some = min(32, owned)
    args = (d_norm, *received, x_rows, proj, scale, ratio, gain)
    return call(
        kernel,
        place,
        owned // some,
        [rows_of(a.shape, some) for a in args[:-1]] + [whole(gain.shape)],
        rows_of((owned, depth + EXTRA), some),
        jax.ShapeDtypeStruct((owned, depth + EXTRA), BF16),
        [],
        10 * owned * depth,
        args,
    )


def input_gradient(place, pieces, turned, seqs):
    hids, steps = len(pieces), len(turned)
    owned, full = pieces[0].shape
    depth = full - EXTRA
    units, rows = turned[0].shape
    part = owned // steps
    slice_wide = depth // seqs
    wide = max(min(256, depth), slice_wide)
    count = wide // slice_wide

    def kernel(place_ref, *refs):
        chunks, extras, turned = refs[:hids], refs[hids : 2 * hids], refs[2 * hids : 2 * hids + steps]
        out, plain, scaled = refs[2 * hids + steps], refs[2 * hids + steps + 1 : -1], refs[-1]
        n, step, j = pl.program_id(0), place_ref[0], place_ref[1]
        columns = pl.ds(pl.multiple_of(n * wide, wide), wide)
        for r in range(hids):
            to = pl.multiple_of(lax.rem(j - r + hids, hids) * part, part)
            for m in range(steps):
                start = pl.multiple_of(lax.rem(step + m, steps) * part, part)
                values = chunks[r][pl.ds(start, part), :]
                plain[m][pl.ds(to, part), columns] = values
                ratio = column_of(extras[r][pl.ds(start, part), :], 0)
                scaled[m, pl.ds(to, part), :] = (values.astype(F32) * ratio).astype(BF16)

        @pl.when(n == 0)
        def _():
            for r in range(hids):
                to = pl.multiple_of(lax.rem(j - r + hids, hids) * part, part)
                for m in range(steps):
                    start = pl.multiple_of(lax.rem(step + m, steps) * part, part)
                    plain[m][pl.ds(to, part), depth:] = extras[r][pl.ds(start, part), :]

        total = jnp.dot(turned[0][...], scaled[0], preferred_element_type=F32)
        for m in range(1, steps):
            total = total + jnp.dot(turned[m][...], scaled[m], preferred_element_type=F32)
        for k in range(count):
            out[k] = total[:, k * slice_wide : (k + 1) * slice_wide].astype(BF16)

    return call(
        kernel,
        place,
        depth // wide,
        [pl.BlockSpec((owned, wide), lambda n, place: (0, n))] * hids
        + [pl.BlockSpec((owned, EXTRA), lambda n, place: (0, depth // EXTRA))] * hids
        + [whole((units, rows))] * steps,
        [pl.BlockSpec((count, units, slice_wide), lambda n, place: (n, 0, 0))]
        + [whole((rows, full))] * steps,
        [jax.ShapeDtypeStruct((seqs, units, slice_wide), BF16)]
        + [jax.ShapeDtypeStruct((rows, full), BF16)] * steps,
        [pltpu.VMEM((steps, rows, wide), BF16)],
        2 * steps * rows * units * depth,
        (*pieces, *pieces, *turned),
    )


def sum_groups(place, received, steps, hids):
    seqs, rows, entries = received.shape
    groups = seqs // steps
    part = rows // hids
    wide = min(256, entries)

    def kernel(place_ref, received, *outs):
        for shift in range(hids):
            start = pl.multiple_of(lax.rem(place_ref[1] + shift, hids) * part, part)
            for s in range(steps):
                total = received[s, pl.ds(start, part), :].astype(F32)
                for g in range(1, groups):
                    total = total + received[g * steps + s, pl.ds(start, part), :].astype(F32)
                outs[shift][s] = total.astype(BF16)

    return call(
        kernel,
        place,
        entries // wide,
        [pl.BlockSpec((seqs, rows, wide), lambda n, place: (0, 0, n))],
        [pl.BlockSpec((steps, part, wide), lambda n, place: (0, 0, n))] * hids,
        [jax.ShapeDtypeStruct((steps, part, entries), BF16)] * hids,
        [],
        seqs * rows * entries,
        (received,),
    )


def head_gradient(place, pieces, halves):
    hids = len(pieces)
    steps, rows, block = pieces[0].shape

    def kernel(place_ref, *refs):
        pieces, out = refs[:-1], refs[-1]
        for r in range(halves):
            which = lax.rem(place_ref[1] - r + hids, halves)
            columns = pl.ds(pl.multiple_of(which * block, block), block)
            for s in range(steps):
                total = pieces[r][s].astype(F32)
                for k in range(r + halves, hids, halves):
                    total = total + pieces[k][s].astype(F32)
                out[:, s, columns] = total

    return call(
        kernel,
        place,
        1,
        [whole((steps, rows, block))] * hids,
        whole((rows, steps, halves * block)),
        jax.ShapeDtypeStruct((rows, steps, halves * block), F32),
        [],
        hids * steps * rows * block,
        tuple(pieces),
    )


def hidden_gradient(place, d_rows, w_in, hidden):
    steps, units, depth = w_in.shape
    rows = hidden.shape[0]
    wide = min(256, units)

    def kernel(place_ref, *refs):
        d_rows, w, hidden, out = refs[:steps], refs[-3], refs[-2], refs[-1]
        total, correction = None, None
        for r in range(steps):
            which = lax.rem(place_ref[0] - r + steps, steps)
            term = lax.dot_general(
                d_rows[r][:, :depth], w[which], (((1,), (1,)), ((), ())), preferred_element_type=F32
            )
            share = column_of(d_rows[r][:, depth:], 1)
            total = term if total is None else total + term
            correction = share if correction is None else correction + share
        ratio = column_of(d_rows[0][:, depth:], 0)
        out[...] = (ratio * total - correction * hidden[...].astype(F32)).astype(BF16)

    return call(
        kernel,
        place,
        units // wide,
        [whole((rows, depth + EXTRA))] * steps
        + [
            pl.BlockSpec((steps, wide, depth), lambda n, place: (0, n, 0)),
            pl.BlockSpec((rows, wide), lambda n, place: (0, n)),
        ],
        pl.BlockSpec((rows, wide), lambda n, place: (0, n)),
        jax.ShapeDtypeStruct((rows, units), BF16),
        [],
        2 * steps * rows * units * depth,
        (*d_rows, w_in, hidden),
    )


def shards(hidden, w_in, embedding, depth_gain, w_out, codebook_ids):
    hids = lax.axis_size("hid")
    seqs = lax.axis_size("seq")
    steps, units, depth = w_in.shape
    entries = w_out.shape[2]
    rows = hidden.shape[0]
    part = rows // hids
    width_in = units * hids
    frames = rows * seqs
    halves = 2 if hids % 2 == 0 else 1
    block = entries // halves
    head_rows = w_out.shape[0]
    groups = seqs // steps
    i = lax.axis_index("seq")
    j = lax.axis_index("hid")
    step = i % steps
    half = j % halves
    owned = steps * part

    def along_hid(values, shift):
        return lax.ppermute(values, "hid", [(a, (a + shift) % hids) for a in range(hids)])

    def turn_hid(values, shift):
        return lax.ppermute(
            values,
            "hid",
            [(a, a - a % halves + (a % halves + shift) % halves) for a in range(hids)],
        )

    def flip_seq(values, flip):
        return lax.ppermute(
            values,
            "seq",
            [(a, a - a % steps + (a % steps + flip) % steps) for a in range(seqs)],
        )

    def gather_flips(values, position):
        out = jnp.broadcast_to(values, (steps,) + values.shape)
        for r in range(1, steps):
            out = lax.dynamic_update_index_in_dim(
                out, flip_seq(values, -r), (position + r) % steps, 0
            )
        return out

    place = jnp.stack([step, j, i // steps]).astype(jnp.int32)

    head_send = w_out.reshape(head_rows, steps, halves, block).transpose(2, 1, 0, 3)
    head_send = jnp.broadcast_to(head_send, (hids // halves,) + head_send.shape)
    head_send = head_send.reshape(hids, steps, head_rows, block)
    head_mid = lax.all_to_all(head_send, "hid", 0, 0).transpose(1, 0, 2, 3)

    ids = gather_flips(codebook_ids, step).transpose(1, 0, 2).reshape(steps, owned)
    ids_rows = [ids] + [turn_hid(ids, -k) for k in range(1, halves)]

    before = jnp.maximum(step - 1, 0)
    looked = jnp.take(pick(embedding, before), pick(ids, before), axis=0)

    group = [hidden] + [flip_seq(hidden, -r) for r in range(1, steps)]
    proj, squares, *send = project(after(place, looked), group, w_in, hids)
    received = [along_hid(send[shift - 1], shift) for shift in range(1, hids)]

    head_send = after(head_mid, *send).reshape(steps, hids * head_rows, block)
    head_send = jnp.broadcast_to(head_send, (groups,) + head_send.shape)
    head_send = head_send.reshape(seqs, hids * head_rows, block)
    head = lax.all_to_all(head_send, "seq", 0, 0).reshape(depth, block)

    gain = pick(depth_gain, step)[None, :]
    proj, x_rows, normed, scale, ratio = normalise(
        place, proj, squares, received, looked, gain, width_in
    )

    normed_rows = jnp.concatenate([normed] + [turn_hid(normed, -k) for k in range(1, halves)])
    targets = jnp.concatenate([pick(r, step) for r in ids_rows])
    logits = matmul(normed_rows, head, ((1,), (0,)))
    top = jnp.max(logits, axis=1)
    total = jnp.sum(jnp.exp(logits - top[:, None]), axis=1)
    stats = jnp.stack([top, total]).reshape(2, halves, -1)
    every = [stats] + [jnp.roll(turn_hid(stats, -t), t, axis=1) for t in range(1, halves)]
    tops = jnp.stack([e[0] for e in every]).reshape(halves, -1)
    totals = jnp.stack([e[1] for e in every]).reshape(halves, -1)
    top_all = jnp.max(tops, axis=0)
    lse = top_all + jnp.log(jnp.sum(totals * jnp.exp(tops - top_all), axis=0))
    entry = lax.broadcasted_iota(jnp.int32, logits.shape, 1) + half * block
    onehot = (targets[:, None] == entry).astype(F32)
    loss_weight = 2.0 * entries / frames
    d_logit = ((jnp.exp(logits - lse[:, None]) - onehot) * loss_weight).astype(BF16)

    d_norm_rows = matmul(d_logit, head, ((1,), (1,)))
    away = [d_norm_rows[k * owned : (k + 1) * owned].astype(BF16) for k in range(1, halves)]
    received = [turn_hid(a, k + 1) for k, a in enumerate(away)]
    d_round = row_gradient(
        place, d_norm_rows, received, x_rows, proj, scale, ratio, gain, width_in
    )

    part_out = matmul(normed_rows, after(d_logit, *received), ((0,), (0,))).astype(BF16)
    part_out = lax.all_to_all(part_out.reshape(seqs, depth // seqs, block), "seq", 0, 0)
    sums = sum_groups(place, part_out, steps, hids)
    sums = [along_hid(p, shift) if shift else p for shift, p in enumerate(sums)]
    grad_out = head_gradient(place, sums, halves)

    turned = [after(h, normed).T for h in group]
    pieces = [d_round] + [along_hid(d_round, shift) for shift in range(1, hids)]
    grad_in, mine, *others = input_gradient(place, pieces, turned, seqs)
    grad_in = lax.all_to_all(grad_in, "seq", 0, 0)
    grad_in = grad_in.reshape(groups, steps, units, depth // seqs).astype(F32).sum(0)
    mine = [mine] + [flip_seq(others[r - 1], r) for r in range(1, steps)]
    grad_hidden = hidden_gradient(place, mine, w_in, hidden)
    return (grad_hidden, grad_in, grad_out)


def solution(mesh):
    placed = (
        P("seq", "hid"),
        P(None, "hid", None),
        P(),
        P(),
        P(("seq", "hid"), None, None),
        P(None, ("seq", "hid")),
    )
    return jax.shard_map(
        shards,
        mesh=mesh,
        in_specs=placed,
        out_specs=(P("seq", "hid"), P(None, "hid", "seq"), P(("seq", "hid"), None, None)),
        check_vma=False,
    )
```

```python
import jax
import jax.numpy as jnp
from jax import lax
from jax.experimental import pallas as pl
from jax.experimental.pallas import tpu as pltpu
from jax.sharding import PartitionSpec as P

F32 = jnp.float32
BF16 = jnp.bfloat16


def pick(values, index):
    return lax.dynamic_index_in_dim(values, index, axis=0, keepdims=False)


def matmul(a, b, contract):
    return lax.dot_general(a, b, (contract, ((), ())), preferred_element_type=F32)


def after(value, *others):
    return lax.optimization_barrier((value, *others))[0]


VMEM = pltpu.CompilerParams(vmem_limit_bytes=16 * 2**20)


def whole(shape):
    return pl.BlockSpec(shape, lambda n, place: (0,) * len(shape))


def call(kernel, place, grid, in_specs, out_specs, out_shape, scratch, flops, args):
    moved = sum(a.size * a.dtype.itemsize for a in args)
    return pl.pallas_call(
        kernel,
        grid_spec=pltpu.PrefetchScalarGridSpec(
            num_scalar_prefetch=1,
            grid=(grid,),
            in_specs=in_specs,
            out_specs=out_specs,
            scratch_shapes=scratch,
        ),
        out_shape=out_shape,
        compiler_params=VMEM,
        cost_estimate=pl.CostEstimate(flops=flops, bytes_accessed=moved, transcendentals=0),
    )(place, *args)


EXACT = 3


def parts_of(values):
    out = []
    for _ in range(EXACT):
        piece = lax.reduce_precision(values, 8, 7)
        values = values - piece
        out.append(piece.astype(BF16))
    return out


def head_gradient(place, pieces, halves):
    hids = len(pieces)
    steps, rows, block = pieces[0].shape

    def kernel(place_ref, *refs):
        pieces, out = refs[:-1], refs[-1]
        for r in range(halves):
            which = lax.rem(place_ref[1] - r + hids, halves)
            columns = pl.ds(pl.multiple_of(which * block, block), block)
            for s in range(steps):
                total = pieces[r][s].astype(F32)
                for k in range(r + halves, hids, halves):
                    total = total + pieces[k][s].astype(F32)
                out[:, s, columns] = total

    return call(
        kernel,
        place,
        1,
        [whole((steps, rows, block))] * hids,
        whole((rows, steps, halves * block)),
        jax.ShapeDtypeStruct((rows, steps, halves * block), F32),
        [],
        hids * steps * rows * block,
        tuple(pieces),
    )


def shards(hidden, w_in, embedding, depth_gain, w_out, codebook_ids):
    hids = lax.axis_size("hid")
    seqs = lax.axis_size("seq")
    steps, units, depth = w_in.shape
    entries = w_out.shape[2]
    rows = hidden.shape[0]
    part = rows // hids
    width_in = units * hids
    frames = rows * seqs
    halves = 2 if hids % 2 == 0 else 1
    block = entries // halves
    head_rows = w_out.shape[0]
    groups = seqs // steps
    i = lax.axis_index("seq")
    j = lax.axis_index("hid")
    step = i % steps
    half = j % halves
    owned = steps * part

    def along_hid(values, shift):
        return lax.ppermute(values, "hid", [(a, (a + shift) % hids) for a in range(hids)])

    def turn_hid(values, shift):
        return lax.ppermute(
            values,
            "hid",
            [(a, a - a % halves + (a % halves + shift) % halves) for a in range(hids)],
        )

    def flip_seq(values, flip):
        return lax.ppermute(
            values,
            "seq",
            [(a, a - a % steps + (a % steps + flip) % steps) for a in range(seqs)],
        )

    place = jnp.stack([step, j]).astype(jnp.int32)
    relations = range(1, steps)

    squares_part = jnp.sum(jnp.square(hidden.astype(F32)), axis=1)
    tail = 8 * block
    small = jnp.concatenate(parts_of(squares_part))
    small = jnp.pad(small, (0, tail - small.size)).reshape(1, 1, 8, block)
    head_send = w_out.reshape(head_rows, steps, halves, block).transpose(2, 1, 0, 3)
    head_send = head_send.reshape(1, halves, steps * head_rows, block)
    small = jnp.broadcast_to(small, (1, halves, 8, block))
    head_send = jnp.concatenate([head_send, small], axis=2)
    head_send = jnp.broadcast_to(head_send, (hids // halves,) + head_send.shape[1:])
    head_send = head_send.reshape(hids, steps * head_rows + 8, block)
    head_got = lax.all_to_all(head_send, "hid", 0, 0)
    head_mid = head_got[:, : steps * head_rows].reshape(hids, steps, head_rows, block)
    squares = head_got[:, steps * head_rows :].reshape(hids, tail)[:, : EXACT * rows]
    squares = jnp.sum(squares.astype(F32).reshape(hids * EXACT, rows), axis=0)

    ids = jnp.concatenate([codebook_ids] + [flip_seq(codebook_ids, -m) for m in relations], axis=1)
    ids_rows = [ids] + [turn_hid(ids, -k) for k in range(1, halves)]
    before = jnp.maximum(step - 1, 0)
    looked = jnp.take(pick(embedding, before), pick(ids, before), axis=0)

    group = [hidden] + [after(flip_seq(hidden, -m), looked) for m in relations]
    w_own = pick(w_in, step)
    proj_parts = matmul(jnp.concatenate(group), w_own, ((1,), (0,)))
    proj_parts = proj_parts.reshape(steps, hids, part, depth)

    def owner_block(index):
        return lax.dynamic_index_in_dim(proj_parts, index, 1, False).reshape(owned, depth)

    send = [owner_block((j + shift) % hids).astype(BF16) for shift in range(1, hids)]
    received = [along_hid(send[shift - 1], shift) for shift in range(1, hids)]

    head_send = after(head_mid, *send).transpose(1, 0, 2, 3)
    head_send = head_send.reshape(steps, hids * head_rows, block)
    head_send = jnp.broadcast_to(head_send, (groups,) + head_send.shape)
    head_send = head_send.reshape(seqs, hids * head_rows, block)
    head = lax.all_to_all(head_send, "seq", 0, 0).reshape(depth, block)

    squares = jnp.stack([squares] + [flip_seq(squares, -m) for m in relations])
    ratio_group = lax.rsqrt(squares / width_in + 1e-06).reshape(steps, hids, part)
    order = [(j - shift) % hids for shift in range(hids)]

    ratio = lax.dynamic_index_in_dim(ratio_group, j, 1, False).reshape(owned, 1)
    proj = owner_block(j)
    for r in received:
        proj += r.astype(F32)
    x_rows = ratio * proj + jnp.where(step > 0, looked.astype(F32), 0.0)
    scale = lax.rsqrt(jnp.mean(x_rows * x_rows, axis=1, keepdims=True) + 1e-06)
    gain = pick(depth_gain, step)[None, :]
    normed = (x_rows * scale * gain).astype(BF16)

    normed_rows = jnp.concatenate([normed] + [turn_hid(normed, -k) for k in range(1, halves)])
    targets = jnp.concatenate([pick(r, step) for r in ids_rows])
    logits = matmul(normed_rows, head, ((1,), (0,)))
    top = jnp.max(logits, axis=1)
    total = jnp.sum(jnp.exp(logits - top[:, None]), axis=1)
    stats = jnp.stack([top, total]).reshape(2, halves, -1)
    every = [stats] + [jnp.roll(turn_hid(stats, -t), t, axis=1) for t in range(1, halves)]
    tops = jnp.stack([e[0] for e in every]).reshape(halves, -1)
    totals = jnp.stack([e[1] for e in every]).reshape(halves, -1)
    top_all = jnp.max(tops, axis=0)
    lse = top_all + jnp.log(jnp.sum(totals * jnp.exp(tops - top_all), axis=0))
    entry = lax.broadcasted_iota(jnp.int32, logits.shape, 1) + half * block
    onehot = (targets[:, None] == entry).astype(F32)
    loss_weight = 2.0 * entries / frames
    d_logit = ((jnp.exp(logits - lse[:, None]) - onehot) * loss_weight).astype(BF16)

    d_norm_rows = matmul(d_logit, head, ((1,), (1,)))
    away = [d_norm_rows[k * owned : (k + 1) * owned].astype(BF16) for k in range(1, halves)]
    received = [turn_hid(a, k + 1) for k, a in enumerate(away)]
    d_norm = d_norm_rows[:owned]
    for r in received:
        d_norm += r.astype(F32)
    gated = gain * d_norm
    d_x = scale * gated - x_rows * scale**3 * jnp.mean(gated * x_rows, axis=1, keepdims=True)
    d_round = d_x.astype(BF16)
    d_ratio_part = jnp.sum(d_x * proj, axis=1).reshape(steps, part)

    part_out = matmul(normed_rows, after(d_logit, *received), ((0,), (0,))).astype(BF16)
    part_out = lax.all_to_all(part_out.reshape(seqs, depth // seqs, block), "seq", 0, 0)
    part_out = part_out.reshape(groups, steps, hids, head_rows, block).astype(F32).sum(0)
    part_out = part_out.astype(BF16)
    sums = [
        lax.dynamic_index_in_dim(part_out, (j + shift) % hids, 1, False) for shift in range(hids)
    ]
    sums = [along_hid(p, shift) if shift else p for shift, p in enumerate(sums)]
    grad_out = head_gradient(place, sums, halves)

    pieces = [d_round] + [along_hid(d_round, shift) for shift in range(1, hids)]
    ordered = [g.reshape(hids, part, units) for g in group]
    hidden_rows = jnp.concatenate([pick(g, o) for o in order for g in ordered])
    ratio_rows = [
        lax.dynamic_index_in_dim(ratio_group, o, 1, False).reshape(owned, 1) for o in order
    ]
    scaled = jnp.concatenate(
        [(r * p.astype(F32)).astype(BF16) for r, p in zip(ratio_rows, pieces)]
    )
    share = matmul(scaled, hidden_rows, ((0,), (0,))).astype(BF16)
    share = lax.all_to_all(share.reshape(seqs, depth // seqs, units), "seq", 0, 0)
    share = share.reshape(groups, steps, depth // seqs, units).astype(F32).sum(0)
    grad_in = share.transpose(0, 2, 1)

    d_ratio = d_ratio_part[0]
    for m in relations:
        d_ratio += flip_seq(d_ratio_part[m], m)
    d_ratio = [d_ratio] + [along_hid(d_ratio, shift) for shift in range(1, hids)]
    d_ratio = jnp.concatenate(d_ratio[::-1])[:, None]
    back_rows = jnp.zeros((steps, rows, depth), BF16)
    for m in range(steps):
        member = jnp.concatenate([p[m * part : (m + 1) * part] for p in pieces[::-1]])
        member = flip_seq(member, m) if m else member
        back_rows = lax.dynamic_update_index_in_dim(back_rows, member, (step - m) % steps, 0)
    back = matmul(back_rows[0], w_in[0], ((1,), (1,)))
    for s in range(1, steps):
        back += matmul(back_rows[s], w_in[s], ((1,), (1,)))
    ratio_own = jnp.concatenate([r[:part] for r in ratio_rows[::-1]])
    hidden_own = jnp.concatenate([pick(ordered[0], o) for o in order[::-1]]).astype(F32)
    correction = ratio_own**3 * d_ratio / width_in
    grad_hidden = (ratio_own * back - correction * hidden_own).astype(BF16)
    grad_hidden = jnp.concatenate([grad_hidden, grad_hidden])
    grad_hidden = lax.dynamic_slice_in_dim(grad_hidden, (hids - 1 - j) * part, rows, 0)
    return (grad_hidden, grad_in, grad_out)


def solution(mesh):
    placed = (
        P("seq", "hid"),
        P(None, "hid", None),
        P(),
        P(),
        P(("seq", "hid"), None, None),
        P(None, ("seq", "hid")),
    )
    return jax.shard_map(
        shards,
        mesh=mesh,
        in_specs=placed,
        out_specs=(P("seq", "hid"), P(None, "hid", "seq"), P(("seq", "hid"), None, None)),
        check_vma=False,
    )
```

```python
import jax
import jax.numpy as jnp
from jax import lax
from jax.experimental import pallas as pl
from jax.experimental.pallas import tpu as pltpu
from jax.sharding import PartitionSpec as P

F32 = jnp.float32
BF16 = jnp.bfloat16


def pick(values, index):
    return lax.dynamic_index_in_dim(values, index, axis=0, keepdims=False)


def matmul(a, b, contract):
    return lax.dot_general(a, b, (contract, ((), ())), preferred_element_type=F32)


def after(value, *others):
    return lax.optimization_barrier((value, *others))[0]


VMEM = pltpu.CompilerParams(vmem_limit_bytes=16 * 2**20)


def whole(shape):
    return pl.BlockSpec(shape, lambda n, place: (0,) * len(shape))


def call(kernel, place, grid, in_specs, out_specs, out_shape, scratch, flops, args):
    moved = sum(a.size * a.dtype.itemsize for a in args)
    return pl.pallas_call(
        kernel,
        grid_spec=pltpu.PrefetchScalarGridSpec(
            num_scalar_prefetch=1,
            grid=(grid,),
            in_specs=in_specs,
            out_specs=out_specs,
            scratch_shapes=scratch,
        ),
        out_shape=out_shape,
        compiler_params=VMEM,
        cost_estimate=pl.CostEstimate(flops=flops, bytes_accessed=moved, transcendentals=0),
    )(place, *args)


EXACT = 3


def parts_of(values):
    out = []
    for _ in range(EXACT):
        piece = lax.reduce_precision(values, 8, 7)
        values = values - piece
        out.append(piece.astype(BF16))
    return out


def head_gradient(place, pieces, halves):
    hids = len(pieces)
    steps, rows, block = pieces[0].shape

    def kernel(place_ref, *refs):
        pieces, out = refs[:-1], refs[-1]
        for r in range(halves):
            which = lax.rem(place_ref[1] - r + hids, halves)
            columns = pl.ds(pl.multiple_of(which * block, block), block)
            for s in range(steps):
                total = pieces[r][s].astype(F32)
                for k in range(r + halves, hids, halves):
                    total = total + pieces[k][s].astype(F32)
                out[:, s, columns] = total

    return call(
        kernel,
        place,
        1,
        [whole((steps, rows, block))] * hids,
        whole((rows, steps, halves * block)),
        jax.ShapeDtypeStruct((rows, steps, halves * block), F32),
        [],
        hids * steps * rows * block,
        tuple(pieces),
    )


def shards(hidden, w_in, embedding, depth_gain, w_out, codebook_ids):
    hids = lax.axis_size("hid")
    seqs = lax.axis_size("seq")
    steps, units, depth = w_in.shape
    entries = w_out.shape[2]
    rows = hidden.shape[0]
    part = rows // hids
    width_in = units * hids
    frames = rows * seqs
    halves = 2 if hids % 2 == 0 else 1
    block = entries // halves
    head_rows = w_out.shape[0]
    groups = seqs // steps
    i = lax.axis_index("seq")
    j = lax.axis_index("hid")
    step = i % steps
    half = j % halves
    owned = steps * part

    def along_hid(values, shift):
        return lax.ppermute(values, "hid", [(a, (a + shift) % hids) for a in range(hids)])

    def turn_hid(values, shift):
        return lax.ppermute(
            values,
            "hid",
            [(a, a - a % halves + (a % halves + shift) % halves) for a in range(hids)],
        )

    def flip_seq(values, flip):
        return lax.ppermute(
            values,
            "seq",
            [(a, a - a % steps + (a % steps + flip) % steps) for a in range(seqs)],
        )

    place = jnp.stack([step, j]).astype(jnp.int32)
    relations = range(1, steps)

    group = [hidden] + [flip_seq(hidden, -m) for m in relations]

    squares_part = jnp.sum(jnp.square(hidden.astype(F32)), axis=1)
    tail = 8 * block
    small = jnp.concatenate(parts_of(squares_part))
    small = jnp.pad(small, (0, tail - small.size)).reshape(1, 1, 8, block)
    head_send = after(w_out, *group[1:]).reshape(head_rows, steps, halves, block)
    head_send = head_send.transpose(2, 1, 0, 3)
    head_send = head_send.reshape(1, halves, steps * head_rows, block)
    small = jnp.broadcast_to(small, (1, halves, 8, block))
    head_send = jnp.concatenate([head_send, small], axis=2)
    head_send = jnp.broadcast_to(head_send, (hids // halves,) + head_send.shape[1:])
    head_send = head_send.reshape(hids, steps * head_rows + 8, block)
    head_got = lax.all_to_all(head_send, "hid", 0, 0)
    head_mid = head_got[:, : steps * head_rows].reshape(hids, steps, head_rows, block)
    squares = head_got[:, steps * head_rows :].reshape(hids, tail)[:, : EXACT * rows]
    squares = jnp.sum(squares.astype(F32).reshape(hids * EXACT, rows), axis=0)

    ids = jnp.concatenate([codebook_ids] + [flip_seq(codebook_ids, -m) for m in relations], axis=1)
    ids_rows = [ids] + [turn_hid(ids, -k) for k in range(1, halves)]
    before = jnp.maximum(step - 1, 0)
    looked = jnp.take(pick(embedding, before), pick(ids, before), axis=0)

    w_own = pick(w_in, step)
    proj_parts = matmul(jnp.concatenate(group), w_own, ((1,), (0,)))
    proj_parts = proj_parts.reshape(steps, hids, part, depth)

    def owner_block(index):
        return lax.dynamic_index_in_dim(proj_parts, index, 1, False).reshape(owned, depth)

    send = [owner_block((j + shift) % hids).astype(BF16) for shift in range(1, hids)]
    received = [along_hid(send[shift - 1], shift) for shift in range(1, hids)]

    head_send = after(head_mid, *send).transpose(1, 0, 2, 3)
    head_send = head_send.reshape(steps, hids * head_rows, block)
    head_send = jnp.broadcast_to(head_send, (groups,) + head_send.shape)
    head_send = head_send.reshape(seqs, hids * head_rows, block)
    head = lax.all_to_all(head_send, "seq", 0, 0).reshape(depth, block)

    squares = jnp.stack([squares] + [flip_seq(squares, -m) for m in relations])
    ratio_group = lax.rsqrt(squares / width_in + 1e-06).reshape(steps, hids, part)
    order = [(j - shift) % hids for shift in range(hids)]

    ratio = lax.dynamic_index_in_dim(ratio_group, j, 1, False).reshape(owned, 1)
    proj = owner_block(j)
    for r in received:
        proj += r.astype(F32)
    x_rows = ratio * proj + jnp.where(step > 0, looked.astype(F32), 0.0)
    scale = lax.rsqrt(jnp.mean(x_rows * x_rows, axis=1, keepdims=True) + 1e-06)
    gain = pick(depth_gain, step)[None, :]
    normed = (x_rows * scale * gain).astype(BF16)

    normed_rows = jnp.concatenate([normed] + [turn_hid(normed, -k) for k in range(1, halves)])
    targets = jnp.concatenate([pick(r, step) for r in ids_rows])
    logits = matmul(normed_rows, head, ((1,), (0,)))
    top = jnp.max(logits, axis=1)
    total = jnp.sum(jnp.exp(logits - top[:, None]), axis=1)
    stats = jnp.stack([top, total]).reshape(2, halves, -1)
    every = [stats] + [jnp.roll(turn_hid(stats, -t), t, axis=1) for t in range(1, halves)]
    tops = jnp.stack([e[0] for e in every]).reshape(halves, -1)
    totals = jnp.stack([e[1] for e in every]).reshape(halves, -1)
    top_all = jnp.max(tops, axis=0)
    lse = top_all + jnp.log(jnp.sum(totals * jnp.exp(tops - top_all), axis=0))
    entry = lax.broadcasted_iota(jnp.int32, logits.shape, 1) + half * block
    onehot = (targets[:, None] == entry).astype(F32)
    loss_weight = 2.0 * entries / frames
    d_logit = ((jnp.exp(logits - lse[:, None]) - onehot) * loss_weight).astype(BF16)

    d_norm_rows = matmul(d_logit, head, ((1,), (1,)))
    away = [d_norm_rows[k * owned : (k + 1) * owned].astype(BF16) for k in range(1, halves)]
    received = [turn_hid(a, k + 1) for k, a in enumerate(away)]
    d_norm = d_norm_rows[:owned]
    for r in received:
        d_norm += r.astype(F32)
    gated = gain * d_norm
    d_x = scale * gated - x_rows * scale**3 * jnp.mean(gated * x_rows, axis=1, keepdims=True)
    d_round = d_x.astype(BF16)
    d_ratio_part = jnp.sum(d_x * proj, axis=1).reshape(steps, part)

    part_out = matmul(normed_rows, after(d_logit, *away), ((0,), (0,))).astype(BF16)
    part_out = lax.all_to_all(part_out.reshape(seqs, depth // seqs, block), "seq", 0, 0)
    part_out = part_out.reshape(groups, steps, hids, head_rows, block).astype(F32).sum(0)
    part_out = part_out.astype(BF16)
    sums = [
        lax.dynamic_index_in_dim(part_out, (j + shift) % hids, 1, False) for shift in range(hids)
    ]
    sums = [along_hid(p, shift) if shift else p for shift, p in enumerate(sums)]
    grad_out = head_gradient(place, sums, halves)

    pieces = [d_round] + [along_hid(d_round, shift) for shift in range(1, hids)]
    ordered = [g.reshape(hids, part, units) for g in group]
    hidden_rows = jnp.concatenate([pick(g, o) for o in order for g in ordered])
    ratio_rows = [
        lax.dynamic_index_in_dim(ratio_group, o, 1, False).reshape(owned, 1) for o in order
    ]
    scaled = jnp.concatenate(
        [(r * p.astype(F32)).astype(BF16) for r, p in zip(ratio_rows, pieces)]
    )
    share = matmul(scaled, hidden_rows, ((0,), (0,))).astype(BF16)
    share = lax.all_to_all(share.reshape(seqs, depth // seqs, units), "seq", 0, 0)
    share = share.reshape(groups, steps, depth // seqs, units).astype(F32).sum(0)
    grad_in = share.transpose(0, 2, 1)

    d_ratio = d_ratio_part[0]
    for m in relations:
        d_ratio += flip_seq(d_ratio_part[m], m)
    d_ratio = [d_ratio] + [along_hid(d_ratio, shift) for shift in range(1, hids)]
    d_ratio = jnp.concatenate(d_ratio[::-1])[:, None]
    back_rows = jnp.zeros((steps, rows, depth), BF16)
    for m in range(steps):
        member = jnp.concatenate([p[m * part : (m + 1) * part] for p in pieces[::-1]])
        member = flip_seq(member, m) if m else member
        back_rows = lax.dynamic_update_index_in_dim(back_rows, member, (step - m) % steps, 0)
    back = matmul(back_rows[0], w_in[0], ((1,), (1,)))
    for s in range(1, steps):
        back += matmul(back_rows[s], w_in[s], ((1,), (1,)))
    ratio_own = jnp.concatenate([r[:part] for r in ratio_rows[::-1]])
    hidden_own = jnp.concatenate([pick(ordered[0], o) for o in order[::-1]]).astype(F32)
    correction = ratio_own**3 * d_ratio / width_in
    grad_hidden = (ratio_own * back - correction * hidden_own).astype(BF16)
    grad_hidden = jnp.concatenate([grad_hidden, grad_hidden])
    grad_hidden = lax.dynamic_slice_in_dim(grad_hidden, (hids - 1 - j) * part, rows, 0)
    return (grad_hidden, grad_in, grad_out)


def solution(mesh):
    placed = (
        P("seq", "hid"),
        P(None, "hid", None),
        P(),
        P(),
        P(("seq", "hid"), None, None),
        P(None, ("seq", "hid")),
    )
    return jax.shard_map(
        shards,
        mesh=mesh,
        in_specs=placed,
        out_specs=(P("seq", "hid"), P(None, "hid", "seq"), P(("seq", "hid"), None, None)),
        check_vma=False,
    )
```

```python
import jax
import jax.numpy as jnp
from jax import lax
from jax.experimental import pallas as pl
from jax.experimental.pallas import tpu as pltpu
from jax.sharding import PartitionSpec as P

F32 = jnp.float32
BF16 = jnp.bfloat16


def pick(values, index):
    return lax.dynamic_index_in_dim(values, index, axis=0, keepdims=False)


def matmul(a, b, contract):
    return lax.dot_general(a, b, (contract, ((), ())), preferred_element_type=F32)


def after(value, *others):
    return lax.optimization_barrier((value, *others))[0]


VMEM = pltpu.CompilerParams(vmem_limit_bytes=32 * 2**20)


def whole(shape):
    return pl.BlockSpec(shape, lambda n, place: (0,) * len(shape))


def call(kernel, place, grid, in_specs, out_specs, out_shape, scratch, flops, args):
    moved = sum(a.size * a.dtype.itemsize for a in args)
    return pl.pallas_call(
        kernel,
        grid_spec=pltpu.PrefetchScalarGridSpec(
            num_scalar_prefetch=1,
            grid=(grid,),
            in_specs=in_specs,
            out_specs=out_specs,
            scratch_shapes=scratch,
        ),
        out_shape=out_shape,
        compiler_params=VMEM,
        cost_estimate=pl.CostEstimate(flops=flops, bytes_accessed=moved, transcendentals=0),
    )(place, *args)


EXACT = 3


def parts_of(values):
    out = []
    for _ in range(EXACT):
        piece = lax.reduce_precision(values, 8, 7)
        values = values - piece
        out.append(piece.astype(BF16))
    return out


def head_gradient(place, pieces, halves):
    hids = len(pieces)
    steps, rows, block = pieces[0].shape

    def kernel(place_ref, *refs):
        pieces, out = refs[:-1], refs[-1]
        for r in range(halves):
            which = lax.rem(place_ref[1] - r + hids, halves)
            columns = pl.ds(pl.multiple_of(which * block, block), block)
            for s in range(steps):
                total = pieces[r][s].astype(F32)
                for k in range(r + halves, hids, halves):
                    total = total + pieces[k][s].astype(F32)
                out[:, s, columns] = total

    return call(
        kernel,
        place,
        1,
        [whole((steps, rows, block))] * hids,
        whole((rows, steps, halves * block)),
        jax.ShapeDtypeStruct((rows, steps, halves * block), F32),
        [],
        hids * steps * rows * block,
        tuple(pieces),
    )


def input_gradient(place, pieces, turned, ratio, seqs):
    hids, steps = len(pieces), len(turned)
    owned, depth = pieces[0].shape
    units, rows = turned[0].shape
    part = owned // steps
    slice_wide = depth // seqs
    wide = max(min(256, depth), slice_wide)
    count = wide // slice_wide

    def kernel(place_ref, *refs):
        chunks, turned, ratio = refs[:hids], refs[hids : hids + steps], refs[hids + steps]
        out, plain, scaled = refs[hids + steps + 1], refs[hids + steps + 2 : -1], refs[-1]
        j = place_ref[1]
        for r in range(hids):
            to = pl.multiple_of(lax.rem(j - r + hids, hids) * part, part)
            for m in range(steps):
                values = chunks[r][m * part : (m + 1) * part, :]
                plain[m][pl.ds(to, part), :] = values
                factor = ratio[m, pl.ds(to, part), :]
                scaled[m, pl.ds(to, part), :] = (values.astype(F32) * factor).astype(BF16)
        total = jnp.dot(turned[0][...], scaled[0], preferred_element_type=F32)
        for m in range(1, steps):
            total = total + jnp.dot(turned[m][...], scaled[m], preferred_element_type=F32)
        for k in range(count):
            out[k] = total[:, k * slice_wide : (k + 1) * slice_wide].astype(BF16)

    return call(
        kernel,
        place,
        depth // wide,
        [pl.BlockSpec((owned, wide), lambda n, place: (0, n))] * hids
        + [whole((units, rows))] * steps
        + [whole((steps, rows, 1))],
        [pl.BlockSpec((count, units, slice_wide), lambda n, place: (n, 0, 0))]
        + [pl.BlockSpec((rows, wide), lambda n, place: (0, n))] * steps,
        [jax.ShapeDtypeStruct((seqs, units, slice_wide), BF16)]
        + [jax.ShapeDtypeStruct((rows, depth), BF16)] * steps,
        [pltpu.VMEM((steps, rows, wide), BF16)],
        2 * steps * rows * units * depth,
        (*pieces, *turned, ratio),
    )


def hidden_gradient(place, d_rows, w_in, hidden, factors):
    steps, units, depth = w_in.shape
    rows = hidden.shape[0]
    wide = min(256, units)

    def kernel(place_ref, *refs):
        d_rows, w, hidden, factors, out = refs[:steps], refs[-4], refs[-3], refs[-2], refs[-1]
        total = None
        for r in range(steps):
            which = lax.rem(place_ref[0] - r + steps, steps)
            term = lax.dot_general(
                d_rows[r][...], w[which], (((1,), (1,)), ((), ())), preferred_element_type=F32
            )
            total = term if total is None else total + term
        out[...] = (factors[0] * total - factors[1] * hidden[...].astype(F32)).astype(BF16)

    return call(
        kernel,
        place,
        units // wide,
        [whole((rows, depth))] * steps
        + [
            pl.BlockSpec((steps, wide, depth), lambda n, place: (0, n, 0)),
            pl.BlockSpec((rows, wide), lambda n, place: (0, n)),
            whole((2, rows, 1)),
        ],
        pl.BlockSpec((rows, wide), lambda n, place: (0, n)),
        jax.ShapeDtypeStruct((rows, units), BF16),
        [],
        2 * steps * rows * units * depth,
        (*d_rows, w_in, hidden, factors),
    )


def shards(hidden, w_in, embedding, depth_gain, w_out, codebook_ids):
    hids = lax.axis_size("hid")
    seqs = lax.axis_size("seq")
    steps, units, depth = w_in.shape
    entries = w_out.shape[2]
    rows = hidden.shape[0]
    part = rows // hids
    width_in = units * hids
    frames = rows * seqs
    halves = 2 if hids % 2 == 0 else 1
    block = entries // halves
    head_rows = w_out.shape[0]
    groups = seqs // steps
    i = lax.axis_index("seq")
    j = lax.axis_index("hid")
    step = i % steps
    half = j % halves
    owned = steps * part

    def along_hid(values, shift):
        return lax.ppermute(values, "hid", [(a, (a + shift) % hids) for a in range(hids)])

    def turn_hid(values, shift):
        return lax.ppermute(
            values,
            "hid",
            [(a, a - a % halves + (a % halves + shift) % halves) for a in range(hids)],
        )

    def flip_seq(values, flip):
        return lax.ppermute(
            values,
            "seq",
            [(a, a - a % steps + (a % steps + flip) % steps) for a in range(seqs)],
        )

    place = jnp.stack([step, j]).astype(jnp.int32)
    relations = range(1, steps)

    group = [hidden] + [flip_seq(hidden, -m) for m in relations]

    squares_part = jnp.sum(jnp.square(hidden.astype(F32)), axis=1)
    tail = 8 * block
    small = jnp.concatenate(parts_of(squares_part))
    small = jnp.pad(small, (0, tail - small.size)).reshape(1, 1, 8, block)
    head_send = after(w_out, *group[1:]).reshape(head_rows, steps, halves, block)
    head_send = head_send.transpose(2, 1, 0, 3)
    head_send = head_send.reshape(1, halves, steps * head_rows, block)
    small = jnp.broadcast_to(small, (1, halves, 8, block))
    head_send = jnp.concatenate([head_send, small], axis=2)
    head_send = jnp.broadcast_to(head_send, (hids // halves,) + head_send.shape[1:])
    head_send = head_send.reshape(hids, steps * head_rows + 8, block)
    head_got = lax.all_to_all(head_send, "hid", 0, 0)
    head_mid = head_got[:, : steps * head_rows].reshape(hids, steps, head_rows, block)
    squares = head_got[:, steps * head_rows :].reshape(hids, tail)[:, : EXACT * rows]
    squares = jnp.sum(squares.astype(F32).reshape(hids * EXACT, rows), axis=0)

    w_own = pick(w_in, step)
    proj_parts = matmul(jnp.concatenate(group), w_own, ((1,), (0,)))
    proj_parts = proj_parts.reshape(steps, hids, part, depth)

    def owner_block(index):
        return lax.dynamic_index_in_dim(proj_parts, index, 1, False).reshape(owned, depth)

    send = [owner_block((j + shift) % hids).astype(BF16) for shift in range(1, hids)]
    received = [along_hid(send[shift - 1], shift) for shift in range(1, hids)]

    ids = after(codebook_ids, *send)
    ids = jnp.concatenate([ids] + [flip_seq(ids, -m) for m in relations], axis=1)
    ids_rows = [ids] + [turn_hid(ids, -k) for k in range(1, halves)]
    before = jnp.maximum(step - 1, 0)
    looked = jnp.take(pick(embedding, before), pick(ids, before), axis=0)

    head_send = after(head_mid, *send).transpose(1, 0, 2, 3)
    head_send = head_send.reshape(steps, hids * head_rows, block)
    head_send = jnp.broadcast_to(head_send, (groups,) + head_send.shape)
    head_send = head_send.reshape(seqs, hids * head_rows, block)
    head = lax.all_to_all(head_send, "seq", 0, 0).reshape(depth, block)

    squares = jnp.stack([squares] + [flip_seq(squares, -m) for m in relations])
    ratio_group = lax.rsqrt(squares / width_in + 1e-06).reshape(steps, hids, part)

    ratio = lax.dynamic_index_in_dim(ratio_group, j, 1, False).reshape(owned, 1)
    proj = owner_block(j)
    for r in received:
        proj += r.astype(F32)
    x_rows = ratio * proj + jnp.where(step > 0, looked.astype(F32), 0.0)
    scale = lax.rsqrt(jnp.mean(x_rows * x_rows, axis=1, keepdims=True) + 1e-06)
    gain = pick(depth_gain, step)[None, :]
    normed = (x_rows * scale * gain).astype(BF16)

    normed_rows = jnp.concatenate([normed] + [turn_hid(normed, -k) for k in range(1, halves)])
    targets = jnp.concatenate([pick(r, step) for r in ids_rows])
    logits = matmul(normed_rows, head, ((1,), (0,)))
    top = jnp.max(logits, axis=1)
    total = jnp.sum(jnp.exp(logits - top[:, None]), axis=1)
    stats = jnp.stack([top, total]).reshape(2, halves, -1)
    every = [stats] + [jnp.roll(turn_hid(stats, -t), t, axis=1) for t in range(1, halves)]
    tops = jnp.stack([e[0] for e in every]).reshape(halves, -1)
    totals = jnp.stack([e[1] for e in every]).reshape(halves, -1)
    top_all = jnp.max(tops, axis=0)
    lse = top_all + jnp.log(jnp.sum(totals * jnp.exp(tops - top_all), axis=0))
    entry = lax.broadcasted_iota(jnp.int32, logits.shape, 1) + half * block
    onehot = (targets[:, None] == entry).astype(F32)
    loss_weight = 2.0 * entries / frames
    d_logit = ((jnp.exp(logits - lse[:, None]) - onehot) * loss_weight).astype(BF16)

    d_norm_rows = matmul(d_logit, head, ((1,), (1,)))
    away = [d_norm_rows[k * owned : (k + 1) * owned].astype(BF16) for k in range(1, halves)]
    received = [turn_hid(a, k + 1) for k, a in enumerate(away)]
    d_norm = d_norm_rows[:owned]
    for r in received:
        d_norm += r.astype(F32)
    gated = gain * d_norm
    d_x = scale * gated - x_rows * scale**3 * jnp.mean(gated * x_rows, axis=1, keepdims=True)
    d_round = d_x.astype(BF16)
    d_ratio_part = jnp.sum(d_x * proj, axis=1).reshape(steps, part)

    part_out = matmul(normed_rows, after(d_logit, *away), ((0,), (0,))).astype(BF16)
    part_out = lax.all_to_all(part_out.reshape(seqs, depth // seqs, block), "seq", 0, 0)
    part_out = part_out.reshape(groups, steps, hids, head_rows, block).astype(F32).sum(0)
    part_out = part_out.astype(BF16)
    sums = [
        lax.dynamic_index_in_dim(part_out, (j + shift) % hids, 1, False) for shift in range(hids)
    ]
    sums = [along_hid(p, shift) if shift else p for shift, p in enumerate(sums)]
    grad_out = head_gradient(place, sums, halves)

    turned = [after(h, normed).T for h in group]
    pieces = [d_round] + [along_hid(d_round, shift) for shift in range(1, hids)]
    ratio_rows = ratio_group.reshape(steps, rows, 1)
    share, mine, *others = input_gradient(place, pieces, turned, ratio_rows, seqs)
    share = lax.all_to_all(share, "seq", 0, 0)
    grad_in = share.reshape(groups, steps, units, depth // seqs).astype(F32).sum(0)

    d_ratio = d_ratio_part[0]
    for m in relations:
        d_ratio += flip_seq(d_ratio_part[m], m)
    d_rows = jnp.broadcast_to(d_ratio, (hids, part))
    for shift in range(1, hids):
        d_rows = lax.dynamic_update_index_in_dim(
            d_rows, along_hid(d_ratio, shift), (j - shift) % hids, 0
        )
    ratio_own = ratio_group[0].reshape(rows)
    correction = ratio_own**3 * d_rows.reshape(rows) / width_in
    factors = jnp.stack([ratio_own, correction])[:, :, None]
    mine = [mine] + [flip_seq(others[m - 1], m) for m in relations]
    grad_hidden = hidden_gradient(place, mine, w_in, hidden, factors)
    return (grad_hidden, grad_in, grad_out)


def solution(mesh):
    placed = (
        P("seq", "hid"),
        P(None, "hid", None),
        P(),
        P(),
        P(("seq", "hid"), None, None),
        P(None, ("seq", "hid")),
    )
    return jax.shard_map(
        shards,
        mesh=mesh,
        in_specs=placed,
        out_specs=(P("seq", "hid"), P(None, "hid", "seq"), P(("seq", "hid"), None, None)),
        check_vma=False,
    )
```

```python
import jax
import jax.numpy as jnp
from jax import lax
from jax.experimental import pallas as pl
from jax.experimental.pallas import tpu as pltpu
from jax.sharding import PartitionSpec as P

F32 = jnp.float32
BF16 = jnp.bfloat16


def pick(values, index):
    return lax.dynamic_index_in_dim(values, index, axis=0, keepdims=False)


def matmul(a, b, contract):
    return lax.dot_general(a, b, (contract, ((), ())), preferred_element_type=F32)


def after(value, *others):
    return lax.optimization_barrier((value, *others))[0]


VMEM = pltpu.CompilerParams(vmem_limit_bytes=60 * 2**20)


def whole(shape):
    return pl.BlockSpec(shape, lambda n, place: (0,) * len(shape))


def call(kernel, place, grid, in_specs, out_specs, out_shape, scratch, flops, args):
    moved = sum(a.size * a.dtype.itemsize for a in args)
    return pl.pallas_call(
        kernel,
        grid_spec=pltpu.PrefetchScalarGridSpec(
            num_scalar_prefetch=1,
            grid=(grid,),
            in_specs=in_specs,
            out_specs=out_specs,
            scratch_shapes=scratch,
        ),
        out_shape=out_shape,
        compiler_params=VMEM,
        cost_estimate=pl.CostEstimate(flops=flops, bytes_accessed=moved, transcendentals=0),
    )(place, *args)


EXACT = 3


def parts_of(values):
    out = []
    for _ in range(EXACT):
        piece = lax.reduce_precision(values, 8, 7)
        values = values - piece
        out.append(piece.astype(BF16))
    return out


def head_gradient(place, pieces, halves):
    hids = len(pieces)
    steps, rows, block = pieces[0].shape

    def kernel(place_ref, *refs):
        pieces, out = refs[:-1], refs[-1]
        for r in range(halves):
            which = lax.rem(place_ref[1] - r + hids, halves)
            columns = pl.ds(pl.multiple_of(which * block, block), block)
            for s in range(steps):
                total = pieces[r][s].astype(F32)
                for k in range(r + halves, hids, halves):
                    total = total + pieces[k][s].astype(F32)
                out[:, s, columns] = total

    return call(
        kernel,
        place,
        1,
        [whole((steps, rows, block))] * hids,
        whole((rows, steps, halves * block)),
        jax.ShapeDtypeStruct((rows, steps, halves * block), F32),
        [],
        hids * steps * rows * block,
        tuple(pieces),
    )


def input_gradient(place, pieces, group, ratio, seqs):
    hids, steps = len(pieces), len(group)
    owned, depth = pieces[0].shape
    rows, units = group[0].shape
    part = owned // steps
    wide = min(512, depth)

    def kernel(place_ref, *refs):
        chunks, group, ratio = refs[:hids], refs[hids : hids + steps], refs[hids + steps]
        out, plain, scaled = refs[hids + steps + 1], refs[hids + steps + 2 : -1], refs[-1]
        j = place_ref[1]
        for r in range(hids):
            to = pl.multiple_of(lax.rem(j - r + hids, hids) * part, part)
            for m in range(steps):
                values = chunks[r][m * part : (m + 1) * part, :]
                plain[m][pl.ds(to, part), :] = values
                factor = ratio[m, pl.ds(to, part), :]
                scaled[m, pl.ds(to, part), :] = (values.astype(F32) * factor).astype(BF16)
        total = None
        for m in range(steps):
            term = lax.dot_general(
                scaled[m], group[m][...], (((0,), (0,)), ((), ())), preferred_element_type=F32
            )
            total = term if total is None else total + term
        out[...] = total.astype(BF16)

    return call(
        kernel,
        place,
        depth // wide,
        [pl.BlockSpec((owned, wide), lambda n, place: (0, n))] * hids
        + [whole((rows, units))] * steps
        + [whole((steps, rows, 1))],
        [pl.BlockSpec((wide, units), lambda n, place: (n, 0))]
        + [pl.BlockSpec((rows, wide), lambda n, place: (0, n))] * steps,
        [jax.ShapeDtypeStruct((depth, units), BF16)]
        + [jax.ShapeDtypeStruct((rows, depth), BF16)] * steps,
        [pltpu.VMEM((steps, rows, wide), BF16)],
        2 * steps * rows * units * depth,
        (*pieces, *group, ratio),
    )


def hidden_gradient(place, d_rows, w_in, hidden, factors):
    steps, units, depth = w_in.shape
    rows = hidden.shape[0]
    wide = min(256, units)

    def kernel(place_ref, *refs):
        d_rows, w, hidden, factors, out = refs[:steps], refs[-4], refs[-3], refs[-2], refs[-1]
        total = None
        for r in range(steps):
            which = lax.rem(place_ref[0] - r + steps, steps)
            term = lax.dot_general(
                d_rows[r][...], w[which], (((1,), (1,)), ((), ())), preferred_element_type=F32
            )
            total = term if total is None else total + term
        out[...] = (factors[0] * total - factors[1] * hidden[...].astype(F32)).astype(BF16)

    return call(
        kernel,
        place,
        units // wide,
        [whole((rows, depth))] * steps
        + [
            pl.BlockSpec((steps, wide, depth), lambda n, place: (0, n, 0)),
            pl.BlockSpec((rows, wide), lambda n, place: (0, n)),
            whole((2, rows, 1)),
        ],
        pl.BlockSpec((rows, wide), lambda n, place: (0, n)),
        jax.ShapeDtypeStruct((rows, units), BF16),
        [],
        2 * steps * rows * units * depth,
        (*d_rows, w_in, hidden, factors),
    )


def shards(hidden, w_in, embedding, depth_gain, w_out, codebook_ids):
    hids = lax.axis_size("hid")
    seqs = lax.axis_size("seq")
    steps, units, depth = w_in.shape
    entries = w_out.shape[2]
    rows = hidden.shape[0]
    part = rows // hids
    width_in = units * hids
    frames = rows * seqs
    halves = 2 if hids % 2 == 0 else 1
    block = entries // halves
    head_rows = w_out.shape[0]
    groups = seqs // steps
    i = lax.axis_index("seq")
    j = lax.axis_index("hid")
    step = i % steps
    half = j % halves
    owned = steps * part

    def along_hid(values, shift):
        return lax.ppermute(values, "hid", [(a, (a + shift) % hids) for a in range(hids)])

    def turn_hid(values, shift):
        return lax.ppermute(
            values,
            "hid",
            [(a, a - a % halves + (a % halves + shift) % halves) for a in range(hids)],
        )

    def flip_seq(values, flip):
        return lax.ppermute(
            values,
            "seq",
            [(a, a - a % steps + (a % steps + flip) % steps) for a in range(seqs)],
        )

    place = jnp.stack([step, j]).astype(jnp.int32)
    relations = range(1, steps)

    group = [hidden] + [flip_seq(hidden, -m) for m in relations]

    squares_part = jnp.sum(jnp.square(hidden.astype(F32)), axis=1)
    tail = 8 * block
    small = jnp.concatenate(parts_of(squares_part))
    small = jnp.pad(small, (0, tail - small.size)).reshape(1, 1, 8, block)
    head_send = after(w_out, *group[1:]).reshape(head_rows, steps, halves, block)
    head_send = head_send.transpose(2, 1, 0, 3)
    head_send = head_send.reshape(1, halves, steps * head_rows, block)
    small = jnp.broadcast_to(small, (1, halves, 8, block))
    head_send = jnp.concatenate([head_send, small], axis=2)
    head_send = jnp.broadcast_to(head_send, (hids // halves,) + head_send.shape[1:])
    head_send = head_send.reshape(hids, steps * head_rows + 8, block)
    head_got = lax.all_to_all(head_send, "hid", 0, 0)
    head_mid = head_got[:, : steps * head_rows].reshape(hids, steps, head_rows, block)
    squares = head_got[:, steps * head_rows :].reshape(hids, tail)[:, : EXACT * rows]
    squares = jnp.sum(squares.astype(F32).reshape(hids * EXACT, rows), axis=0)

    w_own = pick(w_in, step)
    proj_parts = matmul(jnp.concatenate(group), w_own, ((1,), (0,)))
    proj_parts = proj_parts.reshape(steps, hids, part, depth)

    def owner_block(index):
        return lax.dynamic_index_in_dim(proj_parts, index, 1, False).reshape(owned, depth)

    send = [owner_block((j + shift) % hids).astype(BF16) for shift in range(1, hids)]
    send = [after(p, head_got) for p in send]
    received = [along_hid(send[shift - 1], shift) for shift in range(1, hids)]

    ids = after(codebook_ids, *send)
    ids = jnp.concatenate([ids] + [flip_seq(ids, -m) for m in relations], axis=1)
    ids_rows = [ids] + [turn_hid(ids, -k) for k in range(1, halves)]
    before = jnp.maximum(step - 1, 0)
    looked = jnp.take(pick(embedding, before), pick(ids, before), axis=0)

    head_send = after(head_mid, *send).transpose(1, 0, 2, 3)
    head_send = head_send.reshape(steps, hids * head_rows, block)
    head_send = jnp.broadcast_to(head_send, (groups,) + head_send.shape)
    head_send = head_send.reshape(seqs, hids * head_rows, block)
    head = lax.all_to_all(head_send, "seq", 0, 0).reshape(depth, block)

    squares = jnp.stack([squares] + [flip_seq(squares, -m) for m in relations])
    ratio_group = lax.rsqrt(squares / width_in + 1e-06).reshape(steps, hids, part)

    ratio = lax.dynamic_index_in_dim(ratio_group, j, 1, False).reshape(owned, 1)
    proj = owner_block(j)
    for r in received:
        proj += r.astype(F32)
    x_rows = ratio * proj + jnp.where(step > 0, looked.astype(F32), 0.0)
    scale = lax.rsqrt(jnp.mean(x_rows * x_rows, axis=1, keepdims=True) + 1e-06)
    gain = pick(depth_gain, step)[None, :]
    normed = (x_rows * scale * gain).astype(BF16)

    normed_rows = jnp.concatenate([normed] + [turn_hid(normed, -k) for k in range(1, halves)])
    targets = jnp.concatenate([pick(r, step) for r in ids_rows])
    logits = matmul(normed_rows, head, ((1,), (0,)))
    top = jnp.max(logits, axis=1)
    total = jnp.sum(jnp.exp(logits - top[:, None]), axis=1)
    stats = jnp.stack([top, total]).reshape(2, halves, -1)
    every = [stats] + [jnp.roll(turn_hid(stats, -t), t, axis=1) for t in range(1, halves)]
    tops = jnp.stack([e[0] for e in every]).reshape(halves, -1)
    totals = jnp.stack([e[1] for e in every]).reshape(halves, -1)
    top_all = jnp.max(tops, axis=0)
    lse = top_all + jnp.log(jnp.sum(totals * jnp.exp(tops - top_all), axis=0))
    entry = lax.broadcasted_iota(jnp.int32, logits.shape, 1) + half * block
    onehot = (targets[:, None] == entry).astype(F32)
    loss_weight = 2.0 * entries / frames
    d_logit = ((jnp.exp(logits - lse[:, None]) - onehot) * loss_weight).astype(BF16)

    d_norm_rows = matmul(d_logit, head, ((1,), (1,)))
    away = [d_norm_rows[k * owned : (k + 1) * owned].astype(BF16) for k in range(1, halves)]
    received = [turn_hid(a, k + 1) for k, a in enumerate(away)]
    d_norm = d_norm_rows[:owned]
    for r in received:
        d_norm += r.astype(F32)
    gated = gain * d_norm
    d_x = scale * gated - x_rows * scale**3 * jnp.mean(gated * x_rows, axis=1, keepdims=True)
    d_round = d_x.astype(BF16)
    d_ratio_part = jnp.sum(d_x * proj, axis=1).reshape(steps, part)

    part_out = matmul(normed_rows, after(d_logit, *away), ((0,), (0,))).astype(BF16)
    part_out = after(part_out, *received).reshape(seqs, depth // seqs, block)
    part_out = lax.all_to_all(part_out, "seq", 0, 0)
    part_out = part_out.reshape(groups, steps, hids, head_rows, block).astype(F32).sum(0)
    part_out = part_out.astype(BF16)
    sums = [
        lax.dynamic_index_in_dim(part_out, (j + shift) % hids, 1, False) for shift in range(hids)
    ]
    sums = [along_hid(p, shift) if shift else p for shift, p in enumerate(sums)]
    grad_out = head_gradient(place, sums, halves)

    pieces = [d_round] + [along_hid(d_round, shift) for shift in range(1, hids)]
    ratio_rows = ratio_group.reshape(steps, rows, 1)
    share, mine, *others = input_gradient(place, pieces, group, ratio_rows, seqs)
    share = lax.all_to_all(share.reshape(seqs, depth // seqs, units), "seq", 0, 0)
    share = share.reshape(groups, steps, depth // seqs, units).astype(F32).sum(0)
    grad_in = share.transpose(0, 2, 1)

    d_ratio = d_ratio_part[0]
    for m in relations:
        d_ratio += flip_seq(d_ratio_part[m], m)
    d_rows = jnp.broadcast_to(d_ratio, (hids, part))
    for shift in range(1, hids):
        d_rows = lax.dynamic_update_index_in_dim(
            d_rows, along_hid(d_ratio, shift), (j - shift) % hids, 0
        )
    ratio_own = ratio_group[0].reshape(rows)
    correction = ratio_own**3 * d_rows.reshape(rows) / width_in
    factors = jnp.stack([ratio_own, correction])[:, :, None]
    mine = [mine] + [flip_seq(others[m - 1], m) for m in relations]
    grad_hidden = hidden_gradient(place, mine, w_in, hidden, factors)
    return (grad_hidden, grad_in, grad_out)


def solution(mesh):
    placed = (
        P("seq", "hid"),
        P(None, "hid", None),
        P(),
        P(),
        P(("seq", "hid"), None, None),
        P(None, ("seq", "hid")),
    )
    return jax.shard_map(
        shards,
        mesh=mesh,
        in_specs=placed,
        out_specs=(P("seq", "hid"), P(None, "hid", "seq"), P(("seq", "hid"), None, None)),
        check_vma=False,
    )
```

```python
import jax
import jax.numpy as jnp
from jax import lax
from jax.experimental import pallas as pl
from jax.experimental.pallas import tpu as pltpu
from jax.sharding import PartitionSpec as P

F32 = jnp.float32
BF16 = jnp.bfloat16


def pick(values, index):
    return lax.dynamic_index_in_dim(values, index, axis=0, keepdims=False)


def matmul(a, b, contract):
    return lax.dot_general(a, b, (contract, ((), ())), preferred_element_type=F32)


def after(value, *others):
    return lax.optimization_barrier((value, *others))[0]


VMEM = pltpu.CompilerParams(vmem_limit_bytes=60 * 2**20)


def whole(shape):
    return pl.BlockSpec(shape, lambda n, place: (0,) * len(shape))


def call(kernel, place, grid, in_specs, out_specs, out_shape, scratch, flops, args):
    moved = sum(a.size * a.dtype.itemsize for a in args)
    return pl.pallas_call(
        kernel,
        grid_spec=pltpu.PrefetchScalarGridSpec(
            num_scalar_prefetch=1,
            grid=(grid,),
            in_specs=in_specs,
            out_specs=out_specs,
            scratch_shapes=scratch,
        ),
        out_shape=out_shape,
        compiler_params=VMEM,
        cost_estimate=pl.CostEstimate(flops=flops, bytes_accessed=moved, transcendentals=0),
    )(place, *args)


def head_gradient(place, pieces, halves):
    hids = len(pieces)
    steps, rows, block = pieces[0].shape

    def kernel(place_ref, *refs):
        pieces, out = refs[:-1], refs[-1]
        for r in range(halves):
            which = lax.rem(place_ref[1] - r + hids, halves)
            columns = pl.ds(pl.multiple_of(which * block, block), block)
            for s in range(steps):
                total = pieces[r][s].astype(F32)
                for k in range(r + halves, hids, halves):
                    total = total + pieces[k][s].astype(F32)
                out[:, s, columns] = total

    return call(
        kernel,
        place,
        1,
        [whole((steps, rows, block))] * hids,
        whole((rows, steps, halves * block)),
        jax.ShapeDtypeStruct((rows, steps, halves * block), F32),
        [],
        hids * steps * rows * block,
        tuple(pieces),
    )


def input_gradient(place, pieces, group, ratio, seqs):
    hids, steps = len(pieces), len(group)
    owned, depth = pieces[0].shape
    rows, units = group[0].shape
    part = owned // steps
    wide = min(512, depth)

    def kernel(place_ref, *refs):
        chunks, group, ratio = refs[:hids], refs[hids : hids + steps], refs[hids + steps]
        out, plain, scaled = refs[hids + steps + 1], refs[hids + steps + 2 : -1], refs[-1]
        j = place_ref[1]
        for r in range(hids):
            to = pl.multiple_of(lax.rem(j - r + hids, hids) * part, part)
            for m in range(steps):
                values = chunks[r][m * part : (m + 1) * part, :]
                plain[m][pl.ds(to, part), :] = values
                factor = ratio[m, pl.ds(to, part), :]
                scaled[m, pl.ds(to, part), :] = (values.astype(F32) * factor).astype(BF16)
        total = None
        for m in range(steps):
            term = lax.dot_general(
                scaled[m], group[m][...], (((0,), (0,)), ((), ())), preferred_element_type=F32
            )
            total = term if total is None else total + term
        out[...] = total.astype(BF16)

    return call(
        kernel,
        place,
        depth // wide,
        [pl.BlockSpec((owned, wide), lambda n, place: (0, n))] * hids
        + [whole((rows, units))] * steps
        + [whole((steps, rows, 1))],
        [pl.BlockSpec((wide, units), lambda n, place: (n, 0))]
        + [pl.BlockSpec((rows, wide), lambda n, place: (0, n))] * steps,
        [jax.ShapeDtypeStruct((depth, units), BF16)]
        + [jax.ShapeDtypeStruct((rows, depth), BF16)] * steps,
        [pltpu.VMEM((steps, rows, wide), BF16)],
        2 * steps * rows * units * depth,
        (*pieces, *group, ratio),
    )


def hidden_gradient(place, d_rows, w_in, hidden, factors):
    steps, units, depth = w_in.shape
    rows = hidden.shape[0]
    wide = min(256, units)

    def kernel(place_ref, *refs):
        d_rows, w, hidden, factors, out = refs[:steps], refs[-4], refs[-3], refs[-2], refs[-1]
        total = None
        for r in range(steps):
            which = lax.rem(place_ref[0] - r + steps, steps)
            term = lax.dot_general(
                d_rows[r][...], w[which], (((1,), (1,)), ((), ())), preferred_element_type=F32
            )
            total = term if total is None else total + term
        out[...] = (factors[0] * total - factors[1] * hidden[...].astype(F32)).astype(BF16)

    return call(
        kernel,
        place,
        units // wide,
        [whole((rows, depth))] * steps
        + [
            pl.BlockSpec((steps, wide, depth), lambda n, place: (0, n, 0)),
            pl.BlockSpec((rows, wide), lambda n, place: (0, n)),
            whole((2, rows, 1)),
        ],
        pl.BlockSpec((rows, wide), lambda n, place: (0, n)),
        jax.ShapeDtypeStruct((rows, units), BF16),
        [],
        2 * steps * rows * units * depth,
        (*d_rows, w_in, hidden, factors),
    )


def shards(hidden, w_in, embedding, depth_gain, w_out, codebook_ids):
    hids = lax.axis_size("hid")
    seqs = lax.axis_size("seq")
    steps, units, depth = w_in.shape
    entries = w_out.shape[2]
    rows = hidden.shape[0]
    part = rows // hids
    width_in = units * hids
    frames = rows * seqs
    halves = 2 if hids % 2 == 0 else 1
    block = entries // halves
    head_rows = w_out.shape[0]
    groups = seqs // steps
    i = lax.axis_index("seq")
    j = lax.axis_index("hid")
    step = i % steps
    half = j % halves
    owned = steps * part

    def along_hid(values, shift):
        return lax.ppermute(values, "hid", [(a, (a + shift) % hids) for a in range(hids)])

    def turn_hid(values, shift):
        return lax.ppermute(
            values,
            "hid",
            [(a, a - a % halves + (a % halves + shift) % halves) for a in range(hids)],
        )

    def flip_seq(values, flip):
        return lax.ppermute(
            values,
            "seq",
            [(a, a - a % steps + (a % steps + flip) % steps) for a in range(seqs)],
        )

    place = jnp.stack([step, j]).astype(jnp.int32)
    relations = range(1, steps)

    group = [hidden] + [flip_seq(hidden, -m) for m in relations]

    head_send = w_out.reshape(head_rows, steps, halves, block).transpose(2, 1, 0, 3)
    head_send = jnp.broadcast_to(head_send, (hids // halves,) + head_send.shape)
    head_send = head_send.reshape(hids, steps, head_rows, block)
    head_mid = lax.all_to_all(head_send, "hid", 0, 0)

    squares = jnp.sum(jnp.square(hidden.astype(F32)), axis=1)
    squares = [squares] + [along_hid(squares, shift) for shift in range(1, hids)]
    squares = sum(squares[1:], squares[0])
    squares = jnp.stack([squares] + [flip_seq(squares, -m) for m in relations])
    ratio_group = lax.rsqrt(squares / width_in + 1e-06).reshape(steps, hids, part)

    w_own = pick(w_in, step)
    proj_parts = matmul(jnp.concatenate(group), w_own, ((1,), (0,)))
    proj_parts = proj_parts.reshape(steps, hids, part, depth)

    def owner_block(index):
        return lax.dynamic_index_in_dim(proj_parts, index, 1, False).reshape(owned, depth)

    send = [owner_block((j + shift) % hids).astype(BF16) for shift in range(1, hids)]
    send = [after(p, head_mid, ratio_group) for p in send]
    received = [along_hid(send[shift - 1], shift) for shift in range(1, hids)]

    ids = after(codebook_ids, *send)
    ids = jnp.concatenate([ids] + [flip_seq(ids, -m) for m in relations], axis=1)
    ids_rows = [ids] + [turn_hid(ids, -k) for k in range(1, halves)]
    before = jnp.maximum(step - 1, 0)
    looked = jnp.take(pick(embedding, before), pick(ids, before), axis=0)

    head_send = after(head_mid, *send).transpose(1, 0, 2, 3)
    head_send = head_send.reshape(steps, hids * head_rows, block)
    head_send = jnp.broadcast_to(head_send, (groups,) + head_send.shape)
    head_send = head_send.reshape(seqs, hids * head_rows, block)
    head = lax.all_to_all(head_send, "seq", 0, 0).reshape(depth, block)

    ratio = lax.dynamic_index_in_dim(ratio_group, j, 1, False).reshape(owned, 1)
    proj = owner_block(j)
    for r in received:
        proj += r.astype(F32)
    x_rows = ratio * proj + jnp.where(step > 0, looked.astype(F32), 0.0)
    scale = lax.rsqrt(jnp.mean(x_rows * x_rows, axis=1, keepdims=True) + 1e-06)
    x_proj = jnp.sum(x_rows * proj, axis=1, keepdims=True)
    gain = pick(depth_gain, step)[None, :]
    normed = (x_rows * scale * gain).astype(BF16)

    normed_rows = jnp.concatenate([normed] + [turn_hid(normed, -k) for k in range(1, halves)])
    targets = jnp.concatenate([pick(r, step) for r in ids_rows])
    logits = matmul(normed_rows, head, ((1,), (0,)))
    top = jnp.max(logits, axis=1)
    total = jnp.sum(jnp.exp(logits - top[:, None]), axis=1)
    stats = jnp.stack([top, total]).reshape(2, halves, -1)
    every = [stats] + [jnp.roll(turn_hid(stats, -t), t, axis=1) for t in range(1, halves)]
    tops = jnp.stack([e[0] for e in every]).reshape(halves, -1)
    totals = jnp.stack([e[1] for e in every]).reshape(halves, -1)
    top_all = jnp.max(tops, axis=0)
    lse = top_all + jnp.log(jnp.sum(totals * jnp.exp(tops - top_all), axis=0))
    entry = lax.broadcasted_iota(jnp.int32, logits.shape, 1) + half * block
    onehot = (targets[:, None] == entry).astype(F32)
    loss_weight = 2.0 * entries / frames
    d_logit = ((jnp.exp(logits - lse[:, None]) - onehot) * loss_weight).astype(BF16)

    d_norm_rows = matmul(d_logit, head, ((1,), (1,)))
    away = [d_norm_rows[k * owned : (k + 1) * owned].astype(BF16) for k in range(1, halves)]
    received = [turn_hid(a, k + 1) for k, a in enumerate(away)]
    d_norm = d_norm_rows[:owned]
    for r in received:
        d_norm += r.astype(F32)
    gated = gain * d_norm
    back_scale = scale**3 * jnp.mean(gated * x_rows, axis=1, keepdims=True)
    gated_proj = jnp.sum(gated * proj, axis=1, keepdims=True)
    d_round = (scale * gated - x_rows * back_scale).astype(BF16)
    d_ratio_part = (scale * gated_proj - back_scale * x_proj).reshape(steps, part)

    part_out = matmul(normed_rows, after(d_logit, *away), ((0,), (0,))).astype(BF16)
    part_out = after(part_out, *received).reshape(seqs, depth // seqs, block)
    part_out = lax.all_to_all(part_out, "seq", 0, 0)
    part_out = part_out.reshape(groups, steps, hids, head_rows, block).astype(F32).sum(0)
    part_out = part_out.astype(BF16)
    sums = [
        lax.dynamic_index_in_dim(part_out, (j + shift) % hids, 1, False) for shift in range(hids)
    ]
    sums = [along_hid(p, shift) if shift else p for shift, p in enumerate(sums)]
    grad_out = head_gradient(place, sums, halves)

    pieces = [d_round] + [along_hid(d_round, shift) for shift in range(1, hids)]
    ratio_rows = ratio_group.reshape(steps, rows, 1)
    d_ratio = d_ratio_part[0]
    for m in relations:
        d_ratio += flip_seq(d_ratio_part[m], m)
    d_rows = jnp.broadcast_to(d_ratio, (hids, part))
    for shift in range(1, hids):
        d_rows = lax.dynamic_update_index_in_dim(
            d_rows, along_hid(d_ratio, shift), (j - shift) % hids, 0
        )
    share, mine, *others = input_gradient(after(place, d_rows), pieces, group, ratio_rows, seqs)
    share = lax.all_to_all(share.reshape(seqs, depth // seqs, units), "seq", 0, 0)
    share = share.reshape(groups, steps, depth // seqs, units).astype(F32).sum(0)
    grad_in = share.transpose(0, 2, 1)

    ratio_own = ratio_group[0].reshape(rows)
    correction = ratio_own**3 * d_rows.reshape(rows) / width_in
    factors = jnp.stack([ratio_own, correction])[:, :, None]
    mine = [mine] + [flip_seq(others[m - 1], m) for m in relations]
    grad_hidden = hidden_gradient(place, mine, w_in, hidden, factors)
    return (grad_hidden, grad_in, grad_out)


def solution(mesh):
    placed = (
        P("seq", "hid"),
        P(None, "hid", None),
        P(),
        P(),
        P(("seq", "hid"), None, None),
        P(None, ("seq", "hid")),
    )
    return jax.shard_map(
        shards,
        mesh=mesh,
        in_specs=placed,
        out_specs=(P("seq", "hid"), P(None, "hid", "seq"), P(("seq", "hid"), None, None)),
        check_vma=False,
    )
```

```python
import jax
import jax.numpy as jnp
from jax import lax
from jax.experimental import pallas as pl
from jax.experimental.pallas import tpu as pltpu
from jax.sharding import PartitionSpec as P

F32 = jnp.float32
BF16 = jnp.bfloat16


def pick(values, index):
    return lax.dynamic_index_in_dim(values, index, axis=0, keepdims=False)


def matmul(a, b, contract):
    return lax.dot_general(a, b, (contract, ((), ())), preferred_element_type=F32)


def after(value, *others):
    return lax.optimization_barrier((value, *others))[0]


VMEM = pltpu.CompilerParams(vmem_limit_bytes=60 * 2**20)


def whole(shape):
    return pl.BlockSpec(shape, lambda n, place: (0,) * len(shape))


def call(kernel, place, grid, in_specs, out_specs, out_shape, scratch, flops, args):
    moved = sum(a.size * a.dtype.itemsize for a in args)
    return pl.pallas_call(
        kernel,
        grid_spec=pltpu.PrefetchScalarGridSpec(
            num_scalar_prefetch=1,
            grid=(grid,),
            in_specs=in_specs,
            out_specs=out_specs,
            scratch_shapes=scratch,
        ),
        out_shape=out_shape,
        compiler_params=VMEM,
        cost_estimate=pl.CostEstimate(flops=flops, bytes_accessed=moved, transcendentals=0),
    )(place, *args)


EXACT = 3


def parts_of(values):
    out = []
    for _ in range(EXACT):
        piece = lax.reduce_precision(values, 8, 7)
        values = values - piece
        out.append(piece.astype(BF16))
    return out


def head_gradient(place, pieces, halves):
    hids = len(pieces)
    steps, rows, block = pieces[0].shape

    def kernel(place_ref, *refs):
        pieces, out = refs[:-1], refs[-1]
        for r in range(halves):
            which = lax.rem(place_ref[1] - r + hids, halves)
            columns = pl.ds(pl.multiple_of(which * block, block), block)
            for s in range(steps):
                total = pieces[r][s].astype(F32)
                for k in range(r + halves, hids, halves):
                    total = total + pieces[k][s].astype(F32)
                out[:, s, columns] = total

    return call(
        kernel,
        place,
        1,
        [whole((steps, rows, block))] * hids,
        whole((rows, steps, halves * block)),
        jax.ShapeDtypeStruct((rows, steps, halves * block), F32),
        [],
        hids * steps * rows * block,
        tuple(pieces),
    )


def input_gradient(place, pieces, group, ratio, seqs):
    hids, steps = len(pieces), len(group)
    owned, depth = pieces[0].shape
    rows, units = group[0].shape
    part = owned // steps
    wide = min(512, depth)

    def kernel(place_ref, *refs):
        chunks, group, ratio = refs[:hids], refs[hids : hids + steps], refs[hids + steps]
        out, plain, scaled = refs[hids + steps + 1], refs[hids + steps + 2 : -1], refs[-1]
        j = place_ref[1]
        for r in range(hids):
            to = pl.multiple_of(lax.rem(j - r + hids, hids) * part, part)
            for m in range(steps):
                values = chunks[r][m * part : (m + 1) * part, :]
                plain[m][pl.ds(to, part), :] = values
                factor = ratio[m, pl.ds(to, part), :]
                scaled[m, pl.ds(to, part), :] = (values.astype(F32) * factor).astype(BF16)
        total = None
        for m in range(steps):
            term = lax.dot_general(
                scaled[m], group[m][...], (((0,), (0,)), ((), ())), preferred_element_type=F32
            )
            total = term if total is None else total + term
        out[...] = total.astype(BF16)

    return call(
        kernel,
        place,
        depth // wide,
        [pl.BlockSpec((owned, wide), lambda n, place: (0, n))] * hids
        + [whole((rows, units))] * steps
        + [whole((steps, rows, 1))],
        [pl.BlockSpec((wide, units), lambda n, place: (n, 0))]
        + [pl.BlockSpec((rows, wide), lambda n, place: (0, n))] * steps,
        [jax.ShapeDtypeStruct((depth, units), BF16)]
        + [jax.ShapeDtypeStruct((rows, depth), BF16)] * steps,
        [pltpu.VMEM((steps, rows, wide), BF16)],
        2 * steps * rows * units * depth,
        (*pieces, *group, ratio),
    )


def hidden_gradient(place, d_rows, w_in, hidden, factors):
    steps, units, depth = w_in.shape
    rows = hidden.shape[0]
    wide = min(256, units)

    def kernel(place_ref, *refs):
        d_rows, w, hidden, factors, out = refs[:steps], refs[-4], refs[-3], refs[-2], refs[-1]
        total = None
        for r in range(steps):
            which = lax.rem(place_ref[0] - r + steps, steps)
            term = lax.dot_general(
                d_rows[r][...], w[which], (((1,), (1,)), ((), ())), preferred_element_type=F32
            )
            total = term if total is None else total + term
        out[...] = (factors[0] * total - factors[1] * hidden[...].astype(F32)).astype(BF16)

    return call(
        kernel,
        place,
        units // wide,
        [whole((rows, depth))] * steps
        + [
            pl.BlockSpec((steps, wide, depth), lambda n, place: (0, n, 0)),
            pl.BlockSpec((rows, wide), lambda n, place: (0, n)),
            whole((2, rows, 1)),
        ],
        pl.BlockSpec((rows, wide), lambda n, place: (0, n)),
        jax.ShapeDtypeStruct((rows, units), BF16),
        [],
        2 * steps * rows * units * depth,
        (*d_rows, w_in, hidden, factors),
    )


def shards(hidden, w_in, embedding, depth_gain, w_out, codebook_ids):
    hids = lax.axis_size("hid")
    seqs = lax.axis_size("seq")
    steps, units, depth = w_in.shape
    entries = w_out.shape[2]
    rows = hidden.shape[0]
    part = rows // hids
    width_in = units * hids
    frames = rows * seqs
    halves = 2 if hids % 2 == 0 else 1
    block = entries // halves
    head_rows = w_out.shape[0]
    groups = seqs // steps
    i = lax.axis_index("seq")
    j = lax.axis_index("hid")
    step = i % steps
    half = j % halves
    owned = steps * part

    def along_hid(values, shift):
        return lax.ppermute(values, "hid", [(a, (a + shift) % hids) for a in range(hids)])

    def turn_hid(values, shift):
        return lax.ppermute(
            values,
            "hid",
            [(a, a - a % halves + (a % halves + shift) % halves) for a in range(hids)],
        )

    def flip_seq(values, flip):
        return lax.ppermute(
            values,
            "seq",
            [(a, a - a % steps + (a % steps + flip) % steps) for a in range(seqs)],
        )

    place = jnp.stack([step, j]).astype(jnp.int32)
    relations = range(1, steps)
    bits = groups.bit_length() - 1

    def sum_groups(values):
        parts = values.reshape((2,) * bits + (steps,) + values.shape[1:])
        sums = []
        for p in range(steps):
            kept = lax.index_in_dim(parts, p, bits, False)
            left = list(range(bits))
            for k in range(bits):
                bit = (k + p) % bits
                axis = left.index(bit)
                left.remove(bit)
                distance = 2 ** (bits - 1 - bit) * steps
                own = (i // distance) % 2
                send = lax.dynamic_index_in_dim(kept, 1 - own, axis, False).astype(BF16)
                got = lax.ppermute(send, "seq", [(a, a ^ distance) for a in range(seqs)])
                kept = lax.dynamic_index_in_dim(kept, own, axis, False).astype(F32)
                kept = kept + got.astype(F32)
            sums.append(kept)
        sums = jnp.stack(sums)
        mine = pick(sums, step)
        got = [flip_seq(pick(sums, (step + m) % steps).astype(BF16), m) for m in relations]
        out = []
        for s in range(steps):
            value = mine
            for m in relations:
                value = jnp.where(s == (step - m) % steps, got[m - 1].astype(F32), value)
            out.append(value)
        return jnp.stack(out)

    group = [hidden] + [flip_seq(hidden, -m) for m in relations]

    squares_part = jnp.sum(jnp.square(hidden.astype(F32)), axis=1)
    tail = 8 * block
    small = jnp.concatenate(parts_of(squares_part))
    small = jnp.pad(small, (0, tail - small.size)).reshape(1, 1, 8, block)
    head_send = after(w_out, *group[1:]).reshape(head_rows, steps, halves, block)
    head_send = head_send.transpose(2, 1, 0, 3)
    head_send = head_send.reshape(1, halves, steps * head_rows, block)
    small = jnp.broadcast_to(small, (1, halves, 8, block))
    head_send = jnp.concatenate([head_send, small], axis=2)
    head_send = jnp.broadcast_to(head_send, (hids // halves,) + head_send.shape[1:])
    head_send = head_send.reshape(hids, steps * head_rows + 8, block)
    head_got = lax.all_to_all(head_send, "hid", 0, 0)
    head_mid = head_got[:, : steps * head_rows].reshape(hids, steps, head_rows, block)
    squares = head_got[:, steps * head_rows :].reshape(hids, tail)[:, : EXACT * rows]
    squares = jnp.sum(squares.astype(F32).reshape(hids * EXACT, rows), axis=0)

    w_own = pick(w_in, step)
    proj_parts = matmul(jnp.concatenate(group), w_own, ((1,), (0,)))
    proj_parts = proj_parts.reshape(steps, hids, part, depth)

    def owner_block(index):
        return lax.dynamic_index_in_dim(proj_parts, index, 1, False).reshape(owned, depth)

    send = [owner_block((j + shift) % hids).astype(BF16) for shift in range(1, hids)]
    send = [after(p, head_got) for p in send]
    received = [along_hid(send[shift - 1], shift) for shift in range(1, hids)]

    ids = after(codebook_ids, *send)
    ids = jnp.concatenate([ids] + [flip_seq(ids, -m) for m in relations], axis=1)
    ids_rows = [ids] + [turn_hid(ids, -k) for k in range(1, halves)]
    before = jnp.maximum(step - 1, 0)
    looked = jnp.take(pick(embedding, before), pick(ids, before), axis=0)

    head_send = after(head_mid, *send).transpose(1, 0, 2, 3)
    head_send = head_send.reshape(steps, hids * head_rows, block)
    head_send = jnp.broadcast_to(head_send, (groups,) + head_send.shape)
    head_send = head_send.reshape(seqs, hids * head_rows, block)
    head = lax.all_to_all(head_send, "seq", 0, 0).reshape(depth, block)

    squares = jnp.stack([squares] + [flip_seq(squares, -m) for m in relations])
    ratio_group = lax.rsqrt(squares / width_in + 1e-06).reshape(steps, hids, part)

    ratio = lax.dynamic_index_in_dim(ratio_group, j, 1, False).reshape(owned, 1)
    proj = owner_block(j)
    for r in received:
        proj += r.astype(F32)
    x_rows = ratio * proj + jnp.where(step > 0, looked.astype(F32), 0.0)
    scale = lax.rsqrt(jnp.mean(x_rows * x_rows, axis=1, keepdims=True) + 1e-06)
    gain = pick(depth_gain, step)[None, :]
    normed = (x_rows * scale * gain).astype(BF16)

    normed_rows = jnp.concatenate([normed] + [turn_hid(normed, -k) for k in range(1, halves)])
    targets = jnp.concatenate([pick(r, step) for r in ids_rows])
    logits = matmul(normed_rows, head, ((1,), (0,)))
    top = jnp.max(logits, axis=1)
    total = jnp.sum(jnp.exp(logits - top[:, None]), axis=1)
    stats = jnp.stack([top, total]).reshape(2, halves, -1)
    every = [stats] + [jnp.roll(turn_hid(stats, -t), t, axis=1) for t in range(1, halves)]
    tops = jnp.stack([e[0] for e in every]).reshape(halves, -1)
    totals = jnp.stack([e[1] for e in every]).reshape(halves, -1)
    top_all = jnp.max(tops, axis=0)
    lse = top_all + jnp.log(jnp.sum(totals * jnp.exp(tops - top_all), axis=0))
    entry = lax.broadcasted_iota(jnp.int32, logits.shape, 1) + half * block
    onehot = (targets[:, None] == entry).astype(F32)
    loss_weight = 2.0 * entries / frames
    d_logit = ((jnp.exp(logits - lse[:, None]) - onehot) * loss_weight).astype(BF16)

    d_norm_rows = matmul(d_logit, head, ((1,), (1,)))
    away = [d_norm_rows[k * owned : (k + 1) * owned].astype(BF16) for k in range(1, halves)]
    received = [turn_hid(a, k + 1) for k, a in enumerate(away)]
    d_norm = d_norm_rows[:owned]
    for r in received:
        d_norm += r.astype(F32)
    gated = gain * d_norm
    d_x = scale * gated - x_rows * scale**3 * jnp.mean(gated * x_rows, axis=1, keepdims=True)
    d_round = d_x.astype(BF16)
    d_ratio_part = jnp.sum(d_x * proj, axis=1).reshape(steps, part)

    part_out = matmul(normed_rows, after(d_logit, *away), ((0,), (0,))).astype(BF16)
    part_out = after(part_out, *received).reshape(seqs, depth // seqs, block)
    part_out = lax.all_to_all(part_out, "seq", 0, 0)
    part_out = part_out.reshape(groups, steps, hids, head_rows, block).astype(F32).sum(0)
    part_out = part_out.astype(BF16)
    sums = [
        lax.dynamic_index_in_dim(part_out, (j + shift) % hids, 1, False) for shift in range(hids)
    ]
    sums = [along_hid(p, shift) if shift else p for shift, p in enumerate(sums)]
    grad_out = head_gradient(place, sums, halves)

    pieces = [d_round] + [along_hid(d_round, shift) for shift in range(1, hids)]
    ratio_rows = ratio_group.reshape(steps, rows, 1)
    share, mine, *others = input_gradient(place, pieces, group, ratio_rows, seqs)
    share = share.reshape(seqs, depth // seqs, units)
    if groups == 2**bits and steps & (steps - 1) == 0:
        share = sum_groups(share)
    else:
        share = lax.all_to_all(share, "seq", 0, 0)
        share = share.reshape(groups, steps, depth // seqs, units).astype(F32).sum(0)
    grad_in = share.transpose(0, 2, 1)

    d_ratio = d_ratio_part[0]
    for m in relations:
        d_ratio += flip_seq(d_ratio_part[m], m)
    d_rows = jnp.broadcast_to(d_ratio, (hids, part))
    for shift in range(1, hids):
        d_rows = lax.dynamic_update_index_in_dim(
            d_rows, along_hid(d_ratio, shift), (j - shift) % hids, 0
        )
    ratio_own = ratio_group[0].reshape(rows)
    correction = ratio_own**3 * d_rows.reshape(rows) / width_in
    factors = jnp.stack([ratio_own, correction])[:, :, None]
    mine = [mine] + [flip_seq(others[m - 1], m) for m in relations]
    grad_hidden = hidden_gradient(place, mine, w_in, hidden, factors)
    return (grad_hidden, grad_in, grad_out)


def solution(mesh):
    placed = (
        P("seq", "hid"),
        P(None, "hid", None),
        P(),
        P(),
        P(("seq", "hid"), None, None),
        P(None, ("seq", "hid")),
    )
    return jax.shard_map(
        shards,
        mesh=mesh,
        in_specs=placed,
        out_specs=(P("seq", "hid"), P(None, "hid", "seq"), P(("seq", "hid"), None, None)),
        check_vma=False,
    )
```

```python
import jax
import jax.numpy as jnp
from jax import lax
from jax.experimental import pallas as pl
from jax.experimental.pallas import tpu as pltpu
from jax.sharding import PartitionSpec as P

F32 = jnp.float32
BF16 = jnp.bfloat16


def pick(values, index):
    return lax.dynamic_index_in_dim(values, index, axis=0, keepdims=False)


def matmul(a, b, contract):
    return lax.dot_general(a, b, (contract, ((), ())), preferred_element_type=F32)


def after(value, *others):
    return lax.optimization_barrier((value, *others))[0]


VMEM = pltpu.CompilerParams(vmem_limit_bytes=60 * 2**20)


def whole(shape):
    return pl.BlockSpec(shape, lambda n, place: (0,) * len(shape))


def call(kernel, place, grid, in_specs, out_specs, out_shape, scratch, flops, args):
    moved = sum(a.size * a.dtype.itemsize for a in args)
    return pl.pallas_call(
        kernel,
        grid_spec=pltpu.PrefetchScalarGridSpec(
            num_scalar_prefetch=1,
            grid=(grid,),
            in_specs=in_specs,
            out_specs=out_specs,
            scratch_shapes=scratch,
        ),
        out_shape=out_shape,
        compiler_params=VMEM,
        cost_estimate=pl.CostEstimate(flops=flops, bytes_accessed=moved, transcendentals=0),
    )(place, *args)


EXACT = 3


def parts_of(values):
    out = []
    for _ in range(EXACT):
        piece = lax.reduce_precision(values, 8, 7)
        values = values - piece
        out.append(piece.astype(BF16))
    return out


def head_gradient(place, pieces, halves):
    hids = len(pieces)
    steps, rows, block = pieces[0].shape

    def kernel(place_ref, *refs):
        pieces, out = refs[:-1], refs[-1]
        for r in range(halves):
            which = lax.rem(place_ref[1] - r + hids, halves)
            columns = pl.ds(pl.multiple_of(which * block, block), block)
            for s in range(steps):
                total = pieces[r][s].astype(F32)
                for k in range(r + halves, hids, halves):
                    total = total + pieces[k][s].astype(F32)
                out[:, s, columns] = total

    return call(
        kernel,
        place,
        1,
        [whole((steps, rows, block))] * hids,
        whole((rows, steps, halves * block)),
        jax.ShapeDtypeStruct((rows, steps, halves * block), F32),
        [],
        hids * steps * rows * block,
        tuple(pieces),
    )


def input_gradient(place, pieces, group, ratio, seqs):
    hids, steps = len(pieces), len(group)
    owned, depth = pieces[0].shape
    rows, units = group[0].shape
    part = owned // steps
    wide = min(512, depth)

    def kernel(place_ref, *refs):
        chunks, group, ratio = refs[:hids], refs[hids : hids + steps], refs[hids + steps]
        out, plain, scaled = refs[hids + steps + 1], refs[hids + steps + 2 : -1], refs[-1]
        j = place_ref[1]
        for r in range(hids):
            to = pl.multiple_of(lax.rem(j - r + hids, hids) * part, part)
            for m in range(steps):
                values = chunks[r][m * part : (m + 1) * part, :]
                plain[m][pl.ds(to, part), :] = values
                factor = ratio[m, pl.ds(to, part), :]
                scaled[m, pl.ds(to, part), :] = (values.astype(F32) * factor).astype(BF16)
        total = None
        for m in range(steps):
            term = lax.dot_general(
                scaled[m], group[m][...], (((0,), (0,)), ((), ())), preferred_element_type=F32
            )
            total = term if total is None else total + term
        out[...] = total.astype(BF16)

    return call(
        kernel,
        place,
        depth // wide,
        [pl.BlockSpec((owned, wide), lambda n, place: (0, n))] * hids
        + [whole((rows, units))] * steps
        + [whole((steps, rows, 1))],
        [pl.BlockSpec((wide, units), lambda n, place: (n, 0))]
        + [pl.BlockSpec((rows, wide), lambda n, place: (0, n))] * steps,
        [jax.ShapeDtypeStruct((depth, units), BF16)]
        + [jax.ShapeDtypeStruct((rows, depth), BF16)] * steps,
        [pltpu.VMEM((steps, rows, wide), BF16)],
        2 * steps * rows * units * depth,
        (*pieces, *group, ratio),
    )


def hidden_gradient(place, d_rows, w_in, hidden, factors):
    steps, units, depth = w_in.shape
    rows = hidden.shape[0]
    wide = min(256, units)

    def kernel(place_ref, *refs):
        d_rows, w, hidden, factors, out = refs[:steps], refs[-4], refs[-3], refs[-2], refs[-1]
        total = None
        for r in range(steps):
            which = lax.rem(place_ref[0] - r + steps, steps)
            term = lax.dot_general(
                d_rows[r][...], w[which], (((1,), (1,)), ((), ())), preferred_element_type=F32
            )
            total = term if total is None else total + term
        out[...] = (factors[0] * total - factors[1] * hidden[...].astype(F32)).astype(BF16)

    return call(
        kernel,
        place,
        units // wide,
        [whole((rows, depth))] * steps
        + [
            pl.BlockSpec((steps, wide, depth), lambda n, place: (0, n, 0)),
            pl.BlockSpec((rows, wide), lambda n, place: (0, n)),
            whole((2, rows, 1)),
        ],
        pl.BlockSpec((rows, wide), lambda n, place: (0, n)),
        jax.ShapeDtypeStruct((rows, units), BF16),
        [],
        2 * steps * rows * units * depth,
        (*d_rows, w_in, hidden, factors),
    )


def shards(hidden, w_in, embedding, depth_gain, w_out, codebook_ids):
    hids = lax.axis_size("hid")
    seqs = lax.axis_size("seq")
    steps, units, depth = w_in.shape
    entries = w_out.shape[2]
    rows = hidden.shape[0]
    part = rows // hids
    width_in = units * hids
    frames = rows * seqs
    halves = 2 if hids % 2 == 0 else 1
    block = entries // halves
    head_rows = w_out.shape[0]
    groups = seqs // steps
    i = lax.axis_index("seq")
    j = lax.axis_index("hid")
    step = i % steps
    half = j % halves
    owned = steps * part

    def along_hid(values, shift):
        return lax.ppermute(values, "hid", [(a, (a + shift) % hids) for a in range(hids)])

    def turn_hid(values, shift):
        return lax.ppermute(
            values,
            "hid",
            [(a, a - a % halves + (a % halves + shift) % halves) for a in range(hids)],
        )

    def flip_seq(values, flip):
        return lax.ppermute(
            values,
            "seq",
            [(a, a - a % steps + (a % steps + flip) % steps) for a in range(seqs)],
        )

    place = jnp.stack([step, j]).astype(jnp.int32)
    relations = range(1, steps)
    bits = groups.bit_length() - 1
    halving = groups == 2**bits and bits > 0

    def across(values, bit):
        distance = 2 ** (bits - 1 - bit) * steps
        return lax.ppermute(values, "seq", [(a, a ^ distance) for a in range(seqs)])

    def own_bit(bit):
        return (i // (2 ** (bits - 1 - bit) * steps)) % 2

    group = [hidden] + [flip_seq(hidden, -m) for m in relations]

    squares_part = jnp.sum(jnp.square(hidden.astype(F32)), axis=1)
    tail = 8 * block
    small = jnp.concatenate(parts_of(squares_part))
    small = jnp.pad(small, (0, tail - small.size)).reshape(1, 1, 8, block)
    head_send = after(w_out, *group[1:]).reshape(head_rows, steps, halves, block)
    head_send = head_send.transpose(2, 1, 0, 3)
    head_send = head_send.reshape(1, halves, steps * head_rows, block)
    small = jnp.broadcast_to(small, (1, halves, 8, block))
    head_send = jnp.concatenate([head_send, small], axis=2)
    head_send = jnp.broadcast_to(head_send, (hids // halves,) + head_send.shape[1:])
    head_send = head_send.reshape(hids, steps * head_rows + 8, block)
    head_got = lax.all_to_all(head_send, "hid", 0, 0)
    head_mid = head_got[:, : steps * head_rows].reshape(hids, steps, head_rows, block)
    squares = head_got[:, steps * head_rows :].reshape(hids, tail)[:, : EXACT * rows]
    squares = jnp.sum(squares.astype(F32).reshape(hids * EXACT, rows), axis=0)

    w_own = pick(w_in, step)
    proj_parts = matmul(jnp.concatenate(group), w_own, ((1,), (0,)))
    proj_parts = proj_parts.reshape(steps, hids, part, depth)

    def owner_block(index):
        return lax.dynamic_index_in_dim(proj_parts, index, 1, False).reshape(owned, depth)

    send = [owner_block((j + shift) % hids).astype(BF16) for shift in range(1, hids)]
    send = [after(p, head_got) for p in send]
    received = [along_hid(send[shift - 1], shift) for shift in range(1, hids)]

    ids = after(codebook_ids, *send)
    ids = jnp.concatenate([ids] + [flip_seq(ids, -m) for m in relations], axis=1)
    ids_rows = [ids] + [turn_hid(ids, -k) for k in range(1, halves)]
    before = jnp.maximum(step - 1, 0)
    looked = jnp.take(pick(embedding, before), pick(ids, before), axis=0)

    head_send = after(head_mid, *send).transpose(1, 0, 2, 3)
    head_send = head_send.reshape(steps, hids * head_rows, block)
    head_send = jnp.broadcast_to(head_send, (groups,) + head_send.shape)
    head_send = head_send.reshape(seqs, hids * head_rows, block)
    head = lax.all_to_all(head_send, "seq", 0, 0).reshape(depth, block)

    squares = jnp.stack([squares] + [flip_seq(squares, -m) for m in relations])
    ratio_group = lax.rsqrt(squares / width_in + 1e-06).reshape(steps, hids, part)

    ratio = lax.dynamic_index_in_dim(ratio_group, j, 1, False).reshape(owned, 1)
    proj = owner_block(j)
    for r in received:
        proj += r.astype(F32)
    x_rows = ratio * proj + jnp.where(step > 0, looked.astype(F32), 0.0)
    scale = lax.rsqrt(jnp.mean(x_rows * x_rows, axis=1, keepdims=True) + 1e-06)
    gain = pick(depth_gain, step)[None, :]
    normed = (x_rows * scale * gain).astype(BF16)

    normed_rows = jnp.concatenate([normed] + [turn_hid(normed, -k) for k in range(1, halves)])
    targets = jnp.concatenate([pick(r, step) for r in ids_rows])
    logits = matmul(normed_rows, head, ((1,), (0,)))
    top = jnp.max(logits, axis=1)
    total = jnp.sum(jnp.exp(logits - top[:, None]), axis=1)
    stats = jnp.stack([top, total]).reshape(2, halves, -1)
    every = [stats] + [jnp.roll(turn_hid(stats, -t), t, axis=1) for t in range(1, halves)]
    tops = jnp.stack([e[0] for e in every]).reshape(halves, -1)
    totals = jnp.stack([e[1] for e in every]).reshape(halves, -1)
    top_all = jnp.max(tops, axis=0)
    lse = top_all + jnp.log(jnp.sum(totals * jnp.exp(tops - top_all), axis=0))
    entry = lax.broadcasted_iota(jnp.int32, logits.shape, 1) + half * block
    onehot = (targets[:, None] == entry).astype(F32)
    loss_weight = 2.0 * entries / frames
    d_logit = ((jnp.exp(logits - lse[:, None]) - onehot) * loss_weight).astype(BF16)

    d_norm_rows = matmul(d_logit, head, ((1,), (1,)))
    away = [d_norm_rows[k * owned : (k + 1) * owned].astype(BF16) for k in range(1, halves)]
    received = [turn_hid(a, k + 1) for k, a in enumerate(away)]
    d_norm = d_norm_rows[:owned]
    for r in received:
        d_norm += r.astype(F32)
    gated = gain * d_norm
    d_x = scale * gated - x_rows * scale**3 * jnp.mean(gated * x_rows, axis=1, keepdims=True)
    d_round = d_x.astype(BF16)
    d_ratio_part = jnp.sum(d_x * proj, axis=1).reshape(steps, part)

    width = depth // seqs
    d_after = after(d_logit, *away)
    if halving:
        columns = normed_rows.reshape((-1,) + (2,) * bits + (steps, width))
        kept = []
        for p in range(steps):
            mine = lax.index_in_dim(columns, p, 1 + bits, False)
            bit = p % bits
            ends = [
                lax.dynamic_index_in_dim(mine, side, 1 + bit, False).reshape(len(normed_rows), -1)
                for side in (1 - own_bit(bit), own_bit(bit))
            ]
            send, keep = [matmul(e, d_after, ((0,), (0,))) for e in ends]
            kept.append(keep + across(send.astype(BF16), bit).astype(F32))
        first_halves = kept
        sums = []
        for p in range(steps):
            part_sum = kept[p].reshape((2,) * (bits - 1) + (width, block))
            left = [b for b in range(bits) if b != p % bits]
            for k in range(1, bits):
                bit = (p + k) % bits
                axis = left.index(bit)
                left.remove(bit)
                send = lax.dynamic_index_in_dim(part_sum, 1 - own_bit(bit), axis, False)
                part_sum = lax.dynamic_index_in_dim(part_sum, own_bit(bit), axis, False)
                part_sum += across(send.astype(BF16), bit).astype(F32)
            sums.append(part_sum)
        sums = jnp.stack(sums).astype(BF16)
        got = [pick(sums, step)]
        got += [flip_seq(pick(sums, (step + m) % steps), m) for m in relations]
        part_out = []
        for s in range(steps):
            value = got[0]
            for m in relations:
                value = jnp.where(s == (step - m) % steps, got[m], value)
            part_out.append(value)
        part_out = jnp.stack(part_out).reshape(steps, hids, head_rows, block)
    else:
        first_halves = []
        part_out = matmul(normed_rows, d_after, ((0,), (0,))).astype(BF16)
        part_out = lax.all_to_all(part_out.reshape(seqs, width, block), "seq", 0, 0)
        part_out = part_out.reshape(groups, steps, hids, head_rows, block).astype(F32).sum(0)
        part_out = part_out.astype(BF16)
    sums = [
        lax.dynamic_index_in_dim(part_out, (j + shift) % hids, 1, False) for shift in range(hids)
    ]
    sums = [along_hid(p, shift) if shift else p for shift, p in enumerate(sums)]
    grad_out = head_gradient(place, sums, halves)

    pieces = [d_round] + [along_hid(d_round, shift) for shift in range(1, hids)]
    ratio_rows = ratio_group.reshape(steps, rows, 1)
    share, mine, *others = input_gradient(after(place, *first_halves), pieces, group, ratio_rows, seqs)
    share = lax.all_to_all(share.reshape(seqs, depth // seqs, units), "seq", 0, 0)
    share = share.reshape(groups, steps, depth // seqs, units).astype(F32).sum(0)
    grad_in = share.transpose(0, 2, 1)

    d_ratio = d_ratio_part[0]
    for m in relations:
        d_ratio += flip_seq(d_ratio_part[m], m)
    d_rows = jnp.broadcast_to(d_ratio, (hids, part))
    for shift in range(1, hids):
        d_rows = lax.dynamic_update_index_in_dim(
            d_rows, along_hid(d_ratio, shift), (j - shift) % hids, 0
        )
    ratio_own = ratio_group[0].reshape(rows)
    correction = ratio_own**3 * d_rows.reshape(rows) / width_in
    factors = jnp.stack([ratio_own, correction])[:, :, None]
    mine = [mine] + [flip_seq(others[m - 1], m) for m in relations]
    grad_hidden = hidden_gradient(place, mine, w_in, hidden, factors)
    return (grad_hidden, grad_in, grad_out)


def solution(mesh):
    placed = (
        P("seq", "hid"),
        P(None, "hid", None),
        P(),
        P(),
        P(("seq", "hid"), None, None),
        P(None, ("seq", "hid")),
    )
    return jax.shard_map(
        shards,
        mesh=mesh,
        in_specs=placed,
        out_specs=(P("seq", "hid"), P(None, "hid", "seq"), P(("seq", "hid"), None, None)),
        check_vma=False,
    )
```

```python
import jax
import jax.numpy as jnp
from jax import lax
from jax.experimental import pallas as pl
from jax.experimental.pallas import tpu as pltpu
from jax.sharding import PartitionSpec as P

F32 = jnp.float32
BF16 = jnp.bfloat16


def pick(values, index):
    return lax.dynamic_index_in_dim(values, index, axis=0, keepdims=False)


def matmul(a, b, contract):
    return lax.dot_general(a, b, (contract, ((), ())), preferred_element_type=F32)


def after(value, *others):
    return lax.optimization_barrier((value, *others))[0]


VMEM = pltpu.CompilerParams(vmem_limit_bytes=60 * 2**20)


def whole(shape):
    return pl.BlockSpec(shape, lambda n, place: (0,) * len(shape))


def call(kernel, place, grid, in_specs, out_specs, out_shape, scratch, flops, args):
    moved = sum(a.size * a.dtype.itemsize for a in args)
    return pl.pallas_call(
        kernel,
        grid_spec=pltpu.PrefetchScalarGridSpec(
            num_scalar_prefetch=1,
            grid=(grid,),
            in_specs=in_specs,
            out_specs=out_specs,
            scratch_shapes=scratch,
        ),
        out_shape=out_shape,
        compiler_params=VMEM,
        cost_estimate=pl.CostEstimate(flops=flops, bytes_accessed=moved, transcendentals=0),
    )(place, *args)


EXACT = 3


def parts_of(values):
    out = []
    for _ in range(EXACT):
        piece = lax.reduce_precision(values, 8, 7)
        values = values - piece
        out.append(piece.astype(BF16))
    return out


def head_gradient(place, pieces, halves):
    hids = len(pieces)
    steps, rows, block = pieces[0].shape

    def kernel(place_ref, *refs):
        pieces, out = refs[:-1], refs[-1]
        for r in range(halves):
            which = lax.rem(place_ref[1] - r + hids, halves)
            columns = pl.ds(pl.multiple_of(which * block, block), block)
            for s in range(steps):
                total = pieces[r][s].astype(F32)
                for k in range(r + halves, hids, halves):
                    total = total + pieces[k][s].astype(F32)
                out[:, s, columns] = total

    return call(
        kernel,
        place,
        1,
        [whole((steps, rows, block))] * hids,
        whole((rows, steps, halves * block)),
        jax.ShapeDtypeStruct((rows, steps, halves * block), F32),
        [],
        hids * steps * rows * block,
        tuple(pieces),
    )


def input_gradient(place, pieces, group, ratio, seqs):
    hids, steps = len(pieces), len(group)
    owned, depth = pieces[0].shape
    rows, units = group[0].shape
    part = owned // steps
    wide = min(512, depth)

    def kernel(place_ref, *refs):
        chunks, group, ratio = refs[:hids], refs[hids : hids + steps], refs[hids + steps]
        out, plain, scaled = refs[hids + steps + 1], refs[hids + steps + 2 : -1], refs[-1]
        j = place_ref[1]
        for r in range(hids):
            to = pl.multiple_of(lax.rem(j - r + hids, hids) * part, part)
            for m in range(steps):
                values = chunks[r][m * part : (m + 1) * part, :]
                plain[m][pl.ds(to, part), :] = values
                factor = ratio[m, pl.ds(to, part), :]
                scaled[m, pl.ds(to, part), :] = (values.astype(F32) * factor).astype(BF16)
        total = None
        for m in range(steps):
            term = lax.dot_general(
                scaled[m], group[m][...], (((0,), (0,)), ((), ())), preferred_element_type=F32
            )
            total = term if total is None else total + term
        out[...] = total.astype(BF16)

    return call(
        kernel,
        place,
        depth // wide,
        [pl.BlockSpec((owned, wide), lambda n, place: (0, n))] * hids
        + [whole((rows, units))] * steps
        + [whole((steps, rows, 1))],
        [pl.BlockSpec((wide, units), lambda n, place: (n, 0))]
        + [pl.BlockSpec((rows, wide), lambda n, place: (0, n))] * steps,
        [jax.ShapeDtypeStruct((depth, units), BF16)]
        + [jax.ShapeDtypeStruct((rows, depth), BF16)] * steps,
        [pltpu.VMEM((steps, rows, wide), BF16)],
        2 * steps * rows * units * depth,
        (*pieces, *group, ratio),
    )


def hidden_gradient(place, d_rows, w_in, hidden, factors):
    steps, units, depth = w_in.shape
    rows = hidden.shape[0]
    wide = min(256, units)

    def kernel(place_ref, *refs):
        d_rows, w, hidden, factors, out = refs[:steps], refs[-4], refs[-3], refs[-2], refs[-1]
        total = None
        for r in range(steps):
            which = lax.rem(place_ref[0] - r + steps, steps)
            term = lax.dot_general(
                d_rows[r][...], w[which], (((1,), (1,)), ((), ())), preferred_element_type=F32
            )
            total = term if total is None else total + term
        out[...] = (factors[0] * total - factors[1] * hidden[...].astype(F32)).astype(BF16)

    return call(
        kernel,
        place,
        units // wide,
        [whole((rows, depth))] * steps
        + [
            pl.BlockSpec((steps, wide, depth), lambda n, place: (0, n, 0)),
            pl.BlockSpec((rows, wide), lambda n, place: (0, n)),
            whole((2, rows, 1)),
        ],
        pl.BlockSpec((rows, wide), lambda n, place: (0, n)),
        jax.ShapeDtypeStruct((rows, units), BF16),
        [],
        2 * steps * rows * units * depth,
        (*d_rows, w_in, hidden, factors),
    )


def shards(hidden, w_in, embedding, depth_gain, w_out, codebook_ids):
    hids = lax.axis_size("hid")
    seqs = lax.axis_size("seq")
    steps, units, depth = w_in.shape
    entries = w_out.shape[2]
    rows = hidden.shape[0]
    part = rows // hids
    width_in = units * hids
    frames = rows * seqs
    halves = 2 if hids % 2 == 0 else 1
    block = entries // halves
    head_rows = w_out.shape[0]
    groups = seqs // steps
    i = lax.axis_index("seq")
    j = lax.axis_index("hid")
    step = i % steps
    half = j % halves
    owned = steps * part

    def along_hid(values, shift):
        return lax.ppermute(values, "hid", [(a, (a + shift) % hids) for a in range(hids)])

    def turn_hid(values, shift):
        return lax.ppermute(
            values,
            "hid",
            [(a, a - a % halves + (a % halves + shift) % halves) for a in range(hids)],
        )

    def flip_seq(values, flip):
        return lax.ppermute(
            values,
            "seq",
            [(a, a - a % steps + (a % steps + flip) % steps) for a in range(seqs)],
        )

    place = jnp.stack([step, j]).astype(jnp.int32)
    relations = range(1, steps)
    bits = groups.bit_length() - 1
    halving = groups == 2**bits and bits > 0

    def across(values, bit):
        distance = 2 ** (bits - 1 - bit) * steps
        return lax.ppermute(values, "seq", [(a, a ^ distance) for a in range(seqs)])

    def own_bit(bit):
        return (i // (2 ** (bits - 1 - bit) * steps)) % 2

    group = [hidden] + [flip_seq(hidden, -m) for m in relations]

    squares_part = jnp.sum(jnp.square(hidden.astype(F32)), axis=1)
    tail = 8 * block
    small = jnp.concatenate(parts_of(squares_part))
    small = jnp.pad(small, (0, tail - small.size)).reshape(1, 1, 8, block)
    head_send = after(w_out, *group[1:]).reshape(head_rows, steps, halves, block)
    head_send = head_send.transpose(2, 1, 0, 3)
    head_send = head_send.reshape(1, halves, steps * head_rows, block)
    small = jnp.broadcast_to(small, (1, halves, 8, block))
    head_send = jnp.concatenate([head_send, small], axis=2)
    head_send = jnp.broadcast_to(head_send, (hids // halves,) + head_send.shape[1:])
    head_send = head_send.reshape(hids, steps * head_rows + 8, block)
    head_got = lax.all_to_all(head_send, "hid", 0, 0)
    head_mid = head_got[:, : steps * head_rows].reshape(hids, steps, head_rows, block)
    squares = head_got[:, steps * head_rows :].reshape(hids, tail)[:, : EXACT * rows]
    squares = jnp.sum(squares.astype(F32).reshape(hids * EXACT, rows), axis=0)

    w_own = pick(w_in, step)
    proj_parts = matmul(jnp.concatenate(group), w_own, ((1,), (0,)))
    proj_parts = proj_parts.reshape(steps, hids, part, depth)

    def owner_block(index):
        return lax.dynamic_index_in_dim(proj_parts, index, 1, False).reshape(owned, depth)

    send = [owner_block((j + shift) % hids).astype(BF16) for shift in range(1, hids)]
    send = [after(p, head_got) for p in send]
    received = [along_hid(send[shift - 1], shift) for shift in range(1, hids)]

    ids = after(codebook_ids, *send)
    ids = jnp.concatenate([ids] + [flip_seq(ids, -m) for m in relations], axis=1)
    ids_rows = [ids] + [turn_hid(ids, -k) for k in range(1, halves)]
    before = jnp.maximum(step - 1, 0)
    looked = jnp.take(pick(embedding, before), pick(ids, before), axis=0)

    head_send = after(head_mid, *send).transpose(1, 0, 2, 3)
    head_send = head_send.reshape(steps, hids * head_rows, block)
    head_send = jnp.broadcast_to(head_send, (groups,) + head_send.shape)
    head_send = head_send.reshape(seqs, hids * head_rows, block)
    head = lax.all_to_all(head_send, "seq", 0, 0).reshape(depth, block)

    squares = jnp.stack([squares] + [flip_seq(squares, -m) for m in relations])
    ratio_group = lax.rsqrt(squares / width_in + 1e-06).reshape(steps, hids, part)

    ratio = lax.dynamic_index_in_dim(ratio_group, j, 1, False).reshape(owned, 1)
    proj = owner_block(j)
    for r in received:
        proj += r.astype(F32)
    x_rows = ratio * proj + jnp.where(step > 0, looked.astype(F32), 0.0)
    scale = lax.rsqrt(jnp.mean(x_rows * x_rows, axis=1, keepdims=True) + 1e-06)
    gain = pick(depth_gain, step)[None, :]
    normed = (x_rows * scale * gain).astype(BF16)

    normed_rows = jnp.concatenate([normed] + [turn_hid(normed, -k) for k in range(1, halves)])
    targets = jnp.concatenate([pick(r, step) for r in ids_rows])
    logits = matmul(normed_rows, head, ((1,), (0,)))
    top = jnp.max(logits, axis=1)
    total = jnp.sum(jnp.exp(logits - top[:, None]), axis=1)
    stats = jnp.stack([top, total]).reshape(2, halves, -1)
    every = [stats] + [jnp.roll(turn_hid(stats, -t), t, axis=1) for t in range(1, halves)]
    tops = jnp.stack([e[0] for e in every]).reshape(halves, -1)
    totals = jnp.stack([e[1] for e in every]).reshape(halves, -1)
    top_all = jnp.max(tops, axis=0)
    lse = top_all + jnp.log(jnp.sum(totals * jnp.exp(tops - top_all), axis=0))
    entry = lax.broadcasted_iota(jnp.int32, logits.shape, 1) + half * block
    onehot = (targets[:, None] == entry).astype(F32)
    loss_weight = 2.0 * entries / frames
    d_logit = ((jnp.exp(logits - lse[:, None]) - onehot) * loss_weight).astype(BF16)

    d_norm_rows = matmul(d_logit, head, ((1,), (1,)))
    away = [d_norm_rows[k * owned : (k + 1) * owned].astype(BF16) for k in range(1, halves)]
    received = [turn_hid(a, k + 1) for k, a in enumerate(away)]
    d_norm = d_norm_rows[:owned]
    for r in received:
        d_norm += r.astype(F32)
    gated = gain * d_norm
    d_x = scale * gated - x_rows * scale**3 * jnp.mean(gated * x_rows, axis=1, keepdims=True)
    d_round = d_x.astype(BF16)
    d_ratio_part = jnp.sum(d_x * proj, axis=1).reshape(steps, part)

    width = depth // seqs
    d_after = after(d_logit, *away)
    if halving:
        product = matmul(normed_rows, d_after, ((0,), (0,))).astype(BF16)
        product = product.reshape((2,) * bits + (steps, width, block))
        part_sums = [lax.index_in_dim(product, p, bits, False) for p in range(steps)]
        left = [list(range(bits)) for _ in range(steps)]
        first_halves = []
        for k in range(bits):
            for p in range(steps):
                bit = (p + k) % bits
                axis = left[p].index(bit)
                left[p].remove(bit)
                send = lax.dynamic_index_in_dim(part_sums[p], 1 - own_bit(bit), axis, False)
                keep = lax.dynamic_index_in_dim(part_sums[p], own_bit(bit), axis, False)
                got = across(send.astype(BF16), bit)
                part_sums[p] = keep.astype(F32) + got.astype(F32)
            first_halves = first_halves or list(part_sums)
        sums = part_sums
        sums = jnp.stack(sums).astype(BF16)
        group_sums = [sums]
        got = [pick(sums, step)]
        got += [flip_seq(pick(sums, (step + m) % steps), m) for m in relations]
        part_out = []
        for s in range(steps):
            value = got[0]
            for m in relations:
                value = jnp.where(s == (step - m) % steps, got[m], value)
            part_out.append(value)
        part_out = jnp.stack(part_out).reshape(steps, hids, head_rows, block)
    else:
        first_halves, group_sums = [], []
        part_out = matmul(normed_rows, d_after, ((0,), (0,))).astype(BF16)
        part_out = lax.all_to_all(part_out.reshape(seqs, width, block), "seq", 0, 0)
        part_out = part_out.reshape(groups, steps, hids, head_rows, block).astype(F32).sum(0)
        part_out = part_out.astype(BF16)
    sums = [
        lax.dynamic_index_in_dim(part_out, (j + shift) % hids, 1, False) for shift in range(hids)
    ]
    sums = [along_hid(p, shift) if shift else p for shift, p in enumerate(sums)]
    grad_out = head_gradient(place, sums, halves)

    pieces = [d_round] + [along_hid(d_round, shift) for shift in range(1, hids)]
    ratio_rows = ratio_group.reshape(steps, rows, 1)
    share, mine, *others = input_gradient(after(place, *first_halves), pieces, group, ratio_rows, seqs)
    share = after(share, *group_sums).reshape(seqs, depth // seqs, units)
    share = lax.all_to_all(share, "seq", 0, 0)
    share = share.reshape(groups, steps, depth // seqs, units).astype(F32).sum(0)
    grad_in = share.transpose(0, 2, 1)

    d_ratio = d_ratio_part[0]
    for m in relations:
        d_ratio += flip_seq(d_ratio_part[m], m)
    d_rows = jnp.broadcast_to(d_ratio, (hids, part))
    for shift in range(1, hids):
        d_rows = lax.dynamic_update_index_in_dim(
            d_rows, along_hid(d_ratio, shift), (j - shift) % hids, 0
        )
    ratio_own = ratio_group[0].reshape(rows)
    correction = ratio_own**3 * d_rows.reshape(rows) / width_in
    factors = jnp.stack([ratio_own, correction])[:, :, None]
    mine = [mine] + [flip_seq(others[m - 1], m) for m in relations]
    grad_hidden = hidden_gradient(place, mine, w_in, hidden, factors)
    return (grad_hidden, grad_in, grad_out)


def solution(mesh):
    placed = (
        P("seq", "hid"),
        P(None, "hid", None),
        P(),
        P(),
        P(("seq", "hid"), None, None),
        P(None, ("seq", "hid")),
    )
    return jax.shard_map(
        shards,
        mesh=mesh,
        in_specs=placed,
        out_specs=(P("seq", "hid"), P(None, "hid", "seq"), P(("seq", "hid"), None, None)),
        check_vma=False,
    )
```

```python
import jax
import jax.numpy as jnp
from jax import lax
from jax.experimental import pallas as pl
from jax.experimental.pallas import tpu as pltpu
from jax.sharding import PartitionSpec as P

F32 = jnp.float32
BF16 = jnp.bfloat16


def pick(values, index):
    return lax.dynamic_index_in_dim(values, index, axis=0, keepdims=False)


def matmul(a, b, contract):
    return lax.dot_general(a, b, (contract, ((), ())), preferred_element_type=F32)


def after(value, *others):
    return lax.optimization_barrier((value, *others))[0]


VMEM = pltpu.CompilerParams(vmem_limit_bytes=60 * 2**20)


def whole(shape):
    return pl.BlockSpec(shape, lambda n, place: (0,) * len(shape))


def call(kernel, place, grid, in_specs, out_specs, out_shape, scratch, flops, args):
    moved = sum(a.size * a.dtype.itemsize for a in args)
    return pl.pallas_call(
        kernel,
        grid_spec=pltpu.PrefetchScalarGridSpec(
            num_scalar_prefetch=1,
            grid=(grid,),
            in_specs=in_specs,
            out_specs=out_specs,
            scratch_shapes=scratch,
        ),
        out_shape=out_shape,
        compiler_params=VMEM,
        cost_estimate=pl.CostEstimate(flops=flops, bytes_accessed=moved, transcendentals=0),
    )(place, *args)


EXACT = 3


def parts_of(values):
    out = []
    for _ in range(EXACT):
        piece = lax.reduce_precision(values, 8, 7)
        values = values - piece
        out.append(piece.astype(BF16))
    return out


def head_gradient(place, pieces, halves):
    hids = len(pieces)
    steps, rows, block = pieces[0].shape

    def kernel(place_ref, *refs):
        pieces, out = refs[:-1], refs[-1]
        for r in range(halves):
            which = lax.rem(place_ref[1] - r + hids, halves)
            columns = pl.ds(pl.multiple_of(which * block, block), block)
            for s in range(steps):
                total = pieces[r][s].astype(F32)
                for k in range(r + halves, hids, halves):
                    total = total + pieces[k][s].astype(F32)
                out[:, s, columns] = total

    return call(
        kernel,
        place,
        1,
        [whole((steps, rows, block))] * hids,
        whole((rows, steps, halves * block)),
        jax.ShapeDtypeStruct((rows, steps, halves * block), F32),
        [],
        hids * steps * rows * block,
        tuple(pieces),
    )


def input_gradient(place, pieces, group, ratio, seqs, earlier):
    hids, steps = len(pieces), len(group)
    owned, depth = pieces[0].shape
    rows, units = group[0].shape
    part = owned // steps
    wide = min(512, depth)

    def kernel(place_ref, *refs):
        chunks, group, ratio = refs[:hids], refs[hids : hids + steps], refs[hids + steps]
        outs = refs[hids + steps + 1 + len(earlier) :]
        out, plain, scaled = outs[0], outs[1:-1], outs[-1]
        j = place_ref[1]
        for r in range(hids):
            to = pl.multiple_of(lax.rem(j - r + hids, hids) * part, part)
            for m in range(steps):
                values = chunks[r][m * part : (m + 1) * part, :]
                plain[m][pl.ds(to, part), :] = values
                factor = ratio[m, pl.ds(to, part), :]
                scaled[m, pl.ds(to, part), :] = (values.astype(F32) * factor).astype(BF16)
        total = None
        for m in range(steps):
            term = lax.dot_general(
                scaled[m], group[m][...], (((0,), (0,)), ((), ())), preferred_element_type=F32
            )
            total = term if total is None else total + term
        out[...] = total.astype(BF16)

    return call(
        kernel,
        place,
        depth // wide,
        [pl.BlockSpec((owned, wide), lambda n, place: (0, n))] * hids
        + [whole((rows, units))] * steps
        + [whole((steps, rows, 1))]
        + [pl.BlockSpec(memory_space=pl.ANY)] * len(earlier),
        [pl.BlockSpec((wide, units), lambda n, place: (n, 0))]
        + [pl.BlockSpec((rows, wide), lambda n, place: (0, n))] * steps,
        [jax.ShapeDtypeStruct((depth, units), BF16)]
        + [jax.ShapeDtypeStruct((rows, depth), BF16)] * steps,
        [pltpu.VMEM((steps, rows, wide), BF16)],
        2 * steps * rows * units * depth,
        (*pieces, *group, ratio, *earlier),
    )


def hidden_gradient(place, d_rows, w_in, hidden, factors):
    steps, units, depth = w_in.shape
    rows = hidden.shape[0]
    wide = min(256, units)

    def kernel(place_ref, *refs):
        d_rows, w, hidden, factors, out = refs[:steps], refs[-4], refs[-3], refs[-2], refs[-1]
        total = None
        for r in range(steps):
            which = lax.rem(place_ref[0] - r + steps, steps)
            term = lax.dot_general(
                d_rows[r][...], w[which], (((1,), (1,)), ((), ())), preferred_element_type=F32
            )
            total = term if total is None else total + term
        out[...] = (factors[0] * total - factors[1] * hidden[...].astype(F32)).astype(BF16)

    return call(
        kernel,
        place,
        units // wide,
        [whole((rows, depth))] * steps
        + [
            pl.BlockSpec((steps, wide, depth), lambda n, place: (0, n, 0)),
            pl.BlockSpec((rows, wide), lambda n, place: (0, n)),
            whole((2, rows, 1)),
        ],
        pl.BlockSpec((rows, wide), lambda n, place: (0, n)),
        jax.ShapeDtypeStruct((rows, units), BF16),
        [],
        2 * steps * rows * units * depth,
        (*d_rows, w_in, hidden, factors),
    )


def shards(hidden, w_in, embedding, depth_gain, w_out, codebook_ids):
    hids = lax.axis_size("hid")
    seqs = lax.axis_size("seq")
    steps, units, depth = w_in.shape
    entries = w_out.shape[2]
    rows = hidden.shape[0]
    part = rows // hids
    width_in = units * hids
    frames = rows * seqs
    halves = 2 if hids % 2 == 0 else 1
    block = entries // halves
    head_rows = w_out.shape[0]
    groups = seqs // steps
    i = lax.axis_index("seq")
    j = lax.axis_index("hid")
    step = i % steps
    half = j % halves
    owned = steps * part

    def along_hid(values, shift):
        return lax.ppermute(values, "hid", [(a, (a + shift) % hids) for a in range(hids)])

    def turn_hid(values, shift):
        return lax.ppermute(
            values,
            "hid",
            [(a, a - a % halves + (a % halves + shift) % halves) for a in range(hids)],
        )

    def flip_seq(values, flip):
        return lax.ppermute(
            values,
            "seq",
            [(a, a - a % steps + (a % steps + flip) % steps) for a in range(seqs)],
        )

    place = jnp.stack([step, j]).astype(jnp.int32)
    relations = range(1, steps)
    bits = groups.bit_length() - 1
    halving = groups == 2**bits and bits > 0

    def across(values, bit):
        distance = 2 ** (bits - 1 - bit) * steps
        return lax.ppermute(values, "seq", [(a, a ^ distance) for a in range(seqs)])

    def own_bit(bit):
        return (i // (2 ** (bits - 1 - bit) * steps)) % 2

    group = [hidden] + [flip_seq(hidden, -m) for m in relations]

    squares_part = jnp.sum(jnp.square(hidden.astype(F32)), axis=1)
    tail = 8 * block
    small = jnp.concatenate(parts_of(squares_part))
    small = jnp.pad(small, (0, tail - small.size)).reshape(1, 1, 8, block)
    head_send = after(w_out, *group[1:]).reshape(head_rows, steps, halves, block)
    head_send = head_send.transpose(2, 1, 0, 3)
    head_send = head_send.reshape(1, halves, steps * head_rows, block)
    small = jnp.broadcast_to(small, (1, halves, 8, block))
    head_send = jnp.concatenate([head_send, small], axis=2)
    head_send = jnp.broadcast_to(head_send, (hids // halves,) + head_send.shape[1:])
    head_send = head_send.reshape(hids, steps * head_rows + 8, block)
    head_got = lax.all_to_all(head_send, "hid", 0, 0)
    head_mid = head_got[:, : steps * head_rows].reshape(hids, steps, head_rows, block)
    squares = head_got[:, steps * head_rows :].reshape(hids, tail)[:, : EXACT * rows]
    squares = jnp.sum(squares.astype(F32).reshape(hids * EXACT, rows), axis=0)

    ids = jnp.concatenate([codebook_ids] + [flip_seq(codebook_ids, -m) for m in relations], axis=1)
    ids_rows = [ids] + [turn_hid(ids, -k) for k in range(1, halves)]
    before = jnp.maximum(step - 1, 0)
    looked = jnp.take(pick(embedding, before), pick(ids, before), axis=0)

    w_own = pick(w_in, step)
    rows_in = [hidden] + [after(g, looked) for g in group[1:]]
    proj_parts = matmul(jnp.concatenate(rows_in), w_own, ((1,), (0,)))
    proj_parts = proj_parts.reshape(steps, hids, part, depth)

    def owner_block(index):
        return lax.dynamic_index_in_dim(proj_parts, index, 1, False).reshape(owned, depth)

    send = [owner_block((j + shift) % hids).astype(BF16) for shift in range(1, hids)]
    send = [after(p, head_got) for p in send]
    received = [along_hid(send[shift - 1], shift) for shift in range(1, hids)]

    head_send = after(head_mid, *send).transpose(1, 0, 2, 3)
    head_send = head_send.reshape(steps, hids * head_rows, block)
    head_send = jnp.broadcast_to(head_send, (groups,) + head_send.shape)
    head_send = head_send.reshape(seqs, hids * head_rows, block)
    head = lax.all_to_all(head_send, "seq", 0, 0).reshape(depth, block)

    squares = jnp.stack([squares] + [flip_seq(squares, -m) for m in relations])
    ratio_group = lax.rsqrt(squares / width_in + 1e-06).reshape(steps, hids, part)

    ratio = lax.dynamic_index_in_dim(ratio_group, j, 1, False).reshape(owned, 1)
    proj = owner_block(j)
    for r in received:
        proj += r.astype(F32)
    x_rows = ratio * proj + jnp.where(step > 0, looked.astype(F32), 0.0)
    scale = lax.rsqrt(jnp.mean(x_rows * x_rows, axis=1, keepdims=True) + 1e-06)
    gain = pick(depth_gain, step)[None, :]
    normed = (x_rows * scale * gain).astype(BF16)

    normed_rows = jnp.concatenate([normed] + [turn_hid(normed, -k) for k in range(1, halves)])
    targets = jnp.concatenate([pick(r, step) for r in ids_rows])
    logits = matmul(normed_rows, head, ((1,), (0,)))
    top = jnp.max(logits, axis=1)
    total = jnp.sum(jnp.exp(logits - top[:, None]), axis=1)
    stats = jnp.stack([top, total]).reshape(2, halves, -1)
    every = [stats] + [jnp.roll(turn_hid(stats, -t), t, axis=1) for t in range(1, halves)]
    tops = jnp.stack([e[0] for e in every]).reshape(halves, -1)
    totals = jnp.stack([e[1] for e in every]).reshape(halves, -1)
    top_all = jnp.max(tops, axis=0)
    lse = top_all + jnp.log(jnp.sum(totals * jnp.exp(tops - top_all), axis=0))
    entry = lax.broadcasted_iota(jnp.int32, logits.shape, 1) + half * block
    onehot = (targets[:, None] == entry).astype(F32)
    loss_weight = 2.0 * entries / frames
    d_logit = ((jnp.exp(logits - lse[:, None]) - onehot) * loss_weight).astype(BF16)

    d_norm_rows = matmul(d_logit, head, ((1,), (1,)))
    away = [d_norm_rows[k * owned : (k + 1) * owned].astype(BF16) for k in range(1, halves)]
    received = [turn_hid(a, k + 1) for k, a in enumerate(away)]
    d_norm = d_norm_rows[:owned]
    for r in received:
        d_norm += r.astype(F32)
    gated = gain * d_norm
    d_x = scale * gated - x_rows * scale**3 * jnp.mean(gated * x_rows, axis=1, keepdims=True)
    d_round = d_x.astype(BF16)
    d_ratio_part = jnp.sum(d_x * proj, axis=1).reshape(steps, part)

    width = depth // seqs
    d_after = after(d_logit, *away)
    if halving:
        product = matmul(normed_rows, d_after, ((0,), (0,))).astype(BF16)
        product = product.reshape((2,) * bits + (steps, width, block))
        part_sums = [lax.index_in_dim(product, p, bits, False) for p in range(steps)]
        left = [list(range(bits)) for _ in range(steps)]
        for k in range(bits):
            for p in range(steps):
                bit = (p + k) % bits
                axis = left[p].index(bit)
                left[p].remove(bit)
                send = lax.dynamic_index_in_dim(part_sums[p], 1 - own_bit(bit), axis, False)
                keep = lax.dynamic_index_in_dim(part_sums[p], own_bit(bit), axis, False)
                got = across(send.astype(BF16), bit)
                part_sums[p] = keep.astype(F32) + got.astype(F32)
        sums = part_sums
        sums = jnp.stack(sums).astype(BF16)
        group_sums = [sums]
        got = [pick(sums, step)]
        got += [flip_seq(pick(sums, (step + m) % steps), m) for m in relations]
        part_out = []
        for s in range(steps):
            value = got[0]
            for m in relations:
                value = jnp.where(s == (step - m) % steps, got[m], value)
            part_out.append(value)
        part_out = jnp.stack(part_out).reshape(steps, hids, head_rows, block)
    else:
        group_sums = []
        part_out = matmul(normed_rows, d_after, ((0,), (0,))).astype(BF16)
        part_out = lax.all_to_all(part_out.reshape(seqs, width, block), "seq", 0, 0)
        part_out = part_out.reshape(groups, steps, hids, head_rows, block).astype(F32).sum(0)
        part_out = part_out.astype(BF16)
    sums = [
        lax.dynamic_index_in_dim(part_out, (j + shift) % hids, 1, False) for shift in range(hids)
    ]
    sums = [along_hid(p, shift) if shift else p for shift, p in enumerate(sums)]
    grad_out = head_gradient(place, sums, halves)

    pieces = [d_round] + [along_hid(d_round, shift) for shift in range(1, hids)]
    ratio_rows = ratio_group.reshape(steps, rows, 1)
    share, mine, *others = input_gradient(
        place, pieces, group, ratio_rows, seqs, group_sums
    )
    share = share.reshape(seqs, depth // seqs, units)
    share = lax.all_to_all(share, "seq", 0, 0)
    share = share.reshape(groups, steps, depth // seqs, units).astype(F32).sum(0)
    grad_in = share.transpose(0, 2, 1)

    d_ratio = d_ratio_part[0]
    for m in relations:
        d_ratio += flip_seq(d_ratio_part[m], m)
    d_rows = jnp.broadcast_to(d_ratio, (hids, part))
    for shift in range(1, hids):
        d_rows = lax.dynamic_update_index_in_dim(
            d_rows, along_hid(d_ratio, shift), (j - shift) % hids, 0
        )
    ratio_own = ratio_group[0].reshape(rows)
    correction = ratio_own**3 * d_rows.reshape(rows) / width_in
    factors = jnp.stack([ratio_own, correction])[:, :, None]
    mine = [mine] + [flip_seq(others[m - 1], m) for m in relations]
    grad_hidden = hidden_gradient(place, mine, w_in, hidden, factors)
    return (grad_hidden, grad_in, grad_out)


def solution(mesh):
    placed = (
        P("seq", "hid"),
        P(None, "hid", None),
        P(),
        P(),
        P(("seq", "hid"), None, None),
        P(None, ("seq", "hid")),
    )
    return jax.shard_map(
        shards,
        mesh=mesh,
        in_specs=placed,
        out_specs=(P("seq", "hid"), P(None, "hid", "seq"), P(("seq", "hid"), None, None)),
        check_vma=False,
    )
```

```python
import jax
import jax.numpy as jnp
from jax import lax
from jax.experimental import pallas as pl
from jax.experimental.pallas import tpu as pltpu
from jax.sharding import PartitionSpec as P

F32 = jnp.float32
BF16 = jnp.bfloat16


def pick(values, index):
    return lax.dynamic_index_in_dim(values, index, axis=0, keepdims=False)


def matmul(a, b, contract):
    return lax.dot_general(a, b, (contract, ((), ())), preferred_element_type=F32)


def after(value, *others):
    return lax.optimization_barrier((value, *others))[0]


VMEM = pltpu.CompilerParams(vmem_limit_bytes=60 * 2**20)


def whole(shape):
    return pl.BlockSpec(shape, lambda n, place: (0,) * len(shape))


def call(kernel, place, grid, in_specs, out_specs, out_shape, scratch, flops, args):
    moved = sum(a.size * a.dtype.itemsize for a in args)
    return pl.pallas_call(
        kernel,
        grid_spec=pltpu.PrefetchScalarGridSpec(
            num_scalar_prefetch=1,
            grid=(grid,),
            in_specs=in_specs,
            out_specs=out_specs,
            scratch_shapes=scratch,
        ),
        out_shape=out_shape,
        compiler_params=VMEM,
        cost_estimate=pl.CostEstimate(flops=flops, bytes_accessed=moved, transcendentals=0),
    )(place, *args)


EXACT = 3


def parts_of(values):
    out = []
    for _ in range(EXACT):
        piece = lax.reduce_precision(values, 8, 7)
        values = values - piece
        out.append(piece.astype(BF16))
    return out


def head_gradient(place, pieces, halves):
    hids = len(pieces)
    steps, rows, block = pieces[0].shape

    def kernel(place_ref, *refs):
        pieces, out = refs[:-1], refs[-1]
        for r in range(halves):
            which = lax.rem(place_ref[1] - r + hids, halves)
            columns = pl.ds(pl.multiple_of(which * block, block), block)
            for s in range(steps):
                total = pieces[r][s].astype(F32)
                for k in range(r + halves, hids, halves):
                    total = total + pieces[k][s].astype(F32)
                out[:, s, columns] = total

    return call(
        kernel,
        place,
        1,
        [whole((steps, rows, block))] * hids,
        whole((rows, steps, halves * block)),
        jax.ShapeDtypeStruct((rows, steps, halves * block), F32),
        [],
        hids * steps * rows * block,
        tuple(pieces),
    )


def input_gradient(place, pieces, group, ratio, seqs):
    hids, steps = len(pieces), len(group)
    owned, depth = pieces[0].shape
    rows, units = group[0].shape
    part = owned // steps
    wide = min(512, depth)

    def kernel(place_ref, *refs):
        chunks, group, ratio = refs[:hids], refs[hids : hids + steps], refs[hids + steps]
        out, plain, scaled = refs[hids + steps + 1], refs[hids + steps + 2 : -1], refs[-1]
        j = place_ref[1]
        for r in range(hids):
            to = pl.multiple_of(lax.rem(j - r + hids, hids) * part, part)
            for m in range(steps):
                values = chunks[r][m * part : (m + 1) * part, :]
                plain[m][pl.ds(to, part), :] = values
                factor = ratio[m, pl.ds(to, part), :]
                scaled[m, pl.ds(to, part), :] = (values.astype(F32) * factor).astype(BF16)
        total = None
        for m in range(steps):
            term = lax.dot_general(
                scaled[m], group[m][...], (((0,), (0,)), ((), ())), preferred_element_type=F32
            )
            total = term if total is None else total + term
        out[...] = total.astype(BF16)

    return call(
        kernel,
        place,
        depth // wide,
        [pl.BlockSpec((owned, wide), lambda n, place: (0, n))] * hids
        + [whole((rows, units))] * steps
        + [whole((steps, rows, 1))],
        [pl.BlockSpec((wide, units), lambda n, place: (n, 0))]
        + [pl.BlockSpec((rows, wide), lambda n, place: (0, n))] * steps,
        [jax.ShapeDtypeStruct((depth, units), BF16)]
        + [jax.ShapeDtypeStruct((rows, depth), BF16)] * steps,
        [pltpu.VMEM((steps, rows, wide), BF16)],
        2 * steps * rows * units * depth,
        (*pieces, *group, ratio),
    )


def hidden_gradient(place, d_rows, w_in, hidden, factors):
    steps, units, depth = w_in.shape
    rows = hidden.shape[0]
    wide = min(512, units)

    def kernel(place_ref, *refs):
        d_rows, w, hidden, factors, out = refs[:steps], refs[-4], refs[-3], refs[-2], refs[-1]
        total = None
        for r in range(steps):
            which = lax.rem(place_ref[0] - r + steps, steps)
            term = lax.dot_general(
                d_rows[r][...], w[which], (((1,), (1,)), ((), ())), preferred_element_type=F32
            )
            total = term if total is None else total + term
        out[...] = (factors[0] * total - factors[1] * hidden[...].astype(F32)).astype(BF16)

    return call(
        kernel,
        place,
        units // wide,
        [whole((rows, depth))] * steps
        + [
            pl.BlockSpec((steps, wide, depth), lambda n, place: (0, n, 0)),
            pl.BlockSpec((rows, wide), lambda n, place: (0, n)),
            whole((2, rows, 1)),
        ],
        pl.BlockSpec((rows, wide), lambda n, place: (0, n)),
        jax.ShapeDtypeStruct((rows, units), BF16),
        [],
        2 * steps * rows * units * depth,
        (*d_rows, w_in, hidden, factors),
    )


def shards(hidden, w_in, embedding, depth_gain, w_out, codebook_ids):
    hids = lax.axis_size("hid")
    seqs = lax.axis_size("seq")
    steps, units, depth = w_in.shape
    entries = w_out.shape[2]
    rows = hidden.shape[0]
    part = rows // hids
    width_in = units * hids
    frames = rows * seqs
    halves = 2 if hids % 2 == 0 else 1
    block = entries // halves
    head_rows = w_out.shape[0]
    groups = seqs // steps
    i = lax.axis_index("seq")
    j = lax.axis_index("hid")
    step = i % steps
    half = j % halves
    owned = steps * part

    def along_hid(values, shift):
        return lax.ppermute(values, "hid", [(a, (a + shift) % hids) for a in range(hids)])

    def turn_hid(values, shift):
        return lax.ppermute(
            values,
            "hid",
            [(a, a - a % halves + (a % halves + shift) % halves) for a in range(hids)],
        )

    def flip_seq(values, flip):
        return lax.ppermute(
            values,
            "seq",
            [(a, a - a % steps + (a % steps + flip) % steps) for a in range(seqs)],
        )

    place = jnp.stack([step, j]).astype(jnp.int32)
    relations = range(1, steps)

    group = [hidden] + [flip_seq(hidden, -m) for m in relations]

    squares_part = jnp.sum(jnp.square(hidden.astype(F32)), axis=1)
    tail = 8 * block
    small = jnp.concatenate(parts_of(squares_part))
    small = jnp.pad(small, (0, tail - small.size)).reshape(1, 1, 8, block)
    head_send = after(w_out, *group[1:]).reshape(head_rows, steps, halves, block)
    head_send = head_send.transpose(2, 1, 0, 3)
    head_send = head_send.reshape(1, halves, steps * head_rows, block)
    small = jnp.broadcast_to(small, (1, halves, 8, block))
    head_send = jnp.concatenate([head_send, small], axis=2)
    head_send = jnp.broadcast_to(head_send, (hids // halves,) + head_send.shape[1:])
    head_send = head_send.reshape(hids, steps * head_rows + 8, block)
    head_got = lax.all_to_all(head_send, "hid", 0, 0)
    head_mid = head_got[:, : steps * head_rows].reshape(hids, steps, head_rows, block)
    squares = head_got[:, steps * head_rows :].reshape(hids, tail)[:, : EXACT * rows]
    squares = jnp.sum(squares.astype(F32).reshape(hids * EXACT, rows), axis=0)

    w_own = pick(w_in, step)
    proj_parts = matmul(jnp.concatenate(group), w_own, ((1,), (0,)))
    proj_parts = proj_parts.reshape(steps, hids, part, depth)

    def owner_block(index):
        return lax.dynamic_index_in_dim(proj_parts, index, 1, False).reshape(owned, depth)

    send = [owner_block((j + shift) % hids).astype(BF16) for shift in range(1, hids)]
    send = [after(p, head_got) for p in send]
    received = [along_hid(send[shift - 1], shift) for shift in range(1, hids)]

    ids = after(codebook_ids, *send)
    ids = jnp.concatenate([ids] + [flip_seq(ids, -m) for m in relations], axis=1)
    ids_rows = [ids] + [turn_hid(ids, -k) for k in range(1, halves)]
    before = jnp.maximum(step - 1, 0)
    looked = jnp.take(pick(embedding, before), pick(ids, before), axis=0)

    head_send = after(head_mid, *send).transpose(1, 0, 2, 3)
    head_send = head_send.reshape(steps, hids * head_rows, block)
    head_send = jnp.broadcast_to(head_send, (groups,) + head_send.shape)
    head_send = head_send.reshape(seqs, hids * head_rows, block)
    head = lax.all_to_all(head_send, "seq", 0, 0).reshape(depth, block)

    squares = jnp.stack([squares] + [flip_seq(squares, -m) for m in relations])
    ratio_group = lax.rsqrt(squares / width_in + 1e-06).reshape(steps, hids, part)

    ratio = lax.dynamic_index_in_dim(ratio_group, j, 1, False).reshape(owned, 1)
    proj = owner_block(j)
    for r in received:
        proj += r.astype(F32)
    x_rows = ratio * proj + jnp.where(step > 0, looked.astype(F32), 0.0)
    scale = lax.rsqrt(jnp.mean(x_rows * x_rows, axis=1, keepdims=True) + 1e-06)
    x_proj = jnp.sum(x_rows * proj, axis=1, keepdims=True)
    gain = pick(depth_gain, step)[None, :]
    normed = (x_rows * scale * gain).astype(BF16)

    normed_rows = jnp.concatenate([normed] + [turn_hid(normed, -k) for k in range(1, halves)])
    targets = jnp.concatenate([pick(r, step) for r in ids_rows])
    logits = matmul(normed_rows, head, ((1,), (0,)))
    top = jnp.max(logits, axis=1)
    total = jnp.sum(jnp.exp(logits - top[:, None]), axis=1)
    stats = jnp.stack([top, total]).reshape(2, halves, -1)
    every = [stats] + [jnp.roll(turn_hid(stats, -t), t, axis=1) for t in range(1, halves)]
    tops = jnp.stack([e[0] for e in every]).reshape(halves, -1)
    totals = jnp.stack([e[1] for e in every]).reshape(halves, -1)
    top_all = jnp.max(tops, axis=0)
    lse = top_all + jnp.log(jnp.sum(totals * jnp.exp(tops - top_all), axis=0))
    entry = lax.broadcasted_iota(jnp.int32, logits.shape, 1) + half * block
    onehot = (targets[:, None] == entry).astype(F32)
    loss_weight = 2.0 * entries / frames
    d_logit = ((jnp.exp(logits - lse[:, None]) - onehot) * loss_weight).astype(BF16)

    away = [
        matmul(d_logit[k * owned : (k + 1) * owned], head, ((1,), (1,))).astype(BF16)
        for k in range(1, halves)
    ]
    received = [turn_hid(a, k + 1) for k, a in enumerate(away)]
    d_norm = matmul(after(d_logit[:owned], *away), head, ((1,), (1,)))
    for r in received:
        d_norm += r.astype(F32)
    gated = gain * d_norm
    back_scale = scale**3 * jnp.mean(gated * x_rows, axis=1, keepdims=True)
    gated_proj = jnp.sum(gated * proj, axis=1, keepdims=True)
    d_round = (scale * gated - x_rows * back_scale).astype(BF16)
    d_ratio_part = (scale * gated_proj - back_scale * x_proj).reshape(steps, part)

    part_out = matmul(normed_rows, after(d_logit, *away), ((0,), (0,))).astype(BF16)
    part_out = after(part_out, *received).reshape(seqs, depth // seqs, block)
    part_out = lax.all_to_all(part_out, "seq", 0, 0)
    part_out = part_out.reshape(groups, steps, hids, head_rows, block).astype(F32).sum(0)
    part_out = part_out.astype(BF16)
    sums = [
        lax.dynamic_index_in_dim(part_out, (j + shift) % hids, 1, False) for shift in range(hids)
    ]
    sums = [along_hid(p, shift) if shift else p for shift, p in enumerate(sums)]
    grad_out = head_gradient(place, sums, halves)

    pieces = [d_round] + [along_hid(d_round, shift) for shift in range(1, hids)]
    ratio_rows = ratio_group.reshape(steps, rows, 1)
    share, mine, *others = input_gradient(place, pieces, group, ratio_rows, seqs)
    share = lax.all_to_all(share.reshape(seqs, depth // seqs, units), "seq", 0, 0)
    share = share.reshape(groups, steps, depth // seqs, units).astype(F32).sum(0)
    grad_in = share.transpose(0, 2, 1)

    d_ratio = d_ratio_part[0]
    for m in relations:
        d_ratio += flip_seq(d_ratio_part[m], m)
    d_rows = jnp.broadcast_to(d_ratio, (hids, part))
    for shift in range(1, hids):
        d_rows = lax.dynamic_update_index_in_dim(
            d_rows, along_hid(d_ratio, shift), (j - shift) % hids, 0
        )
    ratio_own = ratio_group[0].reshape(rows)
    correction = ratio_own**3 * d_rows.reshape(rows) / width_in
    factors = jnp.stack([ratio_own, correction])[:, :, None]
    mine = [mine] + [flip_seq(others[m - 1], m) for m in relations]
    grad_hidden = hidden_gradient(place, mine, w_in, hidden, factors)
    return (grad_hidden, grad_in, grad_out)


def solution(mesh):
    placed = (
        P("seq", "hid"),
        P(None, "hid", None),
        P(),
        P(),
        P(("seq", "hid"), None, None),
        P(None, ("seq", "hid")),
    )
    return jax.shard_map(
        shards,
        mesh=mesh,
        in_specs=placed,
        out_specs=(P("seq", "hid"), P(None, "hid", "seq"), P(("seq", "hid"), None, None)),
        check_vma=False,
    )
```

```python
import jax
import jax.numpy as jnp
from jax import lax
from jax.experimental import pallas as pl
from jax.experimental.pallas import tpu as pltpu
from jax.sharding import PartitionSpec as P

F32 = jnp.float32
BF16 = jnp.bfloat16


def pick(values, index):
    return lax.dynamic_index_in_dim(values, index, axis=0, keepdims=False)


def matmul(a, b, contract):
    return lax.dot_general(a, b, (contract, ((), ())), preferred_element_type=F32)


def after(value, *others):
    return lax.optimization_barrier((value, *others))[0]


VMEM = pltpu.CompilerParams(vmem_limit_bytes=60 * 2**20)


def whole(shape):
    return pl.BlockSpec(shape, lambda n, place: (0,) * len(shape))


def call(kernel, place, grid, in_specs, out_specs, out_shape, scratch, flops, args):
    moved = sum(a.size * a.dtype.itemsize for a in args)
    return pl.pallas_call(
        kernel,
        grid_spec=pltpu.PrefetchScalarGridSpec(
            num_scalar_prefetch=1,
            grid=(grid,),
            in_specs=in_specs,
            out_specs=out_specs,
            scratch_shapes=scratch,
        ),
        out_shape=out_shape,
        compiler_params=VMEM,
        cost_estimate=pl.CostEstimate(flops=flops, bytes_accessed=moved, transcendentals=0),
    )(place, *args)


EXACT = 3


def parts_of(values):
    out = []
    for _ in range(EXACT):
        piece = lax.reduce_precision(values, 8, 7)
        values = values - piece
        out.append(piece.astype(BF16))
    return out


def head_gradient(place, pieces, halves):
    hids = len(pieces)
    steps, rows, block = pieces[0].shape

    def kernel(place_ref, *refs):
        pieces, out = refs[:-1], refs[-1]
        for r in range(halves):
            which = lax.rem(place_ref[1] - r + hids, halves)
            columns = pl.ds(pl.multiple_of(which * block, block), block)
            for s in range(steps):
                total = pieces[r][s].astype(F32)
                for k in range(r + halves, hids, halves):
                    total = total + pieces[k][s].astype(F32)
                out[:, s, columns] = total

    return call(
        kernel,
        place,
        1,
        [whole((steps, rows, block))] * hids,
        whole((rows, steps, halves * block)),
        jax.ShapeDtypeStruct((rows, steps, halves * block), F32),
        [],
        hids * steps * rows * block,
        tuple(pieces),
    )


def spread(place, pieces, ratio, seqs, earlier):
    hids, steps = len(pieces), ratio.shape[0]
    owned, depth = pieces[0].shape
    part = owned // steps
    rows = part * hids
    wide = depth // seqs

    def kernel(place_ref, *refs):
        pieces, ratio = refs[:hids], refs[hids]
        scaled, *plain = refs[hids + 1 + len(earlier) :]
        step, j = place_ref[0], place_ref[1]
        for r in range(hids):
            block = lax.rem(j - r + hids, hids) * part
            for m in range(steps):
                to = pl.multiple_of(block, part)
                at = pl.multiple_of(lax.rem(step + m, steps) * rows + block, part)
                values = pieces[r][m * part : (m + 1) * part, :]
                plain[m][pl.ds(to, part), :] = values
                values = (values.astype(F32) * ratio[m, pl.ds(to, part), :]).astype(BF16)
                for q in range(seqs):
                    scaled[q, pl.ds(at, part), :] = values[:, q * wide : (q + 1) * wide]

    return call(
        kernel,
        place,
        1,
        [whole((owned, depth))] * hids
        + [whole((steps, rows, 1))]
        + [pl.BlockSpec(memory_space=pl.ANY)] * len(earlier),
        [whole((seqs, steps * rows, wide))] + [whole((rows, depth))] * steps,
        [jax.ShapeDtypeStruct((seqs, steps * rows, wide), BF16)]
        + [jax.ShapeDtypeStruct((rows, depth), BF16)] * steps,
        [],
        steps * rows * depth,
        (*pieces, ratio, *earlier),
    )


def input_gradient(place, blocks, scaled):
    groups, steps = len(blocks), len(blocks[0])
    rows, units = blocks[0][0].shape
    wide = scaled.shape[2]
    tall = min(512, units)

    def kernel(place_ref, *refs):
        hidden, scaled, out = refs[:-2], refs[-2], refs[-1]
        step, group = place_ref[0], place_ref[2]
        total = None
        for r in range(groups):
            source = lax.rem(group - r + groups, groups) * steps
            for m in range(steps):
                at = pl.multiple_of(lax.rem(step + m, steps) * rows, rows)
                left = [scaled[source + s, pl.ds(at, rows), :] for s in range(steps)]
                term = lax.dot_general(
                    jnp.concatenate(left, axis=1),
                    hidden[r * steps + m][...],
                    (((0,), (0,)), ((), ())),
                    preferred_element_type=F32,
                )
                total = term if total is None else total + term
        for s in range(steps):
            out[s] = total[s * wide : (s + 1) * wide, :].T

    flat = [b for line in blocks for b in line]
    return call(
        kernel,
        place,
        units // tall,
        [pl.BlockSpec((rows, tall), lambda n, place: (0, n))] * len(flat) + [whole(scaled.shape)],
        pl.BlockSpec((steps, tall, wide), lambda n, place: (0, n, 0)),
        jax.ShapeDtypeStruct((steps, units, wide), F32),
        [],
        2 * units * rows * len(flat) * wide * steps,
        (*flat, scaled),
    )


def hidden_gradient(place, d_rows, w_in, hidden, factors):
    steps, units, depth = w_in.shape
    rows = hidden.shape[0]
    wide = min(512, units)

    def kernel(place_ref, *refs):
        d_rows, w, hidden, factors, out = refs[:steps], refs[-4], refs[-3], refs[-2], refs[-1]
        total = None
        for r in range(steps):
            which = lax.rem(place_ref[0] - r + steps, steps)
            term = lax.dot_general(
                d_rows[r][...], w[which], (((1,), (1,)), ((), ())), preferred_element_type=F32
            )
            total = term if total is None else total + term
        out[...] = (factors[0] * total - factors[1] * hidden[...].astype(F32)).astype(BF16)

    return call(
        kernel,
        place,
        units // wide,
        [whole((rows, depth))] * steps
        + [
            pl.BlockSpec((steps, wide, depth), lambda n, place: (0, n, 0)),
            pl.BlockSpec((rows, wide), lambda n, place: (0, n)),
            whole((2, rows, 1)),
        ],
        pl.BlockSpec((rows, wide), lambda n, place: (0, n)),
        jax.ShapeDtypeStruct((rows, units), BF16),
        [],
        2 * steps * rows * units * depth,
        (*d_rows, w_in, hidden, factors),
    )


def shards(hidden, w_in, embedding, depth_gain, w_out, codebook_ids):
    hids = lax.axis_size("hid")
    seqs = lax.axis_size("seq")
    steps, units, depth = w_in.shape
    entries = w_out.shape[2]
    rows = hidden.shape[0]
    part = rows // hids
    width_in = units * hids
    frames = rows * seqs
    halves = 2 if hids % 2 == 0 else 1
    block = entries // halves
    head_rows = w_out.shape[0]
    groups = seqs // steps
    i = lax.axis_index("seq")
    j = lax.axis_index("hid")
    step = i % steps
    half = j % halves
    owned = steps * part

    def along_hid(values, shift):
        return lax.ppermute(values, "hid", [(a, (a + shift) % hids) for a in range(hids)])

    def turn_hid(values, shift):
        return lax.ppermute(
            values,
            "hid",
            [(a, a - a % halves + (a % halves + shift) % halves) for a in range(hids)],
        )

    def flip_seq(values, flip):
        return lax.ppermute(
            values,
            "seq",
            [(a, a - a % steps + (a % steps + flip) % steps) for a in range(seqs)],
        )

    place = jnp.stack([step, j, i // steps]).astype(jnp.int32)
    relations = range(1, steps)

    group = [hidden] + [flip_seq(hidden, -m) for m in relations]

    remote = [
        lax.ppermute(hidden, "seq", [(a, (a + r * steps) % seqs) for a in range(seqs)])
        for r in range(1, groups)
    ]

    squares_part = jnp.sum(jnp.square(hidden.astype(F32)), axis=1)
    tail = 8 * block
    small = jnp.concatenate(parts_of(squares_part))
    small = jnp.pad(small, (0, tail - small.size)).reshape(1, 1, 8, block)
    head_send = after(w_out, *group[1:]).reshape(head_rows, steps, halves, block)
    head_send = head_send.transpose(2, 1, 0, 3)
    head_send = head_send.reshape(1, halves, steps * head_rows, block)
    small = jnp.broadcast_to(small, (1, halves, 8, block))
    head_send = jnp.concatenate([head_send, small], axis=2)
    head_send = jnp.broadcast_to(head_send, (hids // halves,) + head_send.shape[1:])
    head_send = head_send.reshape(hids, steps * head_rows + 8, block)
    head_got = lax.all_to_all(head_send, "hid", 0, 0)
    head_mid = head_got[:, : steps * head_rows].reshape(hids, steps, head_rows, block)
    squares = head_got[:, steps * head_rows :].reshape(hids, tail)[:, : EXACT * rows]
    squares = jnp.sum(squares.astype(F32).reshape(hids * EXACT, rows), axis=0)

    w_own = pick(w_in, step)
    rows_in = [hidden] + [after(g, *remote) for g in group[1:]]
    proj_parts = matmul(jnp.concatenate(rows_in), w_own, ((1,), (0,)))
    proj_parts = proj_parts.reshape(steps, hids, part, depth)

    def owner_block(index):
        return lax.dynamic_index_in_dim(proj_parts, index, 1, False).reshape(owned, depth)

    send = [owner_block((j + shift) % hids).astype(BF16) for shift in range(1, hids)]
    send = [after(p, head_got) for p in send]
    received = [along_hid(send[shift - 1], shift) for shift in range(1, hids)]

    ids = after(codebook_ids, *send)
    ids = jnp.concatenate([ids] + [flip_seq(ids, -m) for m in relations], axis=1)
    ids_rows = [ids] + [turn_hid(ids, -k) for k in range(1, halves)]
    before = jnp.maximum(step - 1, 0)
    looked = jnp.take(pick(embedding, before), pick(ids, before), axis=0)

    head_send = after(head_mid, *send).transpose(1, 0, 2, 3)
    head_send = head_send.reshape(steps, hids * head_rows, block)
    head_send = jnp.broadcast_to(head_send, (groups,) + head_send.shape)
    head_send = head_send.reshape(seqs, hids * head_rows, block)
    head = lax.all_to_all(head_send, "seq", 0, 0).reshape(depth, block)

    squares = jnp.stack([squares] + [flip_seq(squares, -m) for m in relations])
    ratio_group = lax.rsqrt(squares / width_in + 1e-06).reshape(steps, hids, part)

    ratio = lax.dynamic_index_in_dim(ratio_group, j, 1, False).reshape(owned, 1)
    proj = owner_block(j)
    for r in received:
        proj += r.astype(F32)
    x_rows = ratio * proj + jnp.where(step > 0, looked.astype(F32), 0.0)
    scale = lax.rsqrt(jnp.mean(x_rows * x_rows, axis=1, keepdims=True) + 1e-06)
    x_proj = jnp.sum(x_rows * proj, axis=1, keepdims=True)
    gain = pick(depth_gain, step)[None, :]
    normed = (x_rows * scale * gain).astype(BF16)

    normed_rows = jnp.concatenate([normed] + [turn_hid(normed, -k) for k in range(1, halves)])
    targets = jnp.concatenate([pick(r, step) for r in ids_rows])
    logits = matmul(normed_rows, head, ((1,), (0,)))
    top = jnp.max(logits, axis=1)
    total = jnp.sum(jnp.exp(logits - top[:, None]), axis=1)
    stats = jnp.stack([top, total]).reshape(2, halves, -1)
    every = [stats] + [jnp.roll(turn_hid(stats, -t), t, axis=1) for t in range(1, halves)]
    tops = jnp.stack([e[0] for e in every]).reshape(halves, -1)
    totals = jnp.stack([e[1] for e in every]).reshape(halves, -1)
    top_all = jnp.max(tops, axis=0)
    lse = top_all + jnp.log(jnp.sum(totals * jnp.exp(tops - top_all), axis=0))
    entry = lax.broadcasted_iota(jnp.int32, logits.shape, 1) + half * block
    onehot = (targets[:, None] == entry).astype(F32)
    loss_weight = 2.0 * entries / frames
    d_logit = ((jnp.exp(logits - lse[:, None]) - onehot) * loss_weight).astype(BF16)

    away = [
        matmul(d_logit[k * owned : (k + 1) * owned], head, ((1,), (1,))).astype(BF16)
        for k in range(1, halves)
    ]
    received = [turn_hid(a, k + 1) for k, a in enumerate(away)]
    d_norm = matmul(after(d_logit[:owned], *away), head, ((1,), (1,)))
    for r in received:
        d_norm += r.astype(F32)
    gated = gain * d_norm
    back_scale = scale**3 * jnp.mean(gated * x_rows, axis=1, keepdims=True)
    gated_proj = jnp.sum(gated * proj, axis=1, keepdims=True)
    d_round = (scale * gated - x_rows * back_scale).astype(BF16)
    d_ratio_part = (scale * gated_proj - back_scale * x_proj).reshape(steps, part)

    part_out = matmul(normed_rows, after(d_logit, *away), ((0,), (0,))).astype(BF16)
    part_out = after(part_out, *received).reshape(seqs, depth // seqs, block)
    part_out = lax.all_to_all(part_out, "seq", 0, 0)
    part_out = part_out.reshape(groups, steps, hids, head_rows, block).astype(F32).sum(0)
    part_out = part_out.astype(BF16)
    sums = [
        lax.dynamic_index_in_dim(part_out, (j + shift) % hids, 1, False) for shift in range(hids)
    ]
    sums = [along_hid(p, shift) if shift else p for shift, p in enumerate(sums)]
    grad_out = head_gradient(place, sums, halves)

    pieces = [d_round] + [along_hid(d_round, shift) for shift in range(1, hids)]
    ratio_rows = ratio_group.reshape(steps, rows, 1)
    flips = [[flip_seq(h, -m) for m in relations] for h in remote]
    blocks = [group] + [[h] + f for h, f in zip(remote, flips)]
    scaled, mine, *others = spread(place, pieces, ratio_rows, seqs, [f for line in flips for f in line])
    scaled = lax.all_to_all(scaled, "seq", 0, 0)
    grad_in = input_gradient(place, blocks, scaled)

    d_ratio = d_ratio_part[0]
    for m in relations:
        d_ratio += flip_seq(d_ratio_part[m], m)
    d_rows = jnp.broadcast_to(d_ratio, (hids, part))
    for shift in range(1, hids):
        d_rows = lax.dynamic_update_index_in_dim(
            d_rows, along_hid(d_ratio, shift), (j - shift) % hids, 0
        )
    ratio_own = ratio_group[0].reshape(rows)
    correction = ratio_own**3 * d_rows.reshape(rows) / width_in
    factors = jnp.stack([ratio_own, correction])[:, :, None]
    mine = [mine] + [flip_seq(others[m - 1], m) for m in relations]
    grad_hidden = hidden_gradient(place, mine, w_in, hidden, factors)
    return (grad_hidden, grad_in, grad_out)


def solution(mesh):
    placed = (
        P("seq", "hid"),
        P(None, "hid", None),
        P(),
        P(),
        P(("seq", "hid"), None, None),
        P(None, ("seq", "hid")),
    )
    return jax.shard_map(
        shards,
        mesh=mesh,
        in_specs=placed,
        out_specs=(P("seq", "hid"), P(None, "hid", "seq"), P(("seq", "hid"), None, None)),
        check_vma=False,
    )
```

```python
import jax
import jax.numpy as jnp
from jax import lax
from jax.experimental import pallas as pl
from jax.experimental.pallas import tpu as pltpu
from jax.sharding import PartitionSpec as P

F32 = jnp.float32
BF16 = jnp.bfloat16


def pick(values, index):
    return lax.dynamic_index_in_dim(values, index, axis=0, keepdims=False)


def matmul(a, b, contract):
    return lax.dot_general(a, b, (contract, ((), ())), preferred_element_type=F32)


def after(value, *others):
    return lax.optimization_barrier((value, *others))[0]


VMEM = pltpu.CompilerParams(vmem_limit_bytes=60 * 2**20)


def whole(shape):
    return pl.BlockSpec(shape, lambda n, place: (0,) * len(shape))


def call(kernel, place, grid, in_specs, out_specs, out_shape, scratch, flops, args):
    moved = sum(a.size * a.dtype.itemsize for a in args)
    return pl.pallas_call(
        kernel,
        grid_spec=pltpu.PrefetchScalarGridSpec(
            num_scalar_prefetch=1,
            grid=(grid,),
            in_specs=in_specs,
            out_specs=out_specs,
            scratch_shapes=scratch,
        ),
        out_shape=out_shape,
        compiler_params=VMEM,
        cost_estimate=pl.CostEstimate(flops=flops, bytes_accessed=moved, transcendentals=0),
    )(place, *args)


EXACT = 3


def parts_of(values):
    out = []
    for _ in range(EXACT):
        piece = lax.reduce_precision(values, 8, 7)
        values = values - piece
        out.append(piece.astype(BF16))
    return out


def head_gradient(place, pieces, halves):
    hids = len(pieces)
    steps, rows, block = pieces[0].shape

    def kernel(place_ref, *refs):
        pieces, out = refs[:-1], refs[-1]
        for r in range(halves):
            which = lax.rem(place_ref[1] - r + hids, halves)
            columns = pl.ds(pl.multiple_of(which * block, block), block)
            for s in range(steps):
                total = pieces[r][s].astype(F32)
                for k in range(r + halves, hids, halves):
                    total = total + pieces[k][s].astype(F32)
                out[:, s, columns] = total

    return call(
        kernel,
        place,
        1,
        [whole((steps, rows, block))] * hids,
        whole((rows, steps, halves * block)),
        jax.ShapeDtypeStruct((rows, steps, halves * block), F32),
        [],
        hids * steps * rows * block,
        tuple(pieces),
    )


def input_gradient(place, pieces, group, ratio, seqs):
    hids, steps = len(pieces), len(group)
    owned, depth = pieces[0].shape
    rows, units = group[0].shape
    part = owned // steps
    wide = min(512, depth)

    def kernel(place_ref, *refs):
        chunks, group, ratio = refs[:hids], refs[hids : hids + steps], refs[hids + steps]
        out, plain, scaled = refs[hids + steps + 1], refs[hids + steps + 2 : -1], refs[-1]
        j = place_ref[1]
        for r in range(hids):
            to = pl.multiple_of(lax.rem(j - r + hids, hids) * part, part)
            for m in range(steps):
                values = chunks[r][m * part : (m + 1) * part, :]
                plain[m][pl.ds(to, part), :] = values
                factor = ratio[m, pl.ds(to, part), :]
                scaled[m, pl.ds(to, part), :] = (values.astype(F32) * factor).astype(BF16)
        total = None
        for m in range(steps):
            term = lax.dot_general(
                scaled[m], group[m][...], (((0,), (0,)), ((), ())), preferred_element_type=F32
            )
            total = term if total is None else total + term
        out[...] = total.astype(BF16)

    return call(
        kernel,
        place,
        depth // wide,
        [pl.BlockSpec((owned, wide), lambda n, place: (0, n))] * hids
        + [whole((rows, units))] * steps
        + [whole((steps, rows, 1))],
        [pl.BlockSpec((wide, units), lambda n, place: (n, 0))]
        + [pl.BlockSpec((rows, wide), lambda n, place: (0, n))] * steps,
        [jax.ShapeDtypeStruct((depth, units), BF16)]
        + [jax.ShapeDtypeStruct((rows, depth), BF16)] * steps,
        [pltpu.VMEM((steps, rows, wide), BF16)],
        2 * steps * rows * units * depth,
        (*pieces, *group, ratio),
    )


def hidden_gradient(place, d_rows, w_in, hidden, factors):
    steps, units, depth = w_in.shape
    rows = hidden.shape[0]
    wide = min(512, units)

    def kernel(place_ref, *refs):
        d_rows, w, hidden, factors, out = refs[:steps], refs[-4], refs[-3], refs[-2], refs[-1]
        total = None
        for r in range(steps):
            which = lax.rem(place_ref[0] - r + steps, steps)
            term = lax.dot_general(
                d_rows[r][...], w[which], (((1,), (1,)), ((), ())), preferred_element_type=F32
            )
            total = term if total is None else total + term
        out[...] = (factors[0] * total - factors[1] * hidden[...].astype(F32)).astype(BF16)

    return call(
        kernel,
        place,
        units // wide,
        [whole((rows, depth))] * steps
        + [
            pl.BlockSpec((steps, wide, depth), lambda n, place: (0, n, 0)),
            pl.BlockSpec((rows, wide), lambda n, place: (0, n)),
            whole((2, rows, 1)),
        ],
        pl.BlockSpec((rows, wide), lambda n, place: (0, n)),
        jax.ShapeDtypeStruct((rows, units), BF16),
        [],
        2 * steps * rows * units * depth,
        (*d_rows, w_in, hidden, factors),
    )


def shards(hidden, w_in, embedding, depth_gain, w_out, codebook_ids):
    hids = lax.axis_size("hid")
    seqs = lax.axis_size("seq")
    steps, units, depth = w_in.shape
    entries = w_out.shape[2]
    rows = hidden.shape[0]
    part = rows // hids
    width_in = units * hids
    frames = rows * seqs
    halves = 2 if hids % 2 == 0 else 1
    block = entries // halves
    head_rows = w_out.shape[0]
    groups = seqs // steps
    i = lax.axis_index("seq")
    j = lax.axis_index("hid")
    step = i % steps
    half = j % halves
    owned = steps * part

    def along_hid(values, shift):
        return lax.ppermute(values, "hid", [(a, (a + shift) % hids) for a in range(hids)])

    def turn_hid(values, shift):
        return lax.ppermute(
            values,
            "hid",
            [(a, a - a % halves + (a % halves + shift) % halves) for a in range(hids)],
        )

    def flip_seq(values, flip):
        return lax.ppermute(
            values,
            "seq",
            [(a, a - a % steps + (a % steps + flip) % steps) for a in range(seqs)],
        )

    place = jnp.stack([step, j]).astype(jnp.int32)
    relations = range(1, steps)

    group = [hidden] + [flip_seq(hidden, -m) for m in relations]

    squares_part = jnp.sum(jnp.square(hidden.astype(F32)), axis=1)
    tail = 8 * block
    small = jnp.concatenate(parts_of(squares_part))
    small = jnp.pad(small, (0, tail - small.size)).reshape(8, block)
    head_parts = w_out.reshape(head_rows, steps, halves, block)
    head_send = []
    for k in range(halves):
        piece = lax.dynamic_index_in_dim(head_parts, (half + k) % halves, 2, False)
        piece = piece.transpose(1, 0, 2).reshape(steps * head_rows, block)
        head_send.append(jnp.concatenate([piece, small]))
    head_got = [head_send[0]]
    head_got += [along_hid(head_send[shift % halves], shift) for shift in range(1, hids)]
    squares = sum(g[steps * head_rows :].astype(F32) for g in head_got).reshape(tail)
    squares = jnp.sum(squares[: EXACT * rows].reshape(EXACT, rows), axis=0)
    head_mid = jnp.stack([g[: steps * head_rows] for g in head_got[::-1]] * 2)
    head_mid = lax.dynamic_slice_in_dim(head_mid, hids - 1 - j, hids, 0)
    head_mid = head_mid.reshape(hids, steps, head_rows, block)

    w_own = pick(w_in, step)
    proj_parts = matmul(jnp.concatenate(group), w_own, ((1,), (0,)))
    proj_parts = proj_parts.reshape(steps, hids, part, depth)

    def owner_block(index):
        return lax.dynamic_index_in_dim(proj_parts, index, 1, False).reshape(owned, depth)

    send = [owner_block((j + shift) % hids).astype(BF16) for shift in range(1, hids)]
    send = [after(p, *head_got[1:]) for p in send]
    received = [along_hid(send[shift - 1], shift) for shift in range(1, hids)]

    ids = after(codebook_ids, *send)
    ids = jnp.concatenate([ids] + [flip_seq(ids, -m) for m in relations], axis=1)
    ids_rows = [ids] + [turn_hid(ids, -k) for k in range(1, halves)]
    before = jnp.maximum(step - 1, 0)
    looked = jnp.take(pick(embedding, before), pick(ids, before), axis=0)

    head_send = after(head_mid, *send).transpose(1, 0, 2, 3)
    head_send = head_send.reshape(steps, hids * head_rows, block)
    head_send = jnp.broadcast_to(head_send, (groups,) + head_send.shape)
    head_send = head_send.reshape(seqs, hids * head_rows, block)
    head = lax.all_to_all(head_send, "seq", 0, 0).reshape(depth, block)

    squares = jnp.stack([squares] + [flip_seq(squares, -m) for m in relations])
    ratio_group = lax.rsqrt(squares / width_in + 1e-06).reshape(steps, hids, part)

    ratio = lax.dynamic_index_in_dim(ratio_group, j, 1, False).reshape(owned, 1)
    proj = owner_block(j)
    for r in received:
        proj += r.astype(F32)
    x_rows = ratio * proj + jnp.where(step > 0, looked.astype(F32), 0.0)
    scale = lax.rsqrt(jnp.mean(x_rows * x_rows, axis=1, keepdims=True) + 1e-06)
    x_proj = jnp.sum(x_rows * proj, axis=1, keepdims=True)
    gain = pick(depth_gain, step)[None, :]
    normed = (x_rows * scale * gain).astype(BF16)

    normed_rows = jnp.concatenate([normed] + [turn_hid(normed, -k) for k in range(1, halves)])
    targets = jnp.concatenate([pick(r, step) for r in ids_rows])
    logits = matmul(normed_rows, head, ((1,), (0,)))
    top = jnp.max(logits, axis=1)
    total = jnp.sum(jnp.exp(logits - top[:, None]), axis=1)
    stats = jnp.stack([top, total]).reshape(2, halves, -1)
    every = [stats] + [jnp.roll(turn_hid(stats, -t), t, axis=1) for t in range(1, halves)]
    tops = jnp.stack([e[0] for e in every]).reshape(halves, -1)
    totals = jnp.stack([e[1] for e in every]).reshape(halves, -1)
    top_all = jnp.max(tops, axis=0)
    lse = top_all + jnp.log(jnp.sum(totals * jnp.exp(tops - top_all), axis=0))
    entry = lax.broadcasted_iota(jnp.int32, logits.shape, 1) + half * block
    onehot = (targets[:, None] == entry).astype(F32)
    loss_weight = 2.0 * entries / frames
    d_logit = ((jnp.exp(logits - lse[:, None]) - onehot) * loss_weight).astype(BF16)

    away = [
        matmul(d_logit[k * owned : (k + 1) * owned], head, ((1,), (1,))).astype(BF16)
        for k in range(1, halves)
    ]
    received = [turn_hid(a, k + 1) for k, a in enumerate(away)]
    d_norm = matmul(after(d_logit[:owned], *away), head, ((1,), (1,)))
    for r in received:
        d_norm += r.astype(F32)
    gated = gain * d_norm
    back_scale = scale**3 * jnp.mean(gated * x_rows, axis=1, keepdims=True)
    gated_proj = jnp.sum(gated * proj, axis=1, keepdims=True)
    d_round = (scale * gated - x_rows * back_scale).astype(BF16)
    d_ratio_part = (scale * gated_proj - back_scale * x_proj).reshape(steps, part)

    part_out = matmul(normed_rows, after(d_logit, *away), ((0,), (0,))).astype(BF16)
    part_out = after(part_out, *received).reshape(seqs, depth // seqs, block)
    part_out = lax.all_to_all(part_out, "seq", 0, 0)
    part_out = part_out.reshape(groups, steps, hids, head_rows, block).astype(F32).sum(0)
    part_out = part_out.astype(BF16)
    sums = [
        lax.dynamic_index_in_dim(part_out, (j + shift) % hids, 1, False) for shift in range(hids)
    ]
    sums = [along_hid(p, shift) if shift else p for shift, p in enumerate(sums)]
    grad_out = head_gradient(place, sums, halves)

    pieces = [d_round] + [along_hid(d_round, shift) for shift in range(1, hids)]
    ratio_rows = ratio_group.reshape(steps, rows, 1)
    share, mine, *others = input_gradient(place, pieces, group, ratio_rows, seqs)
    share = lax.all_to_all(share.reshape(seqs, depth // seqs, units), "seq", 0, 0)
    share = share.reshape(groups, steps, depth // seqs, units).astype(F32).sum(0)
    grad_in = share.transpose(0, 2, 1)

    d_ratio = d_ratio_part[0]
    for m in relations:
        d_ratio += flip_seq(d_ratio_part[m], m)
    d_rows = jnp.broadcast_to(d_ratio, (hids, part))
    for shift in range(1, hids):
        d_rows = lax.dynamic_update_index_in_dim(
            d_rows, along_hid(d_ratio, shift), (j - shift) % hids, 0
        )
    ratio_own = ratio_group[0].reshape(rows)
    correction = ratio_own**3 * d_rows.reshape(rows) / width_in
    factors = jnp.stack([ratio_own, correction])[:, :, None]
    mine = [mine] + [flip_seq(others[m - 1], m) for m in relations]
    grad_hidden = hidden_gradient(place, mine, w_in, hidden, factors)
    return (grad_hidden, grad_in, grad_out)


def solution(mesh):
    placed = (
        P("seq", "hid"),
        P(None, "hid", None),
        P(),
        P(),
        P(("seq", "hid"), None, None),
        P(None, ("seq", "hid")),
    )
    return jax.shard_map(
        shards,
        mesh=mesh,
        in_specs=placed,
        out_specs=(P("seq", "hid"), P(None, "hid", "seq"), P(("seq", "hid"), None, None)),
        check_vma=False,
    )
```

```python
import jax
import jax.numpy as jnp
from jax import lax
from jax.experimental import pallas as pl
from jax.experimental.pallas import tpu as pltpu
from jax.sharding import PartitionSpec as P

F32 = jnp.float32
BF16 = jnp.bfloat16


def pick(values, index):
    return lax.dynamic_index_in_dim(values, index, axis=0, keepdims=False)


def matmul(a, b, contract):
    return lax.dot_general(a, b, (contract, ((), ())), preferred_element_type=F32)


def after(value, *others):
    return lax.optimization_barrier((value, *others))[0]


VMEM = pltpu.CompilerParams(vmem_limit_bytes=60 * 2**20)


def whole(shape):
    return pl.BlockSpec(shape, lambda n, place: (0,) * len(shape))


def call(kernel, place, grid, in_specs, out_specs, out_shape, scratch, flops, args):
    moved = sum(a.size * a.dtype.itemsize for a in args)
    return pl.pallas_call(
        kernel,
        grid_spec=pltpu.PrefetchScalarGridSpec(
            num_scalar_prefetch=1,
            grid=(grid,),
            in_specs=in_specs,
            out_specs=out_specs,
            scratch_shapes=scratch,
        ),
        out_shape=out_shape,
        compiler_params=VMEM,
        cost_estimate=pl.CostEstimate(flops=flops, bytes_accessed=moved, transcendentals=0),
    )(place, *args)


EXACT = 3


def parts_of(values):
    out = []
    for _ in range(EXACT):
        piece = lax.reduce_precision(values, 8, 7)
        values = values - piece
        out.append(piece.astype(BF16))
    return out


def head_gradient(place, pieces, halves):
    hids = len(pieces)
    steps, rows, block = pieces[0].shape

    def kernel(place_ref, *refs):
        pieces, out = refs[:-1], refs[-1]
        for r in range(halves):
            which = lax.rem(place_ref[1] - r + hids, halves)
            columns = pl.ds(pl.multiple_of(which * block, block), block)
            for s in range(steps):
                total = pieces[r][s].astype(F32)
                for k in range(r + halves, hids, halves):
                    total = total + pieces[k][s].astype(F32)
                out[:, s, columns] = total

    return call(
        kernel,
        place,
        1,
        [whole((steps, rows, block))] * hids,
        whole((rows, steps, halves * block)),
        jax.ShapeDtypeStruct((rows, steps, halves * block), F32),
        [],
        hids * steps * rows * block,
        tuple(pieces),
    )


def input_gradient(place, pieces, group, ratio, seqs):
    hids, steps = len(pieces), len(group)
    owned, depth = pieces[0].shape
    rows, units = group[0].shape
    part = owned // steps
    wide = min(512, depth)

    def kernel(place_ref, *refs):
        chunks, group, ratio = refs[:hids], refs[hids : hids + steps], refs[hids + steps]
        out, plain, scaled = refs[hids + steps + 1], refs[hids + steps + 2 : -1], refs[-1]
        j = place_ref[1]
        for r in range(hids):
            to = pl.multiple_of(lax.rem(j - r + hids, hids) * part, part)
            for m in range(steps):
                values = chunks[r][m * part : (m + 1) * part, :]
                plain[m][pl.ds(to, part), :] = values
                factor = ratio[m, pl.ds(to, part), :]
                scaled[m, pl.ds(to, part), :] = (values.astype(F32) * factor).astype(BF16)
        total = None
        for m in range(steps):
            term = lax.dot_general(
                scaled[m], group[m][...], (((0,), (0,)), ((), ())), preferred_element_type=F32
            )
            total = term if total is None else total + term
        out[...] = total.astype(BF16)

    return call(
        kernel,
        place,
        depth // wide,
        [pl.BlockSpec((owned, wide), lambda n, place: (0, n))] * hids
        + [whole((rows, units))] * steps
        + [whole((steps, rows, 1))],
        [pl.BlockSpec((wide, units), lambda n, place: (n, 0))]
        + [pl.BlockSpec((rows, wide), lambda n, place: (0, n))] * steps,
        [jax.ShapeDtypeStruct((depth, units), BF16)]
        + [jax.ShapeDtypeStruct((rows, depth), BF16)] * steps,
        [pltpu.VMEM((steps, rows, wide), BF16)],
        2 * steps * rows * units * depth,
        (*pieces, *group, ratio),
    )


def hidden_gradient(place, d_rows, w_in, hidden, factors):
    steps, units, depth = w_in.shape
    rows = hidden.shape[0]
    wide = min(512, units)

    def kernel(place_ref, *refs):
        d_rows, w, hidden, factors, out = refs[:steps], refs[-4], refs[-3], refs[-2], refs[-1]
        total = None
        for r in range(steps):
            which = lax.rem(place_ref[0] - r + steps, steps)
            term = lax.dot_general(
                d_rows[r][...], w[which], (((1,), (1,)), ((), ())), preferred_element_type=F32
            )
            total = term if total is None else total + term
        out[...] = (factors[0] * total - factors[1] * hidden[...].astype(F32)).astype(BF16)

    return call(
        kernel,
        place,
        units // wide,
        [whole((rows, depth))] * steps
        + [
            pl.BlockSpec((steps, wide, depth), lambda n, place: (0, n, 0)),
            pl.BlockSpec((rows, wide), lambda n, place: (0, n)),
            whole((2, rows, 1)),
        ],
        pl.BlockSpec((rows, wide), lambda n, place: (0, n)),
        jax.ShapeDtypeStruct((rows, units), BF16),
        [],
        2 * steps * rows * units * depth,
        (*d_rows, w_in, hidden, factors),
    )


def shards(hidden, w_in, embedding, depth_gain, w_out, codebook_ids):
    hids = lax.axis_size("hid")
    seqs = lax.axis_size("seq")
    steps, units, depth = w_in.shape
    entries = w_out.shape[2]
    rows = hidden.shape[0]
    part = rows // hids
    width_in = units * hids
    frames = rows * seqs
    halves = 2 if hids % 2 == 0 else 1
    block = entries // halves
    head_rows = w_out.shape[0]
    groups = seqs // steps
    i = lax.axis_index("seq")
    j = lax.axis_index("hid")
    step = i % steps
    half = j % halves
    owned = steps * part

    def along_hid(values, shift):
        return lax.ppermute(values, "hid", [(a, (a + shift) % hids) for a in range(hids)])

    def turn_hid(values, shift):
        return lax.ppermute(
            values,
            "hid",
            [(a, a - a % halves + (a % halves + shift) % halves) for a in range(hids)],
        )

    def flip_seq(values, flip):
        return lax.ppermute(
            values,
            "seq",
            [(a, a - a % steps + (a % steps + flip) % steps) for a in range(seqs)],
        )

    place = jnp.stack([step, j]).astype(jnp.int32)
    relations = range(1, steps)

    group = [hidden] + [flip_seq(hidden, -m) for m in relations]

    squares_part = jnp.sum(jnp.square(hidden.astype(F32)), axis=1)
    tail = 8 * block
    small = jnp.concatenate(parts_of(squares_part))
    small = jnp.pad(small, (0, tail - small.size)).reshape(8, block)
    head_parts = w_out.reshape(head_rows, steps, halves, block)
    head_send = []
    for k in range(halves):
        piece = lax.dynamic_index_in_dim(head_parts, (half + k) % halves, 2, False)
        piece = piece.transpose(1, 0, 2).reshape(steps * head_rows, block)
        head_send.append(jnp.concatenate([piece, small]))
    head_got = [head_send[0]]
    head_got += [along_hid(head_send[shift % halves], shift) for shift in range(1, hids)]
    squares = sum(g[steps * head_rows :].astype(F32) for g in head_got).reshape(tail)
    squares = jnp.sum(squares[: EXACT * rows].reshape(EXACT, rows), axis=0)
    head_mid = jnp.stack([g[: steps * head_rows] for g in head_got[::-1]] * 2)
    head_mid = lax.dynamic_slice_in_dim(head_mid, hids - 1 - j, hids, 0)
    head_mid = head_mid.reshape(hids, steps, head_rows, block)

    w_own = pick(w_in, step)
    proj_parts = matmul(jnp.concatenate(group), w_own, ((1,), (0,)))
    proj_parts = proj_parts.reshape(steps, hids, part, depth)

    def owner_block(index):
        return lax.dynamic_index_in_dim(proj_parts, index, 1, False).reshape(owned, depth)

    send = [owner_block((j + shift) % hids).astype(BF16) for shift in range(1, hids)]
    received = [along_hid(send[shift - 1], shift) for shift in range(1, hids)]

    ids = after(codebook_ids, *send)
    ids = jnp.concatenate([ids] + [flip_seq(ids, -m) for m in relations], axis=1)
    ids_rows = [ids] + [turn_hid(ids, -k) for k in range(1, halves)]
    before = jnp.maximum(step - 1, 0)
    looked = jnp.take(pick(embedding, before), pick(ids, before), axis=0)

    head_send = after(head_mid, *send).transpose(1, 0, 2, 3)
    head_send = head_send.reshape(steps, hids * head_rows, block)
    head_send = jnp.broadcast_to(head_send, (groups,) + head_send.shape)
    head_send = head_send.reshape(seqs, hids * head_rows, block)
    head = lax.all_to_all(head_send, "seq", 0, 0).reshape(depth, block)

    squares = jnp.stack([squares] + [flip_seq(squares, -m) for m in relations])
    ratio_group = lax.rsqrt(squares / width_in + 1e-06).reshape(steps, hids, part)

    ratio = lax.dynamic_index_in_dim(ratio_group, j, 1, False).reshape(owned, 1)
    proj = owner_block(j)
    for r in received:
        proj += r.astype(F32)
    x_rows = ratio * proj + jnp.where(step > 0, looked.astype(F32), 0.0)
    scale = lax.rsqrt(jnp.mean(x_rows * x_rows, axis=1, keepdims=True) + 1e-06)
    x_proj = jnp.sum(x_rows * proj, axis=1, keepdims=True)
    gain = pick(depth_gain, step)[None, :]
    normed = (x_rows * scale * gain).astype(BF16)

    normed_rows = jnp.concatenate([normed] + [turn_hid(normed, -k) for k in range(1, halves)])
    targets = jnp.concatenate([pick(r, step) for r in ids_rows])
    logits = matmul(normed_rows, head, ((1,), (0,)))
    top = jnp.max(logits, axis=1)
    total = jnp.sum(jnp.exp(logits - top[:, None]), axis=1)
    stats = jnp.stack([top, total]).reshape(2, halves, -1)
    every = [stats] + [jnp.roll(turn_hid(stats, -t), t, axis=1) for t in range(1, halves)]
    tops = jnp.stack([e[0] for e in every]).reshape(halves, -1)
    totals = jnp.stack([e[1] for e in every]).reshape(halves, -1)
    top_all = jnp.max(tops, axis=0)
    lse = top_all + jnp.log(jnp.sum(totals * jnp.exp(tops - top_all), axis=0))
    entry = lax.broadcasted_iota(jnp.int32, logits.shape, 1) + half * block
    onehot = (targets[:, None] == entry).astype(F32)
    loss_weight = 2.0 * entries / frames
    d_logit = ((jnp.exp(logits - lse[:, None]) - onehot) * loss_weight).astype(BF16)

    away = [
        matmul(d_logit[k * owned : (k + 1) * owned], head, ((1,), (1,))).astype(BF16)
        for k in range(1, halves)
    ]
    received = [turn_hid(a, k + 1) for k, a in enumerate(away)]
    d_norm = matmul(after(d_logit[:owned], *away), head, ((1,), (1,)))
    for r in received:
        d_norm += r.astype(F32)
    gated = gain * d_norm
    back_scale = scale**3 * jnp.mean(gated * x_rows, axis=1, keepdims=True)
    gated_proj = jnp.sum(gated * proj, axis=1, keepdims=True)
    d_round = (scale * gated - x_rows * back_scale).astype(BF16)
    d_ratio_part = (scale * gated_proj - back_scale * x_proj).reshape(steps, part)

    part_out = matmul(normed_rows, after(d_logit, *away), ((0,), (0,))).astype(BF16)
    part_out = after(part_out, *received).reshape(seqs, depth // seqs, block)
    part_out = lax.all_to_all(part_out, "seq", 0, 0)
    part_out = part_out.reshape(groups, steps, hids, head_rows, block).astype(F32).sum(0)
    part_out = part_out.astype(BF16)
    sums = [
        lax.dynamic_index_in_dim(part_out, (j + shift) % hids, 1, False) for shift in range(hids)
    ]
    sums = [along_hid(p, shift) if shift else p for shift, p in enumerate(sums)]
    grad_out = head_gradient(place, sums, halves)

    pieces = [d_round] + [along_hid(d_round, shift) for shift in range(1, hids)]
    ratio_rows = ratio_group.reshape(steps, rows, 1)
    share, mine, *others = input_gradient(place, pieces, group, ratio_rows, seqs)
    share = lax.all_to_all(share.reshape(seqs, depth // seqs, units), "seq", 0, 0)
    share = share.reshape(groups, steps, depth // seqs, units).astype(F32).sum(0)
    grad_in = share.transpose(0, 2, 1)

    d_ratio = d_ratio_part[0]
    for m in relations:
        d_ratio += flip_seq(d_ratio_part[m], m)
    d_rows = jnp.broadcast_to(d_ratio, (hids, part))
    for shift in range(1, hids):
        d_rows = lax.dynamic_update_index_in_dim(
            d_rows, along_hid(d_ratio, shift), (j - shift) % hids, 0
        )
    ratio_own = ratio_group[0].reshape(rows)
    correction = ratio_own**3 * d_rows.reshape(rows) / width_in
    factors = jnp.stack([ratio_own, correction])[:, :, None]
    mine = [mine] + [flip_seq(others[m - 1], m) for m in relations]
    grad_hidden = hidden_gradient(place, mine, w_in, hidden, factors)
    return (grad_hidden, grad_in, grad_out)


def solution(mesh):
    placed = (
        P("seq", "hid"),
        P(None, "hid", None),
        P(),
        P(),
        P(("seq", "hid"), None, None),
        P(None, ("seq", "hid")),
    )
    return jax.shard_map(
        shards,
        mesh=mesh,
        in_specs=placed,
        out_specs=(P("seq", "hid"), P(None, "hid", "seq"), P(("seq", "hid"), None, None)),
        check_vma=False,
    )
```

```python
import jax
import jax.numpy as jnp
from jax import lax
from jax.experimental import pallas as pl
from jax.experimental.pallas import tpu as pltpu
from jax.sharding import PartitionSpec as P

F32 = jnp.float32
BF16 = jnp.bfloat16


def pick(values, index):
    return lax.dynamic_index_in_dim(values, index, axis=0, keepdims=False)


def matmul(a, b, contract):
    return lax.dot_general(a, b, (contract, ((), ())), preferred_element_type=F32)


def after(value, *others):
    return lax.optimization_barrier((value, *others))[0]


VMEM = pltpu.CompilerParams(vmem_limit_bytes=60 * 2**20)


def whole(shape):
    return pl.BlockSpec(shape, lambda n, place: (0,) * len(shape))


def call(kernel, place, grid, in_specs, out_specs, out_shape, scratch, flops, args):
    moved = sum(a.size * a.dtype.itemsize for a in args)
    return pl.pallas_call(
        kernel,
        grid_spec=pltpu.PrefetchScalarGridSpec(
            num_scalar_prefetch=1,
            grid=(grid,),
            in_specs=in_specs,
            out_specs=out_specs,
            scratch_shapes=scratch,
        ),
        out_shape=out_shape,
        compiler_params=VMEM,
        cost_estimate=pl.CostEstimate(flops=flops, bytes_accessed=moved, transcendentals=0),
    )(place, *args)


EXACT = 3


def parts_of(values):
    out = []
    for _ in range(EXACT):
        piece = lax.reduce_precision(values, 8, 7)
        values = values - piece
        out.append(piece.astype(BF16))
    return out


def head_gradient(place, pieces, halves):
    hids = len(pieces)
    steps, rows, block = pieces[0].shape

    def kernel(place_ref, *refs):
        pieces, out = refs[:-1], refs[-1]
        for r in range(halves):
            which = lax.rem(place_ref[1] - r + hids, halves)
            columns = pl.ds(pl.multiple_of(which * block, block), block)
            for s in range(steps):
                total = pieces[r][s].astype(F32)
                for k in range(r + halves, hids, halves):
                    total = total + pieces[k][s].astype(F32)
                out[:, s, columns] = total

    return call(
        kernel,
        place,
        1,
        [whole((steps, rows, block))] * hids,
        whole((rows, steps, halves * block)),
        jax.ShapeDtypeStruct((rows, steps, halves * block), F32),
        [],
        hids * steps * rows * block,
        tuple(pieces),
    )


def input_gradient(place, pieces, group, ratio, seqs):
    hids, steps = len(pieces), len(group)
    owned, depth = pieces[0].shape
    rows, units = group[0].shape
    part = owned // steps
    wide = min(512, depth)

    def kernel(place_ref, *refs):
        chunks, group, ratio = refs[:hids], refs[hids : hids + steps], refs[hids + steps]
        out, plain, scaled = refs[hids + steps + 1], refs[hids + steps + 2 : -1], refs[-1]
        j = place_ref[1]
        for r in range(hids):
            to = pl.multiple_of(lax.rem(j - r + hids, hids) * part, part)
            for m in range(steps):
                values = chunks[r][m * part : (m + 1) * part, :]
                plain[m][pl.ds(to, part), :] = values
                factor = ratio[m, pl.ds(to, part), :]
                scaled[m, pl.ds(to, part), :] = (values.astype(F32) * factor).astype(BF16)
        total = None
        for m in range(steps):
            term = lax.dot_general(
                scaled[m], group[m][...], (((0,), (0,)), ((), ())), preferred_element_type=F32
            )
            total = term if total is None else total + term
        out[...] = total.astype(BF16)

    return call(
        kernel,
        place,
        depth // wide,
        [pl.BlockSpec((owned, wide), lambda n, place: (0, n))] * hids
        + [whole((rows, units))] * steps
        + [whole((steps, rows, 1))],
        [pl.BlockSpec((wide, units), lambda n, place: (n, 0))]
        + [pl.BlockSpec((rows, wide), lambda n, place: (0, n))] * steps,
        [jax.ShapeDtypeStruct((depth, units), BF16)]
        + [jax.ShapeDtypeStruct((rows, depth), BF16)] * steps,
        [pltpu.VMEM((steps, rows, wide), BF16)],
        2 * steps * rows * units * depth,
        (*pieces, *group, ratio),
    )


def hidden_gradient(place, d_rows, w_in, hidden, factors):
    steps, units, depth = w_in.shape
    rows = hidden.shape[0]
    wide = min(512, units)

    def kernel(place_ref, *refs):
        d_rows, w, hidden, factors, out = refs[:steps], refs[-4], refs[-3], refs[-2], refs[-1]
        total = None
        for r in range(steps):
            which = lax.rem(place_ref[0] - r + steps, steps)
            term = lax.dot_general(
                d_rows[r][...], w[which], (((1,), (1,)), ((), ())), preferred_element_type=F32
            )
            total = term if total is None else total + term
        out[...] = (factors[0] * total - factors[1] * hidden[...].astype(F32)).astype(BF16)

    return call(
        kernel,
        place,
        units // wide,
        [whole((rows, depth))] * steps
        + [
            pl.BlockSpec((steps, wide, depth), lambda n, place: (0, n, 0)),
            pl.BlockSpec((rows, wide), lambda n, place: (0, n)),
            whole((2, rows, 1)),
        ],
        pl.BlockSpec((rows, wide), lambda n, place: (0, n)),
        jax.ShapeDtypeStruct((rows, units), BF16),
        [],
        2 * steps * rows * units * depth,
        (*d_rows, w_in, hidden, factors),
    )


def shards(hidden, w_in, embedding, depth_gain, w_out, codebook_ids):
    hids = lax.axis_size("hid")
    seqs = lax.axis_size("seq")
    steps, units, depth = w_in.shape
    entries = w_out.shape[2]
    rows = hidden.shape[0]
    part = rows // hids
    width_in = units * hids
    frames = rows * seqs
    halves = 2 if hids % 2 == 0 else 1
    block = entries // halves
    head_rows = w_out.shape[0]
    groups = seqs // steps
    i = lax.axis_index("seq")
    j = lax.axis_index("hid")
    step = i % steps
    half = j % halves
    owned = steps * part

    def along_hid(values, shift):
        return lax.ppermute(values, "hid", [(a, (a + shift) % hids) for a in range(hids)])

    def turn_hid(values, shift):
        return lax.ppermute(
            values,
            "hid",
            [(a, a - a % halves + (a % halves + shift) % halves) for a in range(hids)],
        )

    def flip_seq(values, flip):
        return lax.ppermute(
            values,
            "seq",
            [(a, a - a % steps + (a % steps + flip) % steps) for a in range(seqs)],
        )

    place = jnp.stack([step, j]).astype(jnp.int32)
    relations = range(1, steps)

    group = [hidden] + [flip_seq(hidden, -m) for m in relations]

    squares_part = jnp.sum(jnp.square(hidden.astype(F32)), axis=1)
    tail = 8 * block
    small = jnp.concatenate(parts_of(squares_part))
    small = jnp.pad(small, (0, tail - small.size)).reshape(8, block)
    head_parts = w_out.reshape(head_rows, steps, halves, block)
    head_send = []
    for k in range(halves):
        piece = lax.dynamic_index_in_dim(head_parts, (half + k) % halves, 2, False)
        piece = piece.transpose(1, 0, 2).reshape(steps * head_rows, block)
        head_send.append(jnp.concatenate([piece, small]))
    head_got = [head_send[0]]
    head_got += [along_hid(head_send[shift % halves], shift) for shift in range(1, hids)]
    w_own = pick(w_in, step)
    proj_parts = matmul(jnp.concatenate(group), w_own, ((1,), (0,)))
    proj_parts = proj_parts.reshape(steps, hids, part, depth)

    def owner_block(index):
        return lax.dynamic_index_in_dim(proj_parts, index, 1, False).reshape(owned, depth)

    send = [owner_block((j + shift) % hids).astype(BF16) for shift in range(1, hids)]
    received = [along_hid(send[shift - 1], shift) for shift in range(1, hids)]

    head_got = [head_got[0]] + [after(g, received[0]) for g in head_got[1:]]
    squares = sum(g[steps * head_rows :].astype(F32) for g in head_got).reshape(tail)
    squares = jnp.sum(squares[: EXACT * rows].reshape(EXACT, rows), axis=0)
    head_mid = jnp.stack([g[: steps * head_rows] for g in head_got[::-1]] * 2)
    head_mid = lax.dynamic_slice_in_dim(head_mid, hids - 1 - j, hids, 0)
    head_mid = head_mid.reshape(hids, steps, head_rows, block)

    ids = after(codebook_ids, *send)
    ids = jnp.concatenate([ids] + [flip_seq(ids, -m) for m in relations], axis=1)
    ids_rows = [ids] + [turn_hid(ids, -k) for k in range(1, halves)]
    before = jnp.maximum(step - 1, 0)
    looked = jnp.take(pick(embedding, before), pick(ids, before), axis=0)

    head_send = head_mid.transpose(1, 0, 2, 3)
    head_send = head_send.reshape(steps, hids * head_rows, block)
    head_send = jnp.broadcast_to(head_send, (groups,) + head_send.shape)
    head_send = head_send.reshape(seqs, hids * head_rows, block)
    head = lax.all_to_all(head_send, "seq", 0, 0).reshape(depth, block)

    squares = jnp.stack([squares] + [flip_seq(squares, -m) for m in relations])
    ratio_group = lax.rsqrt(squares / width_in + 1e-06).reshape(steps, hids, part)

    ratio = lax.dynamic_index_in_dim(ratio_group, j, 1, False).reshape(owned, 1)
    proj = owner_block(j)
    for r in received:
        proj += r.astype(F32)
    x_rows = ratio * proj + jnp.where(step > 0, looked.astype(F32), 0.0)
    scale = lax.rsqrt(jnp.mean(x_rows * x_rows, axis=1, keepdims=True) + 1e-06)
    x_proj = jnp.sum(x_rows * proj, axis=1, keepdims=True)
    gain = pick(depth_gain, step)[None, :]
    normed = (x_rows * scale * gain).astype(BF16)

    normed_rows = jnp.concatenate([normed] + [turn_hid(normed, -k) for k in range(1, halves)])
    targets = jnp.concatenate([pick(r, step) for r in ids_rows])
    logits = matmul(normed_rows, head, ((1,), (0,)))
    top = jnp.max(logits, axis=1)
    total = jnp.sum(jnp.exp(logits - top[:, None]), axis=1)
    stats = jnp.stack([top, total]).reshape(2, halves, -1)
    every = [stats] + [jnp.roll(turn_hid(stats, -t), t, axis=1) for t in range(1, halves)]
    tops = jnp.stack([e[0] for e in every]).reshape(halves, -1)
    totals = jnp.stack([e[1] for e in every]).reshape(halves, -1)
    top_all = jnp.max(tops, axis=0)
    lse = top_all + jnp.log(jnp.sum(totals * jnp.exp(tops - top_all), axis=0))
    entry = lax.broadcasted_iota(jnp.int32, logits.shape, 1) + half * block
    onehot = (targets[:, None] == entry).astype(F32)
    loss_weight = 2.0 * entries / frames
    d_logit = ((jnp.exp(logits - lse[:, None]) - onehot) * loss_weight).astype(BF16)

    away = [
        matmul(d_logit[k * owned : (k + 1) * owned], head, ((1,), (1,))).astype(BF16)
        for k in range(1, halves)
    ]
    received = [turn_hid(a, k + 1) for k, a in enumerate(away)]
    d_norm = matmul(after(d_logit[:owned], *away), head, ((1,), (1,)))
    for r in received:
        d_norm += r.astype(F32)
    gated = gain * d_norm
    back_scale = scale**3 * jnp.mean(gated * x_rows, axis=1, keepdims=True)
    gated_proj = jnp.sum(gated * proj, axis=1, keepdims=True)
    d_round = (scale * gated - x_rows * back_scale).astype(BF16)
    d_ratio_part = (scale * gated_proj - back_scale * x_proj).reshape(steps, part)

    part_out = matmul(normed_rows, after(d_logit, *away), ((0,), (0,))).astype(BF16)
    part_out = after(part_out, *received).reshape(seqs, depth // seqs, block)
    part_out = lax.all_to_all(part_out, "seq", 0, 0)
    part_out = part_out.reshape(groups, steps, hids, head_rows, block).astype(F32).sum(0)
    part_out = part_out.astype(BF16)
    sums = [
        lax.dynamic_index_in_dim(part_out, (j + shift) % hids, 1, False) for shift in range(hids)
    ]
    sums = [along_hid(p, shift) if shift else p for shift, p in enumerate(sums)]
    grad_out = head_gradient(place, sums, halves)

    pieces = [d_round] + [along_hid(d_round, shift) for shift in range(1, hids)]
    ratio_rows = ratio_group.reshape(steps, rows, 1)
    share, mine, *others = input_gradient(place, pieces, group, ratio_rows, seqs)
    share = lax.all_to_all(share.reshape(seqs, depth // seqs, units), "seq", 0, 0)
    share = share.reshape(groups, steps, depth // seqs, units).astype(F32).sum(0)
    grad_in = share.transpose(0, 2, 1)

    d_ratio = d_ratio_part[0]
    for m in relations:
        d_ratio += flip_seq(d_ratio_part[m], m)
    d_rows = jnp.broadcast_to(d_ratio, (hids, part))
    for shift in range(1, hids):
        d_rows = lax.dynamic_update_index_in_dim(
            d_rows, along_hid(d_ratio, shift), (j - shift) % hids, 0
        )
    ratio_own = ratio_group[0].reshape(rows)
    correction = ratio_own**3 * d_rows.reshape(rows) / width_in
    factors = jnp.stack([ratio_own, correction])[:, :, None]
    mine = [mine] + [flip_seq(others[m - 1], m) for m in relations]
    grad_hidden = hidden_gradient(place, mine, w_in, hidden, factors)
    return (grad_hidden, grad_in, grad_out)


def solution(mesh):
    placed = (
        P("seq", "hid"),
        P(None, "hid", None),
        P(),
        P(),
        P(("seq", "hid"), None, None),
        P(None, ("seq", "hid")),
    )
    return jax.shard_map(
        shards,
        mesh=mesh,
        in_specs=placed,
        out_specs=(P("seq", "hid"), P(None, "hid", "seq"), P(("seq", "hid"), None, None)),
        check_vma=False,
    )
```

```python
import jax
import jax.numpy as jnp
from jax import lax
from jax.experimental import pallas as pl
from jax.experimental.pallas import tpu as pltpu
from jax.sharding import PartitionSpec as P

F32 = jnp.float32
BF16 = jnp.bfloat16


def pick(values, index):
    return lax.dynamic_index_in_dim(values, index, axis=0, keepdims=False)


def matmul(a, b, contract):
    return lax.dot_general(a, b, (contract, ((), ())), preferred_element_type=F32)


def after(value, *others):
    return lax.optimization_barrier((value, *others))[0]


VMEM = pltpu.CompilerParams(vmem_limit_bytes=60 * 2**20)


def whole(shape):
    return pl.BlockSpec(shape, lambda n, place: (0,) * len(shape))


def call(kernel, place, grid, in_specs, out_specs, out_shape, scratch, flops, args):
    moved = sum(a.size * a.dtype.itemsize for a in args)
    return pl.pallas_call(
        kernel,
        grid_spec=pltpu.PrefetchScalarGridSpec(
            num_scalar_prefetch=1,
            grid=(grid,),
            in_specs=in_specs,
            out_specs=out_specs,
            scratch_shapes=scratch,
        ),
        out_shape=out_shape,
        compiler_params=VMEM,
        cost_estimate=pl.CostEstimate(flops=flops, bytes_accessed=moved, transcendentals=0),
    )(place, *args)


EXACT = 3


def parts_of(values):
    out = []
    for _ in range(EXACT):
        piece = lax.reduce_precision(values, 8, 7)
        values = values - piece
        out.append(piece.astype(BF16))
    return out


def head_gradient(place, pieces, halves):
    hids = len(pieces)
    steps, rows, block = pieces[0].shape

    def kernel(place_ref, *refs):
        pieces, out = refs[:-1], refs[-1]
        for r in range(halves):
            which = lax.rem(place_ref[1] - r + hids, halves)
            columns = pl.ds(pl.multiple_of(which * block, block), block)
            for s in range(steps):
                total = pieces[r][s].astype(F32)
                for k in range(r + halves, hids, halves):
                    total = total + pieces[k][s].astype(F32)
                out[:, s, columns] = total

    return call(
        kernel,
        place,
        1,
        [whole((steps, rows, block))] * hids,
        whole((rows, steps, halves * block)),
        jax.ShapeDtypeStruct((rows, steps, halves * block), F32),
        [],
        hids * steps * rows * block,
        tuple(pieces),
    )


def input_gradient(place, pieces, group, ratio, seqs):
    hids, steps = len(pieces), len(group)
    owned, depth = pieces[0].shape
    rows, units = group[0].shape
    part = owned // steps
    wide = min(512, depth)

    def kernel(place_ref, *refs):
        chunks, group, ratio = refs[:hids], refs[hids : hids + steps], refs[hids + steps]
        out, plain, scaled = refs[hids + steps + 1], refs[hids + steps + 2 : -1], refs[-1]
        j = place_ref[1]
        for r in range(hids):
            to = pl.multiple_of(lax.rem(j - r + hids, hids) * part, part)
            for m in range(steps):
                values = chunks[r][m * part : (m + 1) * part, :]
                plain[m][pl.ds(to, part), :] = values
                factor = ratio[m, pl.ds(to, part), :]
                scaled[m, pl.ds(to, part), :] = (values.astype(F32) * factor).astype(BF16)
        total = None
        for m in range(steps):
            term = lax.dot_general(
                scaled[m], group[m][...], (((0,), (0,)), ((), ())), preferred_element_type=F32
            )
            total = term if total is None else total + term
        out[...] = total.astype(BF16)

    return call(
        kernel,
        place,
        depth // wide,
        [pl.BlockSpec((owned, wide), lambda n, place: (0, n))] * hids
        + [whole((rows, units))] * steps
        + [whole((steps, rows, 1))],
        [pl.BlockSpec((wide, units), lambda n, place: (n, 0))]
        + [pl.BlockSpec((rows, wide), lambda n, place: (0, n))] * steps,
        [jax.ShapeDtypeStruct((depth, units), BF16)]
        + [jax.ShapeDtypeStruct((rows, depth), BF16)] * steps,
        [pltpu.VMEM((steps, rows, wide), BF16)],
        2 * steps * rows * units * depth,
        (*pieces, *group, ratio),
    )


def hidden_gradient(place, d_rows, w_in, hidden, factors):
    steps, units, depth = w_in.shape
    rows = hidden.shape[0]
    wide = min(512, units)

    def kernel(place_ref, *refs):
        d_rows, w, hidden, factors, out = refs[:steps], refs[-4], refs[-3], refs[-2], refs[-1]
        total = None
        for r in range(steps):
            which = lax.rem(place_ref[0] - r + steps, steps)
            term = lax.dot_general(
                d_rows[r][...], w[which], (((1,), (1,)), ((), ())), preferred_element_type=F32
            )
            total = term if total is None else total + term
        out[...] = (factors[0] * total - factors[1] * hidden[...].astype(F32)).astype(BF16)

    return call(
        kernel,
        place,
        units // wide,
        [whole((rows, depth))] * steps
        + [
            pl.BlockSpec((steps, wide, depth), lambda n, place: (0, n, 0)),
            pl.BlockSpec((rows, wide), lambda n, place: (0, n)),
            whole((2, rows, 1)),
        ],
        pl.BlockSpec((rows, wide), lambda n, place: (0, n)),
        jax.ShapeDtypeStruct((rows, units), BF16),
        [],
        2 * steps * rows * units * depth,
        (*d_rows, w_in, hidden, factors),
    )


def shards(hidden, w_in, embedding, depth_gain, w_out, codebook_ids):
    hids = lax.axis_size("hid")
    seqs = lax.axis_size("seq")
    steps, units, depth = w_in.shape
    entries = w_out.shape[2]
    rows = hidden.shape[0]
    part = rows // hids
    width_in = units * hids
    frames = rows * seqs
    halves = 2 if hids % 2 == 0 else 1
    block = entries // halves
    head_rows = w_out.shape[0]
    groups = seqs // steps
    i = lax.axis_index("seq")
    j = lax.axis_index("hid")
    step = i % steps
    half = j % halves
    owned = steps * part

    def along_hid(values, shift):
        return lax.ppermute(values, "hid", [(a, (a + shift) % hids) for a in range(hids)])

    def turn_hid(values, shift):
        return lax.ppermute(
            values,
            "hid",
            [(a, a - a % halves + (a % halves + shift) % halves) for a in range(hids)],
        )

    def flip_seq(values, flip):
        return lax.ppermute(
            values,
            "seq",
            [(a, a - a % steps + (a % steps + flip) % steps) for a in range(seqs)],
        )

    place = jnp.stack([step, j]).astype(jnp.int32)
    relations = range(1, steps)

    group = [hidden] + [flip_seq(hidden, -m) for m in relations]

    squares_part = jnp.sum(jnp.square(hidden.astype(F32)), axis=1)
    tail = 8 * block
    small = jnp.concatenate(parts_of(squares_part))
    small = jnp.pad(small, (0, tail - small.size)).reshape(8, block)
    head_parts = w_out.reshape(head_rows, steps, halves, block)
    head_send = []
    for k in range(halves):
        piece = lax.dynamic_index_in_dim(head_parts, (half + k) % halves, 2, False)
        piece = piece.transpose(1, 0, 2).reshape(steps * head_rows, block)
        head_send.append(jnp.concatenate([piece, small]))
    head_got = [head_send[0]]
    head_got += [along_hid(head_send[shift % halves], shift) for shift in range(1, hids)]
    w_own = pick(w_in, step)
    proj_parts = matmul(jnp.concatenate(group), w_own, ((1,), (0,)))
    proj_parts = proj_parts.reshape(steps, hids, part, depth)

    def owner_block(index):
        return lax.dynamic_index_in_dim(proj_parts, index, 1, False).reshape(owned, depth)

    send = [owner_block((j + shift) % hids).astype(BF16) for shift in range(1, hids)]
    ready = [after(p, *head_got[1:]) for p in send]
    received = [along_hid(ready[shift - 1], shift) for shift in range(1, hids)]

    head_got = [head_got[0]] + [after(g, *send) for g in head_got[1:]]
    squares = sum(g[steps * head_rows :].astype(F32) for g in head_got).reshape(tail)
    squares = jnp.sum(squares[: EXACT * rows].reshape(EXACT, rows), axis=0)
    head_mid = jnp.stack([g[: steps * head_rows] for g in head_got[::-1]] * 2)
    head_mid = lax.dynamic_slice_in_dim(head_mid, hids - 1 - j, hids, 0)
    head_mid = head_mid.reshape(hids, steps, head_rows, block)

    ids = after(codebook_ids, *send)
    ids = jnp.concatenate([ids] + [flip_seq(ids, -m) for m in relations], axis=1)
    ids_rows = [ids] + [turn_hid(ids, -k) for k in range(1, halves)]
    before = jnp.maximum(step - 1, 0)
    looked = jnp.take(pick(embedding, before), pick(ids, before), axis=0)

    head_send = head_mid.transpose(1, 0, 2, 3)
    head_send = head_send.reshape(steps, hids * head_rows, block)
    head_send = jnp.broadcast_to(head_send, (groups,) + head_send.shape)
    head_send = head_send.reshape(seqs, hids * head_rows, block)
    head = lax.all_to_all(head_send, "seq", 0, 0).reshape(depth, block)

    squares = jnp.stack([squares] + [flip_seq(squares, -m) for m in relations])
    ratio_group = lax.rsqrt(squares / width_in + 1e-06).reshape(steps, hids, part)

    ratio = lax.dynamic_index_in_dim(ratio_group, j, 1, False).reshape(owned, 1)
    proj = owner_block(j)
    for r in received:
        proj += r.astype(F32)
    x_rows = ratio * proj + jnp.where(step > 0, looked.astype(F32), 0.0)
    scale = lax.rsqrt(jnp.mean(x_rows * x_rows, axis=1, keepdims=True) + 1e-06)
    x_proj = jnp.sum(x_rows * proj, axis=1, keepdims=True)
    gain = pick(depth_gain, step)[None, :]
    normed = (x_rows * scale * gain).astype(BF16)

    normed_rows = jnp.concatenate([normed] + [turn_hid(normed, -k) for k in range(1, halves)])
    targets = jnp.concatenate([pick(r, step) for r in ids_rows])
    logits = matmul(normed_rows, head, ((1,), (0,)))
    top = jnp.max(logits, axis=1)
    total = jnp.sum(jnp.exp(logits - top[:, None]), axis=1)
    stats = jnp.stack([top, total]).reshape(2, halves, -1)
    every = [stats] + [jnp.roll(turn_hid(stats, -t), t, axis=1) for t in range(1, halves)]
    tops = jnp.stack([e[0] for e in every]).reshape(halves, -1)
    totals = jnp.stack([e[1] for e in every]).reshape(halves, -1)
    top_all = jnp.max(tops, axis=0)
    lse = top_all + jnp.log(jnp.sum(totals * jnp.exp(tops - top_all), axis=0))
    entry = lax.broadcasted_iota(jnp.int32, logits.shape, 1) + half * block
    onehot = (targets[:, None] == entry).astype(F32)
    loss_weight = 2.0 * entries / frames
    d_logit = ((jnp.exp(logits - lse[:, None]) - onehot) * loss_weight).astype(BF16)

    away = [
        matmul(d_logit[k * owned : (k + 1) * owned], head, ((1,), (1,))).astype(BF16)
        for k in range(1, halves)
    ]
    received = [turn_hid(a, k + 1) for k, a in enumerate(away)]
    d_norm = matmul(after(d_logit[:owned], *away), head, ((1,), (1,)))
    for r in received:
        d_norm += r.astype(F32)
    gated = gain * d_norm
    back_scale = scale**3 * jnp.mean(gated * x_rows, axis=1, keepdims=True)
    gated_proj = jnp.sum(gated * proj, axis=1, keepdims=True)
    d_round = (scale * gated - x_rows * back_scale).astype(BF16)
    d_ratio_part = (scale * gated_proj - back_scale * x_proj).reshape(steps, part)

    part_out = matmul(normed_rows, after(d_logit, *away), ((0,), (0,))).astype(BF16)
    part_out = after(part_out, *received).reshape(seqs, depth // seqs, block)
    part_out = lax.all_to_all(part_out, "seq", 0, 0)
    part_out = part_out.reshape(groups, steps, hids, head_rows, block).astype(F32).sum(0)
    part_out = part_out.astype(BF16)
    sums = [
        lax.dynamic_index_in_dim(part_out, (j + shift) % hids, 1, False) for shift in range(hids)
    ]
    sums = [along_hid(p, shift) if shift else p for shift, p in enumerate(sums)]
    grad_out = head_gradient(place, sums, halves)

    pieces = [d_round] + [along_hid(d_round, shift) for shift in range(1, hids)]
    ratio_rows = ratio_group.reshape(steps, rows, 1)
    share, mine, *others = input_gradient(place, pieces, group, ratio_rows, seqs)
    share = lax.all_to_all(share.reshape(seqs, depth // seqs, units), "seq", 0, 0)
    share = share.reshape(groups, steps, depth // seqs, units).astype(F32).sum(0)
    grad_in = share.transpose(0, 2, 1)

    d_ratio = d_ratio_part[0]
    for m in relations:
        d_ratio += flip_seq(d_ratio_part[m], m)
    d_rows = jnp.broadcast_to(d_ratio, (hids, part))
    for shift in range(1, hids):
        d_rows = lax.dynamic_update_index_in_dim(
            d_rows, along_hid(d_ratio, shift), (j - shift) % hids, 0
        )
    ratio_own = ratio_group[0].reshape(rows)
    correction = ratio_own**3 * d_rows.reshape(rows) / width_in
    factors = jnp.stack([ratio_own, correction])[:, :, None]
    mine = [mine] + [flip_seq(others[m - 1], m) for m in relations]
    grad_hidden = hidden_gradient(place, mine, w_in, hidden, factors)
    return (grad_hidden, grad_in, grad_out)


def solution(mesh):
    placed = (
        P("seq", "hid"),
        P(None, "hid", None),
        P(),
        P(),
        P(("seq", "hid"), None, None),
        P(None, ("seq", "hid")),
    )
    return jax.shard_map(
        shards,
        mesh=mesh,
        in_specs=placed,
        out_specs=(P("seq", "hid"), P(None, "hid", "seq"), P(("seq", "hid"), None, None)),
        check_vma=False,
    )
```

```python
import jax
import jax.numpy as jnp
from jax import lax
from jax.experimental import pallas as pl
from jax.experimental.pallas import tpu as pltpu
from jax.sharding import PartitionSpec as P

F32 = jnp.float32
BF16 = jnp.bfloat16


def pick(values, index):
    return lax.dynamic_index_in_dim(values, index, axis=0, keepdims=False)


def matmul(a, b, contract):
    return lax.dot_general(a, b, (contract, ((), ())), preferred_element_type=F32)


def after(value, *others):
    return lax.optimization_barrier((value, *others))[0]


VMEM = pltpu.CompilerParams(vmem_limit_bytes=60 * 2**20)


def whole(shape):
    return pl.BlockSpec(shape, lambda n, place: (0,) * len(shape))


def call(kernel, place, grid, in_specs, out_specs, out_shape, scratch, flops, args):
    moved = sum(a.size * a.dtype.itemsize for a in args)
    return pl.pallas_call(
        kernel,
        grid_spec=pltpu.PrefetchScalarGridSpec(
            num_scalar_prefetch=1,
            grid=(grid,),
            in_specs=in_specs,
            out_specs=out_specs,
            scratch_shapes=scratch,
        ),
        out_shape=out_shape,
        compiler_params=VMEM,
        cost_estimate=pl.CostEstimate(flops=flops, bytes_accessed=moved, transcendentals=0),
    )(place, *args)


EXACT = 3


def parts_of(values):
    out = []
    for _ in range(EXACT):
        piece = lax.reduce_precision(values, 8, 7)
        values = values - piece
        out.append(piece.astype(BF16))
    return out


def head_gradient(place, pieces, halves):
    hids = len(pieces)
    steps, rows, block = pieces[0].shape

    def kernel(place_ref, *refs):
        pieces, out = refs[:-1], refs[-1]
        for r in range(halves):
            which = lax.rem(place_ref[1] - r + hids, halves)
            columns = pl.ds(pl.multiple_of(which * block, block), block)
            for s in range(steps):
                total = pieces[r][s].astype(F32)
                for k in range(r + halves, hids, halves):
                    total = total + pieces[k][s].astype(F32)
                out[:, s, columns] = total

    return call(
        kernel,
        place,
        1,
        [whole((steps, rows, block))] * hids,
        whole((rows, steps, halves * block)),
        jax.ShapeDtypeStruct((rows, steps, halves * block), F32),
        [],
        hids * steps * rows * block,
        tuple(pieces),
    )


def input_gradient(place, pieces, group, ratio, seqs):
    hids, steps = len(pieces), len(group)
    owned, depth = pieces[0].shape
    rows, units = group[0].shape
    part = owned // steps
    wide = min(512, depth)

    def kernel(place_ref, *refs):
        chunks, group, ratio = refs[:hids], refs[hids : hids + steps], refs[hids + steps]
        out, plain, scaled = refs[hids + steps + 1], refs[hids + steps + 2 : -1], refs[-1]
        j = place_ref[1]
        for r in range(hids):
            to = pl.multiple_of(lax.rem(j - r + hids, hids) * part, part)
            for m in range(steps):
                values = chunks[r][m * part : (m + 1) * part, :]
                plain[m][pl.ds(to, part), :] = values
                factor = ratio[m, pl.ds(to, part), :]
                scaled[m, pl.ds(to, part), :] = (values.astype(F32) * factor).astype(BF16)
        total = None
        for m in range(steps):
            term = lax.dot_general(
                scaled[m], group[m][...], (((0,), (0,)), ((), ())), preferred_element_type=F32
            )
            total = term if total is None else total + term
        out[...] = total.astype(BF16)

    return call(
        kernel,
        place,
        depth // wide,
        [pl.BlockSpec((owned, wide), lambda n, place: (0, n))] * hids
        + [whole((rows, units))] * steps
        + [whole((steps, rows, 1))],
        [pl.BlockSpec((wide, units), lambda n, place: (n, 0))]
        + [pl.BlockSpec((rows, wide), lambda n, place: (0, n))] * steps,
        [jax.ShapeDtypeStruct((depth, units), BF16)]
        + [jax.ShapeDtypeStruct((rows, depth), BF16)] * steps,
        [pltpu.VMEM((steps, rows, wide), BF16)],
        2 * steps * rows * units * depth,
        (*pieces, *group, ratio),
    )


def hidden_gradient(place, d_rows, w_in, hidden, factors):
    steps, units, depth = w_in.shape
    rows = hidden.shape[0]
    wide = min(512, units)

    def kernel(place_ref, *refs):
        d_rows, w, hidden, factors, out = refs[:steps], refs[-4], refs[-3], refs[-2], refs[-1]
        total = None
        for r in range(steps):
            which = lax.rem(place_ref[0] - r + steps, steps)
            term = lax.dot_general(
                d_rows[r][...], w[which], (((1,), (1,)), ((), ())), preferred_element_type=F32
            )
            total = term if total is None else total + term
        out[...] = (factors[0] * total - factors[1] * hidden[...].astype(F32)).astype(BF16)

    return call(
        kernel,
        place,
        units // wide,
        [whole((rows, depth))] * steps
        + [
            pl.BlockSpec((steps, wide, depth), lambda n, place: (0, n, 0)),
            pl.BlockSpec((rows, wide), lambda n, place: (0, n)),
            whole((2, rows, 1)),
        ],
        pl.BlockSpec((rows, wide), lambda n, place: (0, n)),
        jax.ShapeDtypeStruct((rows, units), BF16),
        [],
        2 * steps * rows * units * depth,
        (*d_rows, w_in, hidden, factors),
    )


def shards(hidden, w_in, embedding, depth_gain, w_out, codebook_ids):
    hids = lax.axis_size("hid")
    seqs = lax.axis_size("seq")
    steps, units, depth = w_in.shape
    entries = w_out.shape[2]
    rows = hidden.shape[0]
    part = rows // hids
    width_in = units * hids
    frames = rows * seqs
    halves = 2 if hids % 2 == 0 else 1
    block = entries // halves
    head_rows = w_out.shape[0]
    groups = seqs // steps
    i = lax.axis_index("seq")
    j = lax.axis_index("hid")
    step = i % steps
    half = j % halves
    owned = steps * part

    def along_hid(values, shift):
        return lax.ppermute(values, "hid", [(a, (a + shift) % hids) for a in range(hids)])

    def turn_hid(values, shift):
        return lax.ppermute(
            values,
            "hid",
            [(a, a - a % halves + (a % halves + shift) % halves) for a in range(hids)],
        )

    def flip_seq(values, flip):
        return lax.ppermute(
            values,
            "seq",
            [(a, a - a % steps + (a % steps + flip) % steps) for a in range(seqs)],
        )

    place = jnp.stack([step, j]).astype(jnp.int32)
    relations = range(1, steps)

    group = [hidden] + [flip_seq(hidden, -m) for m in relations]

    squares_part = jnp.sum(jnp.square(hidden.astype(F32)), axis=1)
    tail = 8 * block
    small = jnp.concatenate(parts_of(squares_part))
    small = jnp.pad(small, (0, tail - small.size)).reshape(8, block)
    head_parts = w_out.reshape(head_rows, steps, halves, block)
    head_send = []
    for k in range(halves):
        piece = lax.dynamic_index_in_dim(head_parts, (half + k) % halves, 2, False)
        piece = piece.transpose(1, 0, 2).reshape(steps * head_rows, block)
        head_send.append(jnp.concatenate([piece, small]))
    head_got = [head_send[0]]
    head_got += [along_hid(head_send[shift % halves], shift) for shift in range(1, hids)]
    w_own = pick(w_in, step)
    proj_parts = matmul(jnp.concatenate(group), w_own, ((1,), (0,)))
    proj_parts = proj_parts.reshape(steps, hids, part, depth)

    def owner_block(index):
        return lax.dynamic_index_in_dim(proj_parts, index, 1, False).reshape(owned, depth)

    send = [owner_block((j + shift) % hids).astype(BF16) for shift in range(1, hids)]
    ready = [after(p, *head_got[1:]) for p in send]
    received = [along_hid(ready[shift - 1], shift) for shift in range(1, hids)]

    head_got = [head_got[0]] + [after(g, *send) for g in head_got[1:]]
    squares = sum(g[steps * head_rows :].astype(F32) for g in head_got).reshape(tail)
    squares = jnp.sum(squares[: EXACT * rows].reshape(EXACT, rows), axis=0)
    head_mid = jnp.stack([g[: steps * head_rows] for g in head_got[::-1]] * 2)
    head_mid = lax.dynamic_slice_in_dim(head_mid, hids - 1 - j, hids, 0)
    head_mid = head_mid.reshape(hids, steps, head_rows, block)

    ids = after(codebook_ids, *send)
    ids = jnp.concatenate([ids] + [flip_seq(ids, -m) for m in relations], axis=1)
    ids_rows = [ids] + [turn_hid(ids, -k) for k in range(1, halves)]
    before = jnp.maximum(step - 1, 0)
    looked = jnp.take(pick(embedding, before), pick(ids, before), axis=0)

    head_send = head_mid.transpose(1, 0, 2, 3)
    head_send = head_send.reshape(steps, hids * head_rows, block)
    head_send = jnp.broadcast_to(head_send, (groups,) + head_send.shape)
    head_send = head_send.reshape(seqs, hids * head_rows, block)
    head = lax.all_to_all(head_send, "seq", 0, 0).reshape(depth, block)

    squares = jnp.stack([squares] + [flip_seq(squares, -m) for m in relations])
    ratio_group = lax.rsqrt(squares / width_in + 1e-06).reshape(steps, hids, part)

    ratio = lax.dynamic_index_in_dim(ratio_group, j, 1, False).reshape(owned, 1)
    proj = owner_block(j)
    for r in received:
        proj += r.astype(F32)
    x_rows = ratio * proj + jnp.where(step > 0, looked.astype(F32), 0.0)
    scale = lax.rsqrt(jnp.mean(x_rows * x_rows, axis=1, keepdims=True) + 1e-06)
    x_proj = jnp.sum(x_rows * proj, axis=1, keepdims=True)
    gain = pick(depth_gain, step)[None, :]
    normed = (x_rows * scale * gain).astype(BF16)

    normed_rows = jnp.concatenate([normed] + [turn_hid(normed, -k) for k in range(1, halves)])
    targets = jnp.concatenate([pick(r, step) for r in ids_rows])
    logits = matmul(normed_rows, head, ((1,), (0,)))
    top = jnp.max(logits, axis=1)
    total = jnp.sum(jnp.exp(logits - top[:, None]), axis=1)
    stats = jnp.stack([top, total]).reshape(2, halves, -1)
    every = [stats] + [jnp.roll(turn_hid(stats, -t), t, axis=1) for t in range(1, halves)]
    tops = jnp.stack([e[0] for e in every]).reshape(halves, -1)
    totals = jnp.stack([e[1] for e in every]).reshape(halves, -1)
    top_all = jnp.max(tops, axis=0)
    lse = top_all + jnp.log(jnp.sum(totals * jnp.exp(tops - top_all), axis=0))
    entry = lax.broadcasted_iota(jnp.int32, logits.shape, 1) + half * block
    onehot = (targets[:, None] == entry).astype(F32)
    loss_weight = 2.0 * entries / frames
    d_logit = ((jnp.exp(logits - lse[:, None]) - onehot) * loss_weight).astype(BF16)

    away = [
        matmul(d_logit[k * owned : (k + 1) * owned], head, ((1,), (1,))).astype(BF16)
        for k in range(1, halves)
    ]
    received = [turn_hid(a, k + 1) for k, a in enumerate(away)]
    d_norm = matmul(after(d_logit[:owned], *away), head, ((1,), (1,)))
    for r in received:
        d_norm += r.astype(F32)
    gated = gain * d_norm
    back_scale = scale**3 * jnp.mean(gated * x_rows, axis=1, keepdims=True)
    gated_proj = jnp.sum(gated * proj, axis=1, keepdims=True)
    d_round = (scale * gated - x_rows * back_scale).astype(BF16)
    d_ratio_part = (scale * gated_proj - back_scale * x_proj).reshape(steps, part)

    part_out = matmul(normed_rows, after(d_logit, *away), ((0,), (0,))).astype(BF16)
    part_out = part_out.reshape(seqs, depth // seqs, block)
    part_out = lax.all_to_all(part_out, "seq", 0, 0)
    part_out = part_out.reshape(groups, steps, hids, head_rows, block).astype(F32).sum(0)
    part_out = part_out.astype(BF16)
    sums = [
        lax.dynamic_index_in_dim(part_out, (j + shift) % hids, 1, False) for shift in range(hids)
    ]
    sums = [along_hid(p, shift) if shift else p for shift, p in enumerate(sums)]
    grad_out = head_gradient(place, sums, halves)

    pieces = [d_round] + [along_hid(d_round, shift) for shift in range(1, hids)]
    ratio_rows = ratio_group.reshape(steps, rows, 1)
    d_ratio_part = after(d_ratio_part, pieces[1])
    d_ratio = d_ratio_part[0]
    for m in relations:
        d_ratio += flip_seq(d_ratio_part[m], m)
    d_rows = jnp.broadcast_to(d_ratio, (hids, part))
    for shift in range(1, hids):
        d_rows = lax.dynamic_update_index_in_dim(
            d_rows, along_hid(d_ratio, shift), (j - shift) % hids, 0
        )
    share, mine, *others = input_gradient(after(place, d_rows), pieces, group, ratio_rows, seqs)
    share = lax.all_to_all(share.reshape(seqs, depth // seqs, units), "seq", 0, 0)
    share = share.reshape(groups, steps, depth // seqs, units).astype(F32).sum(0)
    grad_in = share.transpose(0, 2, 1)

    ratio_own = ratio_group[0].reshape(rows)
    correction = ratio_own**3 * d_rows.reshape(rows) / width_in
    factors = jnp.stack([ratio_own, correction])[:, :, None]
    mine = [mine] + [flip_seq(others[m - 1], m) for m in relations]
    grad_hidden = hidden_gradient(place, mine, w_in, hidden, factors)
    return (grad_hidden, grad_in, grad_out)


def solution(mesh):
    placed = (
        P("seq", "hid"),
        P(None, "hid", None),
        P(),
        P(),
        P(("seq", "hid"), None, None),
        P(None, ("seq", "hid")),
    )
    return jax.shard_map(
        shards,
        mesh=mesh,
        in_specs=placed,
        out_specs=(P("seq", "hid"), P(None, "hid", "seq"), P(("seq", "hid"), None, None)),
        check_vma=False,
    )
```

```python
import jax
import jax.numpy as jnp
from jax import lax
from jax.experimental import pallas as pl
from jax.experimental.pallas import tpu as pltpu
from jax.sharding import PartitionSpec as P

F32 = jnp.float32
BF16 = jnp.bfloat16


def pick(values, index):
    return lax.dynamic_index_in_dim(values, index, axis=0, keepdims=False)


def matmul(a, b, contract):
    return lax.dot_general(a, b, (contract, ((), ())), preferred_element_type=F32)


def after(value, *others):
    return lax.optimization_barrier((value, *others))[0]


VMEM = pltpu.CompilerParams(vmem_limit_bytes=60 * 2**20)


def whole(shape):
    return pl.BlockSpec(shape, lambda n, place: (0,) * len(shape))


def call(kernel, place, grid, in_specs, out_specs, out_shape, scratch, flops, args):
    moved = sum(a.size * a.dtype.itemsize for a in args)
    return pl.pallas_call(
        kernel,
        grid_spec=pltpu.PrefetchScalarGridSpec(
            num_scalar_prefetch=1,
            grid=(grid,),
            in_specs=in_specs,
            out_specs=out_specs,
            scratch_shapes=scratch,
        ),
        out_shape=out_shape,
        compiler_params=VMEM,
        cost_estimate=pl.CostEstimate(flops=flops, bytes_accessed=moved, transcendentals=0),
    )(place, *args)


EXACT = 3


def parts_of(values):
    out = []
    for _ in range(EXACT):
        piece = lax.reduce_precision(values, 8, 7)
        values = values - piece
        out.append(piece.astype(BF16))
    return out


def head_gradient(place, pieces, halves):
    hids = len(pieces)
    steps, rows, block = pieces[0].shape

    def kernel(place_ref, *refs):
        pieces, out = refs[:-1], refs[-1]
        for r in range(halves):
            which = lax.rem(place_ref[1] - r + hids, halves)
            columns = pl.ds(pl.multiple_of(which * block, block), block)
            for s in range(steps):
                total = pieces[r][s].astype(F32)
                for k in range(r + halves, hids, halves):
                    total = total + pieces[k][s].astype(F32)
                out[:, s, columns] = total

    return call(
        kernel,
        place,
        1,
        [whole((steps, rows, block))] * hids,
        whole((rows, steps, halves * block)),
        jax.ShapeDtypeStruct((rows, steps, halves * block), F32),
        [],
        hids * steps * rows * block,
        tuple(pieces),
    )


def input_gradient(place, pieces, group, ratio, seqs):
    hids, steps = len(pieces), len(group)
    owned, depth = pieces[0].shape
    rows, units = group[0].shape
    part = owned // steps
    wide = min(512, depth)

    def kernel(place_ref, *refs):
        chunks, group, ratio = refs[:hids], refs[hids : hids + steps], refs[hids + steps]
        out, plain, scaled = refs[hids + steps + 1], refs[hids + steps + 2 : -1], refs[-1]
        j = place_ref[1]
        for r in range(hids):
            to = pl.multiple_of(lax.rem(j - r + hids, hids) * part, part)
            for m in range(steps):
                values = chunks[r][m * part : (m + 1) * part, :]
                plain[m][pl.ds(to, part), :] = values
                factor = ratio[m, pl.ds(to, part), :]
                scaled[m, pl.ds(to, part), :] = (values.astype(F32) * factor).astype(BF16)
        total = None
        for m in range(steps):
            term = lax.dot_general(
                scaled[m], group[m][...], (((0,), (0,)), ((), ())), preferred_element_type=F32
            )
            total = term if total is None else total + term
        out[...] = total.astype(BF16)

    return call(
        kernel,
        place,
        depth // wide,
        [pl.BlockSpec((owned, wide), lambda n, place: (0, n))] * hids
        + [whole((rows, units))] * steps
        + [whole((steps, rows, 1))],
        [pl.BlockSpec((wide, units), lambda n, place: (n, 0))]
        + [pl.BlockSpec((rows, wide), lambda n, place: (0, n))] * steps,
        [jax.ShapeDtypeStruct((depth, units), BF16)]
        + [jax.ShapeDtypeStruct((rows, depth), BF16)] * steps,
        [pltpu.VMEM((steps, rows, wide), BF16)],
        2 * steps * rows * units * depth,
        (*pieces, *group, ratio),
    )


def hidden_gradient(place, d_rows, w_in, hidden, factors):
    steps, units, depth = w_in.shape
    rows = hidden.shape[0]
    wide = min(512, units)

    def kernel(place_ref, *refs):
        d_rows, w, hidden, factors, out = refs[:steps], refs[-4], refs[-3], refs[-2], refs[-1]
        total = None
        for r in range(steps):
            which = lax.rem(place_ref[0] - r + steps, steps)
            term = lax.dot_general(
                d_rows[r][...], w[which], (((1,), (1,)), ((), ())), preferred_element_type=F32
            )
            total = term if total is None else total + term
        out[...] = (factors[0] * total - factors[1] * hidden[...].astype(F32)).astype(BF16)

    return call(
        kernel,
        place,
        units // wide,
        [whole((rows, depth))] * steps
        + [
            pl.BlockSpec((steps, wide, depth), lambda n, place: (0, n, 0)),
            pl.BlockSpec((rows, wide), lambda n, place: (0, n)),
            whole((2, rows, 1)),
        ],
        pl.BlockSpec((rows, wide), lambda n, place: (0, n)),
        jax.ShapeDtypeStruct((rows, units), BF16),
        [],
        2 * steps * rows * units * depth,
        (*d_rows, w_in, hidden, factors),
    )


def shards(hidden, w_in, embedding, depth_gain, w_out, codebook_ids):
    hids = lax.axis_size("hid")
    seqs = lax.axis_size("seq")
    steps, units, depth = w_in.shape
    entries = w_out.shape[2]
    rows = hidden.shape[0]
    part = rows // hids
    width_in = units * hids
    frames = rows * seqs
    halves = 2 if hids % 2 == 0 else 1
    block = entries // halves
    head_rows = w_out.shape[0]
    groups = seqs // steps
    i = lax.axis_index("seq")
    j = lax.axis_index("hid")
    step = i % steps
    half = j % halves
    owned = steps * part

    def along_hid(values, shift):
        return lax.ppermute(values, "hid", [(a, (a + shift) % hids) for a in range(hids)])

    def turn_hid(values, shift):
        return lax.ppermute(
            values,
            "hid",
            [(a, a - a % halves + (a % halves + shift) % halves) for a in range(hids)],
        )

    def flip_seq(values, flip):
        return lax.ppermute(
            values,
            "seq",
            [(a, a - a % steps + (a % steps + flip) % steps) for a in range(seqs)],
        )

    place = jnp.stack([step, j]).astype(jnp.int32)
    relations = range(1, steps)

    group = [hidden] + [flip_seq(hidden, -m) for m in relations]

    squares_part = jnp.sum(jnp.square(hidden.astype(F32)), axis=1)
    tail = 8 * block
    small = jnp.concatenate(parts_of(squares_part))
    small = jnp.pad(small, (0, tail - small.size)).reshape(8, block)
    head_parts = w_out.reshape(head_rows, steps, halves, block)
    head_send = []
    for k in range(halves):
        piece = lax.dynamic_index_in_dim(head_parts, (half + k) % halves, 2, False)
        piece = piece.transpose(1, 0, 2).reshape(steps * head_rows, block)
        head_send.append(jnp.concatenate([piece, small]))
    head_got = [head_send[0]]
    head_got += [along_hid(head_send[shift % halves], shift) for shift in range(1, hids)]
    w_own = pick(w_in, step)
    proj_parts = matmul(jnp.concatenate(group), w_own, ((1,), (0,)))
    proj_parts = proj_parts.reshape(steps, hids, part, depth)

    def owner_block(index):
        return lax.dynamic_index_in_dim(proj_parts, index, 1, False).reshape(owned, depth)

    send = [owner_block((j + shift) % hids).astype(BF16) for shift in range(1, hids)]
    ready = [after(p, *head_got[1:]) for p in send]
    received = [along_hid(ready[shift - 1], shift) for shift in range(1, hids)]

    head_got = [head_got[0]] + [after(g, *send) for g in head_got[1:]]
    squares = sum(g[steps * head_rows :].astype(F32) for g in head_got).reshape(tail)
    squares = jnp.sum(squares[: EXACT * rows].reshape(EXACT, rows), axis=0)
    head_mid = jnp.stack([g[: steps * head_rows] for g in head_got[::-1]] * 2)
    head_mid = lax.dynamic_slice_in_dim(head_mid, hids - 1 - j, hids, 0)
    head_mid = head_mid.reshape(hids, steps, head_rows, block)

    ids = after(codebook_ids, *send)
    ids = jnp.concatenate([ids] + [flip_seq(ids, -m) for m in relations], axis=1)
    ids_rows = [ids] + [turn_hid(ids, -k) for k in range(1, halves)]
    before = jnp.maximum(step - 1, 0)
    looked = jnp.take(pick(embedding, before), pick(ids, before), axis=0)

    head_send = head_mid.transpose(1, 0, 2, 3)
    head_send = head_send.reshape(steps, hids * head_rows, block)
    head_send = jnp.broadcast_to(head_send, (groups,) + head_send.shape)
    head_send = head_send.reshape(seqs, hids * head_rows, block)
    head = lax.all_to_all(head_send, "seq", 0, 0).reshape(depth, block)

    squares = jnp.stack([squares] + [flip_seq(squares, -m) for m in relations])
    ratio_group = lax.rsqrt(squares / width_in + 1e-06).reshape(steps, hids, part)

    ratio = lax.dynamic_index_in_dim(ratio_group, j, 1, False).reshape(owned, 1)
    proj = owner_block(j)
    for r in received:
        proj += r.astype(F32)
    x_rows = ratio * proj + jnp.where(step > 0, looked.astype(F32), 0.0)
    scale = lax.rsqrt(jnp.mean(x_rows * x_rows, axis=1, keepdims=True) + 1e-06)
    x_proj = jnp.sum(x_rows * proj, axis=1, keepdims=True)
    gain = pick(depth_gain, step)[None, :]
    normed = (x_rows * scale * gain).astype(BF16)

    normed_rows = jnp.concatenate([normed] + [turn_hid(normed, -k) for k in range(1, halves)])
    targets = jnp.concatenate([pick(r, step) for r in ids_rows])
    logits = matmul(normed_rows, head, ((1,), (0,)))
    top = jnp.max(logits, axis=1)
    total = jnp.sum(jnp.exp(logits - top[:, None]), axis=1)
    stats = jnp.stack([top, total]).reshape(2, halves, -1)
    every = [stats] + [jnp.roll(turn_hid(stats, -t), t, axis=1) for t in range(1, halves)]
    tops = jnp.stack([e[0] for e in every]).reshape(halves, -1)
    totals = jnp.stack([e[1] for e in every]).reshape(halves, -1)
    top_all = jnp.max(tops, axis=0)
    lse = top_all + jnp.log(jnp.sum(totals * jnp.exp(tops - top_all), axis=0))
    entry = lax.broadcasted_iota(jnp.int32, logits.shape, 1) + half * block
    onehot = (targets[:, None] == entry).astype(F32)
    loss_weight = 2.0 * entries / frames
    d_logit = ((jnp.exp(logits - lse[:, None]) - onehot) * loss_weight).astype(BF16)

    away = [
        matmul(d_logit[k * owned : (k + 1) * owned], head, ((1,), (1,))).astype(BF16)
        for k in range(1, halves)
    ]
    received = [turn_hid(a, k + 1) for k, a in enumerate(away)]
    d_norm = matmul(after(d_logit[:owned], *away), head, ((1,), (1,)))
    for r in received:
        d_norm += r.astype(F32)
    gated = gain * d_norm
    back_scale = scale**3 * jnp.mean(gated * x_rows, axis=1, keepdims=True)
    gated_proj = jnp.sum(gated * proj, axis=1, keepdims=True)
    d_round = (scale * gated - x_rows * back_scale).astype(BF16)
    d_ratio_part = (scale * gated_proj - back_scale * x_proj).reshape(steps, part)

    part_out = matmul(normed_rows, after(d_logit, *away), ((0,), (0,))).astype(BF16)
    part_out = part_out.reshape(seqs, depth // seqs, block)
    part_out = lax.all_to_all(part_out, "seq", 0, 0)
    part_out = part_out.reshape(groups, steps, hids, head_rows, block).astype(F32).sum(0)
    part_out = part_out.astype(BF16)
    sums = [
        lax.dynamic_index_in_dim(part_out, (j + shift) % hids, 1, False) for shift in range(hids)
    ]
    sums = [along_hid(p, shift) if shift else p for shift, p in enumerate(sums)]
    grad_out = head_gradient(place, sums, halves)

    pieces = [d_round] + [along_hid(d_round, shift) for shift in range(1, hids)]
    ratio_rows = ratio_group.reshape(steps, rows, 1)
    d_ratio_part = after(d_ratio_part, d_round)
    d_ratio = d_ratio_part[0]
    for m in relations:
        d_ratio += flip_seq(d_ratio_part[m], m)
    d_rows = jnp.broadcast_to(d_ratio, (hids, part))
    for shift in range(1, hids):
        d_rows = lax.dynamic_update_index_in_dim(
            d_rows, along_hid(d_ratio, shift), (j - shift) % hids, 0
        )
    share, mine, *others = input_gradient(after(place, d_rows), pieces, group, ratio_rows, seqs)
    share = lax.all_to_all(share.reshape(seqs, depth // seqs, units), "seq", 0, 0)
    share = share.reshape(groups, steps, depth // seqs, units).astype(F32).sum(0)
    grad_in = share.transpose(0, 2, 1)

    ratio_own = ratio_group[0].reshape(rows)
    correction = ratio_own**3 * d_rows.reshape(rows) / width_in
    factors = jnp.stack([ratio_own, correction])[:, :, None]
    mine = [mine] + [flip_seq(others[m - 1], m) for m in relations]
    grad_hidden = hidden_gradient(place, mine, w_in, hidden, factors)
    return (grad_hidden, grad_in, grad_out)


def solution(mesh):
    placed = (
        P("seq", "hid"),
        P(None, "hid", None),
        P(),
        P(),
        P(("seq", "hid"), None, None),
        P(None, ("seq", "hid")),
    )
    return jax.shard_map(
        shards,
        mesh=mesh,
        in_specs=placed,
        out_specs=(P("seq", "hid"), P(None, "hid", "seq"), P(("seq", "hid"), None, None)),
        check_vma=False,
    )
```

```python
import jax
import jax.numpy as jnp
from jax import lax
from jax.experimental import pallas as pl
from jax.experimental.pallas import tpu as pltpu
from jax.sharding import PartitionSpec as P

F32 = jnp.float32
BF16 = jnp.bfloat16


def pick(values, index):
    return lax.dynamic_index_in_dim(values, index, axis=0, keepdims=False)


def matmul(a, b, contract):
    return lax.dot_general(a, b, (contract, ((), ())), preferred_element_type=F32)


def after(value, *others):
    return lax.optimization_barrier((value, *others))[0]


VMEM = pltpu.CompilerParams(vmem_limit_bytes=60 * 2**20)


def whole(shape):
    return pl.BlockSpec(shape, lambda n, place: (0,) * len(shape))


def call(kernel, place, grid, in_specs, out_specs, out_shape, scratch, flops, args):
    moved = sum(a.size * a.dtype.itemsize for a in args)
    return pl.pallas_call(
        kernel,
        grid_spec=pltpu.PrefetchScalarGridSpec(
            num_scalar_prefetch=1,
            grid=(grid,),
            in_specs=in_specs,
            out_specs=out_specs,
            scratch_shapes=scratch,
        ),
        out_shape=out_shape,
        compiler_params=VMEM,
        cost_estimate=pl.CostEstimate(flops=flops, bytes_accessed=moved, transcendentals=0),
    )(place, *args)


EXACT = 3


def parts_of(values):
    out = []
    for _ in range(EXACT):
        piece = lax.reduce_precision(values, 8, 7)
        values = values - piece
        out.append(piece.astype(BF16))
    return out


def head_gradient(place, pieces, halves):
    hids = len(pieces)
    steps, rows, block = pieces[0].shape

    def kernel(place_ref, *refs):
        pieces, out = refs[:-1], refs[-1]
        for r in range(halves):
            which = lax.rem(place_ref[1] - r + hids, halves)
            columns = pl.ds(pl.multiple_of(which * block, block), block)
            for s in range(steps):
                total = pieces[r][s].astype(F32)
                for k in range(r + halves, hids, halves):
                    total = total + pieces[k][s].astype(F32)
                out[:, s, columns] = total

    return call(
        kernel,
        place,
        1,
        [whole((steps, rows, block))] * hids,
        whole((rows, steps, halves * block)),
        jax.ShapeDtypeStruct((rows, steps, halves * block), F32),
        [],
        hids * steps * rows * block,
        tuple(pieces),
    )


def input_gradient(place, pieces, group, ratio, seqs):
    hids, steps = len(pieces), len(group)
    taller, depth = pieces[0].shape
    rows, units = group[0].shape
    part = rows // hids
    wide = min(512, depth)

    def kernel(place_ref, *refs):
        chunks, group, ratio = refs[:hids], refs[hids : hids + steps], refs[hids + steps]
        out, plain, scaled = refs[hids + steps + 1], refs[hids + steps + 2 : -1], refs[-1]
        j = place_ref[1]
        for r in range(hids):
            to = pl.multiple_of(lax.rem(j - r + hids, hids) * part, part)
            for m in range(steps):
                values = chunks[r][m * part : (m + 1) * part, :]
                plain[m][pl.ds(to, part), :] = values
                factor = ratio[m, pl.ds(to, part), :]
                scaled[m, pl.ds(to, part), :] = (values.astype(F32) * factor).astype(BF16)
        total = None
        for m in range(steps):
            term = lax.dot_general(
                scaled[m], group[m][...], (((0,), (0,)), ((), ())), preferred_element_type=F32
            )
            total = term if total is None else total + term
        out[...] = total.astype(BF16)

    return call(
        kernel,
        place,
        depth // wide,
        [pl.BlockSpec((taller, wide), lambda n, place: (0, n))] * hids
        + [whole((rows, units))] * steps
        + [whole((steps, rows, 1))],
        [pl.BlockSpec((wide, units), lambda n, place: (n, 0))]
        + [pl.BlockSpec((rows, wide), lambda n, place: (0, n))] * steps,
        [jax.ShapeDtypeStruct((depth, units), BF16)]
        + [jax.ShapeDtypeStruct((rows, depth), BF16)] * steps,
        [pltpu.VMEM((steps, rows, wide), BF16)],
        2 * steps * rows * units * depth,
        (*pieces, *group, ratio),
    )


def hidden_gradient(place, d_rows, w_in, hidden, factors):
    steps, units, depth = w_in.shape
    rows = hidden.shape[0]
    wide = min(512, units)

    def kernel(place_ref, *refs):
        d_rows, w, hidden, factors, out = refs[:steps], refs[-4], refs[-3], refs[-2], refs[-1]
        total = None
        for r in range(steps):
            which = lax.rem(place_ref[0] - r + steps, steps)
            term = lax.dot_general(
                d_rows[r][...], w[which], (((1,), (1,)), ((), ())), preferred_element_type=F32
            )
            total = term if total is None else total + term
        out[...] = (factors[0] * total - factors[1] * hidden[...].astype(F32)).astype(BF16)

    return call(
        kernel,
        place,
        units // wide,
        [whole((rows, depth))] * steps
        + [
            pl.BlockSpec((steps, wide, depth), lambda n, place: (0, n, 0)),
            pl.BlockSpec((rows, wide), lambda n, place: (0, n)),
            whole((2, rows, 1)),
        ],
        pl.BlockSpec((rows, wide), lambda n, place: (0, n)),
        jax.ShapeDtypeStruct((rows, units), BF16),
        [],
        2 * steps * rows * units * depth,
        (*d_rows, w_in, hidden, factors),
    )


def shards(hidden, w_in, embedding, depth_gain, w_out, codebook_ids):
    hids = lax.axis_size("hid")
    seqs = lax.axis_size("seq")
    steps, units, depth = w_in.shape
    entries = w_out.shape[2]
    rows = hidden.shape[0]
    part = rows // hids
    width_in = units * hids
    frames = rows * seqs
    halves = 2 if hids % 2 == 0 else 1
    block = entries // halves
    head_rows = w_out.shape[0]
    groups = seqs // steps
    i = lax.axis_index("seq")
    j = lax.axis_index("hid")
    step = i % steps
    half = j % halves
    owned = steps * part

    def along_hid(values, shift):
        return lax.ppermute(values, "hid", [(a, (a + shift) % hids) for a in range(hids)])

    def turn_hid(values, shift):
        return lax.ppermute(
            values,
            "hid",
            [(a, a - a % halves + (a % halves + shift) % halves) for a in range(hids)],
        )

    def flip_seq(values, flip):
        return lax.ppermute(
            values,
            "seq",
            [(a, a - a % steps + (a % steps + flip) % steps) for a in range(seqs)],
        )

    place = jnp.stack([step, j]).astype(jnp.int32)
    relations = range(1, steps)

    group = [hidden] + [flip_seq(hidden, -m) for m in relations]

    squares_part = jnp.sum(jnp.square(hidden.astype(F32)), axis=1)
    tail = 8 * block
    small = jnp.concatenate(parts_of(squares_part))
    small = jnp.pad(small, (0, tail - small.size)).reshape(8, block)
    head_parts = w_out.reshape(head_rows, steps, halves, block)
    head_send = []
    for k in range(halves):
        piece = lax.dynamic_index_in_dim(head_parts, (half + k) % halves, 2, False)
        piece = piece.transpose(1, 0, 2).reshape(steps * head_rows, block)
        head_send.append(jnp.concatenate([piece, small]))
    head_got = [head_send[0]]
    head_got += [along_hid(head_send[shift % halves], shift) for shift in range(1, hids)]
    w_own = pick(w_in, step)
    proj_parts = matmul(jnp.concatenate(group), w_own, ((1,), (0,)))
    proj_parts = proj_parts.reshape(steps, hids, part, depth)

    def owner_block(index):
        return lax.dynamic_index_in_dim(proj_parts, index, 1, False).reshape(owned, depth)

    send = [owner_block((j + shift) % hids).astype(BF16) for shift in range(1, hids)]
    ready = [after(p, *head_got[1:]) for p in send]
    received = [along_hid(ready[shift - 1], shift) for shift in range(1, hids)]

    head_got = [head_got[0]] + [after(g, *send) for g in head_got[1:]]
    squares = sum(g[steps * head_rows :].astype(F32) for g in head_got).reshape(tail)
    squares = jnp.sum(squares[: EXACT * rows].reshape(EXACT, rows), axis=0)
    head_mid = jnp.stack([g[: steps * head_rows] for g in head_got[::-1]] * 2)
    head_mid = lax.dynamic_slice_in_dim(head_mid, hids - 1 - j, hids, 0)
    head_mid = head_mid.reshape(hids, steps, head_rows, block)

    ids = after(codebook_ids, *send)
    ids = jnp.concatenate([ids] + [flip_seq(ids, -m) for m in relations], axis=1)
    ids_rows = [ids] + [turn_hid(ids, -k) for k in range(1, halves)]
    before = jnp.maximum(step - 1, 0)
    looked = jnp.take(pick(embedding, before), pick(ids, before), axis=0)

    head_send = head_mid.transpose(1, 0, 2, 3)
    head_send = head_send.reshape(steps, hids * head_rows, block)
    head_send = jnp.broadcast_to(head_send, (groups,) + head_send.shape)
    head_send = head_send.reshape(seqs, hids * head_rows, block)
    head = lax.all_to_all(head_send, "seq", 0, 0).reshape(depth, block)

    squares = jnp.stack([squares] + [flip_seq(squares, -m) for m in relations])
    ratio_group = lax.rsqrt(squares / width_in + 1e-06).reshape(steps, hids, part)

    ratio = lax.dynamic_index_in_dim(ratio_group, j, 1, False).reshape(owned, 1)
    proj = owner_block(j)
    for r in received:
        proj += r.astype(F32)
    x_rows = ratio * proj + jnp.where(step > 0, looked.astype(F32), 0.0)
    scale = lax.rsqrt(jnp.mean(x_rows * x_rows, axis=1, keepdims=True) + 1e-06)
    x_proj = jnp.sum(x_rows * proj, axis=1, keepdims=True)
    gain = pick(depth_gain, step)[None, :]
    normed = (x_rows * scale * gain).astype(BF16)

    normed_rows = jnp.concatenate([normed] + [turn_hid(normed, -k) for k in range(1, halves)])
    targets = jnp.concatenate([pick(r, step) for r in ids_rows])
    logits = matmul(normed_rows, head, ((1,), (0,)))
    top = jnp.max(logits, axis=1)
    total = jnp.sum(jnp.exp(logits - top[:, None]), axis=1)
    stats = jnp.stack([top, total]).reshape(2, halves, -1)
    every = [stats] + [jnp.roll(turn_hid(stats, -t), t, axis=1) for t in range(1, halves)]
    tops = jnp.stack([e[0] for e in every]).reshape(halves, -1)
    totals = jnp.stack([e[1] for e in every]).reshape(halves, -1)
    top_all = jnp.max(tops, axis=0)
    lse = top_all + jnp.log(jnp.sum(totals * jnp.exp(tops - top_all), axis=0))
    entry = lax.broadcasted_iota(jnp.int32, logits.shape, 1) + half * block
    onehot = (targets[:, None] == entry).astype(F32)
    loss_weight = 2.0 * entries / frames
    d_logit = ((jnp.exp(logits - lse[:, None]) - onehot) * loss_weight).astype(BF16)

    away = [
        matmul(d_logit[k * owned : (k + 1) * owned], head, ((1,), (1,))).astype(BF16)
        for k in range(1, halves)
    ]
    received = [turn_hid(a, k + 1) for k, a in enumerate(away)]
    d_norm = matmul(after(d_logit[:owned], *away), head, ((1,), (1,)))
    for r in received:
        d_norm += r.astype(F32)
    gated = gain * d_norm
    back_scale = scale**3 * jnp.mean(gated * x_rows, axis=1, keepdims=True)
    gated_proj = jnp.sum(gated * proj, axis=1, keepdims=True)
    d_round = (scale * gated - x_rows * back_scale).astype(BF16)
    d_ratio_part = (scale * gated_proj - back_scale * x_proj).reshape(steps, part)

    part_out = matmul(normed_rows, after(d_logit, *away), ((0,), (0,))).astype(BF16)
    part_out = part_out.reshape(seqs, depth // seqs, block)
    part_out = lax.all_to_all(part_out, "seq", 0, 0)
    part_out = part_out.reshape(groups, steps, hids, head_rows, block).astype(F32).sum(0)
    part_out = part_out.astype(BF16)
    sums = [
        lax.dynamic_index_in_dim(part_out, (j + shift) % hids, 1, False) for shift in range(hids)
    ]
    sums = [along_hid(p, shift) if shift else p for shift, p in enumerate(sums)]
    grad_out = head_gradient(place, sums, halves)

    below = jnp.concatenate(parts_of(d_ratio_part.reshape(owned)))
    below = jnp.pad(below, (0, 8 * depth - below.size)).reshape(8, depth)
    payload = jnp.concatenate([d_round, below])
    pieces = [payload] + [along_hid(payload, shift) for shift in range(1, hids)]
    ratio_rows = ratio_group.reshape(steps, rows, 1)
    share, mine, *others = input_gradient(place, pieces, group, ratio_rows, seqs)
    share = lax.all_to_all(share.reshape(seqs, depth // seqs, units), "seq", 0, 0)
    share = share.reshape(groups, steps, depth // seqs, units).astype(F32).sum(0)
    grad_in = share.transpose(0, 2, 1)

    shares = [p[owned:].reshape(-1)[: EXACT * owned].reshape(EXACT, steps, part) for p in pieces]
    shares = [jnp.sum(p.astype(F32), axis=0) for p in shares]
    shares = lax.dynamic_slice_in_dim(jnp.stack(shares[::-1] * 2), hids - 1 - j, hids, 0)
    d_rows = shares[:, 0]
    for m in relations:
        d_rows += flip_seq(shares[:, m], m)
    ratio_own = ratio_group[0].reshape(rows)
    correction = ratio_own**3 * d_rows.reshape(rows) / width_in
    factors = jnp.stack([ratio_own, correction])[:, :, None]
    mine = [mine] + [flip_seq(others[m - 1], m) for m in relations]
    grad_hidden = hidden_gradient(place, mine, w_in, hidden, factors)
    return (grad_hidden, grad_in, grad_out)


def solution(mesh):
    placed = (
        P("seq", "hid"),
        P(None, "hid", None),
        P(),
        P(),
        P(("seq", "hid"), None, None),
        P(None, ("seq", "hid")),
    )
    return jax.shard_map(
        shards,
        mesh=mesh,
        in_specs=placed,
        out_specs=(P("seq", "hid"), P(None, "hid", "seq"), P(("seq", "hid"), None, None)),
        check_vma=False,
    )
```

```python
import jax
import jax.numpy as jnp
from jax import lax
from jax.experimental import pallas as pl
from jax.experimental.pallas import tpu as pltpu
from jax.sharding import PartitionSpec as P

F32 = jnp.float32
BF16 = jnp.bfloat16


def pick(values, index):
    return lax.dynamic_index_in_dim(values, index, axis=0, keepdims=False)


def matmul(a, b, contract):
    return lax.dot_general(a, b, (contract, ((), ())), preferred_element_type=F32)


def after(value, *others):
    return lax.optimization_barrier((value, *others))[0]


VMEM = pltpu.CompilerParams(vmem_limit_bytes=60 * 2**20)


def whole(shape):
    return pl.BlockSpec(shape, lambda n, place: (0,) * len(shape))


def call(kernel, place, grid, in_specs, out_specs, out_shape, scratch, flops, args):
    moved = sum(a.size * a.dtype.itemsize for a in args)
    return pl.pallas_call(
        kernel,
        grid_spec=pltpu.PrefetchScalarGridSpec(
            num_scalar_prefetch=1,
            grid=(grid,),
            in_specs=in_specs,
            out_specs=out_specs,
            scratch_shapes=scratch,
        ),
        out_shape=out_shape,
        compiler_params=VMEM,
        cost_estimate=pl.CostEstimate(flops=flops, bytes_accessed=moved, transcendentals=0),
    )(place, *args)


EXACT = 3


def parts_of(values):
    out = []
    for _ in range(EXACT):
        piece = lax.reduce_precision(values, 8, 7)
        values = values - piece
        out.append(piece.astype(BF16))
    return out


def head_gradient(place, pieces, halves):
    hids = len(pieces)
    steps, rows, block = pieces[0].shape

    def kernel(place_ref, *refs):
        pieces, out = refs[:-1], refs[-1]
        for r in range(halves):
            which = lax.rem(place_ref[1] - r + hids, halves)
            columns = pl.ds(pl.multiple_of(which * block, block), block)
            for s in range(steps):
                total = pieces[r][s].astype(F32)
                for k in range(r + halves, hids, halves):
                    total = total + pieces[k][s].astype(F32)
                out[:, s, columns] = total

    return call(
        kernel,
        place,
        1,
        [whole((steps, rows, block))] * hids,
        whole((rows, steps, halves * block)),
        jax.ShapeDtypeStruct((rows, steps, halves * block), F32),
        [],
        hids * steps * rows * block,
        tuple(pieces),
    )


def input_gradient(place, pieces, group, ratio, seqs):
    hids, steps = len(pieces), len(group)
    owned, depth = pieces[0].shape
    rows, units = group[0].shape
    part = owned // steps
    wide = min(512, depth)

    def kernel(place_ref, *refs):
        chunks, group, ratio = refs[:hids], refs[hids : hids + steps], refs[hids + steps]
        out, plain, scaled = refs[hids + steps + 1], refs[hids + steps + 2 : -1], refs[-1]
        j = place_ref[1]
        for r in range(hids):
            to = pl.multiple_of(lax.rem(j - r + hids, hids) * part, part)
            for m in range(steps):
                values = chunks[r][m * part : (m + 1) * part, :]
                plain[m][pl.ds(to, part), :] = values
                factor = ratio[m, pl.ds(to, part), :]
                scaled[m, pl.ds(to, part), :] = (values.astype(F32) * factor).astype(BF16)
        total = None
        for m in range(steps):
            term = lax.dot_general(
                scaled[m], group[m][...], (((0,), (0,)), ((), ())), preferred_element_type=F32
            )
            total = term if total is None else total + term
        out[...] = total.astype(BF16)

    return call(
        kernel,
        place,
        depth // wide,
        [pl.BlockSpec((owned, wide), lambda n, place: (0, n))] * hids
        + [whole((rows, units))] * steps
        + [whole((steps, rows, 1))],
        [pl.BlockSpec((wide, units), lambda n, place: (n, 0))]
        + [pl.BlockSpec((rows, wide), lambda n, place: (0, n))] * steps,
        [jax.ShapeDtypeStruct((depth, units), BF16)]
        + [jax.ShapeDtypeStruct((rows, depth), BF16)] * steps,
        [pltpu.VMEM((steps, rows, wide), BF16)],
        2 * steps * rows * units * depth,
        (*pieces, *group, ratio),
    )


def hidden_gradient(place, d_rows, w_in, hidden, factors):
    steps, units, depth = w_in.shape
    rows = hidden.shape[0]
    wide = min(512, units)

    def kernel(place_ref, *refs):
        d_rows, w, hidden, factors, out = refs[:steps], refs[-4], refs[-3], refs[-2], refs[-1]
        total = None
        for r in range(steps):
            which = lax.rem(place_ref[0] - r + steps, steps)
            term = lax.dot_general(
                d_rows[r][...], w[which], (((1,), (1,)), ((), ())), preferred_element_type=F32
            )
            total = term if total is None else total + term
        out[...] = (factors[0] * total - factors[1] * hidden[...].astype(F32)).astype(BF16)

    return call(
        kernel,
        place,
        units // wide,
        [whole((rows, depth))] * steps
        + [
            pl.BlockSpec((steps, wide, depth), lambda n, place: (0, n, 0)),
            pl.BlockSpec((rows, wide), lambda n, place: (0, n)),
            whole((2, rows, 1)),
        ],
        pl.BlockSpec((rows, wide), lambda n, place: (0, n)),
        jax.ShapeDtypeStruct((rows, units), BF16),
        [],
        2 * steps * rows * units * depth,
        (*d_rows, w_in, hidden, factors),
    )


def shards(hidden, w_in, embedding, depth_gain, w_out, codebook_ids):
    hids = lax.axis_size("hid")
    seqs = lax.axis_size("seq")
    steps, units, depth = w_in.shape
    entries = w_out.shape[2]
    rows = hidden.shape[0]
    part = rows // hids
    width_in = units * hids
    frames = rows * seqs
    halves = 2 if hids % 2 == 0 else 1
    block = entries // halves
    head_rows = w_out.shape[0]
    groups = seqs // steps
    i = lax.axis_index("seq")
    j = lax.axis_index("hid")
    step = i % steps
    half = j % halves
    owned = steps * part

    def along_hid(values, shift):
        return lax.ppermute(values, "hid", [(a, (a + shift) % hids) for a in range(hids)])

    def turn_hid(values, shift):
        return lax.ppermute(
            values,
            "hid",
            [(a, a - a % halves + (a % halves + shift) % halves) for a in range(hids)],
        )

    def flip_seq(values, flip):
        return lax.ppermute(
            values,
            "seq",
            [(a, a - a % steps + (a % steps + flip) % steps) for a in range(seqs)],
        )

    place = jnp.stack([step, j]).astype(jnp.int32)
    relations = range(1, steps)

    group = [hidden] + [flip_seq(hidden, -m) for m in relations]

    squares_part = jnp.sum(jnp.square(hidden.astype(F32)), axis=1)
    tail = 8 * block
    small = jnp.concatenate(parts_of(squares_part))
    small = jnp.pad(small, (0, tail - small.size)).reshape(8, block)
    head_parts = w_out.reshape(head_rows, steps, halves, block)
    head_send = []
    for k in range(halves):
        piece = lax.dynamic_index_in_dim(head_parts, (half + k) % halves, 2, False)
        piece = piece.transpose(1, 0, 2).reshape(steps * head_rows, block)
        head_send.append(jnp.concatenate([piece, small]))
    head_got = [head_send[0]]
    head_got += [along_hid(head_send[shift % halves], shift) for shift in range(1, hids)]
    w_own = pick(w_in, step)
    proj_parts = matmul(jnp.concatenate(group), w_own, ((1,), (0,)))
    proj_parts = proj_parts.reshape(steps, hids, part, depth)

    def owner_block(index):
        return lax.dynamic_index_in_dim(proj_parts, index, 1, False).reshape(owned, depth)

    send = [owner_block((j + shift) % hids).astype(BF16) for shift in range(1, hids)]
    ready = [after(p, *head_got[1:]) for p in send]
    received = [along_hid(ready[shift - 1], shift) for shift in range(1, hids)]

    head_got = [head_got[0]] + [after(g, *send) for g in head_got[1:]]
    squares = sum(g[steps * head_rows :].astype(F32) for g in head_got).reshape(tail)
    squares = jnp.sum(squares[: EXACT * rows].reshape(EXACT, rows), axis=0)
    head_mid = jnp.stack([g[: steps * head_rows] for g in head_got[::-1]] * 2)
    head_mid = lax.dynamic_slice_in_dim(head_mid, hids - 1 - j, hids, 0)
    head_mid = head_mid.reshape(hids, steps, head_rows, block)

    ids = after(codebook_ids, *send)
    ids = jnp.concatenate([ids] + [flip_seq(ids, -m) for m in relations], axis=1)
    ids_rows = [ids] + [turn_hid(ids, -k) for k in range(1, halves)]
    before = jnp.maximum(step - 1, 0)
    looked = jnp.take(pick(embedding, before), pick(ids, before), axis=0)

    head_send = head_mid.transpose(1, 0, 2, 3)
    head_send = head_send.reshape(steps, hids * head_rows, block)
    head_send = jnp.broadcast_to(head_send, (groups,) + head_send.shape)
    head_send = head_send.reshape(seqs, hids * head_rows, block)
    head = lax.all_to_all(head_send, "seq", 0, 0).reshape(depth, block)

    squares = jnp.stack([squares] + [flip_seq(squares, -m) for m in relations])
    ratio_group = lax.rsqrt(squares / width_in + 1e-06).reshape(steps, hids, part)

    ratio = lax.dynamic_index_in_dim(ratio_group, j, 1, False).reshape(owned, 1)
    proj = owner_block(j)
    for r in received:
        proj += r.astype(F32)
    x_rows = ratio * proj + jnp.where(step > 0, looked.astype(F32), 0.0)
    scale = lax.rsqrt(jnp.mean(x_rows * x_rows, axis=1, keepdims=True) + 1e-06)
    x_proj = jnp.sum(x_rows * proj, axis=1, keepdims=True)
    gain = pick(depth_gain, step)[None, :]
    normed = (x_rows * scale * gain).astype(BF16)

    normed_rows = jnp.concatenate([normed] + [turn_hid(normed, -k) for k in range(1, halves)])
    targets = jnp.concatenate([pick(r, step) for r in ids_rows])
    logits = matmul(normed_rows, head, ((1,), (0,)))
    top = jnp.max(logits, axis=1)
    total = jnp.sum(jnp.exp(logits - top[:, None]), axis=1)
    stats = jnp.stack([top, total]).reshape(2, halves, -1)
    every = [stats] + [jnp.roll(turn_hid(stats, -t), t, axis=1) for t in range(1, halves)]
    tops = jnp.stack([e[0] for e in every]).reshape(halves, -1)
    totals = jnp.stack([e[1] for e in every]).reshape(halves, -1)
    top_all = jnp.max(tops, axis=0)
    lse = top_all + jnp.log(jnp.sum(totals * jnp.exp(tops - top_all), axis=0))
    entry = lax.broadcasted_iota(jnp.int32, logits.shape, 1) + half * block
    onehot = (targets[:, None] == entry).astype(F32)
    loss_weight = 2.0 * entries / frames
    d_logit = ((jnp.exp(logits - lse[:, None]) - onehot) * loss_weight).astype(BF16)

    away = [
        matmul(d_logit[k * owned : (k + 1) * owned], head, ((1,), (1,))).astype(BF16)
        for k in range(1, halves)
    ]
    received = [turn_hid(a, k + 1) for k, a in enumerate(away)]
    d_norm = matmul(after(d_logit[:owned], *away), head, ((1,), (1,)))
    for r in received:
        d_norm += r.astype(F32)
    gated = gain * d_norm
    back_scale = scale**3 * jnp.mean(gated * x_rows, axis=1, keepdims=True)
    gated_proj = jnp.sum(gated * proj, axis=1, keepdims=True)
    d_round = (scale * gated - x_rows * back_scale).astype(BF16)
    d_ratio_part = (scale * gated_proj - back_scale * x_proj).reshape(steps, part)

    part_out = matmul(normed_rows, after(d_logit, *away), ((0,), (0,))).astype(BF16)
    part_out = part_out.reshape(seqs, depth // seqs, block)
    part_out = lax.all_to_all(part_out, "seq", 0, 0)
    part_out = part_out.reshape(groups, steps, hids, head_rows, block).astype(F32).sum(0)
    part_out = part_out.astype(BF16)
    sums = [
        lax.dynamic_index_in_dim(part_out, (j + shift) % hids, 1, False) for shift in range(hids)
    ]
    sums = [along_hid(p, shift) if shift else p for shift, p in enumerate(sums)]
    grad_out = head_gradient(place, sums, halves)

    pieces = [d_round] + [along_hid(d_round, shift) for shift in range(1, hids)]
    ratio_rows = ratio_group.reshape(steps, rows, 1)
    share, mine, *others = input_gradient(place, pieces, group, ratio_rows, seqs)
    share = lax.all_to_all(share.reshape(seqs, depth // seqs, units), "seq", 0, 0)
    share = share.reshape(groups, steps, depth // seqs, units).astype(F32).sum(0)
    grad_in = share.transpose(0, 2, 1)

    d_ratio = d_ratio_part[0]
    for m in relations:
        d_ratio += flip_seq(d_ratio_part[m], m)
    d_rows = jnp.broadcast_to(d_ratio, (hids, part))
    for shift in range(1, hids):
        d_rows = lax.dynamic_update_index_in_dim(
            d_rows, along_hid(d_ratio, shift), (j - shift) % hids, 0
        )
    ratio_own = ratio_group[0].reshape(rows)
    correction = ratio_own**3 * d_rows.reshape(rows) / width_in
    factors = jnp.stack([ratio_own, correction])[:, :, None]
    mine = [mine] + [flip_seq(others[m - 1], m) for m in relations]
    grad_hidden = hidden_gradient(place, mine, w_in, hidden, factors)
    return (grad_hidden, grad_in, grad_out)


def solution(mesh):
    placed = (
        P("seq", "hid"),
        P(None, "hid", None),
        P(),
        P(),
        P(("seq", "hid"), None, None),
        P(None, ("seq", "hid")),
    )
    return jax.shard_map(
        shards,
        mesh=mesh,
        in_specs=placed,
        out_specs=(P("seq", "hid"), P(None, "hid", "seq"), P(("seq", "hid"), None, None)),
        check_vma=False,
    )
```

```python
import jax
import jax.numpy as jnp
from jax import lax
from jax.experimental import pallas as pl
from jax.experimental.pallas import tpu as pltpu
from jax.sharding import PartitionSpec as P

F32 = jnp.float32
BF16 = jnp.bfloat16


def pick(values, index):
    return lax.dynamic_index_in_dim(values, index, axis=0, keepdims=False)


def matmul(a, b, contract):
    return lax.dot_general(a, b, (contract, ((), ())), preferred_element_type=F32)


def after(value, *others):
    return lax.optimization_barrier((value, *others))[0]


VMEM = pltpu.CompilerParams(vmem_limit_bytes=60 * 2**20)


def whole(shape):
    return pl.BlockSpec(shape, lambda n, place: (0,) * len(shape))


def call(kernel, place, grid, in_specs, out_specs, out_shape, scratch, flops, args):
    moved = sum(a.size * a.dtype.itemsize for a in args)
    return pl.pallas_call(
        kernel,
        grid_spec=pltpu.PrefetchScalarGridSpec(
            num_scalar_prefetch=1,
            grid=(grid,),
            in_specs=in_specs,
            out_specs=out_specs,
            scratch_shapes=scratch,
        ),
        out_shape=out_shape,
        compiler_params=VMEM,
        cost_estimate=pl.CostEstimate(flops=flops, bytes_accessed=moved, transcendentals=0),
    )(place, *args)


EXACT = 3


def parts_of(values):
    out = []
    for _ in range(EXACT):
        piece = lax.reduce_precision(values, 8, 7)
        values = values - piece
        out.append(piece.astype(BF16))
    return out


def head_gradient(place, pieces, halves):
    hids = len(pieces)
    steps, rows, block = pieces[0].shape

    def kernel(place_ref, *refs):
        pieces, out = refs[:-1], refs[-1]
        for r in range(halves):
            which = lax.rem(place_ref[1] - r + hids, halves)
            columns = pl.ds(pl.multiple_of(which * block, block), block)
            for s in range(steps):
                total = pieces[r][s].astype(F32)
                for k in range(r + halves, hids, halves):
                    total = total + pieces[k][s].astype(F32)
                out[:, s, columns] = total

    return call(
        kernel,
        place,
        1,
        [whole((steps, rows, block))] * hids,
        whole((rows, steps, halves * block)),
        jax.ShapeDtypeStruct((rows, steps, halves * block), F32),
        [],
        hids * steps * rows * block,
        tuple(pieces),
    )


def input_gradient(place, pieces, group, ratio, seqs):
    hids, steps = len(pieces), len(group)
    owned, depth = pieces[0].shape
    rows, units = group[0].shape
    part = owned // steps
    wide = min(512, depth)

    def kernel(place_ref, *refs):
        chunks, group, ratio = refs[:hids], refs[hids : hids + steps], refs[hids + steps]
        out, plain, scaled = refs[hids + steps + 1], refs[hids + steps + 2 : -1], refs[-1]
        j = place_ref[1]
        for r in range(hids):
            to = pl.multiple_of(lax.rem(j - r + hids, hids) * part, part)
            for m in range(steps):
                values = chunks[r][m * part : (m + 1) * part, :]
                plain[m][pl.ds(to, part), :] = values
                factor = ratio[m, pl.ds(to, part), :]
                scaled[m, pl.ds(to, part), :] = (values.astype(F32) * factor).astype(BF16)
        total = None
        for m in range(steps):
            term = lax.dot_general(
                scaled[m], group[m][...], (((0,), (0,)), ((), ())), preferred_element_type=F32
            )
            total = term if total is None else total + term
        out[...] = total.astype(BF16)

    return call(
        kernel,
        place,
        depth // wide,
        [pl.BlockSpec((owned, wide), lambda n, place: (0, n))] * hids
        + [whole((rows, units))] * steps
        + [whole((steps, rows, 1))],
        [pl.BlockSpec((wide, units), lambda n, place: (n, 0))]
        + [pl.BlockSpec((rows, wide), lambda n, place: (0, n))] * steps,
        [jax.ShapeDtypeStruct((depth, units), BF16)]
        + [jax.ShapeDtypeStruct((rows, depth), BF16)] * steps,
        [pltpu.VMEM((steps, rows, wide), BF16)],
        2 * steps * rows * units * depth,
        (*pieces, *group, ratio),
    )


def hidden_gradient(place, d_rows, w_in, hidden, factors):
    steps, units, depth = w_in.shape
    rows = hidden.shape[0]
    wide = min(512, units)

    def kernel(place_ref, *refs):
        d_rows, w, hidden, factors, out = refs[:steps], refs[-4], refs[-3], refs[-2], refs[-1]
        total = None
        for r in range(steps):
            which = lax.rem(place_ref[0] - r + steps, steps)
            term = lax.dot_general(
                d_rows[r][...], w[which], (((1,), (1,)), ((), ())), preferred_element_type=F32
            )
            total = term if total is None else total + term
        out[...] = (factors[0] * total - factors[1] * hidden[...].astype(F32)).astype(BF16)

    return call(
        kernel,
        place,
        units // wide,
        [whole((rows, depth))] * steps
        + [
            pl.BlockSpec((steps, wide, depth), lambda n, place: (0, n, 0)),
            pl.BlockSpec((rows, wide), lambda n, place: (0, n)),
            whole((2, rows, 1)),
        ],
        pl.BlockSpec((rows, wide), lambda n, place: (0, n)),
        jax.ShapeDtypeStruct((rows, units), BF16),
        [],
        2 * steps * rows * units * depth,
        (*d_rows, w_in, hidden, factors),
    )


def shards(hidden, w_in, embedding, depth_gain, w_out, codebook_ids):
    hids = lax.axis_size("hid")
    seqs = lax.axis_size("seq")
    steps, units, depth = w_in.shape
    entries = w_out.shape[2]
    rows = hidden.shape[0]
    part = rows // hids
    width_in = units * hids
    frames = rows * seqs
    halves = 2 if hids % 2 == 0 else 1
    block = entries // halves
    head_rows = w_out.shape[0]
    groups = seqs // steps
    i = lax.axis_index("seq")
    j = lax.axis_index("hid")
    step = i % steps
    half = j % halves
    owned = steps * part

    def along_hid(values, shift):
        return lax.ppermute(values, "hid", [(a, (a + shift) % hids) for a in range(hids)])

    def turn_hid(values, shift):
        return lax.ppermute(
            values,
            "hid",
            [(a, a - a % halves + (a % halves + shift) % halves) for a in range(hids)],
        )

    def flip_seq(values, flip):
        return lax.ppermute(
            values,
            "seq",
            [(a, a - a % steps + (a % steps + flip) % steps) for a in range(seqs)],
        )

    place = jnp.stack([step, j]).astype(jnp.int32)
    relations = range(1, steps)

    group = [hidden] + [flip_seq(hidden, -m) for m in relations]

    squares_part = jnp.sum(jnp.square(hidden.astype(F32)), axis=1)
    tail = 8 * block
    small = jnp.concatenate(parts_of(squares_part))
    small = jnp.pad(small, (0, tail - small.size)).reshape(8, block)
    head_parts = w_out.reshape(head_rows, steps, halves, block)
    head_send = []
    for k in range(halves):
        piece = lax.dynamic_index_in_dim(head_parts, (half + k) % halves, 2, False)
        piece = piece.transpose(1, 0, 2).reshape(steps * head_rows, block)
        head_send.append(jnp.concatenate([piece, small]))
    head_got = [head_send[0]]
    head_got += [along_hid(head_send[shift % halves], shift) for shift in range(1, hids)]
    w_own = pick(w_in, step)
    proj_parts = matmul(jnp.concatenate(group), w_own, ((1,), (0,)))
    proj_parts = proj_parts.reshape(steps, hids, part, depth)

    def owner_block(index):
        return lax.dynamic_index_in_dim(proj_parts, index, 1, False).reshape(owned, depth)

    send = [owner_block((j + shift) % hids).astype(BF16) for shift in range(1, hids)]
    ready = [after(p, *head_got[1:]) for p in send]
    received = [along_hid(ready[shift - 1], shift) for shift in range(1, hids)]

    head_got = [head_got[0]] + [after(g, *send) for g in head_got[1:]]
    squares = sum(g[steps * head_rows :].astype(F32) for g in head_got).reshape(tail)
    squares = jnp.sum(squares[: EXACT * rows].reshape(EXACT, rows), axis=0)
    head_mid = jnp.stack([g[: steps * head_rows] for g in head_got[::-1]] * 2)
    head_mid = lax.dynamic_slice_in_dim(head_mid, hids - 1 - j, hids, 0)
    head_mid = head_mid.reshape(hids, steps, head_rows, block)

    ids = after(codebook_ids, *send)
    ids = jnp.concatenate([ids] + [flip_seq(ids, -m) for m in relations], axis=1)
    ids_rows = [ids] + [turn_hid(ids, -k) for k in range(1, halves)]
    before = jnp.maximum(step - 1, 0)
    looked = jnp.take(pick(embedding, before), pick(ids, before), axis=0)

    head_send = head_mid.transpose(1, 0, 2, 3)
    head_send = head_send.reshape(steps, hids * head_rows, block)
    head_send = jnp.broadcast_to(head_send, (groups,) + head_send.shape)
    head_send = head_send.reshape(seqs, hids * head_rows, block)
    head = lax.all_to_all(head_send, "seq", 0, 0).reshape(depth, block)

    squares = jnp.stack([squares] + [flip_seq(squares, -m) for m in relations])
    ratio_group = lax.rsqrt(squares / width_in + 1e-06).reshape(steps, hids, part)

    ratio = lax.dynamic_index_in_dim(ratio_group, j, 1, False).reshape(owned, 1)
    proj = owner_block(j)
    for r in received:
        proj += r.astype(F32)
    x_rows = ratio * proj + jnp.where(step > 0, looked.astype(F32), 0.0)
    scale = lax.rsqrt(jnp.mean(x_rows * x_rows, axis=1, keepdims=True) + 1e-06)
    x_proj = jnp.sum(x_rows * proj, axis=1, keepdims=True)
    gain = pick(depth_gain, step)[None, :]
    normed = (x_rows * scale * gain).astype(BF16)

    normed_rows = jnp.concatenate([normed] + [turn_hid(normed, -k) for k in range(1, halves)])
    targets = jnp.concatenate([pick(r, step) for r in ids_rows])
    logits = matmul(normed_rows, head, ((1,), (0,)))
    top = jnp.max(logits, axis=1)
    total = jnp.sum(jnp.exp(logits - top[:, None]), axis=1)
    stats = jnp.stack([top, total]).reshape(2, halves, -1)
    every = [stats] + [jnp.roll(turn_hid(stats, -t), t, axis=1) for t in range(1, halves)]
    tops = jnp.stack([e[0] for e in every]).reshape(halves, -1)
    totals = jnp.stack([e[1] for e in every]).reshape(halves, -1)
    top_all = jnp.max(tops, axis=0)
    lse = top_all + jnp.log(jnp.sum(totals * jnp.exp(tops - top_all), axis=0))
    entry = lax.broadcasted_iota(jnp.int32, logits.shape, 1) + half * block
    onehot = (targets[:, None] == entry).astype(F32)
    loss_weight = 2.0 * entries / frames
    d_logit = ((jnp.exp(logits - lse[:, None]) - onehot) * loss_weight).astype(BF16)

    away = [
        matmul(d_logit[k * owned : (k + 1) * owned], head, ((1,), (1,))).astype(BF16)
        for k in range(1, halves)
    ]
    received = [turn_hid(a, k + 1) for k, a in enumerate(away)]
    d_norm = matmul(after(d_logit[:owned], *away), head, ((1,), (1,)))
    for r in received:
        d_norm += r.astype(F32)
    gated = gain * d_norm
    back_scale = scale**3 * jnp.mean(gated * x_rows, axis=1, keepdims=True)
    gated_proj = jnp.sum(gated * proj, axis=1, keepdims=True)
    d_round = (scale * gated - x_rows * back_scale).astype(BF16)
    d_ratio_part = (scale * gated_proj - back_scale * x_proj).reshape(steps, part)

    part_out = matmul(normed_rows, after(d_logit, *away), ((0,), (0,))).astype(BF16)
    part_out = part_out.reshape(seqs, depth // seqs, block)
    part_out = lax.all_to_all(part_out, "seq", 0, 0)
    part_out = part_out.reshape(groups, steps, hids, head_rows, block).astype(F32).sum(0)
    part_out = part_out.astype(BF16)
    sums = [
        lax.dynamic_index_in_dim(part_out, (j + shift) % hids, 1, False) for shift in range(hids)
    ]
    sums = [along_hid(p, shift) if shift else p for shift, p in enumerate(sums)]
    grad_out = head_gradient(place, sums, halves)

    pieces = [d_round] + [along_hid(d_round, shift) for shift in range(1, hids)]
    ratio_rows = ratio_group.reshape(steps, rows, 1)
    d_ratio_part = after(d_ratio_part, *pieces[1:])
    d_ratio = d_ratio_part[0]
    for m in relations:
        d_ratio += flip_seq(d_ratio_part[m], m)
    d_rows = jnp.broadcast_to(d_ratio, (hids, part))
    for shift in range(1, hids):
        d_rows = lax.dynamic_update_index_in_dim(
            d_rows, along_hid(d_ratio, shift), (j - shift) % hids, 0
        )
    share, mine, *others = input_gradient(place, pieces, group, ratio_rows, seqs)
    share = lax.all_to_all(share.reshape(seqs, depth // seqs, units), "seq", 0, 0)
    share = share.reshape(groups, steps, depth // seqs, units).astype(F32).sum(0)
    grad_in = share.transpose(0, 2, 1)

    ratio_own = ratio_group[0].reshape(rows)
    correction = ratio_own**3 * d_rows.reshape(rows) / width_in
    factors = jnp.stack([ratio_own, correction])[:, :, None]
    mine = [mine] + [flip_seq(others[m - 1], m) for m in relations]
    grad_hidden = hidden_gradient(place, mine, w_in, hidden, factors)
    return (grad_hidden, grad_in, grad_out)


def solution(mesh):
    placed = (
        P("seq", "hid"),
        P(None, "hid", None),
        P(),
        P(),
        P(("seq", "hid"), None, None),
        P(None, ("seq", "hid")),
    )
    return jax.shard_map(
        shards,
        mesh=mesh,
        in_specs=placed,
        out_specs=(P("seq", "hid"), P(None, "hid", "seq"), P(("seq", "hid"), None, None)),
        check_vma=False,
    )
```

```python
import jax
import jax.numpy as jnp
from jax import lax
from jax.experimental import pallas as pl
from jax.experimental.pallas import tpu as pltpu
from jax.sharding import PartitionSpec as P

F32 = jnp.float32
BF16 = jnp.bfloat16


def pick(values, index):
    return lax.dynamic_index_in_dim(values, index, axis=0, keepdims=False)


def matmul(a, b, contract):
    return lax.dot_general(a, b, (contract, ((), ())), preferred_element_type=F32)


def after(value, *others):
    return lax.optimization_barrier((value, *others))[0]


VMEM = pltpu.CompilerParams(vmem_limit_bytes=60 * 2**20)


def whole(shape):
    return pl.BlockSpec(shape, lambda n, place: (0,) * len(shape))


def call(kernel, place, grid, in_specs, out_specs, out_shape, scratch, flops, args):
    moved = sum(a.size * a.dtype.itemsize for a in args)
    return pl.pallas_call(
        kernel,
        grid_spec=pltpu.PrefetchScalarGridSpec(
            num_scalar_prefetch=1,
            grid=(grid,),
            in_specs=in_specs,
            out_specs=out_specs,
            scratch_shapes=scratch,
        ),
        out_shape=out_shape,
        compiler_params=VMEM,
        cost_estimate=pl.CostEstimate(flops=flops, bytes_accessed=moved, transcendentals=0),
    )(place, *args)


EXACT = 3


def parts_of(values):
    out = []
    for _ in range(EXACT):
        piece = lax.reduce_precision(values, 8, 7)
        values = values - piece
        out.append(piece.astype(BF16))
    return out


def head_gradient(place, pieces, halves):
    hids = len(pieces)
    steps, rows, block = pieces[0].shape

    def kernel(place_ref, *refs):
        pieces, out = refs[:-1], refs[-1]
        for r in range(halves):
            which = lax.rem(place_ref[1] - r + hids, halves)
            columns = pl.ds(pl.multiple_of(which * block, block), block)
            for s in range(steps):
                total = pieces[r][s].astype(F32)
                for k in range(r + halves, hids, halves):
                    total = total + pieces[k][s].astype(F32)
                out[:, s, columns] = total

    return call(
        kernel,
        place,
        1,
        [whole((steps, rows, block))] * hids,
        whole((rows, steps, halves * block)),
        jax.ShapeDtypeStruct((rows, steps, halves * block), F32),
        [],
        hids * steps * rows * block,
        tuple(pieces),
    )


def input_gradient(place, pieces, group, ratio, seqs):
    hids, steps = len(pieces), len(group)
    owned, depth = pieces[0].shape
    rows, units = group[0].shape
    part = owned // steps
    wide = min(512, depth)

    def kernel(place_ref, *refs):
        chunks, group, ratio = refs[:hids], refs[hids : hids + steps], refs[hids + steps]
        out, plain, scaled = refs[hids + steps + 1], refs[hids + steps + 2 : -1], refs[-1]
        j = place_ref[1]
        for r in range(hids):
            to = pl.multiple_of(lax.rem(j - r + hids, hids) * part, part)
            for m in range(steps):
                values = chunks[r][m * part : (m + 1) * part, :]
                plain[m][pl.ds(to, part), :] = values
                factor = ratio[m, pl.ds(to, part), :]
                scaled[m, pl.ds(to, part), :] = (values.astype(F32) * factor).astype(BF16)
        total = None
        for m in range(steps):
            term = lax.dot_general(
                scaled[m], group[m][...], (((0,), (0,)), ((), ())), preferred_element_type=F32
            )
            total = term if total is None else total + term
        out[...] = total.astype(BF16)

    return call(
        kernel,
        place,
        depth // wide,
        [pl.BlockSpec((owned, wide), lambda n, place: (0, n))] * hids
        + [whole((rows, units))] * steps
        + [whole((steps, rows, 1))],
        [pl.BlockSpec((wide, units), lambda n, place: (n, 0))]
        + [pl.BlockSpec((rows, wide), lambda n, place: (0, n))] * steps,
        [jax.ShapeDtypeStruct((depth, units), BF16)]
        + [jax.ShapeDtypeStruct((rows, depth), BF16)] * steps,
        [pltpu.VMEM((steps, rows, wide), BF16)],
        2 * steps * rows * units * depth,
        (*pieces, *group, ratio),
    )


def hidden_gradient(place, d_rows, w_in, hidden, factors):
    steps, units, depth = w_in.shape
    rows = hidden.shape[0]
    wide = min(512, units)

    def kernel(place_ref, *refs):
        d_rows, w, hidden, factors, out = refs[:steps], refs[-4], refs[-3], refs[-2], refs[-1]
        total = None
        for r in range(steps):
            which = lax.rem(place_ref[0] - r + steps, steps)
            term = lax.dot_general(
                d_rows[r][...], w[which], (((1,), (1,)), ((), ())), preferred_element_type=F32
            )
            total = term if total is None else total + term
        out[...] = (factors[0] * total - factors[1] * hidden[...].astype(F32)).astype(BF16)

    return call(
        kernel,
        place,
        units // wide,
        [whole((rows, depth))] * steps
        + [
            pl.BlockSpec((steps, wide, depth), lambda n, place: (0, n, 0)),
            pl.BlockSpec((rows, wide), lambda n, place: (0, n)),
            whole((2, rows, 1)),
        ],
        pl.BlockSpec((rows, wide), lambda n, place: (0, n)),
        jax.ShapeDtypeStruct((rows, units), BF16),
        [],
        2 * steps * rows * units * depth,
        (*d_rows, w_in, hidden, factors),
    )


def shards(hidden, w_in, embedding, depth_gain, w_out, codebook_ids):
    hids = lax.axis_size("hid")
    seqs = lax.axis_size("seq")
    steps, units, depth = w_in.shape
    entries = w_out.shape[2]
    rows = hidden.shape[0]
    part = rows // hids
    width_in = units * hids
    frames = rows * seqs
    halves = 2 if hids % 2 == 0 else 1
    block = entries // halves
    head_rows = w_out.shape[0]
    groups = seqs // steps
    i = lax.axis_index("seq")
    j = lax.axis_index("hid")
    step = i % steps
    half = j % halves
    owned = steps * part

    def along_hid(values, shift):
        return lax.ppermute(values, "hid", [(a, (a + shift) % hids) for a in range(hids)])

    def turn_hid(values, shift):
        return lax.ppermute(
            values,
            "hid",
            [(a, a - a % halves + (a % halves + shift) % halves) for a in range(hids)],
        )

    def flip_seq(values, flip):
        return lax.ppermute(
            values,
            "seq",
            [(a, a - a % steps + (a % steps + flip) % steps) for a in range(seqs)],
        )

    place = jnp.stack([step, j]).astype(jnp.int32)
    relations = range(1, steps)

    group = [hidden] + [flip_seq(hidden, -m) for m in relations]

    squares_part = jnp.sum(jnp.square(hidden.astype(F32)), axis=1)
    tail = 8 * block
    small = jnp.concatenate(parts_of(squares_part))
    small = jnp.pad(small, (0, tail - small.size)).reshape(8, block)
    head_parts = w_out.reshape(head_rows, steps, halves, block)
    head_send = []
    for k in range(halves):
        piece = lax.dynamic_index_in_dim(head_parts, (half + k) % halves, 2, False)
        piece = piece.transpose(1, 0, 2).reshape(steps * head_rows, block)
        head_send.append(jnp.concatenate([piece, small]))
    head_got = [head_send[0]]
    head_got += [along_hid(head_send[shift % halves], shift) for shift in range(1, hids)]
    w_own = pick(w_in, step)
    proj_parts = matmul(jnp.concatenate(group), w_own, ((1,), (0,)))
    proj_parts = proj_parts.reshape(steps, hids, part, depth)

    def owner_block(index):
        return lax.dynamic_index_in_dim(proj_parts, index, 1, False).reshape(owned, depth)

    send = [owner_block((j + shift) % hids).astype(BF16) for shift in range(1, hids)]
    ready = [after(p, *head_got[1:]) for p in send]
    received = [along_hid(ready[shift - 1], shift) for shift in range(1, hids)]

    head_got = [head_got[0]] + [after(g, *send) for g in head_got[1:]]
    squares = sum(g[steps * head_rows :].astype(F32) for g in head_got).reshape(tail)
    squares = jnp.sum(squares[: EXACT * rows].reshape(EXACT, rows), axis=0)
    head_mid = jnp.stack([g[: steps * head_rows] for g in head_got[::-1]] * 2)
    head_mid = lax.dynamic_slice_in_dim(head_mid, hids - 1 - j, hids, 0)
    head_mid = head_mid.reshape(hids, steps, head_rows, block)

    ids = after(codebook_ids, *send)
    ids = jnp.concatenate([ids] + [flip_seq(ids, -m) for m in relations], axis=1)
    ids_rows = [ids] + [turn_hid(ids, -k) for k in range(1, halves)]
    before = jnp.maximum(step - 1, 0)
    looked = jnp.take(pick(embedding, before), pick(ids, before), axis=0)

    head_send = head_mid.transpose(1, 0, 2, 3)
    head_send = head_send.reshape(steps, hids * head_rows, block)
    head_send = jnp.broadcast_to(head_send, (groups,) + head_send.shape)
    head_send = head_send.reshape(seqs, hids * head_rows, block)
    head = lax.all_to_all(head_send, "seq", 0, 0).reshape(depth, block)

    squares = jnp.stack([squares] + [flip_seq(squares, -m) for m in relations])
    ratio_group = lax.rsqrt(squares / width_in + 1e-06).reshape(steps, hids, part)

    ratio = lax.dynamic_index_in_dim(ratio_group, j, 1, False).reshape(owned, 1)
    proj = owner_block(j)
    for r in received:
        proj += r.astype(F32)
    x_rows = ratio * proj + jnp.where(step > 0, looked.astype(F32), 0.0)
    scale = lax.rsqrt(jnp.mean(x_rows * x_rows, axis=1, keepdims=True) + 1e-06)
    x_proj = jnp.sum(x_rows * proj, axis=1, keepdims=True)
    gain = pick(depth_gain, step)[None, :]
    normed = (x_rows * scale * gain).astype(BF16)

    normed_rows = jnp.concatenate([normed] + [turn_hid(normed, -k) for k in range(1, halves)])
    targets = jnp.concatenate([pick(r, step) for r in ids_rows])
    logits = matmul(normed_rows, head, ((1,), (0,)))
    top = jnp.max(logits, axis=1)
    total = jnp.sum(jnp.exp(logits - top[:, None]), axis=1)
    stats = jnp.stack([top, total]).reshape(2, halves, -1)
    every = [stats] + [jnp.roll(turn_hid(stats, -t), t, axis=1) for t in range(1, halves)]
    tops = jnp.stack([e[0] for e in every]).reshape(halves, -1)
    totals = jnp.stack([e[1] for e in every]).reshape(halves, -1)
    top_all = jnp.max(tops, axis=0)
    lse = top_all + jnp.log(jnp.sum(totals * jnp.exp(tops - top_all), axis=0))
    entry = lax.broadcasted_iota(jnp.int32, logits.shape, 1) + half * block
    onehot = (targets[:, None] == entry).astype(F32)
    loss_weight = 2.0 * entries / frames
    d_logit = ((jnp.exp(logits - lse[:, None]) - onehot) * loss_weight).astype(BF16)

    away = [
        matmul(d_logit[k * owned : (k + 1) * owned], head, ((1,), (1,))).astype(BF16)
        for k in range(1, halves)
    ]
    received = [turn_hid(a, k + 1) for k, a in enumerate(away)]
    d_norm = matmul(after(d_logit[:owned], *away), head, ((1,), (1,)))
    for r in received:
        d_norm += r.astype(F32)
    gated = gain * d_norm
    back_scale = scale**3 * jnp.mean(gated * x_rows, axis=1, keepdims=True)
    gated_proj = jnp.sum(gated * proj, axis=1, keepdims=True)
    d_round = (scale * gated - x_rows * back_scale).astype(BF16)
    d_ratio_part = (scale * gated_proj - back_scale * x_proj).reshape(steps, part)

    part_out = matmul(normed_rows, after(d_logit, *away), ((0,), (0,))).astype(BF16)
    part_out = after(part_out, *received).reshape(seqs, depth // seqs, block)
    part_out = lax.all_to_all(part_out, "seq", 0, 0)
    part_out = part_out.reshape(groups, steps, hids, head_rows, block).astype(F32).sum(0)
    part_out = part_out.astype(BF16)
    sums = [
        lax.dynamic_index_in_dim(part_out, (j + shift) % hids, 1, False) for shift in range(hids)
    ]
    cut = sums
    sums = [along_hid(p, shift) if shift else p for shift, p in enumerate(sums)]
    grad_out = head_gradient(place, sums, halves)

    pieces = [d_round] + [along_hid(d_round, shift) for shift in range(1, hids)]
    ratio_rows = ratio_group.reshape(steps, rows, 1)
    share, mine, *others = input_gradient(place, pieces, group, ratio_rows, seqs)
    share = lax.all_to_all(share.reshape(seqs, depth // seqs, units), "seq", 0, 0)
    share = share.reshape(groups, steps, depth // seqs, units).astype(F32).sum(0)
    grad_in = share.transpose(0, 2, 1)

    d_ratio_part = after(d_ratio_part, *cut)
    d_ratio = d_ratio_part[0]
    for m in relations:
        d_ratio += flip_seq(d_ratio_part[m], m)
    d_rows = jnp.broadcast_to(d_ratio, (hids, part))
    for shift in range(1, hids):
        d_rows = lax.dynamic_update_index_in_dim(
            d_rows, along_hid(d_ratio, shift), (j - shift) % hids, 0
        )
    ratio_own = ratio_group[0].reshape(rows)
    correction = ratio_own**3 * d_rows.reshape(rows) / width_in
    factors = jnp.stack([ratio_own, correction])[:, :, None]
    mine = [mine] + [flip_seq(others[m - 1], m) for m in relations]
    grad_hidden = hidden_gradient(place, mine, w_in, hidden, factors)
    return (grad_hidden, grad_in, grad_out)


def solution(mesh):
    placed = (
        P("seq", "hid"),
        P(None, "hid", None),
        P(),
        P(),
        P(("seq", "hid"), None, None),
        P(None, ("seq", "hid")),
    )
    return jax.shard_map(
        shards,
        mesh=mesh,
        in_specs=placed,
        out_specs=(P("seq", "hid"), P(None, "hid", "seq"), P(("seq", "hid"), None, None)),
        check_vma=False,
    )
```

```python
import jax
import jax.numpy as jnp
from jax import lax
from jax.experimental import pallas as pl
from jax.experimental.pallas import tpu as pltpu
from jax.sharding import PartitionSpec as P

F32 = jnp.float32
BF16 = jnp.bfloat16


def pick(values, index):
    return lax.dynamic_index_in_dim(values, index, axis=0, keepdims=False)


def matmul(a, b, contract):
    return lax.dot_general(a, b, (contract, ((), ())), preferred_element_type=F32)


def after(value, *others):
    return lax.optimization_barrier((value, *others))[0]


VMEM = pltpu.CompilerParams(vmem_limit_bytes=60 * 2**20)


def whole(shape):
    return pl.BlockSpec(shape, lambda n, place: (0,) * len(shape))


def call(kernel, place, grid, in_specs, out_specs, out_shape, scratch, flops, args):
    moved = sum(a.size * a.dtype.itemsize for a in args)
    return pl.pallas_call(
        kernel,
        grid_spec=pltpu.PrefetchScalarGridSpec(
            num_scalar_prefetch=1,
            grid=(grid,),
            in_specs=in_specs,
            out_specs=out_specs,
            scratch_shapes=scratch,
        ),
        out_shape=out_shape,
        compiler_params=VMEM,
        cost_estimate=pl.CostEstimate(flops=flops, bytes_accessed=moved, transcendentals=0),
    )(place, *args)


EXACT = 3


def parts_of(values):
    out = []
    for _ in range(EXACT):
        piece = lax.reduce_precision(values, 8, 7)
        values = values - piece
        out.append(piece.astype(BF16))
    return out


def head_gradient(place, pieces, halves):
    hids = len(pieces)
    steps, rows, block = pieces[0].shape

    def kernel(place_ref, *refs):
        pieces, out = refs[:-1], refs[-1]
        for r in range(halves):
            which = lax.rem(place_ref[1] - r + hids, halves)
            columns = pl.ds(pl.multiple_of(which * block, block), block)
            for s in range(steps):
                total = pieces[r][s].astype(F32)
                for k in range(r + halves, hids, halves):
                    total = total + pieces[k][s].astype(F32)
                out[:, s, columns] = total

    return call(
        kernel,
        place,
        1,
        [whole((steps, rows, block))] * hids,
        whole((rows, steps, halves * block)),
        jax.ShapeDtypeStruct((rows, steps, halves * block), F32),
        [],
        hids * steps * rows * block,
        tuple(pieces),
    )


def input_gradient(place, pieces, group, ratio, seqs):
    hids, steps = len(pieces), len(group)
    owned, depth = pieces[0].shape
    rows, units = group[0].shape
    part = owned // steps
    wide = min(512, depth)

    def kernel(place_ref, *refs):
        chunks, group, ratio = refs[:hids], refs[hids : hids + steps], refs[hids + steps]
        out, plain, scaled = refs[hids + steps + 1], refs[hids + steps + 2 : -1], refs[-1]
        j = place_ref[1]
        for r in range(hids):
            to = pl.multiple_of(lax.rem(j - r + hids, hids) * part, part)
            for m in range(steps):
                values = chunks[r][m * part : (m + 1) * part, :]
                plain[m][pl.ds(to, part), :] = values
                factor = ratio[m, pl.ds(to, part), :]
                scaled[m, pl.ds(to, part), :] = (values.astype(F32) * factor).astype(BF16)
        total = None
        for m in range(steps):
            term = lax.dot_general(
                scaled[m], group[m][...], (((0,), (0,)), ((), ())), preferred_element_type=F32
            )
            total = term if total is None else total + term
        out[...] = total.astype(BF16)

    return call(
        kernel,
        place,
        depth // wide,
        [pl.BlockSpec((owned, wide), lambda n, place: (0, n))] * hids
        + [whole((rows, units))] * steps
        + [whole((steps, rows, 1))],
        [pl.BlockSpec((wide, units), lambda n, place: (n, 0))]
        + [pl.BlockSpec((rows, wide), lambda n, place: (0, n))] * steps,
        [jax.ShapeDtypeStruct((depth, units), BF16)]
        + [jax.ShapeDtypeStruct((rows, depth), BF16)] * steps,
        [pltpu.VMEM((steps, rows, wide), BF16)],
        2 * steps * rows * units * depth,
        (*pieces, *group, ratio),
    )


def hidden_gradient(place, d_rows, w_in, hidden, factors):
    steps, units, depth = w_in.shape
    rows = hidden.shape[0]
    wide = min(512, units)

    def kernel(place_ref, *refs):
        d_rows, w, hidden, factors, out = refs[:steps], refs[-4], refs[-3], refs[-2], refs[-1]
        total = None
        for r in range(steps):
            which = lax.rem(place_ref[0] - r + steps, steps)
            term = lax.dot_general(
                d_rows[r][...], w[which], (((1,), (1,)), ((), ())), preferred_element_type=F32
            )
            total = term if total is None else total + term
        out[...] = (factors[0] * total - factors[1] * hidden[...].astype(F32)).astype(BF16)

    return call(
        kernel,
        place,
        units // wide,
        [whole((rows, depth))] * steps
        + [
            pl.BlockSpec((steps, wide, depth), lambda n, place: (0, n, 0)),
            pl.BlockSpec((rows, wide), lambda n, place: (0, n)),
            whole((2, rows, 1)),
        ],
        pl.BlockSpec((rows, wide), lambda n, place: (0, n)),
        jax.ShapeDtypeStruct((rows, units), BF16),
        [],
        2 * steps * rows * units * depth,
        (*d_rows, w_in, hidden, factors),
    )


def shards(hidden, w_in, embedding, depth_gain, w_out, codebook_ids):
    hids = lax.axis_size("hid")
    seqs = lax.axis_size("seq")
    steps, units, depth = w_in.shape
    entries = w_out.shape[2]
    rows = hidden.shape[0]
    part = rows // hids
    width_in = units * hids
    frames = rows * seqs
    halves = 2 if hids % 2 == 0 else 1
    block = entries // halves
    head_rows = w_out.shape[0]
    groups = seqs // steps
    i = lax.axis_index("seq")
    j = lax.axis_index("hid")
    step = i % steps
    half = j % halves
    owned = steps * part

    def along_hid(values, shift):
        return lax.ppermute(values, "hid", [(a, (a + shift) % hids) for a in range(hids)])

    def turn_hid(values, shift):
        return lax.ppermute(
            values,
            "hid",
            [(a, a - a % halves + (a % halves + shift) % halves) for a in range(hids)],
        )

    def flip_seq(values, flip):
        return lax.ppermute(
            values,
            "seq",
            [(a, a - a % steps + (a % steps + flip) % steps) for a in range(seqs)],
        )

    place = jnp.stack([step, j]).astype(jnp.int32)
    relations = range(1, steps)

    group = [hidden] + [flip_seq(hidden, -m) for m in relations]

    squares_part = jnp.sum(jnp.square(hidden.astype(F32)), axis=1)
    tail = 8 * block
    small = jnp.concatenate(parts_of(squares_part))
    small = jnp.pad(small, (0, tail - small.size)).reshape(8, block)
    head_parts = w_out.reshape(head_rows, steps, halves, block)
    head_send = []
    for k in range(halves):
        piece = lax.dynamic_index_in_dim(head_parts, (half + k) % halves, 2, False)
        piece = piece.transpose(1, 0, 2).reshape(steps * head_rows, block)
        head_send.append(jnp.concatenate([piece, small]))
    head_got = [head_send[0]]
    head_got += [along_hid(head_send[shift % halves], shift) for shift in range(1, hids)]
    w_own = pick(w_in, step)
    proj_parts = matmul(jnp.concatenate(group), w_own, ((1,), (0,)))
    proj_parts = proj_parts.reshape(steps, hids, part, depth)

    def owner_block(index):
        return lax.dynamic_index_in_dim(proj_parts, index, 1, False).reshape(owned, depth)

    send = [owner_block((j + shift) % hids).astype(BF16) for shift in range(1, hids)]
    ready = [after(p, *head_got[1:]) for p in send]
    received = [along_hid(ready[shift - 1], shift) for shift in range(1, hids)]

    head_got = [head_got[0]] + [after(g, *send) for g in head_got[1:]]
    squares = sum(g[steps * head_rows :].astype(F32) for g in head_got).reshape(tail)
    squares = jnp.sum(squares[: EXACT * rows].reshape(EXACT, rows), axis=0)
    head_mid = jnp.stack([g[: steps * head_rows] for g in head_got[::-1]] * 2)
    head_mid = lax.dynamic_slice_in_dim(head_mid, hids - 1 - j, hids, 0)
    head_mid = head_mid.reshape(hids, steps, head_rows, block)

    ids = after(codebook_ids, *send)
    ids = jnp.concatenate([ids] + [flip_seq(ids, -m) for m in relations], axis=1)
    ids_rows = [ids] + [turn_hid(ids, -k) for k in range(1, halves)]
    before = jnp.maximum(step - 1, 0)
    looked = jnp.take(pick(embedding, before), pick(ids, before), axis=0)

    head_send = head_mid.transpose(1, 0, 2, 3)
    head_send = head_send.reshape(steps, hids * head_rows, block)
    head_send = jnp.broadcast_to(head_send, (groups,) + head_send.shape)
    head_send = head_send.reshape(seqs, hids * head_rows, block)
    head = lax.all_to_all(head_send, "seq", 0, 0).reshape(depth, block)

    squares = jnp.stack([squares] + [flip_seq(squares, -m) for m in relations])
    ratio_group = lax.rsqrt(squares / width_in + 1e-06).reshape(steps, hids, part)

    ratio = lax.dynamic_index_in_dim(ratio_group, j, 1, False).reshape(owned, 1)
    proj = owner_block(j)
    for r in received:
        proj += r.astype(F32)
    x_rows = ratio * proj + jnp.where(step > 0, looked.astype(F32), 0.0)
    scale = lax.rsqrt(jnp.mean(x_rows * x_rows, axis=1, keepdims=True) + 1e-06)
    x_proj = jnp.sum(x_rows * proj, axis=1, keepdims=True)
    gain = pick(depth_gain, step)[None, :]
    normed = (x_rows * scale * gain).astype(BF16)

    normed_rows = jnp.concatenate([normed] + [turn_hid(normed, -k) for k in range(1, halves)])
    targets = jnp.concatenate([pick(r, step) for r in ids_rows])
    logits = matmul(normed_rows, head, ((1,), (0,)))
    top = jnp.max(logits, axis=1)
    total = jnp.sum(jnp.exp(logits - top[:, None]), axis=1)
    stats = jnp.stack([top, total]).reshape(2, halves, -1)
    every = [stats] + [jnp.roll(turn_hid(stats, -t), t, axis=1) for t in range(1, halves)]
    tops = jnp.stack([e[0] for e in every]).reshape(halves, -1)
    totals = jnp.stack([e[1] for e in every]).reshape(halves, -1)
    top_all = jnp.max(tops, axis=0)
    lse = top_all + jnp.log(jnp.sum(totals * jnp.exp(tops - top_all), axis=0))
    entry = lax.broadcasted_iota(jnp.int32, logits.shape, 1) + half * block
    onehot = (targets[:, None] == entry).astype(F32)
    loss_weight = 2.0 * entries / frames
    d_logit = ((jnp.exp(logits - lse[:, None]) - onehot) * loss_weight).astype(BF16)

    away = [
        matmul(d_logit[k * owned : (k + 1) * owned], head, ((1,), (1,))).astype(BF16)
        for k in range(1, halves)
    ]
    received = [turn_hid(a, k + 1) for k, a in enumerate(away)]
    d_norm = matmul(after(d_logit[:owned], *away), head, ((1,), (1,)))
    for r in received:
        d_norm += r.astype(F32)
    gated = gain * d_norm
    back_scale = scale**3 * jnp.mean(gated * x_rows, axis=1, keepdims=True)
    gated_proj = jnp.sum(gated * proj, axis=1, keepdims=True)
    d_round = (scale * gated - x_rows * back_scale).astype(BF16)
    d_ratio_part = (scale * gated_proj - back_scale * x_proj).reshape(steps, part)

    part_out = matmul(normed_rows, after(d_logit, *away), ((0,), (0,))).astype(BF16)
    part_out = part_out.reshape(seqs, depth // seqs, block)
    part_out = lax.all_to_all(part_out, "seq", 0, 0)
    part_out = part_out.reshape(groups, steps, hids, head_rows, block).astype(F32).sum(0)
    part_out = part_out.astype(BF16)
    sums = [
        lax.dynamic_index_in_dim(part_out, (j + shift) % hids, 1, False) for shift in range(hids)
    ]
    sums = [along_hid(p, shift) if shift else p for shift, p in enumerate(sums)]
    grad_out = head_gradient(place, sums, halves)

    pieces = [d_round] + [along_hid(d_round, shift) for shift in range(1, hids)]
    ratio_rows = ratio_group.reshape(steps, rows, 1)
    d_ratio_part = after(d_ratio_part, d_round)
    d_ratio = d_ratio_part[0]
    for m in relations:
        d_ratio += flip_seq(d_ratio_part[m], m)
    d_rows = jnp.broadcast_to(d_ratio, (hids, part))
    for shift in range(1, hids):
        d_rows = lax.dynamic_update_index_in_dim(
            d_rows, along_hid(d_ratio, shift), (j - shift) % hids, 0
        )
    share, mine, *others = input_gradient(after(place, d_ratio), pieces, group, ratio_rows, seqs)
    share = lax.all_to_all(share.reshape(seqs, depth // seqs, units), "seq", 0, 0)
    share = share.reshape(groups, steps, depth // seqs, units).astype(F32).sum(0)
    grad_in = share.transpose(0, 2, 1)

    ratio_own = ratio_group[0].reshape(rows)
    correction = ratio_own**3 * d_rows.reshape(rows) / width_in
    factors = jnp.stack([ratio_own, correction])[:, :, None]
    mine = [mine] + [flip_seq(others[m - 1], m) for m in relations]
    grad_hidden = hidden_gradient(place, mine, w_in, hidden, factors)
    return (grad_hidden, grad_in, grad_out)


def solution(mesh):
    placed = (
        P("seq", "hid"),
        P(None, "hid", None),
        P(),
        P(),
        P(("seq", "hid"), None, None),
        P(None, ("seq", "hid")),
    )
    return jax.shard_map(
        shards,
        mesh=mesh,
        in_specs=placed,
        out_specs=(P("seq", "hid"), P(None, "hid", "seq"), P(("seq", "hid"), None, None)),
        check_vma=False,
    )
```

```python
import jax
import jax.numpy as jnp
from jax import lax
from jax.experimental import pallas as pl
from jax.experimental.pallas import tpu as pltpu
from jax.sharding import PartitionSpec as P

F32 = jnp.float32
BF16 = jnp.bfloat16


def pick(values, index):
    return lax.dynamic_index_in_dim(values, index, axis=0, keepdims=False)


def matmul(a, b, contract):
    return lax.dot_general(a, b, (contract, ((), ())), preferred_element_type=F32)


def after(value, *others):
    return lax.optimization_barrier((value, *others))[0]


VMEM = pltpu.CompilerParams(vmem_limit_bytes=60 * 2**20)


def whole(shape):
    return pl.BlockSpec(shape, lambda n, place: (0,) * len(shape))


def call(kernel, place, grid, in_specs, out_specs, out_shape, scratch, flops, args):
    moved = sum(a.size * a.dtype.itemsize for a in args)
    return pl.pallas_call(
        kernel,
        grid_spec=pltpu.PrefetchScalarGridSpec(
            num_scalar_prefetch=1,
            grid=(grid,),
            in_specs=in_specs,
            out_specs=out_specs,
            scratch_shapes=scratch,
        ),
        out_shape=out_shape,
        compiler_params=VMEM,
        cost_estimate=pl.CostEstimate(flops=flops, bytes_accessed=moved, transcendentals=0),
    )(place, *args)


EXACT = 3


def parts_of(values):
    out = []
    for _ in range(EXACT):
        piece = lax.reduce_precision(values, 8, 7)
        values = values - piece
        out.append(piece.astype(BF16))
    return out


def head_gradient(place, pieces, halves):
    hids = len(pieces)
    steps, rows, block = pieces[0].shape

    def kernel(place_ref, *refs):
        pieces, out = refs[:-1], refs[-1]
        for r in range(halves):
            which = lax.rem(place_ref[1] - r + hids, halves)
            columns = pl.ds(pl.multiple_of(which * block, block), block)
            for s in range(steps):
                total = pieces[r][s].astype(F32)
                for k in range(r + halves, hids, halves):
                    total = total + pieces[k][s].astype(F32)
                out[:, s, columns] = total

    return call(
        kernel,
        place,
        1,
        [whole((steps, rows, block))] * hids,
        whole((rows, steps, halves * block)),
        jax.ShapeDtypeStruct((rows, steps, halves * block), F32),
        [],
        hids * steps * rows * block,
        tuple(pieces),
    )


def input_gradient(place, pieces, group, ratio, seqs):
    hids, steps = len(pieces), len(group)
    owned, depth = pieces[0].shape
    rows, units = group[0].shape
    part = owned // steps
    wide = depth

    def kernel(place_ref, *refs):
        chunks, group, ratio = refs[:hids], refs[hids : hids + steps], refs[hids + steps]
        out, plain, scaled = refs[hids + steps + 1], refs[hids + steps + 2 : -1], refs[-1]
        j = place_ref[1]
        for r in range(hids):
            to = pl.multiple_of(lax.rem(j - r + hids, hids) * part, part)
            for m in range(steps):
                values = chunks[r][m * part : (m + 1) * part, :]
                plain[m][pl.ds(to, part), :] = values
                factor = ratio[m, pl.ds(to, part), :]
                scaled[m, pl.ds(to, part), :] = (values.astype(F32) * factor).astype(BF16)
        total = None
        for m in range(steps):
            term = lax.dot_general(
                scaled[m], group[m][...], (((0,), (0,)), ((), ())), preferred_element_type=F32
            )
            total = term if total is None else total + term
        out[...] = total.astype(BF16)

    return call(
        kernel,
        place,
        depth // wide,
        [pl.BlockSpec((owned, wide), lambda n, place: (0, n))] * hids
        + [whole((rows, units))] * steps
        + [whole((steps, rows, 1))],
        [pl.BlockSpec((wide, units), lambda n, place: (n, 0))]
        + [pl.BlockSpec((rows, wide), lambda n, place: (0, n))] * steps,
        [jax.ShapeDtypeStruct((depth, units), BF16)]
        + [jax.ShapeDtypeStruct((rows, depth), BF16)] * steps,
        [pltpu.VMEM((steps, rows, wide), BF16)],
        2 * steps * rows * units * depth,
        (*pieces, *group, ratio),
    )


def hidden_gradient(place, d_rows, w_in, hidden, factors):
    steps, units, depth = w_in.shape
    rows = hidden.shape[0]
    wide = min(512, units)

    def kernel(place_ref, *refs):
        d_rows, w, hidden, factors, out = refs[:steps], refs[-4], refs[-3], refs[-2], refs[-1]
        total = None
        for r in range(steps):
            which = lax.rem(place_ref[0] - r + steps, steps)
            term = lax.dot_general(
                d_rows[r][...], w[which], (((1,), (1,)), ((), ())), preferred_element_type=F32
            )
            total = term if total is None else total + term
        out[...] = (factors[0] * total - factors[1] * hidden[...].astype(F32)).astype(BF16)

    return call(
        kernel,
        place,
        units // wide,
        [whole((rows, depth))] * steps
        + [
            pl.BlockSpec((steps, wide, depth), lambda n, place: (0, n, 0)),
            pl.BlockSpec((rows, wide), lambda n, place: (0, n)),
            whole((2, rows, 1)),
        ],
        pl.BlockSpec((rows, wide), lambda n, place: (0, n)),
        jax.ShapeDtypeStruct((rows, units), BF16),
        [],
        2 * steps * rows * units * depth,
        (*d_rows, w_in, hidden, factors),
    )


def shards(hidden, w_in, embedding, depth_gain, w_out, codebook_ids):
    hids = lax.axis_size("hid")
    seqs = lax.axis_size("seq")
    steps, units, depth = w_in.shape
    entries = w_out.shape[2]
    rows = hidden.shape[0]
    part = rows // hids
    width_in = units * hids
    frames = rows * seqs
    halves = 2 if hids % 2 == 0 else 1
    block = entries // halves
    head_rows = w_out.shape[0]
    groups = seqs // steps
    i = lax.axis_index("seq")
    j = lax.axis_index("hid")
    step = i % steps
    half = j % halves
    owned = steps * part

    def along_hid(values, shift):
        return lax.ppermute(values, "hid", [(a, (a + shift) % hids) for a in range(hids)])

    def turn_hid(values, shift):
        return lax.ppermute(
            values,
            "hid",
            [(a, a - a % halves + (a % halves + shift) % halves) for a in range(hids)],
        )

    def flip_seq(values, flip):
        return lax.ppermute(
            values,
            "seq",
            [(a, a - a % steps + (a % steps + flip) % steps) for a in range(seqs)],
        )

    place = jnp.stack([step, j]).astype(jnp.int32)
    relations = range(1, steps)

    group = [hidden] + [flip_seq(hidden, -m) for m in relations]

    squares_part = jnp.sum(jnp.square(hidden.astype(F32)), axis=1)
    tail = 8 * block
    small = jnp.concatenate(parts_of(squares_part))
    small = jnp.pad(small, (0, tail - small.size)).reshape(8, block)
    head_parts = w_out.reshape(head_rows, steps, halves, block)
    head_send = []
    for k in range(halves):
        piece = lax.dynamic_index_in_dim(head_parts, (half + k) % halves, 2, False)
        piece = piece.transpose(1, 0, 2).reshape(steps * head_rows, block)
        head_send.append(jnp.concatenate([piece, small]))
    head_got = [head_send[0]]
    head_got += [along_hid(head_send[shift % halves], shift) for shift in range(1, hids)]
    w_own = pick(w_in, step)
    proj_parts = matmul(jnp.concatenate(group), w_own, ((1,), (0,)))
    proj_parts = proj_parts.reshape(steps, hids, part, depth)

    def owner_block(index):
        return lax.dynamic_index_in_dim(proj_parts, index, 1, False).reshape(owned, depth)

    send = [owner_block((j + shift) % hids).astype(BF16) for shift in range(1, hids)]
    ready = [after(p, *head_got[1:]) for p in send]
    received = [along_hid(ready[shift - 1], shift) for shift in range(1, hids)]

    head_got = [head_got[0]] + [after(g, *send) for g in head_got[1:]]
    squares = sum(g[steps * head_rows :].astype(F32) for g in head_got).reshape(tail)
    squares = jnp.sum(squares[: EXACT * rows].reshape(EXACT, rows), axis=0)
    head_mid = jnp.stack([g[: steps * head_rows] for g in head_got[::-1]] * 2)
    head_mid = lax.dynamic_slice_in_dim(head_mid, hids - 1 - j, hids, 0)
    head_mid = head_mid.reshape(hids, steps, head_rows, block)

    ids = after(codebook_ids, *send)
    ids = jnp.concatenate([ids] + [flip_seq(ids, -m) for m in relations], axis=1)
    ids_rows = [ids] + [turn_hid(ids, -k) for k in range(1, halves)]
    before = jnp.maximum(step - 1, 0)
    looked = jnp.take(pick(embedding, before), pick(ids, before), axis=0)

    head_send = head_mid.transpose(1, 0, 2, 3)
    head_send = head_send.reshape(steps, hids * head_rows, block)
    head_send = jnp.broadcast_to(head_send, (groups,) + head_send.shape)
    head_send = head_send.reshape(seqs, hids * head_rows, block)
    head = lax.all_to_all(head_send, "seq", 0, 0).reshape(depth, block)

    squares = jnp.stack([squares] + [flip_seq(squares, -m) for m in relations])
    ratio_group = lax.rsqrt(squares / width_in + 1e-06).reshape(steps, hids, part)

    ratio = lax.dynamic_index_in_dim(ratio_group, j, 1, False).reshape(owned, 1)
    proj = owner_block(j)
    for r in received:
        proj += r.astype(F32)
    x_rows = ratio * proj + jnp.where(step > 0, looked.astype(F32), 0.0)
    scale = lax.rsqrt(jnp.mean(x_rows * x_rows, axis=1, keepdims=True) + 1e-06)
    x_proj = jnp.sum(x_rows * proj, axis=1, keepdims=True)
    gain = pick(depth_gain, step)[None, :]
    normed = (x_rows * scale * gain).astype(BF16)

    normed_rows = jnp.concatenate([normed] + [turn_hid(normed, -k) for k in range(1, halves)])
    targets = jnp.concatenate([pick(r, step) for r in ids_rows])
    logits = matmul(normed_rows, head, ((1,), (0,)))
    top = jnp.max(logits, axis=1)
    total = jnp.sum(jnp.exp(logits - top[:, None]), axis=1)
    stats = jnp.stack([top, total]).reshape(2, halves, -1)
    every = [stats] + [jnp.roll(turn_hid(stats, -t), t, axis=1) for t in range(1, halves)]
    tops = jnp.stack([e[0] for e in every]).reshape(halves, -1)
    totals = jnp.stack([e[1] for e in every]).reshape(halves, -1)
    top_all = jnp.max(tops, axis=0)
    lse = top_all + jnp.log(jnp.sum(totals * jnp.exp(tops - top_all), axis=0))
    entry = lax.broadcasted_iota(jnp.int32, logits.shape, 1) + half * block
    onehot = (targets[:, None] == entry).astype(F32)
    loss_weight = 2.0 * entries / frames
    d_logit = ((jnp.exp(logits - lse[:, None]) - onehot) * loss_weight).astype(BF16)

    away = [
        matmul(d_logit[k * owned : (k + 1) * owned], head, ((1,), (1,))).astype(BF16)
        for k in range(1, halves)
    ]
    received = [turn_hid(a, k + 1) for k, a in enumerate(away)]
    d_norm = matmul(after(d_logit[:owned], *away), head, ((1,), (1,)))
    for r in received:
        d_norm += r.astype(F32)
    gated = gain * d_norm
    back_scale = scale**3 * jnp.mean(gated * x_rows, axis=1, keepdims=True)
    gated_proj = jnp.sum(gated * proj, axis=1, keepdims=True)
    d_round = (scale * gated - x_rows * back_scale).astype(BF16)
    d_ratio_part = (scale * gated_proj - back_scale * x_proj).reshape(steps, part)

    part_out = matmul(normed_rows, after(d_logit, *away), ((0,), (0,))).astype(BF16)
    part_out = part_out.reshape(seqs, depth // seqs, block)
    part_out = lax.all_to_all(part_out, "seq", 0, 0)
    part_out = part_out.reshape(groups, steps, hids, head_rows, block).astype(F32).sum(0)
    part_out = part_out.astype(BF16)
    sums = [
        lax.dynamic_index_in_dim(part_out, (j + shift) % hids, 1, False) for shift in range(hids)
    ]
    sums = [along_hid(p, shift) if shift else p for shift, p in enumerate(sums)]
    grad_out = head_gradient(place, sums, halves)

    pieces = [d_round] + [along_hid(d_round, shift) for shift in range(1, hids)]
    ratio_rows = ratio_group.reshape(steps, rows, 1)
    d_ratio_part = after(d_ratio_part, d_round)
    d_ratio = d_ratio_part[0]
    for m in relations:
        d_ratio += flip_seq(d_ratio_part[m], m)
    d_rows = jnp.broadcast_to(d_ratio, (hids, part))
    for shift in range(1, hids):
        d_rows = lax.dynamic_update_index_in_dim(
            d_rows, along_hid(d_ratio, shift), (j - shift) % hids, 0
        )
    share, mine, *others = input_gradient(after(place, d_ratio), pieces, group, ratio_rows, seqs)
    share = lax.all_to_all(share.reshape(seqs, depth // seqs, units), "seq", 0, 0)
    share = share.reshape(groups, steps, depth // seqs, units).astype(F32).sum(0)
    grad_in = share.transpose(0, 2, 1)

    ratio_own = ratio_group[0].reshape(rows)
    correction = ratio_own**3 * d_rows.reshape(rows) / width_in
    factors = jnp.stack([ratio_own, correction])[:, :, None]
    mine = [mine] + [flip_seq(others[m - 1], m) for m in relations]
    grad_hidden = hidden_gradient(place, mine, w_in, hidden, factors)
    return (grad_hidden, grad_in, grad_out)


def solution(mesh):
    placed = (
        P("seq", "hid"),
        P(None, "hid", None),
        P(),
        P(),
        P(("seq", "hid"), None, None),
        P(None, ("seq", "hid")),
    )
    return jax.shard_map(
        shards,
        mesh=mesh,
        in_specs=placed,
        out_specs=(P("seq", "hid"), P(None, "hid", "seq"), P(("seq", "hid"), None, None)),
        check_vma=False,
    )
```

```python
import jax
import jax.numpy as jnp
from jax import lax
from jax.experimental import pallas as pl
from jax.experimental.pallas import tpu as pltpu
from jax.sharding import PartitionSpec as P

F32 = jnp.float32
BF16 = jnp.bfloat16


def pick(values, index):
    return lax.dynamic_index_in_dim(values, index, axis=0, keepdims=False)


def matmul(a, b, contract):
    return lax.dot_general(a, b, (contract, ((), ())), preferred_element_type=F32)


def after(value, *others):
    return lax.optimization_barrier((value, *others))[0]


VMEM = pltpu.CompilerParams(vmem_limit_bytes=60 * 2**20)


def whole(shape):
    return pl.BlockSpec(shape, lambda n, place: (0,) * len(shape))


def call(kernel, place, grid, in_specs, out_specs, out_shape, scratch, flops, args):
    moved = sum(a.size * a.dtype.itemsize for a in args)
    return pl.pallas_call(
        kernel,
        grid_spec=pltpu.PrefetchScalarGridSpec(
            num_scalar_prefetch=1,
            grid=(grid,),
            in_specs=in_specs,
            out_specs=out_specs,
            scratch_shapes=scratch,
        ),
        out_shape=out_shape,
        compiler_params=VMEM,
        cost_estimate=pl.CostEstimate(flops=flops, bytes_accessed=moved, transcendentals=0),
    )(place, *args)


EXACT = 3


def parts_of(values):
    out = []
    for _ in range(EXACT):
        piece = lax.reduce_precision(values, 8, 7)
        values = values - piece
        out.append(piece.astype(BF16))
    return out


def head_gradient(place, pieces, halves):
    hids = len(pieces)
    steps, rows, block = pieces[0].shape

    def kernel(place_ref, *refs):
        pieces, out = refs[:-1], refs[-1]
        for r in range(halves):
            which = lax.rem(place_ref[1] - r + hids, halves)
            columns = pl.ds(pl.multiple_of(which * block, block), block)
            for s in range(steps):
                total = pieces[r][s].astype(F32)
                for k in range(r + halves, hids, halves):
                    total = total + pieces[k][s].astype(F32)
                out[:, s, columns] = total

    return call(
        kernel,
        place,
        1,
        [whole((steps, rows, block))] * hids,
        whole((rows, steps, halves * block)),
        jax.ShapeDtypeStruct((rows, steps, halves * block), F32),
        [],
        hids * steps * rows * block,
        tuple(pieces),
    )


def input_gradient(place, pieces, group, ratio, seqs):
    hids, steps = len(pieces), len(group)
    owned, depth = pieces[0].shape
    rows, units = group[0].shape
    part = owned // steps
    wide = depth

    def kernel(place_ref, *refs):
        chunks, group, ratio = refs[:hids], refs[hids : hids + steps], refs[hids + steps]
        out, plain, scaled = refs[hids + steps + 1], refs[hids + steps + 2 : -1], refs[-1]
        j = place_ref[1]
        for r in range(hids):
            to = pl.multiple_of(lax.rem(j - r + hids, hids) * part, part)
            for m in range(steps):
                values = chunks[r][m * part : (m + 1) * part, :]
                plain[m][pl.ds(to, part), :] = values
                factor = ratio[m, pl.ds(to, part), :]
                scaled[m, pl.ds(to, part), :] = (values.astype(F32) * factor).astype(BF16)
        total = None
        for m in range(steps):
            term = lax.dot_general(
                scaled[m], group[m][...], (((0,), (0,)), ((), ())), preferred_element_type=F32
            )
            total = term if total is None else total + term
        out[...] = total.astype(BF16)

    return call(
        kernel,
        place,
        depth // wide,
        [pl.BlockSpec((owned, wide), lambda n, place: (0, n))] * hids
        + [whole((rows, units))] * steps
        + [whole((steps, rows, 1))],
        [pl.BlockSpec((wide, units), lambda n, place: (n, 0))]
        + [pl.BlockSpec((rows, wide), lambda n, place: (0, n))] * steps,
        [jax.ShapeDtypeStruct((depth, units), BF16)]
        + [jax.ShapeDtypeStruct((rows, depth), BF16)] * steps,
        [pltpu.VMEM((steps, rows, wide), BF16)],
        2 * steps * rows * units * depth,
        (*pieces, *group, ratio),
    )


def hidden_gradient(place, d_rows, w_in, hidden, factors):
    steps, units, depth = w_in.shape
    rows = hidden.shape[0]
    wide = min(512, units)

    def kernel(place_ref, *refs):
        d_rows, w, hidden, factors, out = refs[:steps], refs[-4], refs[-3], refs[-2], refs[-1]
        total = None
        for r in range(steps):
            which = lax.rem(place_ref[0] - r + steps, steps)
            term = lax.dot_general(
                d_rows[r][...], w[which], (((1,), (1,)), ((), ())), preferred_element_type=F32
            )
            total = term if total is None else total + term
        out[...] = (factors[0] * total - factors[1] * hidden[...].astype(F32)).astype(BF16)

    return call(
        kernel,
        place,
        units // wide,
        [whole((rows, depth))] * steps
        + [
            pl.BlockSpec((steps, wide, depth), lambda n, place: (0, n, 0)),
            pl.BlockSpec((rows, wide), lambda n, place: (0, n)),
            whole((2, rows, 1)),
        ],
        pl.BlockSpec((rows, wide), lambda n, place: (0, n)),
        jax.ShapeDtypeStruct((rows, units), BF16),
        [],
        2 * steps * rows * units * depth,
        (*d_rows, w_in, hidden, factors),
    )


def shards(hidden, w_in, embedding, depth_gain, w_out, codebook_ids):
    hids = lax.axis_size("hid")
    seqs = lax.axis_size("seq")
    steps, units, depth = w_in.shape
    entries = w_out.shape[2]
    rows = hidden.shape[0]
    part = rows // hids
    width_in = units * hids
    frames = rows * seqs
    halves = 2 if hids % 2 == 0 else 1
    block = entries // halves
    head_rows = w_out.shape[0]
    groups = seqs // steps
    i = lax.axis_index("seq")
    j = lax.axis_index("hid")
    step = i % steps
    half = j % halves
    owned = steps * part

    def along_hid(values, shift):
        return lax.ppermute(values, "hid", [(a, (a + shift) % hids) for a in range(hids)])

    def turn_hid(values, shift):
        return lax.ppermute(
            values,
            "hid",
            [(a, a - a % halves + (a % halves + shift) % halves) for a in range(hids)],
        )

    def flip_seq(values, flip):
        return lax.ppermute(
            values,
            "seq",
            [(a, a - a % steps + (a % steps + flip) % steps) for a in range(seqs)],
        )

    place = jnp.stack([step, j]).astype(jnp.int32)
    relations = range(1, steps)

    group = [hidden] + [flip_seq(hidden, -m) for m in relations]

    squares_part = jnp.sum(jnp.square(hidden.astype(F32)), axis=1)
    tail = 8 * block
    small = jnp.concatenate(parts_of(squares_part))
    small = jnp.pad(small, (0, tail - small.size)).reshape(8, block)
    head_send = []
    for k in range(halves):
        piece = lax.dynamic_slice_in_dim(w_out, (half + k) % halves * block, block, 2)
        piece = piece.transpose(1, 0, 2).reshape(steps * head_rows, block)
        head_send.append(jnp.concatenate([piece, small]))
    head_got = [head_send[0]]
    head_got += [along_hid(head_send[shift % halves], shift) for shift in range(1, hids)]
    w_own = pick(w_in, step)
    proj_parts = matmul(jnp.concatenate(group), w_own, ((1,), (0,)))
    proj_parts = proj_parts.reshape(steps, hids, part, depth)

    def owner_block(index):
        return lax.dynamic_index_in_dim(proj_parts, index, 1, False).reshape(owned, depth)

    send = [owner_block((j + shift) % hids).astype(BF16) for shift in range(1, hids)]
    ready = [after(p, *head_got[1:]) for p in send]
    received = [along_hid(ready[shift - 1], shift) for shift in range(1, hids)]

    head_got = [head_got[0]] + [after(g, *send) for g in head_got[1:]]
    squares = sum(g[steps * head_rows :].astype(F32) for g in head_got).reshape(tail)
    squares = jnp.sum(squares[: EXACT * rows].reshape(EXACT, rows), axis=0)
    head_mid = jnp.stack([g[: steps * head_rows] for g in head_got[::-1]] * 2)
    head_mid = lax.dynamic_slice_in_dim(head_mid, hids - 1 - j, hids, 0)
    head_mid = head_mid.reshape(hids, steps, head_rows, block)

    ids = after(codebook_ids, *send)
    ids = jnp.concatenate([ids] + [flip_seq(ids, -m) for m in relations], axis=1)
    ids_rows = [ids] + [turn_hid(ids, -k) for k in range(1, halves)]
    before = jnp.maximum(step - 1, 0)
    looked = jnp.take(pick(embedding, before), pick(ids, before), axis=0)

    head_send = head_mid.transpose(1, 0, 2, 3)
    head_send = head_send.reshape(steps, hids * head_rows, block)
    head_send = jnp.broadcast_to(head_send, (groups,) + head_send.shape)
    head_send = head_send.reshape(seqs, hids * head_rows, block)
    head = lax.all_to_all(head_send, "seq", 0, 0).reshape(depth, block)

    squares = jnp.stack([squares] + [flip_seq(squares, -m) for m in relations])
    ratio_group = lax.rsqrt(squares / width_in + 1e-06).reshape(steps, hids, part)

    ratio = lax.dynamic_index_in_dim(ratio_group, j, 1, False).reshape(owned, 1)
    proj = owner_block(j)
    for r in received:
        proj += r.astype(F32)
    x_rows = ratio * proj + jnp.where(step > 0, looked.astype(F32), 0.0)
    scale = lax.rsqrt(jnp.mean(x_rows * x_rows, axis=1, keepdims=True) + 1e-06)
    x_proj = jnp.sum(x_rows * proj, axis=1, keepdims=True)
    gain = pick(depth_gain, step)[None, :]
    normed = (x_rows * scale * gain).astype(BF16)

    normed_rows = jnp.concatenate([normed] + [turn_hid(normed, -k) for k in range(1, halves)])
    targets = jnp.concatenate([pick(r, step) for r in ids_rows])
    logits = matmul(normed_rows, head, ((1,), (0,)))
    top = jnp.max(logits, axis=1)
    total = jnp.sum(jnp.exp(logits - top[:, None]), axis=1)
    stats = jnp.stack([top, total]).reshape(2, halves, -1)
    every = [stats] + [jnp.roll(turn_hid(stats, -t), t, axis=1) for t in range(1, halves)]
    tops = jnp.stack([e[0] for e in every]).reshape(halves, -1)
    totals = jnp.stack([e[1] for e in every]).reshape(halves, -1)
    top_all = jnp.max(tops, axis=0)
    lse = top_all + jnp.log(jnp.sum(totals * jnp.exp(tops - top_all), axis=0))
    entry = lax.broadcasted_iota(jnp.int32, logits.shape, 1) + half * block
    onehot = (targets[:, None] == entry).astype(F32)
    loss_weight = 2.0 * entries / frames
    d_logit = ((jnp.exp(logits - lse[:, None]) - onehot) * loss_weight).astype(BF16)

    away = [
        matmul(d_logit[k * owned : (k + 1) * owned], head, ((1,), (1,))).astype(BF16)
        for k in range(1, halves)
    ]
    received = [turn_hid(a, k + 1) for k, a in enumerate(away)]
    d_norm = matmul(after(d_logit[:owned], *away), head, ((1,), (1,)))
    for r in received:
        d_norm += r.astype(F32)
    gated = gain * d_norm
    back_scale = scale**3 * jnp.mean(gated * x_rows, axis=1, keepdims=True)
    gated_proj = jnp.sum(gated * proj, axis=1, keepdims=True)
    d_round = (scale * gated - x_rows * back_scale).astype(BF16)
    d_ratio_part = (scale * gated_proj - back_scale * x_proj).reshape(steps, part)

    part_out = matmul(normed_rows, after(d_logit, *away), ((0,), (0,))).astype(BF16)
    part_out = part_out.reshape(seqs, depth // seqs, block)
    part_out = lax.all_to_all(part_out, "seq", 0, 0)
    part_out = part_out.reshape(groups, steps, hids, head_rows, block).astype(F32).sum(0)
    part_out = part_out.astype(BF16)
    sums = [
        lax.dynamic_index_in_dim(part_out, (j + shift) % hids, 1, False) for shift in range(hids)
    ]
    sums = [along_hid(p, shift) if shift else p for shift, p in enumerate(sums)]
    grad_out = head_gradient(place, sums, halves)

    pieces = [d_round] + [along_hid(d_round, shift) for shift in range(1, hids)]
    ratio_rows = ratio_group.reshape(steps, rows, 1)
    d_ratio_part = after(d_ratio_part, d_round)
    d_ratio = d_ratio_part[0]
    for m in relations:
        d_ratio += flip_seq(d_ratio_part[m], m)
    d_rows = jnp.broadcast_to(d_ratio, (hids, part))
    for shift in range(1, hids):
        d_rows = lax.dynamic_update_index_in_dim(
            d_rows, along_hid(d_ratio, shift), (j - shift) % hids, 0
        )
    share, mine, *others = input_gradient(after(place, d_ratio), pieces, group, ratio_rows, seqs)
    share = lax.all_to_all(share.reshape(seqs, depth // seqs, units), "seq", 0, 0)
    share = share.reshape(groups, steps, depth // seqs, units).astype(F32).sum(0)
    grad_in = share.transpose(0, 2, 1)

    ratio_own = ratio_group[0].reshape(rows)
    correction = ratio_own**3 * d_rows.reshape(rows) / width_in
    factors = jnp.stack([ratio_own, correction])[:, :, None]
    mine = [mine] + [flip_seq(others[m - 1], m) for m in relations]
    grad_hidden = hidden_gradient(place, mine, w_in, hidden, factors)
    return (grad_hidden, grad_in, grad_out)


def solution(mesh):
    placed = (
        P("seq", "hid"),
        P(None, "hid", None),
        P(),
        P(),
        P(("seq", "hid"), None, None),
        P(None, ("seq", "hid")),
    )
    return jax.shard_map(
        shards,
        mesh=mesh,
        in_specs=placed,
        out_specs=(P("seq", "hid"), P(None, "hid", "seq"), P(("seq", "hid"), None, None)),
        check_vma=False,
    )
```
